32 devices in a mesh: dp: 4 (over y, x), row: 2 (over core), col: 4 (over z).
Axes of the slice: x: 2, y: 2, z: 4, core: 2. Of those that a mesh axis runs over, the one named last changes fastest.
Arguments:
- tokens_in: bfloat16 [16384, 2048], P(('dp', 'col'), 'row'), may hold values from -6 to 6
- out_grad: bfloat16 [16384, 2048], P(('dp', 'col'), 'row'), may hold values from -6 to 6
- segment_ids: int32 [16, 1024], P('dp'), may hold values from 0 to 3, never falling along the last dimension, each value on 1 to 800 neighbouring positions
- active_lengths: int32 [16, 4], P('dp'), may hold values from 1 to 800
- norm1_gain: float32 [2048], P('row'), may hold values from 0.5 to 1.5
- norm1_shift: float32 [2048], P('row'), may hold values from -1.5 to 1.5
- query_weight: bfloat16 [2048, 2048], P('row', 'col'), may hold values from -0.125 to 0.125
- query_bias: float32 [2048], P('col'), may hold values from -1.5 to 1.5
- key_weight: bfloat16 [2048, 2048], P('row', 'col'), may hold values from -0.125 to 0.125
- value_weight: bfloat16 [2048, 2048], P('row', 'col'), may hold values from -0.125 to 0.125
- value_bias: float32 [2048], P('col'), may hold values from -1.5 to 1.5
- out_weight: bfloat16 [2048, 2048], P('col', 'row'), may hold values from -0.5 to 0.5
- out_bias: float32 [2048], P('row'), may hold values from -1.5 to 1.5
- norm2_gain: float32 [2048], P('row'), may hold values from 0.5 to 1.5
- norm2_shift: float32 [2048], P('row'), may hold values from -1.5 to 1.5
- up_weight: bfloat16 [2048, 8192], P('row', 'col'), may hold values from -0.125 to 0.125
- up_bias: float32 [8192], P('col'), may hold values from -1.5 to 1.5
- down_weight: bfloat16 [8192, 2048], P('col', 'row'), may hold values from -0.09375 to 0.09375
- down_bias: float32 [2048], P('row'), may hold values from -1.5 to 1.5
Outputs:
- layer_out: float32 [16384, 2048], P(('dp', 'col'), 'row')
- input_grad: float32 [16384, 2048], P(('dp', 'col'), 'row')
- norm1_gain_grad: float32 [2048], P('row')
- norm1_shift_grad: float32 [2048], P('row')
- query_weight_grad: float32 [2048, 2048], P('row', 'col')
- query_bias_grad: float32 [2048], P('col')
- key_weight_grad: float32 [2048, 2048], P('row', 'col')
- value_weight_grad: float32 [2048, 2048], P('row', 'col')
- value_bias_grad: float32 [2048], P('col')
- out_weight_grad: float32 [2048, 2048], P('col', 'row')
- out_bias_grad: float32 [2048], P('row')
- norm2_gain_grad: float32 [2048], P('row')
- norm2_shift_grad: float32 [2048], P('row')
- up_weight_grad: float32 [2048, 8192], P('row', 'col')
- up_bias_grad: float32 [8192], P('col')
- down_weight_grad: float32 [8192, 2048], P('col', 'row')
- down_bias_grad: float32 [2048], P('row')
The draws below stay inside these ranges and needn't reach their ends.
Inputs may be any that keep to these rules, and one draw needn't show every extreme that they name: `segment_ids`: each sequence holds documents numbered 0 to 3 in order, each of 1 to 800 tokens, one of exactly 800. active_lengths[s, j] is the number of leading tokens of document j of sequence s that are active; the whole document is active where it is shorter.
All inputs are finite; a program needn't handle non-finite values.
Results may differ from the reference program's by a relative error of at most 0.013.
Values may be sent and summed in bfloat16 or wider, within the bound.
No kernel may reach another device: no remote copies, remote signals or barrier semaphores. Data moves between devices by JAX's collectives and lax.ppermute only.
A program may use at most 384 MiB of HBM per device.

```python
import math
import jax
import jax.numpy as jnp
import numpy as np
from jax import lax

D = 2048
HEADS = 32
FF = 8192
HEAD_DIM = 64
SEQ_LEN = 1024
SEQ_DP = 4
DOCS = 4
DOC_MAX = 800
SEQS = 16
TOKENS = 16384


def touch_ends(drawn, key, least, top_value):
    place = [jax.random.randint(jax.random.fold_in(key, axis), (), 0, length) for axis, length in enumerate(drawn.shape)]
    main_axis = drawn.shape.index(max(drawn.shape))
    beside = place[:main_axis] + [(place[main_axis] + 1) % drawn.shape[main_axis]] + place[main_axis + 1:]
    return drawn.at[tuple(place)].set(least).at[tuple(beside)].set(top_value)


def block_scale(own_key, dims, cuts, low, top_value):
    level = 1.0
    for dim, shards_of in cuts:
        heights = jax.random.uniform(jax.random.fold_in(jax.random.fold_in(own_key, 6), dim), (shards_of,), jnp.float32, low / len(cuts), top_value / len(cuts))
        level = level * jnp.repeat(jnp.exp(heights), dims[dim] // shards_of).reshape((-1,) + (1,) * (len(dims) - 1 - dim))
    return level


def length_profile(amount, total, bound, lean):
    portions = [(1 << 20) // math.isqrt(rank ** lean) + 1 for rank in range(2, amount + 1)]
    spare, holding = total - bound - (amount - 1), [1] * (amount - 1)
    while spare > 0:
        candidates = [i for i in range(amount - 1) if holding[i] < bound]
        pool, budget = sum([portions[i] for i in candidates]), spare
        for i in candidates:
            extra = min(bound - holding[i], max(1, budget * portions[i] // pool), spare)
            holding[i] = holding[i] + extra
            spare = spare - extra
    return np.array([bound] + holding)


def ragged_sizes(stream_key, amount, total, limit, skew):
    if amount == 2:
        one = jax.random.randint(stream_key, (), max(1, total - limit), min(limit, total - 1) + 1)
        return jnp.stack([one, total - one])
    sizes = jnp.asarray(length_profile(amount, total, limit, skew), jnp.int32)
    pairs = (amount - 1) // 2
    source_of, taker = sizes[1:1 + 2 * pairs:2], sizes[2:2 + 2 * pairs:2]
    margin = jnp.minimum(source_of - 1, limit - taker)
    shifted = jax.random.randint(jax.random.fold_in(stream_key, 1), (pairs,), 0, 1 << 20) % (margin + 1)
    sizes = sizes.at[1:1 + 2 * pairs:2].set(source_of - shifted).at[2:2 + 2 * pairs:2].set(taker + shifted)
    return sizes[jax.random.permutation(jax.random.fold_in(stream_key, 2), amount)]


def normal_values(key, extent, deviation, limit, pieces=(), kind=jnp.bfloat16):
    gain = block_scale(key, extent, pieces, -0.22, 0.18) if pieces else 1.0
    values = jax.random.normal(key, extent, jnp.float32) * deviation * gain
    return jnp.minimum(jnp.maximum(values, -limit), limit).astype(kind)


def setup_inputs(seed: int = 0) -> dict:
    arg_keys = jax.random.split(jax.random.key(seed), 20)
    tokens_in = normal_values(arg_keys[0], (TOKENS, D), 1.0, 6.0, ((0, 16), (1, 2)))
    out_grad = normal_values(arg_keys[1], (TOKENS, D), 1.0, 6.0, ((0, 16), (1, 2)))
    segment_ids = jax.vmap(lambda own: jnp.searchsorted(jnp.cumsum(ragged_sizes(own, DOCS, SEQ_LEN, DOC_MAX, 0)), jnp.arange(SEQ_LEN), side="right"))(jax.random.split(arg_keys[2], SEQS)).reshape((SEQS, SEQ_LEN)).astype(jnp.int32)
    active_lengths = touch_ends(jax.random.randint(arg_keys[3], (SEQS, DOCS), 1, DOC_MAX + 1), jax.random.fold_in(arg_keys[3], 1), 1, DOC_MAX).astype(jnp.int32)
    norm1_gain = jnp.clip(1.0 + 0.1 * jax.random.normal(arg_keys[4], (D,), jnp.float32), 0.5, 1.5)
    norm1_shift = normal_values(arg_keys[5], (D,), 0.3, 1.5, ((0, 2),), jnp.float32)
    query_weight = normal_values(arg_keys[6], (D, D), D ** -0.5, 0.125, ((0, 2), (1, 4)))
    query_bias = normal_values(arg_keys[7], (D,), 0.3, 1.5, ((0, 4),), jnp.float32)
    key_weight = normal_values(arg_keys[8], (D, D), D ** -0.5, 0.125, ((0, 2), (1, 4)))
    value_weight = normal_values(arg_keys[9], (D, D), D ** -0.5, 0.125, ((0, 2), (1, 4)))
    value_bias = normal_values(arg_keys[10], (D,), 0.3, 1.5, ((0, 4),), jnp.float32)
    out_weight = normal_values(arg_keys[11], (D, D), (D // 16) ** -0.5, 0.5, ((0, 4), (1, 2)))
    out_bias = normal_values(arg_keys[12], (D,), 0.3, 1.5, ((0, 2),), jnp.float32)
    norm2_gain = jnp.clip(1.0 + 0.1 * jax.random.normal(arg_keys[13], (D,), jnp.float32), 0.5, 1.5)
    norm2_shift = normal_values(arg_keys[14], (D,), 0.3, 1.5, ((0, 2),), jnp.float32)
    up_weight = normal_values(arg_keys[15], (D, FF), D ** -0.5, 0.125, ((0, 2), (1, 4)))
    up_bias = normal_values(arg_keys[16], (FF,), 0.3, 1.5, ((0, 4),), jnp.float32)
    down_weight = normal_values(arg_keys[17], (FF, D), (FF // 2) ** -0.5, 0.09375, ((0, 4), (1, 2)))
    down_bias = normal_values(arg_keys[18], (D,), 0.3, 1.5, ((0, 2),), jnp.float32)
    return dict(tokens_in=tokens_in, out_grad=out_grad, segment_ids=segment_ids, active_lengths=active_lengths, norm1_gain=norm1_gain, norm1_shift=norm1_shift, query_weight=query_weight, query_bias=query_bias, key_weight=key_weight, value_weight=value_weight, value_bias=value_bias, out_weight=out_weight, out_bias=out_bias, norm2_gain=norm2_gain, norm2_shift=norm2_shift, up_weight=up_weight, up_bias=up_bias, down_weight=down_weight, down_bias=down_bias)


@jax.custom_vjp
def low(v):
    return lax.optimization_barrier(v.astype(jnp.bfloat16)).astype(jnp.float32)

@jax.custom_vjp
def low_back(v):
    return v

def low_keep(v):
    return (low(v), None)

def low_pass(kept, grad):
    return (grad,)

def back_keep(v):
    return (v, None)

def back_low(kept, grad):
    return (low(grad),)
low.defvjp(low_keep, low_pass)
low_back.defvjp(back_keep, back_low)
norm_eps = 1e-05
masked_fill = -1e+30

def matmul_high(left_side, right_side):
    return jnp.dot(left_side, right_side, precision=lax.Precision.HIGHEST)

def layer_norm(values, gain_vec, shift_vec):
    average = lax.optimization_barrier(jnp.mean(values, axis=-1, keepdims=True))
    centered = values - average
    variance = lax.optimization_barrier(jnp.mean(centered * centered, axis=-1, keepdims=True))
    return centered * lax.rsqrt(variance + norm_eps) * gain_vec + shift_vec

def active_rows(segment_rows, keep_lengths):
    doc_index = jnp.arange(keep_lengths.shape[-1], dtype=jnp.int32)
    member = (segment_rows[:, :, None] == doc_index).astype(jnp.int32)
    counts = lax.optimization_barrier(jnp.sum(member, axis=1)).astype(jnp.int32)
    starts = (jnp.cumsum(counts, axis=1).astype(jnp.int32) - counts).astype(jnp.int32)
    first_pos = lax.optimization_barrier(jnp.sum(member * starts[:, None, :], axis=2)).astype(jnp.int32)
    keep_here = lax.optimization_barrier(jnp.sum(member * keep_lengths[:, None, :], axis=2)).astype(jnp.int32)
    position_in = jnp.arange(segment_rows.shape[1], dtype=jnp.int32)[None, :] - first_pos
    return (position_in < keep_here).reshape(-1)

def attend_sequence(seq_items):
    query_rows, key_rows, value_rows, segment_row = seq_items
    scores = jnp.einsum('qhd,khd->hqk', query_rows, key_rows, precision=lax.Precision.HIGHEST) * HEAD_DIM ** (-0.5)
    scores = low_back(scores)
    positions = jnp.arange(segment_row.shape[0], dtype=jnp.int32)
    allowed = (positions[None, :] <= positions[:, None]) & (segment_row[None, :] == segment_row[:, None])
    scores = jnp.where(allowed[None], scores, masked_fill)
    weights = low(jax.nn.softmax(scores, axis=-1))
    return jnp.einsum('hqk,khd->qhd', weights, value_rows, precision=lax.Precision.HIGHEST)

def forward(group_input, params, segment_rows, active):
    gain_one, shift_one, query_weight, query_bias, key_weight, value_weight, value_bias, out_weight, out_bias, gain_two, shift_two, up_weight, up_bias, down_weight, down_bias = params
    normed = low(layer_norm(group_input, gain_one, shift_one))
    queries = low(low_back(matmul_high(normed, query_weight) + query_bias))
    key_vals = low(low_back(matmul_high(normed, key_weight)))
    value_vals = low(low_back(matmul_high(normed, value_weight) + value_bias))
    shaped = (segment_rows.shape[0], segment_rows.shape[1], HEADS, HEAD_DIM)
    attended = lax.map(jax.checkpoint(attend_sequence), (queries.reshape(shaped), key_vals.reshape(shaped), value_vals.reshape(shaped), segment_rows))
    attended = low(low_back(attended.reshape(group_input.shape[0], D)))
    attention_out = matmul_high(attended, out_weight) + out_bias
    hidden_one = group_input + low_back(attention_out)
    normed_two = low(layer_norm(hidden_one, gain_two, shift_two))
    pre_act = low_back(matmul_high(normed_two, up_weight) + up_bias)
    activated = low(jax.nn.gelu(pre_act, approximate=True))
    ffn_out = matmul_high(activated, down_weight) + down_bias
    return jnp.where(active[:, None], hidden_one + low_back(ffn_out), group_input)

def reference(tokens_in, out_grad, segment_ids, active_lengths, norm1_gain, norm1_shift, query_weight, query_bias, key_weight, value_weight, value_bias, out_weight, out_bias, norm2_gain, norm2_shift, up_weight, up_bias, down_weight, down_bias):
    params = (norm1_gain.astype(jnp.float32), norm1_shift.astype(jnp.float32), query_weight.astype(jnp.float32), query_bias.astype(jnp.float32), key_weight.astype(jnp.float32), value_weight.astype(jnp.float32), value_bias.astype(jnp.float32), out_weight.astype(jnp.float32), out_bias.astype(jnp.float32), norm2_gain.astype(jnp.float32), norm2_shift.astype(jnp.float32), up_weight.astype(jnp.float32), up_bias.astype(jnp.float32), down_weight.astype(jnp.float32), down_bias.astype(jnp.float32))
    group_count = SEQS // SEQ_DP
    group_rows = SEQ_DP * SEQ_LEN
    scan_inputs = (tokens_in.astype(jnp.float32).reshape(group_count, group_rows, D), out_grad.astype(jnp.float32).reshape(group_count, group_rows, D), segment_ids.reshape(group_count, SEQ_DP, SEQ_LEN), active_lengths.reshape(group_count, SEQ_DP, DOCS))

    def group_step(totals, group_items):
        group_input, cotangent, segment_rows, keep_lengths = group_items
        active = active_rows(segment_rows, keep_lengths)
        result, pullback = jax.vjp(lambda rows_given, weight_set: forward(rows_given, weight_set, segment_rows, active), group_input, params)
        rows_grad, params_grad = pullback(cotangent)
        summed = jax.tree.map(lambda first_term, second_term: first_term + second_term, totals, params_grad)
        return (summed, (result, rows_grad))
    zero_grads = jax.tree.map(jnp.zeros_like, params)
    totals, (outputs, input_grads) = lax.scan(group_step, zero_grads, scan_inputs)
    return (outputs.reshape(TOKENS, D), input_grads.reshape(TOKENS, D), totals[0], totals[1], totals[2], totals[3], totals[4], totals[5], totals[6], totals[7], totals[8], totals[9], totals[10], totals[11], totals[12], totals[13], totals[14])
```

```python
import jax
import jax.numpy as jnp
from jax import lax
from jax.sharding import PartitionSpec as P

D = 2048
HEAD_DIM = 64


norm_eps = 1e-05
masked_fill = -1e30


def width_totals(total_one, total_two):
    return lax.psum((total_one, total_two), "row")


def token_gather(values):
    return lax.all_gather(values, "col", axis=0, tiled=True)


def token_sums(partial_rows):
    return lax.psum_scatter(partial_rows, "col", scatter_dimension=0, tiled=True)


def unit_gather(values):
    return lax.all_gather(values, "row", axis=1, tiled=True)


def unit_sums(partial_units):
    return lax.psum_scatter(partial_units, "row", scatter_dimension=1, tiled=True)


def gelu_value(values):
    return jax.nn.gelu(values, approximate=True)


def gelu_slope(values):
    result, pullback = jax.vjp(gelu_value, values)
    return pullback(jnp.ones_like(values))[0]


def active_rows(segment_rows, keep_lengths):
    doc_index = jnp.arange(keep_lengths.shape[-1], dtype=jnp.int32)
    member = (segment_rows[:, :, None] == doc_index).astype(jnp.int32)
    counts = jnp.sum(member, axis=1)
    starts = jnp.cumsum(counts, axis=1) - counts
    first_pos = jnp.sum(member * starts[:, None, :], axis=2)
    keep_here = jnp.sum(member * keep_lengths[:, None, :], axis=2)
    position_in = jnp.arange(segment_rows.shape[1], dtype=jnp.int32)[None, :] - first_pos
    return (position_in < keep_here).reshape(-1)


def norm_forward(values, gain_part, shift_part):
    total_one, total_two = width_totals(jnp.sum(values, axis=1), jnp.sum(values * values, axis=1))
    average = total_one / D
    variance = total_two / D - average * average
    inverse = lax.rsqrt(variance + norm_eps)
    normal = (values - average[:, None]) * inverse[:, None]
    return ((normal * gain_part + shift_part).astype(jnp.bfloat16), normal, inverse)


def norm_backward(grad_rows, normal, inverse, gain_part):
    scaled = grad_rows * gain_part
    total_one, total_two = width_totals(jnp.sum(scaled, axis=1), jnp.sum(scaled * normal, axis=1))
    grad_in = inverse[:, None] * (
        scaled - total_one[:, None] / D - normal * (total_two[:, None] / D)
    )
    return (grad_in, jnp.sum(grad_rows * normal, axis=0), jnp.sum(grad_rows, axis=0))


def allowed_mask(segment_row, offset, block_rows):
    key_pos = jnp.arange(segment_row.shape[0], dtype=jnp.int32)
    query_pos = key_pos[offset : offset + block_rows]
    same_doc = segment_row[None, :] == segment_row[offset : offset + block_rows, None]
    return (key_pos[None, :] <= query_pos[:, None]) & same_doc


def attend_forward(query_seq, key_seq, value_seq, segment_row, score_scale):
    seq_length = query_seq.shape[2]
    block_rows = min(512, seq_length)
    outputs = []
    log_parts = []
    for offset in range(0, seq_length, block_rows):
        query_block = query_seq[:, :, offset : offset + block_rows]
        scores = (
            jnp.einsum("hdq,hdk->hqk", query_block, key_seq, preferred_element_type=jnp.float32)
            * score_scale
        )
        scores = jnp.where(allowed_mask(segment_row, offset, block_rows)[None], scores, masked_fill)
        row_max = jnp.max(scores, axis=2, keepdims=True)
        exp_scores = jnp.exp(scores - row_max)
        row_total = jnp.sum(exp_scores, axis=2, keepdims=True)
        weights = (exp_scores / row_total).astype(jnp.bfloat16)
        outputs.append(
            jnp.einsum("hqk,hdk->hdq", weights, value_seq, preferred_element_type=jnp.float32)
        )
        log_parts.append((row_max + jnp.log(row_total))[:, :, 0])
    return (jnp.concatenate(outputs, axis=2), jnp.concatenate(log_parts, axis=1))


def attend_backward(query_seq, key_seq, value_seq, grad_seq, segment_row, log_sums, score_scale):
    seq_length = query_seq.shape[2]
    block_rows = min(512, seq_length)
    key_grad = jnp.zeros(key_seq.shape, jnp.float32)
    value_grad = jnp.zeros(value_seq.shape, jnp.float32)
    query_grads = []
    for offset in range(0, seq_length, block_rows):
        query_block = query_seq[:, :, offset : offset + block_rows]
        grad_block = grad_seq[:, :, offset : offset + block_rows]
        scores = (
            jnp.einsum("hdq,hdk->hqk", query_block, key_seq, preferred_element_type=jnp.float32)
            * score_scale
        )
        scores = jnp.where(allowed_mask(segment_row, offset, block_rows)[None], scores, masked_fill)
        probs = jnp.exp(scores - log_sums[:, offset : offset + block_rows, None])
        prob_grad = jnp.einsum(
            "hdq,hdk->hqk", grad_block, value_seq, preferred_element_type=jnp.float32
        )
        row_dot = jnp.sum(probs * prob_grad, axis=2, keepdims=True)
        score_grad = (probs * (prob_grad - row_dot)).astype(jnp.bfloat16)
        query_grads.append(
            jnp.einsum("hqk,hdk->hdq", score_grad, key_seq, preferred_element_type=jnp.float32)
            * score_scale
        )
        key_grad = (
            key_grad
            + jnp.einsum(
                "hqk,hdq->hdk", score_grad, query_block, preferred_element_type=jnp.float32
            )
            * score_scale
        )
        value_grad = value_grad + jnp.einsum(
            "hqk,hdq->hdk",
            probs.astype(jnp.bfloat16),
            grad_block,
            preferred_element_type=jnp.float32,
        )
    return (jnp.concatenate(query_grads, axis=2), key_grad, value_grad)


def body_general(
    tokens_in,
    out_grad,
    segment_ids,
    active_lengths,
    norm1_gain,
    norm1_shift,
    query_weight,
    query_bias,
    key_weight,
    value_weight,
    value_bias,
    out_weight,
    out_bias,
    norm2_gain,
    norm2_shift,
    up_weight,
    up_bias,
    down_weight,
    down_bias,
):
    local_rows = tokens_in.shape[0]
    seq_here = segment_ids.shape[0]
    seq_length = segment_ids.shape[1]
    group_rows = seq_here * seq_length
    row_index = lax.axis_index("row")
    col_index = lax.axis_index("col")
    active_all = active_rows(segment_ids, active_lengths)
    active_here = lax.dynamic_slice_in_dim(active_all, col_index * local_rows, local_rows)
    keep_mask = active_here.astype(jnp.float32)[:, None]
    score_scale = HEAD_DIM ** (-0.5)
    rows_in = tokens_in.astype(jnp.float32)
    normed_one, normal_one, inverse_one = norm_forward(rows_in, norm1_gain, norm1_shift)
    gathered_one = token_gather(normed_one)
    stacked_weight = jnp.stack([query_weight, key_weight, value_weight])
    projected = unit_sums(
        jnp.einsum("td,kdh->kht", gathered_one, stacked_weight, preferred_element_type=jnp.float32)
    )
    head_width = projected.shape[1]
    head_count = head_width // HEAD_DIM
    query_part = lax.dynamic_slice_in_dim(query_bias, row_index * head_width, head_width)
    value_part = lax.dynamic_slice_in_dim(value_bias, row_index * head_width, head_width)
    bias_stack = jnp.stack([query_part, jnp.zeros_like(query_part), value_part])
    heads_all = (projected + bias_stack[:, :, None]).astype(jnp.bfloat16)

    def to_seqs(values):
        return jnp.moveaxis(values.reshape(head_count, HEAD_DIM, seq_here, seq_length), 2, 0)

    def from_seqs(values):
        return jnp.moveaxis(values, 0, 2).reshape(head_width, group_rows)

    query_seqs = to_seqs(heads_all[0])
    key_seqs = to_seqs(heads_all[1])
    value_seqs = to_seqs(heads_all[2])
    attended_seqs, log_sums = lax.map(
        lambda seq_items: attend_forward(
            seq_items[0], seq_items[1], seq_items[2], seq_items[3], score_scale
        ),
        (query_seqs, key_seqs, value_seqs, segment_ids),
    )
    attended = from_seqs(attended_seqs).astype(jnp.bfloat16)
    gathered_heads = unit_gather(attended[None])
    attention_rows = (
        token_sums(
            jnp.einsum("kht,hd->td", gathered_heads, out_weight, preferred_element_type=jnp.float32)
        )
        + out_bias
    )
    hidden_one = rows_in + attention_rows
    normed_two, normal_two, inverse_two = norm_forward(hidden_one, norm2_gain, norm2_shift)
    gathered_two = token_gather(normed_two)
    up_part = jnp.einsum("td,df->ft", gathered_two, up_weight, preferred_element_type=jnp.float32)[
        None
    ]
    unit_width = up_part.shape[1] // lax.axis_size("row")
    up_slice = lax.dynamic_slice_in_dim(up_bias, row_index * unit_width, unit_width)
    pre_act = unit_sums(up_part)[0] + up_slice[:, None]
    gathered_act = unit_gather(gelu_value(pre_act).astype(jnp.bfloat16)[None])
    ffn_rows = (
        token_sums(
            jnp.einsum("kft,fd->td", gathered_act, down_weight, preferred_element_type=jnp.float32)
        )
        + down_bias
    )
    layer_out = jnp.where(active_here[:, None], hidden_one + ffn_rows, rows_in)
    grad_rows = out_grad.astype(jnp.float32) * keep_mask
    branch_grad = token_gather(grad_rows.astype(jnp.bfloat16))
    down_grad = jnp.einsum(
        "kft,td->fd", gathered_act, branch_grad, preferred_element_type=jnp.float32
    )
    down_bias_grad = jnp.sum(branch_grad, axis=0, dtype=jnp.float32)
    act_part = jnp.einsum(
        "td,fd->ft", branch_grad, down_weight, preferred_element_type=jnp.float32
    )[None]
    act_grad = unit_sums(act_part)[0]
    pre_grad = (act_grad * gelu_slope(pre_act)).astype(jnp.bfloat16)
    gathered_pre = unit_gather(pre_grad[None])
    up_grad = jnp.einsum(
        "td,kft->df", gathered_two, gathered_pre, preferred_element_type=jnp.float32
    )
    up_bias_grad = jnp.sum(gathered_pre[0], axis=1, dtype=jnp.float32)
    normed_grad_two = token_sums(
        jnp.einsum("kft,df->td", gathered_pre, up_weight, preferred_element_type=jnp.float32)
    )
    back_two, gain_two_grad, shift_two_grad = norm_backward(
        normed_grad_two, normal_two, inverse_two, norm2_gain
    )
    hidden_grad = grad_rows + back_two
    attention_grad = token_gather(hidden_grad.astype(jnp.bfloat16))
    out_weight_grad = jnp.einsum(
        "kht,td->hd", gathered_heads, attention_grad, preferred_element_type=jnp.float32
    )
    out_bias_grad = jnp.sum(attention_grad, axis=0, dtype=jnp.float32)
    head_grad = unit_sums(
        jnp.einsum("td,hd->ht", attention_grad, out_weight, preferred_element_type=jnp.float32)[
            None
        ]
    )[0].astype(jnp.bfloat16)
    query_grads, key_grads, value_grads = lax.map(
        lambda seq_items: attend_backward(
            seq_items[0],
            seq_items[1],
            seq_items[2],
            seq_items[3],
            seq_items[4],
            seq_items[5],
            score_scale,
        ),
        (query_seqs, key_seqs, value_seqs, to_seqs(head_grad), segment_ids, log_sums),
    )
    stacked_grad = jnp.stack(
        [from_seqs(query_grads), from_seqs(key_grads), from_seqs(value_grads)]
    ).astype(jnp.bfloat16)
    gathered_grad = unit_gather(stacked_grad)
    stacked_weight_grad = jnp.einsum(
        "td,kht->kdh", gathered_one, gathered_grad, preferred_element_type=jnp.float32
    )
    query_bias_grad = jnp.sum(gathered_grad[0], axis=1, dtype=jnp.float32)
    value_bias_grad = jnp.sum(gathered_grad[2], axis=1, dtype=jnp.float32)
    normed_grad_one = token_sums(
        jnp.einsum("kht,kdh->td", gathered_grad, stacked_weight, preferred_element_type=jnp.float32)
    )
    back_one, gain_one_grad, shift_one_grad = norm_backward(
        normed_grad_one, normal_one, inverse_one, norm1_gain
    )
    input_grad = out_grad.astype(jnp.float32) * (1.0 - keep_mask) + hidden_grad + back_one
    (
        stacked_weight_grad,
        query_bias_grad,
        value_bias_grad,
        out_weight_grad,
        out_bias_grad,
        down_grad,
        down_bias_grad,
        up_grad,
        up_bias_grad,
    ) = lax.psum(
        (
            stacked_weight_grad,
            query_bias_grad,
            value_bias_grad,
            out_weight_grad,
            out_bias_grad,
            down_grad,
            down_bias_grad,
            up_grad,
            up_bias_grad,
        ),
        "dp",
    )
    gain_one_grad, shift_one_grad, gain_two_grad, shift_two_grad = lax.psum(
        (gain_one_grad, shift_one_grad, gain_two_grad, shift_two_grad), ("dp", "col")
    )
    return (
        layer_out,
        input_grad,
        gain_one_grad,
        shift_one_grad,
        stacked_weight_grad[0],
        query_bias_grad,
        stacked_weight_grad[1],
        stacked_weight_grad[2],
        value_bias_grad,
        out_weight_grad,
        out_bias_grad,
        gain_two_grad,
        shift_two_grad,
        up_grad,
        up_bias_grad,
        down_grad,
        down_bias_grad,
    )


def swap(values):
    return lax.ppermute(values, "row", [(0, 1), (1, 0)])


def step_x(values):
    return lax.ppermute(values, "dp", [(0, 1), (1, 0), (2, 3), (3, 2)])


def step_y(values):
    return lax.ppermute(values, "dp", [(0, 2), (2, 0), (1, 3), (3, 1)])


def step_up(values):
    count = lax.axis_size("col")
    return lax.ppermute(values, "col", [(i, (i + 1) % count) for i in range(count)])


def step_down(values):
    count = lax.axis_size("col")
    return lax.ppermute(values, "col", [(i, (i - 1) % count) for i in range(count)])


def plane_gather(values):
    half = values.shape[0] // 2
    from_x = step_x(values)
    from_y = step_y(values)
    far_one = step_y(from_x[:half])
    far_two = step_x(from_y[half:])
    return (values, from_x, from_y, jnp.concatenate([far_one, far_two], axis=0))


def plane_sum(here, to_x, to_y, to_far):
    half = here.shape[0] // 2
    f32 = jnp.float32
    via_x = step_x(to_far[:half])
    via_y = step_y(to_far[half:])
    x_top = step_x(to_x[:half])
    y_bottom = step_y(to_y[half:])
    x_bottom = step_x((to_x[half:].astype(f32) + via_y.astype(f32)).astype(jnp.bfloat16))
    y_top = step_y((to_y[:half].astype(f32) + via_x.astype(f32)).astype(jnp.bfloat16))
    top = here[:half].astype(f32) + x_top.astype(f32) + y_top.astype(f32)
    bottom = here[half:].astype(f32) + x_bottom.astype(f32) + y_bottom.astype(f32)
    return jnp.concatenate([top, bottom], axis=0)


def ring_gather(values):
    held = [values]
    for _ in range(lax.axis_size("col") - 1):
        held.append(jax.tree.map(step_up, held[-1]))
    return held


def ring_sum(blocks):
    total = blocks[-1]
    for block in blocks[-2::-1]:
        arrived = jax.tree.map(step_down, total)
        total = jax.tree.map(
            lambda a, b: (a.astype(jnp.float32) + b.astype(jnp.float32)).astype(jnp.bfloat16),
            arrived,
            block,
        )
    return total


def butterfly_sum(values):
    count = lax.axis_size("col")
    values = values + step_x(values)
    values = values + step_y(values)
    step = 1
    while step < count:
        values = values + lax.ppermute(values, "col", [(i, i ^ step) for i in range(count)])
        step *= 2
    return values


def picked(stacked, index):
    return lax.dynamic_index_in_dim(stacked, index, 0, keepdims=False)


def reordered(stacked, index, count):
    return jnp.stack([picked(stacked, jnp.bitwise_xor(index, i)) for i in range(count)])


def row_norm(values):
    average = jnp.mean(values, axis=1, keepdims=True)
    centered = values - average
    inverse = lax.rsqrt(jnp.mean(centered * centered, axis=1, keepdims=True) + norm_eps)
    return (average, inverse)


def mm(left, right, dims, dtype=jnp.float32):
    return lax.dot_general(
        left, right, (dims, ((), ())), preferred_element_type=jnp.float32
    ).astype(dtype)


def body_local(
    tokens_in,
    out_grad,
    segment_ids,
    active_lengths,
    norm1_gain,
    norm1_shift,
    query_weight,
    query_bias,
    key_weight,
    value_weight,
    value_bias,
    out_weight,
    out_bias,
    norm2_gain,
    norm2_shift,
    up_weight,
    up_bias,
    down_weight,
    down_bias,
):
    f32, bf16 = jnp.float32, jnp.bfloat16
    rows, width = tokens_in.shape
    ring = lax.axis_size("col")
    row_i = lax.axis_index("row")
    plane_i = lax.axis_index("dp")
    col_i = lax.axis_index("col")
    own_units = query_weight.shape[1] // 2
    head_units = own_units // 4
    quarter = up_weight.shape[1] // 4
    unit_width = quarter // 2
    score_scale = HEAD_DIM ** (-0.5)

    active_all = active_rows(segment_ids, active_lengths)
    active_here = lax.dynamic_slice_in_dim(active_all, col_i * rows, rows)
    keep_mask = active_here.astype(f32)[:, None]
    segment_row = picked(segment_ids, col_i)

    vectors = jnp.stack([norm1_gain, norm1_shift, norm2_gain, norm2_shift, out_bias])
    vectors = jnp.concatenate([vectors, swap(vectors)], axis=1)
    gain_one, shift_one, gain_two, shift_two, attention_bias = [vectors[i] for i in range(5)]
    tokens = jnp.concatenate([tokens_in, swap(tokens_in)], axis=1).astype(f32)

    def column_part(weight, which, offset, size):
        return lax.dynamic_slice_in_dim(weight, offset + which * size, size, axis=1)

    def row_part(weight, which, offset, size):
        return lax.dynamic_slice_in_dim(weight, offset + which * size, size, axis=0)

    projections = (query_weight, key_weight, value_weight)
    mine = [column_part(w, row_i, 0, own_units).T for w in projections]
    mine.append(row_part(out_weight, row_i, 0, own_units))
    other = [column_part(w, 1 - row_i, 0, own_units).T for w in projections]
    other.append(row_part(out_weight, 1 - row_i, 0, own_units))
    head_weights = jnp.concatenate([jnp.stack(mine), swap(jnp.stack(other))], axis=2)
    head_weights = head_weights.reshape(4, 4, head_units, 2 * width).transpose(1, 0, 2, 3)
    head_weights = reordered(head_weights, plane_i, 4)
    groups = [head_weights]
    for piece in ring_gather(head_weights[0])[1:]:
        groups.append(jnp.stack(plane_gather(piece)))

    ff_offset = plane_i * quarter
    ff_mine = (
        column_part(up_weight, row_i, ff_offset, unit_width),
        column_part(up_weight, 1 - row_i, ff_offset, unit_width),
        row_part(down_weight, row_i, ff_offset, unit_width),
        row_part(down_weight, 1 - row_i, ff_offset, unit_width),
    )
    ff_all = ring_gather(ff_mine)
    up_own = jnp.concatenate([p[0] for p in ff_all], axis=1)
    up_sib = jnp.concatenate([p[1] for p in ff_all], axis=1)
    down_own = jnp.concatenate([p[2] for p in ff_all], axis=0)
    down_sib = jnp.concatenate([p[3] for p in ff_all], axis=0)
    up_full = jnp.concatenate([up_own, swap(up_sib)], axis=0)
    down_full = jnp.concatenate([down_own, swap(down_sib)], axis=1)
    up_half = jnp.concatenate([up_own, up_sib], axis=1)
    down_half = jnp.concatenate([down_own, down_sib], axis=0)

    query_heads = reordered(
        lax.dynamic_slice_in_dim(query_bias, row_i * own_units, own_units).reshape(4, head_units),
        plane_i,
        4,
    )
    value_heads = reordered(
        lax.dynamic_slice_in_dim(value_bias, row_i * own_units, own_units).reshape(4, head_units),
        plane_i,
        4,
    )
    up_part = lax.dynamic_slice_in_dim(up_bias, ff_offset + row_i * unit_width, unit_width)
    small = ring_gather(jnp.concatenate([query_heads.reshape(-1), value_heads.reshape(-1), up_part]))
    up_biases = jnp.concatenate([s[2 * own_units :] for s in small])

    average_one, inverse_one = row_norm(tokens)
    normal_one = (tokens - average_one) * inverse_one
    normed_one = (normal_one * gain_one + shift_one).astype(bf16)
    heads, attended, log_sums = [], [], []
    for weights, biases in zip(groups, small):
        projected = jnp.einsum("jmud,td->jmut", weights[:, :3], normed_one, preferred_element_type=f32)
        bias_q = biases[:own_units].reshape(4, head_units, 1)
        bias_v = biases[own_units : 2 * own_units].reshape(4, head_units, 1)
        query = (projected[:, 0] + bias_q).astype(bf16)
        key = projected[:, 1].astype(bf16)
        value = (projected[:, 2] + bias_v).astype(bf16)
        result, log_sum = attend_forward(query, key, value, segment_row, score_scale)
        heads.append((query, key, value))
        log_sums.append(log_sum)
        attended.append(result.astype(bf16).reshape(own_units, rows))
    attended_both = jnp.concatenate(attended + [swap(a) for a in attended], axis=0)
    out_own = [g[:, 3].reshape(own_units, 2 * width) for g in groups]
    out_sib = [swap(w) for w in out_own]
    out_sib = [jnp.concatenate([w[:, width:], w[:, :width]], axis=1) for w in out_sib]
    out_both = jnp.concatenate(out_own + out_sib, axis=0)
    hidden_one = tokens + mm(attended_both, out_both, ((0,), (0,))) + attention_bias

    average_two, inverse_two = row_norm(hidden_one)
    normal_two = (hidden_one - average_two) * inverse_two
    normed_two = (normal_two * gain_two + shift_two).astype(bf16)
    normed_own = jnp.concatenate(plane_gather(normed_two[:, :width]), axis=0)
    normed_sib = jnp.concatenate([normed_two[:, width:], swap(normed_own[rows:])], axis=0)
    normed_all = jnp.concatenate([normed_own, normed_sib], axis=1)
    branch_mine = (out_grad.astype(f32) * keep_mask).astype(bf16)
    branch_own = jnp.concatenate(plane_gather(branch_mine), axis=0)
    branch_sib = swap(branch_own)
    branch_all = jnp.concatenate([branch_own, branch_sib], axis=1)
    pre_act = mm(normed_all, up_full, ((1,), (0,))) + up_biases
    activated = gelu_value(pre_act).astype(bf16)
    pre_grad = (mm(branch_all, down_full, ((1,), (1,))) * gelu_slope(pre_act)).astype(bf16)
    pre_grad_chip = jnp.concatenate([pre_grad, swap(pre_grad)], axis=1)
    activated_chip = jnp.concatenate([activated, swap(activated)], axis=1)
    grad_parts = mm(pre_grad_chip, up_half, ((1,), (1,)), bf16).reshape(4, rows, width)
    normed_grad_two = plane_sum(*[grad_parts[i] for i in range(4)])
    down_parts = mm(activated_chip, down_half, ((1,), (0,)), bf16).reshape(4, rows, width)
    ffn_rows = plane_sum(*[down_parts[i] for i in range(4)]) + down_bias
    layer_out = jnp.where(active_here[:, None], hidden_one[:, :width] + ffn_rows, tokens[:, :width])
    up_grad = mm(normed_own, pre_grad_chip, ((0,), (0,)), bf16)
    down_grad = mm(activated_chip, branch_own, ((0,), (0,)), bf16)

    units = ring * unit_width
    ff_blocks = []
    for k in range(ring):
        span_own = slice(k * unit_width, (k + 1) * unit_width)
        span_sib = slice(units + k * unit_width, units + (k + 1) * unit_width)
        ff_blocks.append(
            (up_grad[:, span_own], up_grad[:, span_sib], down_grad[span_own], down_grad[span_sib])
        )
    ff_sums = ring_sum(ff_blocks)

    def placed_blocks(own, sib):
        own_all = jnp.stack(plane_gather(own))
        sib_all = jnp.stack(plane_gather(sib))
        both = jnp.stack([own_all, sib_all])
        both = reordered(both, row_i, 2)
        return [
            picked(both[r], jnp.bitwise_xor(plane_i, q)).astype(f32)
            for q in range(4)
            for r in range(2)
        ]

    up_weight_grad = jnp.concatenate(placed_blocks(ff_sums[0], ff_sums[1]), axis=1)
    down_weight_grad = jnp.concatenate(placed_blocks(ff_sums[2], ff_sums[3]), axis=0)

    normed_grad_sib = swap(normed_grad_two.astype(bf16)).astype(f32)
    normed_grad_full = jnp.concatenate([normed_grad_two, normed_grad_sib], axis=1)
    grad_rows = jnp.concatenate([branch_own[:rows], branch_sib[:rows]], axis=1).astype(f32)
    scaled = normed_grad_full * gain_two
    back_two = inverse_two * (
        scaled
        - jnp.mean(scaled, axis=1, keepdims=True)
        - normal_two * jnp.mean(scaled * normal_two, axis=1, keepdims=True)
    )
    hidden_grad = grad_rows + back_two
    attention_grad = hidden_grad.astype(bf16)
    gain_two_grad = jnp.sum(normed_grad_two * normal_two[:, :width], axis=0)
    shift_two_grad = jnp.sum(normed_grad_two, axis=0)

    reduced = [None] * ring
    normed_grad_one = None
    bias_rows = [None] * ring
    for k in range(ring - 1, -1, -1):
        weights = groups[k]
        query, key, value = heads[k]
        head_grad = mm(out_own[k], attention_grad, ((1,), (1,)), bf16).reshape(query.shape)
        grads = attend_backward(
            query, key, value, head_grad, segment_row, log_sums[k], score_scale
        )
        stacked = jnp.stack(grads, axis=1).astype(bf16)
        part = jnp.einsum("jmut,jmud->td", stacked, weights[:, :3], preferred_element_type=f32)
        normed_grad_one = part if normed_grad_one is None else normed_grad_one + part
        weight_grads = jnp.einsum("jmut,td->jmud", stacked, normed_one, preferred_element_type=f32)
        out_grads = mm(attended[k], attention_grad, ((1,), (0,)))
        out_grads = out_grads.reshape(4, 1, head_units, 2 * width)
        blocks = jnp.concatenate([weight_grads, out_grads], axis=1).astype(bf16)
        reduced[k] = plane_sum(*[blocks[i] for i in range(4)]).astype(bf16)
        bias_rows[k] = jnp.stack(
            [
                jnp.sum(stacked[:, 0].astype(f32), axis=2),
                jnp.sum(stacked[:, 2].astype(f32), axis=2),
            ]
        )
    head_sum = ring_sum(reduced)
    head_other = swap(head_sum[:, :, width:])
    head_both = jnp.stack([head_sum[:, :, :width], head_other])
    head_all = jnp.stack(plane_gather(head_both.transpose(1, 0, 2, 3)))
    head_all = reordered(head_all, plane_i, 4).transpose(1, 2, 0, 3, 4)
    head_all = jnp.stack([reordered(head_all[m], row_i, 2) for m in range(4)])
    head_all = head_all.reshape(4, 2 * own_units, width)
    query_weight_grad = head_all[0].T.astype(f32)
    key_weight_grad = head_all[1].T.astype(f32)
    value_weight_grad = head_all[2].T.astype(f32)
    out_weight_grad = head_all[3].astype(f32)

    normed_grad_one = normed_grad_one[:, :width] + swap(
        normed_grad_one[:, width:].astype(bf16)
    ).astype(f32)
    normal_own = normal_one[:, :width]
    scaled = normed_grad_one * gain_one[:width]
    sums = jnp.stack([jnp.sum(scaled, axis=1), jnp.sum(scaled * normal_own, axis=1)])
    sums = (sums + swap(sums)) / (2 * width)
    back_one = inverse_one * (scaled - sums[0][:, None] - normal_own * sums[1][:, None])
    gain_one_grad = jnp.sum(normed_grad_one * normal_own, axis=0)
    shift_one_grad = jnp.sum(normed_grad_one, axis=0)
    input_grad = out_grad.astype(f32) * (1.0 - keep_mask) + hidden_grad[:, :width] + back_one

    def by_column(relative):
        index = jnp.mod(col_i - jnp.arange(ring), ring)
        return jnp.take(jnp.stack(relative), index, axis=0)

    row_hot = (jnp.arange(2) == row_i).astype(f32)
    plane_hot = (jnp.arange(4) == plane_i).astype(f32)
    plane_order = jnp.bitwise_xor(plane_i, jnp.arange(4))
    head_bias = jnp.take(by_column(bias_rows), plane_order, axis=2)
    head_bias = head_bias.transpose(0, 1, 2, 3)[:, :, None] * row_hot[None, None, :, None, None]
    up_bias_part = jnp.sum(pre_grad.astype(f32), axis=0).reshape(ring, unit_width)
    up_bias_part = by_column([up_bias_part[k] for k in range(ring)])
    up_bias_part = (
        up_bias_part[:, None, None, :] * plane_hot[None, :, None, None] * row_hot[None, None, :, None]
    )
    bias_vector = jnp.concatenate([head_bias.reshape(ring, -1), up_bias_part.reshape(ring, -1)], axis=1)
    bias_vector = bias_vector + swap(bias_vector)
    out_bias_part = jnp.sum(attention_grad[:, :width].astype(f32), axis=0)
    down_bias_part = jnp.sum(branch_mine.astype(f32), axis=0)
    own_vector = jnp.concatenate(
        [gain_one_grad, shift_one_grad, gain_two_grad, shift_two_grad, out_bias_part, down_bias_part]
    )
    summed = butterfly_sum(jnp.concatenate([bias_vector.reshape(-1), own_vector]))
    bias_size = bias_vector.size
    bias_here = picked(summed[:bias_size].reshape(ring, -1), col_i)
    own_here = summed[bias_size:].reshape(6, width)
    head_size = 2 * own_units
    return (
        layer_out,
        input_grad,
        own_here[0],
        own_here[1],
        query_weight_grad,
        bias_here[:head_size],
        key_weight_grad,
        value_weight_grad,
        bias_here[head_size : 2 * head_size],
        out_weight_grad,
        own_here[4],
        own_here[2],
        own_here[3],
        up_weight_grad,
        bias_here[2 * head_size :],
        down_weight_grad,
        own_here[5],
    )


def body(tokens_in, out_grad, segment_ids, *rest):
    ring = lax.axis_size("col")
    local = (
        lax.axis_size("dp") == 4
        and lax.axis_size("row") == 2
        and ring & (ring - 1) == 0
        and tokens_in.shape[0] == segment_ids.shape[1]
    )
    chosen = body_local if local else body_general
    return chosen(tokens_in, out_grad, segment_ids, *rest)


def solution(mesh):
    placed = (
        P(("dp", "col"), "row"),
        P(("dp", "col"), "row"),
        P("dp", None),
        P("dp", None),
        P("row"),
        P("row"),
        P("row", "col"),
        P("col"),
        P("row", "col"),
        P("row", "col"),
        P("col"),
        P("col", "row"),
        P("row"),
        P("row"),
        P("row"),
        P("row", "col"),
        P("col"),
        P("col", "row"),
        P("row"),
    )
    return jax.shard_map(
        body,
        mesh=mesh,
        in_specs=placed,
        out_specs=(
            P(("dp", "col"), "row"),
            P(("dp", "col"), "row"),
            P("row"),
            P("row"),
            P("row", "col"),
            P("col"),
            P("row", "col"),
            P("row", "col"),
            P("col"),
            P("col", "row"),
            P("row"),
            P("row"),
            P("row"),
            P("row", "col"),
            P("col"),
            P("col", "row"),
            P("row"),
        ),
        check_vma=False,
    )
```

```python
import functools

import jax
import jax.numpy as jnp
from jax import lax
from jax.experimental import pallas as pl
from jax.experimental.pallas import tpu as pltpu
from jax.sharding import PartitionSpec as P

D = 2048
HEAD_DIM = 64


norm_eps = 1e-05
masked_fill = -1e30


def width_totals(total_one, total_two):
    return lax.psum((total_one, total_two), "row")


def token_gather(values):
    return lax.all_gather(values, "col", axis=0, tiled=True)


def token_sums(partial_rows):
    return lax.psum_scatter(partial_rows, "col", scatter_dimension=0, tiled=True)


def unit_gather(values):
    return lax.all_gather(values, "row", axis=1, tiled=True)


def unit_sums(partial_units):
    return lax.psum_scatter(partial_units, "row", scatter_dimension=1, tiled=True)


def gelu_value(values):
    return jax.nn.gelu(values, approximate=True)


def gelu_slope(values):
    result, pullback = jax.vjp(gelu_value, values)
    return pullback(jnp.ones_like(values))[0]


def active_rows(segment_rows, keep_lengths):
    doc_index = jnp.arange(keep_lengths.shape[-1], dtype=jnp.int32)
    member = (segment_rows[:, :, None] == doc_index).astype(jnp.int32)
    counts = jnp.sum(member, axis=1)
    starts = jnp.cumsum(counts, axis=1) - counts
    first_pos = jnp.sum(member * starts[:, None, :], axis=2)
    keep_here = jnp.sum(member * keep_lengths[:, None, :], axis=2)
    position_in = jnp.arange(segment_rows.shape[1], dtype=jnp.int32)[None, :] - first_pos
    return (position_in < keep_here).reshape(-1)


def norm_forward(values, gain_part, shift_part):
    total_one, total_two = width_totals(jnp.sum(values, axis=1), jnp.sum(values * values, axis=1))
    average = total_one / D
    variance = total_two / D - average * average
    inverse = lax.rsqrt(variance + norm_eps)
    normal = (values - average[:, None]) * inverse[:, None]
    return ((normal * gain_part + shift_part).astype(jnp.bfloat16), normal, inverse)


def norm_backward(grad_rows, normal, inverse, gain_part):
    scaled = grad_rows * gain_part
    total_one, total_two = width_totals(jnp.sum(scaled, axis=1), jnp.sum(scaled * normal, axis=1))
    grad_in = inverse[:, None] * (
        scaled - total_one[:, None] / D - normal * (total_two[:, None] / D)
    )
    return (grad_in, jnp.sum(grad_rows * normal, axis=0), jnp.sum(grad_rows, axis=0))


def allowed_mask(segment_row, offset, block_rows):
    key_pos = jnp.arange(segment_row.shape[0], dtype=jnp.int32)
    query_pos = key_pos[offset : offset + block_rows]
    same_doc = segment_row[None, :] == segment_row[offset : offset + block_rows, None]
    return (key_pos[None, :] <= query_pos[:, None]) & same_doc


def attend_forward(query_seq, key_seq, value_seq, segment_row, score_scale):
    seq_length = query_seq.shape[2]
    block_rows = min(512, seq_length)
    outputs = []
    log_parts = []
    for offset in range(0, seq_length, block_rows):
        query_block = query_seq[:, :, offset : offset + block_rows]
        scores = (
            jnp.einsum("hdq,hdk->hqk", query_block, key_seq, preferred_element_type=jnp.float32)
            * score_scale
        )
        scores = jnp.where(allowed_mask(segment_row, offset, block_rows)[None], scores, masked_fill)
        row_max = jnp.max(scores, axis=2, keepdims=True)
        exp_scores = jnp.exp(scores - row_max)
        row_total = jnp.sum(exp_scores, axis=2, keepdims=True)
        weights = (exp_scores / row_total).astype(jnp.bfloat16)
        outputs.append(
            jnp.einsum("hqk,hdk->hdq", weights, value_seq, preferred_element_type=jnp.float32)
        )
        log_parts.append((row_max + jnp.log(row_total))[:, :, 0])
    return (jnp.concatenate(outputs, axis=2), jnp.concatenate(log_parts, axis=1))


def attend_backward(query_seq, key_seq, value_seq, grad_seq, segment_row, log_sums, score_scale):
    seq_length = query_seq.shape[2]
    block_rows = min(512, seq_length)
    key_grad = jnp.zeros(key_seq.shape, jnp.float32)
    value_grad = jnp.zeros(value_seq.shape, jnp.float32)
    query_grads = []
    for offset in range(0, seq_length, block_rows):
        query_block = query_seq[:, :, offset : offset + block_rows]
        grad_block = grad_seq[:, :, offset : offset + block_rows]
        scores = (
            jnp.einsum("hdq,hdk->hqk", query_block, key_seq, preferred_element_type=jnp.float32)
            * score_scale
        )
        scores = jnp.where(allowed_mask(segment_row, offset, block_rows)[None], scores, masked_fill)
        probs = jnp.exp(scores - log_sums[:, offset : offset + block_rows, None])
        prob_grad = jnp.einsum(
            "hdq,hdk->hqk", grad_block, value_seq, preferred_element_type=jnp.float32
        )
        row_dot = jnp.sum(probs * prob_grad, axis=2, keepdims=True)
        score_grad = (probs * (prob_grad - row_dot)).astype(jnp.bfloat16)
        query_grads.append(
            jnp.einsum("hqk,hdk->hdq", score_grad, key_seq, preferred_element_type=jnp.float32)
            * score_scale
        )
        key_grad = (
            key_grad
            + jnp.einsum(
                "hqk,hdq->hdk", score_grad, query_block, preferred_element_type=jnp.float32
            )
            * score_scale
        )
        value_grad = value_grad + jnp.einsum(
            "hqk,hdq->hdk",
            probs.astype(jnp.bfloat16),
            grad_block,
            preferred_element_type=jnp.float32,
        )
    return (jnp.concatenate(query_grads, axis=2), key_grad, value_grad)


def body_general(
    tokens_in,
    out_grad,
    segment_ids,
    active_lengths,
    norm1_gain,
    norm1_shift,
    query_weight,
    query_bias,
    key_weight,
    value_weight,
    value_bias,
    out_weight,
    out_bias,
    norm2_gain,
    norm2_shift,
    up_weight,
    up_bias,
    down_weight,
    down_bias,
):
    local_rows = tokens_in.shape[0]
    seq_here = segment_ids.shape[0]
    seq_length = segment_ids.shape[1]
    group_rows = seq_here * seq_length
    row_index = lax.axis_index("row")
    col_index = lax.axis_index("col")
    active_all = active_rows(segment_ids, active_lengths)
    active_here = lax.dynamic_slice_in_dim(active_all, col_index * local_rows, local_rows)
    keep_mask = active_here.astype(jnp.float32)[:, None]
    score_scale = HEAD_DIM ** (-0.5)
    rows_in = tokens_in.astype(jnp.float32)
    normed_one, normal_one, inverse_one = norm_forward(rows_in, norm1_gain, norm1_shift)
    gathered_one = token_gather(normed_one)
    stacked_weight = jnp.stack([query_weight, key_weight, value_weight])
    projected = unit_sums(
        jnp.einsum("td,kdh->kht", gathered_one, stacked_weight, preferred_element_type=jnp.float32)
    )
    head_width = projected.shape[1]
    head_count = head_width // HEAD_DIM
    query_part = lax.dynamic_slice_in_dim(query_bias, row_index * head_width, head_width)
    value_part = lax.dynamic_slice_in_dim(value_bias, row_index * head_width, head_width)
    bias_stack = jnp.stack([query_part, jnp.zeros_like(query_part), value_part])
    heads_all = (projected + bias_stack[:, :, None]).astype(jnp.bfloat16)

    def to_seqs(values):
        return jnp.moveaxis(values.reshape(head_count, HEAD_DIM, seq_here, seq_length), 2, 0)

    def from_seqs(values):
        return jnp.moveaxis(values, 0, 2).reshape(head_width, group_rows)

    query_seqs = to_seqs(heads_all[0])
    key_seqs = to_seqs(heads_all[1])
    value_seqs = to_seqs(heads_all[2])
    attended_seqs, log_sums = lax.map(
        lambda seq_items: attend_forward(
            seq_items[0], seq_items[1], seq_items[2], seq_items[3], score_scale
        ),
        (query_seqs, key_seqs, value_seqs, segment_ids),
    )
    attended = from_seqs(attended_seqs).astype(jnp.bfloat16)
    gathered_heads = unit_gather(attended[None])
    attention_rows = (
        token_sums(
            jnp.einsum("kht,hd->td", gathered_heads, out_weight, preferred_element_type=jnp.float32)
        )
        + out_bias
    )
    hidden_one = rows_in + attention_rows
    normed_two, normal_two, inverse_two = norm_forward(hidden_one, norm2_gain, norm2_shift)
    gathered_two = token_gather(normed_two)
    up_part = jnp.einsum("td,df->ft", gathered_two, up_weight, preferred_element_type=jnp.float32)[
        None
    ]
    unit_width = up_part.shape[1] // lax.axis_size("row")
    up_slice = lax.dynamic_slice_in_dim(up_bias, row_index * unit_width, unit_width)
    pre_act = unit_sums(up_part)[0] + up_slice[:, None]
    gathered_act = unit_gather(gelu_value(pre_act).astype(jnp.bfloat16)[None])
    ffn_rows = (
        token_sums(
            jnp.einsum("kft,fd->td", gathered_act, down_weight, preferred_element_type=jnp.float32)
        )
        + down_bias
    )
    layer_out = jnp.where(active_here[:, None], hidden_one + ffn_rows, rows_in)
    grad_rows = out_grad.astype(jnp.float32) * keep_mask
    branch_grad = token_gather(grad_rows.astype(jnp.bfloat16))
    down_grad = jnp.einsum(
        "kft,td->fd", gathered_act, branch_grad, preferred_element_type=jnp.float32
    )
    down_bias_grad = jnp.sum(branch_grad, axis=0, dtype=jnp.float32)
    act_part = jnp.einsum(
        "td,fd->ft", branch_grad, down_weight, preferred_element_type=jnp.float32
    )[None]
    act_grad = unit_sums(act_part)[0]
    pre_grad = (act_grad * gelu_slope(pre_act)).astype(jnp.bfloat16)
    gathered_pre = unit_gather(pre_grad[None])
    up_grad = jnp.einsum(
        "td,kft->df", gathered_two, gathered_pre, preferred_element_type=jnp.float32
    )
    up_bias_grad = jnp.sum(gathered_pre[0], axis=1, dtype=jnp.float32)
    normed_grad_two = token_sums(
        jnp.einsum("kft,df->td", gathered_pre, up_weight, preferred_element_type=jnp.float32)
    )
    back_two, gain_two_grad, shift_two_grad = norm_backward(
        normed_grad_two, normal_two, inverse_two, norm2_gain
    )
    hidden_grad = grad_rows + back_two
    attention_grad = token_gather(hidden_grad.astype(jnp.bfloat16))
    out_weight_grad = jnp.einsum(
        "kht,td->hd", gathered_heads, attention_grad, preferred_element_type=jnp.float32
    )
    out_bias_grad = jnp.sum(attention_grad, axis=0, dtype=jnp.float32)
    head_grad = unit_sums(
        jnp.einsum("td,hd->ht", attention_grad, out_weight, preferred_element_type=jnp.float32)[
            None
        ]
    )[0].astype(jnp.bfloat16)
    query_grads, key_grads, value_grads = lax.map(
        lambda seq_items: attend_backward(
            seq_items[0],
            seq_items[1],
            seq_items[2],
            seq_items[3],
            seq_items[4],
            seq_items[5],
            score_scale,
        ),
        (query_seqs, key_seqs, value_seqs, to_seqs(head_grad), segment_ids, log_sums),
    )
    stacked_grad = jnp.stack(
        [from_seqs(query_grads), from_seqs(key_grads), from_seqs(value_grads)]
    ).astype(jnp.bfloat16)
    gathered_grad = unit_gather(stacked_grad)
    stacked_weight_grad = jnp.einsum(
        "td,kht->kdh", gathered_one, gathered_grad, preferred_element_type=jnp.float32
    )
    query_bias_grad = jnp.sum(gathered_grad[0], axis=1, dtype=jnp.float32)
    value_bias_grad = jnp.sum(gathered_grad[2], axis=1, dtype=jnp.float32)
    normed_grad_one = token_sums(
        jnp.einsum("kht,kdh->td", gathered_grad, stacked_weight, preferred_element_type=jnp.float32)
    )
    back_one, gain_one_grad, shift_one_grad = norm_backward(
        normed_grad_one, normal_one, inverse_one, norm1_gain
    )
    input_grad = out_grad.astype(jnp.float32) * (1.0 - keep_mask) + hidden_grad + back_one
    (
        stacked_weight_grad,
        query_bias_grad,
        value_bias_grad,
        out_weight_grad,
        out_bias_grad,
        down_grad,
        down_bias_grad,
        up_grad,
        up_bias_grad,
    ) = lax.psum(
        (
            stacked_weight_grad,
            query_bias_grad,
            value_bias_grad,
            out_weight_grad,
            out_bias_grad,
            down_grad,
            down_bias_grad,
            up_grad,
            up_bias_grad,
        ),
        "dp",
    )
    gain_one_grad, shift_one_grad, gain_two_grad, shift_two_grad = lax.psum(
        (gain_one_grad, shift_one_grad, gain_two_grad, shift_two_grad), ("dp", "col")
    )
    return (
        layer_out,
        input_grad,
        gain_one_grad,
        shift_one_grad,
        stacked_weight_grad[0],
        query_bias_grad,
        stacked_weight_grad[1],
        stacked_weight_grad[2],
        value_bias_grad,
        out_weight_grad,
        out_bias_grad,
        gain_two_grad,
        shift_two_grad,
        up_grad,
        up_bias_grad,
        down_grad,
        down_bias_grad,
    )


def after(values, *others):
    return lax.optimization_barrier((values, others))[0]


def swap(values):
    return lax.ppermute(values, "row", [(0, 1), (1, 0)])


def step_x(values):
    return lax.ppermute(values, "dp", [(0, 1), (1, 0), (2, 3), (3, 2)])


def step_y(values):
    return lax.ppermute(values, "dp", [(0, 2), (2, 0), (1, 3), (3, 1)])


def step_up(values):
    count = lax.axis_size("col")
    return lax.ppermute(values, "col", [(i, (i + 1) % count) for i in range(count)])


def step_down(values):
    count = lax.axis_size("col")
    return lax.ppermute(values, "col", [(i, (i - 1) % count) for i in range(count)])


def plane_gather(values):
    half = values.shape[0] // 2
    from_x = step_x(values)
    from_y = step_y(values)
    far_one = step_y(from_x[:half])
    far_two = step_x(from_y[half:])
    return [values, from_x, from_y, far_one, far_two]


def add_rounded(left, right):
    return (left.astype(jnp.float32) + right.astype(jnp.float32)).astype(jnp.bfloat16)


def plane_sum(parts):
    f32 = jnp.float32
    first, second = parts
    via_x = step_x(first[3])
    via_y = step_y(second[3])
    first_x = step_x(first[1])
    second_y = step_y(second[2])
    second_x = step_x(add_rounded(second[1], via_y))
    first_y = step_y(add_rounded(first[2], via_x))
    return (
        first[0].astype(f32) + first_x.astype(f32) + first_y.astype(f32),
        second[0].astype(f32) + second_x.astype(f32) + second_y.astype(f32),
    )


def ring_gather(values):
    held = [values]
    for _ in range(lax.axis_size("col") - 1):
        held.append(jax.tree.map(step_up, held[-1]))
    return held


def ring_sum(blocks):
    total = blocks[-1]
    for block in blocks[-2::-1]:
        total = jax.tree.map(lambda a, b: add_rounded(step_down(a), b), total, block)
    return total


def butterfly_sum(values):
    count = lax.axis_size("col")
    values = values + step_x(values)
    values = values + step_y(values)
    step = 1
    while step < count:
        values = values + lax.ppermute(values, "col", [(i, i ^ step) for i in range(count)])
        step *= 2
    return values


def picked(stacked, index):
    return lax.dynamic_index_in_dim(stacked, index, 0, keepdims=False)


def exchanged(values, index, axis):
    size = values.shape[axis] // 4
    return jnp.concatenate(
        [
            lax.dynamic_slice_in_dim(values, jnp.bitwise_xor(index, i) * size, size, axis=axis)
            for i in range(4)
        ],
        axis=axis,
    )


def row_norm(values):
    average = jnp.mean(values, axis=1, keepdims=True)
    centered = values - average
    inverse = lax.rsqrt(jnp.mean(centered * centered, axis=1, keepdims=True) + norm_eps)
    return (average, inverse)


def mm(left, right, left_dim, right_dim, dtype=jnp.float32):
    return lax.dot_general(
        left, right, (((left_dim,), (right_dim,)), ((), ())), preferred_element_type=jnp.float32
    ).astype(dtype)


PAIR = 2 * HEAD_DIM
vmem_bytes = 48 * 1024 * 1024


def head_lanes(head, value):
    lane = lax.broadcasted_iota(jnp.int32, (1, PAIR), 1)
    return jnp.where(lane // HEAD_DIM == head, value, 0.0).astype(jnp.bfloat16)


def allowed_keys(first_row, low, high):
    key_pos = lax.broadcasted_iota(jnp.int32, (high, high - low), 0)
    query_pos = lax.broadcasted_iota(jnp.int32, (high, high - low), 1) + low
    return (key_pos >= first_row) & (key_pos <= query_pos)


def local_forward_kernel(size, first_ref, query_ref, key_ref, value_ref, out_ref):
    lane = lax.broadcasted_iota(jnp.int32, (size, PAIR), 1)
    for low in range(0, key_ref.shape[0], size):
        high = low + size
        keys = key_ref[:high, :]
        values = value_ref[:high, :]
        queries = query_ref[low:high, :]
        allowed = allowed_keys(first_ref[:, low:high], low, high)
        results = []
        for head in range(2):
            scores = mm(keys, queries * head_lanes(head, HEAD_DIM ** (-0.5)), 1, 1)
            scores = jnp.where(allowed, scores, masked_fill)
            exp_scores = jnp.exp(scores - jnp.max(scores, axis=0, keepdims=True))
            inverse = 1.0 / jnp.sum(exp_scores, axis=0, keepdims=True)
            results.append(mm((exp_scores * inverse).astype(jnp.bfloat16), values, 0, 0))
        out_ref[low:high, :] = jnp.where(lane < HEAD_DIM, results[0], results[1]).astype(
            jnp.bfloat16
        )


def local_forward(heads, first_row):
    length = heads.shape[0]
    pairs = heads.shape[1] // (3 * PAIR)
    return pl.pallas_call(
        functools.partial(local_forward_kernel, min(256, length)),
        grid=(pairs,),
        in_specs=[
            pl.BlockSpec((1, length), lambda p: (0, 0)),
            pl.BlockSpec((length, PAIR), lambda p: (0, p)),
            pl.BlockSpec((length, PAIR), lambda p: (0, pairs + p)),
            pl.BlockSpec((length, PAIR), lambda p: (0, 2 * pairs + p)),
        ],
        out_specs=pl.BlockSpec((length, PAIR), lambda p: (0, p)),
        out_shape=jax.ShapeDtypeStruct((length, pairs * PAIR), jnp.bfloat16),
        compiler_params=pltpu.CompilerParams(vmem_limit_bytes=vmem_bytes),
        cost_estimate=pl.CostEstimate(
            flops=16 * length * length * pairs * PAIR, bytes_accessed=8 * heads.size, transcendentals=0
        ),
    )(first_row, heads, heads, heads)


def local_backward_kernel(
    size, first_ref, query_ref, grad_ref, key_ref, value_ref, out_ref, key_sum, value_sum
):
    length = key_ref.shape[0]
    pair = pl.program_id(0)
    pairs = out_ref.shape[1] // (3 * PAIR)
    scale = HEAD_DIM ** (-0.5)
    lane = lax.broadcasted_iota(jnp.int32, (size, PAIR), 1)

    def lanes(part):
        return pl.ds(pl.multiple_of((part * pairs + pair) * PAIR, PAIR), PAIR)

    for low in range(length - size, -1, -size):
        high = low + size
        keys = key_ref[:high, :]
        values = value_ref[:high, :]
        queries = query_ref[low:high, :]
        grads = grad_ref[low:high, :]
        allowed = allowed_keys(first_ref[:, low:high], low, high)
        query_grads = []
        for head in range(2):
            scaled = queries * head_lanes(head, scale)
            grad = grads * head_lanes(head, 1.0)
            scores = jnp.where(allowed, mm(keys, scaled, 1, 1), masked_fill)
            exp_scores = jnp.exp(scores - jnp.max(scores, axis=0, keepdims=True))
            probs = exp_scores * (1.0 / jnp.sum(exp_scores, axis=0, keepdims=True))
            prob_grad = mm(values, grad, 1, 1)
            row_dot = jnp.sum(probs * prob_grad, axis=0, keepdims=True)
            score_grad = (probs * (prob_grad - row_dot)).astype(jnp.bfloat16)
            value_part = mm(probs.astype(jnp.bfloat16), grad, 1, 0)
            key_part = mm(score_grad, scaled, 1, 0)
            query_grads.append(mm(score_grad, keys, 0, 0) * scale)
            if head == 0:
                key_add, value_add = key_part, value_part
            else:
                key_add, value_add = key_add + key_part, value_add + value_part
        if high == length:
            key_sum[...] = key_add
            value_sum[...] = value_add
        else:
            key_sum[:high, :] += key_add
            value_sum[:high, :] += value_add
        out_ref[low:high, lanes(0)] = jnp.where(
            lane < HEAD_DIM, query_grads[0], query_grads[1]
        ).astype(jnp.bfloat16)
    out_ref[:, lanes(1)] = key_sum[...].astype(jnp.bfloat16)
    out_ref[:, lanes(2)] = value_sum[...].astype(jnp.bfloat16)


def local_backward(heads, head_grad, first_row):
    length = heads.shape[0]
    pairs = heads.shape[1] // (3 * PAIR)
    return pl.pallas_call(
        functools.partial(local_backward_kernel, min(512, length)),
        grid=(pairs,),
        in_specs=[
            pl.BlockSpec((1, length), lambda p: (0, 0)),
            pl.BlockSpec((length, PAIR), lambda p: (0, p)),
            pl.BlockSpec((length, PAIR), lambda p: (0, p)),
            pl.BlockSpec((length, PAIR), lambda p: (0, pairs + p)),
            pl.BlockSpec((length, PAIR), lambda p: (0, 2 * pairs + p)),
        ],
        out_specs=pl.BlockSpec(heads.shape, lambda p: (0, 0)),
        out_shape=jax.ShapeDtypeStruct(heads.shape, jnp.bfloat16),
        scratch_shapes=[pltpu.VMEM((length, PAIR), jnp.float32)] * 2,
        compiler_params=pltpu.CompilerParams(vmem_limit_bytes=vmem_bytes),
        cost_estimate=pl.CostEstimate(
            flops=32 * length * length * pairs * PAIR, bytes_accessed=8 * heads.size, transcendentals=0
        ),
    )(first_row, heads, head_grad, heads, heads)


def token_products_kernel(*refs):
    out_ref = refs[-1]
    count = (len(refs) - 1) // 2
    total = mm(refs[0][...], refs[count][...], 0, 0)
    for i in range(1, count):
        total += mm(refs[i][...], refs[count + i][...], 0, 0)
    out_ref[...] = total.astype(out_ref.dtype)


def token_products(lefts, rights):
    tokens, left_width = lefts[0].shape
    right_width = rights[0].shape[1]
    size = min(256, left_width)
    count = len(lefts)
    flops = 2 * count * tokens * left_width * right_width
    return pl.pallas_call(
        token_products_kernel,
        grid=(left_width // size,),
        in_specs=[pl.BlockSpec((tokens, size), lambda i: (0, i))] * count
        + [pl.BlockSpec((tokens, right_width), lambda i: (0, 0))] * count,
        out_specs=pl.BlockSpec((size, right_width), lambda i: (i, 0)),
        out_shape=jax.ShapeDtypeStruct((left_width, right_width), jnp.bfloat16),
        compiler_params=pltpu.CompilerParams(vmem_limit_bytes=vmem_bytes),
        cost_estimate=pl.CostEstimate(
            flops=flops, bytes_accessed=2 * count * tokens * (left_width + right_width), transcendentals=0
        ),
    )(*lefts, *rights)


def body_local(
    tokens_in,
    out_grad,
    segment_ids,
    active_lengths,
    norm1_gain,
    norm1_shift,
    query_weight,
    query_bias,
    key_weight,
    value_weight,
    value_bias,
    out_weight,
    out_bias,
    norm2_gain,
    norm2_shift,
    up_weight,
    up_bias,
    down_weight,
    down_bias,
):
    f32, bf16 = jnp.float32, jnp.bfloat16
    rows, width = tokens_in.shape
    ring = lax.axis_size("col")
    row_i = lax.axis_index("row")
    plane_i = lax.axis_index("dp")
    col_i = lax.axis_index("col")
    own = query_weight.shape[1] // 2
    block = width // 4
    quarter = up_weight.shape[1] // 4
    unit = quarter // 2

    def by_core(weight, size, offset=0):
        return [
            lax.dynamic_slice_in_dim(weight, offset + which * size, size, axis=1)
            for which in (row_i, 1 - row_i)
        ]

    four = [by_core(w, own) for w in (query_weight, key_weight, value_weight, out_weight.T)]
    four = jnp.concatenate([w[0] for w in four] + [w[1] for w in four], axis=1)
    four = exchanged(four, plane_i, 0)

    tokens_sib = swap(tokens_in)

    ff_offset = plane_i * quarter
    up_piece = jnp.concatenate(by_core(up_weight, unit, ff_offset), axis=1)
    down_piece = jnp.concatenate(
        [
            lax.dynamic_slice_in_dim(down_weight, ff_offset + which * unit, unit, axis=0)
            for which in (row_i, 1 - row_i)
        ],
        axis=0,
    )

    active_all = active_rows(segment_ids, active_lengths)
    active_here = lax.dynamic_slice_in_dim(active_all, col_i * rows, rows)
    keep_mask = active_here.astype(f32)[:, None]
    segment_row = picked(segment_ids, col_i)
    member = (segment_row[:, None] == jnp.arange(active_lengths.shape[1])).astype(jnp.int32)
    counts = jnp.sum(member, axis=0)
    first_row = jnp.sum(member * (jnp.cumsum(counts) - counts), axis=1)[None, :]

    branch_mine = (out_grad.astype(f32) * keep_mask).astype(bf16)

    query_part = lax.dynamic_slice_in_dim(query_bias, row_i * own, own)
    value_part = lax.dynamic_slice_in_dim(value_bias, row_i * own, own)
    up_part = lax.dynamic_slice_in_dim(up_bias, ff_offset + row_i * unit, unit)
    small = ring_gather(
        jnp.concatenate([query_part, jnp.zeros_like(query_part), value_part, up_part])
    )
    up_biases = jnp.concatenate([s[3 * own :] for s in small])

    pieces = ring_gather(four[:block])
    own_rows, other_units = [four[:, : 4 * own]], [four[:, 4 * own :]]
    for piece in pieces[1:]:
        gathered = plane_gather(piece)
        own_rows.append(jnp.concatenate([p[:, : 4 * own] for p in gathered], axis=0))
        other_units.append(jnp.concatenate([p[:, 4 * own :] for p in gathered], axis=0))
    groups = [jnp.concatenate([a, swap(b)], axis=0) for a, b in zip(own_rows, other_units)]

    gains = jnp.stack([norm1_gain, norm1_shift])
    gains_sib = swap(gains)
    tokens_own = tokens_in.astype(f32)
    tokens_all = jnp.concatenate([tokens_own, tokens_sib.astype(f32)], axis=1)
    average_one, inverse_one = row_norm(tokens_all)
    normed_one = jnp.concatenate(
        [
            exchanged(
                (((t - average_one) * inverse_one) * g[0] + g[1]).astype(bf16), plane_i, 1
            )
            for t, g in ((tokens_own, gains), (tokens_sib.astype(f32), gains_sib))
        ],
        axis=1,
    )
    heads, attended = [], []
    attention_rows = None
    for k in range(ring):
        weights = groups[k]
        head = (mm(normed_one, weights[:, : 3 * own], 1, 0) + small[k][: 3 * own]).astype(bf16)
        result = local_forward(head, first_row)
        heads.append(head)
        attended.append(result)
        both = jnp.concatenate([result, swap(result)], axis=1)
        out_both = jnp.concatenate([own_rows[k][:, 3 * own :], other_units[k][:, 3 * own :]], axis=1)
        part = mm(both, out_both, 1, 1)
        attention_rows = part if k == 0 else attention_rows + part
    hidden_one = tokens_own + exchanged(attention_rows, plane_i, 1) + out_bias

    def both_sums(one, two):
        sums = jnp.stack([jnp.sum(one, axis=1), jnp.sum(two, axis=1)])
        sums = (sums + swap(sums)) / (2 * width)
        return sums[0][:, None], sums[1][:, None]

    half_mean = jnp.mean(hidden_one, axis=1, keepdims=True)
    centered = hidden_one - half_mean
    half_square = jnp.mean(centered * centered, axis=1, keepdims=True)
    half_stats = jnp.concatenate([half_mean, half_square], axis=1).T
    other_stats = swap(half_stats)
    gap = half_stats[0] - other_stats[0]
    average_two = (0.5 * (half_stats[0] + other_stats[0]))[:, None]
    variance_two = (0.5 * (half_stats[1] + other_stats[1]) + 0.25 * gap * gap)[:, None]
    inverse_two = lax.rsqrt(variance_two + norm_eps)
    normal_two = (hidden_one - average_two) * inverse_two
    normed_two = (normal_two * norm2_gain + norm2_shift).astype(bf16)

    ff_pieces = ring_gather((up_piece, down_piece))
    up_own = jnp.concatenate([p[0][:, :unit] for p in ff_pieces], axis=1)
    up_sib = jnp.concatenate([p[0][:, unit:] for p in ff_pieces], axis=1)
    down_own = jnp.concatenate([p[1][:unit] for p in ff_pieces], axis=0)
    down_sib = jnp.concatenate([p[1][unit:] for p in ff_pieces], axis=0)
    up_full = jnp.concatenate([up_own, swap(up_sib)], axis=0)
    down_full = jnp.concatenate([down_own, swap(down_sib)], axis=1)
    up_half = jnp.concatenate([up_own, up_sib], axis=1)
    down_half = jnp.concatenate([down_own, down_sib], axis=0)

    def gathered_tokens(values):
        here, from_x, from_y, far_one, far_two = plane_gather(values)
        own_parts = [here, from_x, from_y, jnp.concatenate([far_one, far_two], axis=0)]
        return own_parts, [jnp.concatenate([p, swap(p)], axis=1) for p in own_parts]

    branch_own, branch_all = gathered_tokens(branch_mine)
    normed_own, normed_all = gathered_tokens(normed_two)
    half_rows = rows // 2
    acts, act_sibs, pre_grads, pre_sibs, grad_parts, down_parts = [], [], [], [], [], []
    for j in range(4):
        pre_act = mm(normed_all[j], up_full, 1, 0) + up_biases
        act = gelu_value(pre_act).astype(bf16)
        pre_grad = (mm(branch_all[j], down_full, 1, 1) * gelu_slope(pre_act)).astype(bf16)
        acts.append(act)
        pre_grads.append(pre_grad)
        pre_sibs.append(swap(pre_grad))
        act_sibs.append(swap(act))
        chip = jnp.concatenate([pre_grad, pre_sibs[j]], axis=1)
        grad_parts.append(mm(chip, up_half, 1, 1, bf16))
    normed_grad_two = jnp.concatenate(
        plane_sum([[g[:half_rows] for g in grad_parts], [g[half_rows:] for g in grad_parts]]), axis=0
    )
    for j in range(4):
        chip = jnp.concatenate([acts[j], act_sibs[j]], axis=1)
        down_parts.append(mm(chip, down_half, 1, 0, bf16))
    up_grads = (token_products(normed_own, pre_grads), token_products(normed_own, pre_sibs))
    down_grads = (token_products(acts, branch_own), token_products(act_sibs, branch_own))

    scaled = normed_grad_two * norm2_gain
    mean_one, mean_two = both_sums(scaled, scaled * normal_two)
    hidden_grad = branch_mine.astype(f32) + inverse_two * (scaled - mean_one - normal_two * mean_two)
    attention_grad = hidden_grad.astype(bf16)
    gain_two_grad = jnp.sum(normed_grad_two * normal_two, axis=0)
    shift_two_grad = jnp.sum(normed_grad_two, axis=0)

    grad_blocks = exchanged(attention_grad, plane_i, 1)
    grad_blocks = jnp.concatenate([grad_blocks, swap(grad_blocks)], axis=1)
    reduced = [None] * ring
    normed_grad_one = None
    bias_rows = [None] * ring
    for k in range(ring - 1, -1, -1):
        weights = groups[k]
        head_grad = mm(grad_blocks, weights[:, 3 * own :], 1, 0, bf16)
        grads = local_backward(heads[k], head_grad, first_row)
        part = mm(grads, weights[:, : 3 * own], 1, 1)
        normed_grad_one = part if normed_grad_one is None else normed_grad_one + part
        weight_grads = jnp.concatenate(
            [mm(normed_one, grads, 0, 0, bf16), mm(grad_blocks, attended[k], 0, 0, bf16)], axis=1
        )
        mine = weight_grads[:width]
        arrived = swap(weight_grads[width:])
        reduced[k] = [
            r.astype(bf16)
            for r in plane_sum(
                [[m[j * block : (j + 1) * block] for j in range(4)] for m in (mine, arrived)]
            )
        ]
        bias_rows[k] = jnp.sum(grads.astype(f32), axis=0)
    head_sum = ring_sum(reduced)
    head_mine, head_sib = [
        exchanged(jnp.concatenate(plane_gather(h), axis=0), plane_i, 0) for h in head_sum
    ]

    def by_row(mine, sib, axis):
        return jnp.where(
            row_i == 0,
            jnp.concatenate([mine, sib], axis=axis),
            jnp.concatenate([sib, mine], axis=axis),
        )

    query_weight_grad, key_weight_grad, value_weight_grad, out_weight_grad = [
        by_row(head_mine[:, m * own : (m + 1) * own], head_sib[:, m * own : (m + 1) * own], 1).astype(f32)
        for m in range(4)
    ]
    out_weight_grad = out_weight_grad.T

    ffn_rows = plane_sum([[d[:half_rows] for d in down_parts], [d[half_rows:] for d in down_parts]])
    ffn_rows = jnp.concatenate(ffn_rows, axis=0) + down_bias
    layer_out = jnp.where(active_here[:, None], hidden_one + ffn_rows, tokens_own)
    ff_sums = ring_sum(
        [
            (
                up_grads[0][:, k * unit : (k + 1) * unit],
                up_grads[1][:, k * unit : (k + 1) * unit],
                down_grads[0][k * unit : (k + 1) * unit],
                down_grads[1][k * unit : (k + 1) * unit],
            )
            for k in range(ring)
        ]
    )
    ff_gathered = []
    for total in ff_sums:
        here, from_x, from_y, far_one, far_two = plane_gather(total)
        ff_gathered.append(jnp.stack([here, from_x, from_y, jnp.concatenate([far_one, far_two])]))

    def placed(mine, sib, axis):
        return jnp.concatenate(
            [by_row(picked(mine, plane_i ^ q), picked(sib, plane_i ^ q), axis) for q in range(4)], axis=axis
        ).astype(f32)

    up_weight_grad = placed(ff_gathered[0], ff_gathered[1], 1)
    down_weight_grad = placed(ff_gathered[2], ff_gathered[3], 0)

    normed_grad_one = normed_grad_one[:, :width] + swap(
        normed_grad_one[:, width:].astype(bf16)
    ).astype(f32)
    normed_grad_one = exchanged(normed_grad_one, plane_i, 1)
    normal_own = (tokens_own - average_one) * inverse_one
    scaled = normed_grad_one * norm1_gain
    mean_one, mean_two = both_sums(scaled, scaled * normal_own)
    back_one = inverse_one * (scaled - mean_one - normal_own * mean_two)
    gain_one_grad = jnp.sum(normed_grad_one * normal_own, axis=0)
    shift_one_grad = jnp.sum(normed_grad_one, axis=0)
    input_grad = out_grad.astype(f32) * (1.0 - keep_mask) + hidden_grad + back_one

    def by_column(relative):
        index = jnp.mod(col_i - jnp.arange(ring), ring)
        return jnp.take(relative, index, axis=0)

    row_hot = (jnp.arange(2) == row_i).astype(f32)
    plane_hot = (jnp.arange(4) == plane_i).astype(f32)
    head_bias = by_column(jnp.stack(bias_rows)).reshape(ring, 3, 1, own) * row_hot[:, None]
    up_bias_part = sum(jnp.sum(p.astype(f32), axis=0) for p in pre_grads).reshape(ring, unit)
    up_bias_part = by_column(up_bias_part).reshape(ring, 1, 1, unit)
    up_bias_part = up_bias_part * plane_hot[:, None, None] * row_hot[:, None]
    bias_vector = jnp.concatenate([head_bias.reshape(ring, -1), up_bias_part.reshape(ring, -1)], axis=1)
    bias_vector = bias_vector + swap(bias_vector)
    out_bias_part = jnp.sum(attention_grad.astype(f32), axis=0)
    down_bias_part = jnp.sum(branch_mine.astype(f32), axis=0)
    own_vector = jnp.concatenate(
        [gain_one_grad, shift_one_grad, gain_two_grad, shift_two_grad, out_bias_part, down_bias_part]
    )
    summed = butterfly_sum(jnp.concatenate([bias_vector.reshape(-1), own_vector]))
    bias_here = picked(summed[: bias_vector.size].reshape(ring, -1), col_i)
    own_here = summed[bias_vector.size :].reshape(6, width)
    size = 2 * own
    return (
        layer_out,
        input_grad,
        own_here[0],
        own_here[1],
        query_weight_grad,
        bias_here[:size],
        key_weight_grad,
        value_weight_grad,
        bias_here[2 * size : 3 * size],
        out_weight_grad,
        own_here[4],
        own_here[2],
        own_here[3],
        up_weight_grad,
        bias_here[3 * size :],
        down_weight_grad,
        own_here[5],
    )


def body(tokens_in, out_grad, segment_ids, *rest):
    ring = lax.axis_size("col")
    local = (
        lax.axis_size("dp") == 4
        and lax.axis_size("row") == 2
        and ring & (ring - 1) == 0
        and tokens_in.shape[0] == segment_ids.shape[1]
    )
    chosen = body_local if local else body_general
    return chosen(tokens_in, out_grad, segment_ids, *rest)


def solution(mesh):
    placed = (
        P(("dp", "col"), "row"),
        P(("dp", "col"), "row"),
        P("dp", None),
        P("dp", None),
        P("row"),
        P("row"),
        P("row", "col"),
        P("col"),
        P("row", "col"),
        P("row", "col"),
        P("col"),
        P("col", "row"),
        P("row"),
        P("row"),
        P("row"),
        P("row", "col"),
        P("col"),
        P("col", "row"),
        P("row"),
    )
    return jax.shard_map(
        body,
        mesh=mesh,
        in_specs=placed,
        out_specs=(
            P(("dp", "col"), "row"),
            P(("dp", "col"), "row"),
            P("row"),
            P("row"),
            P("row", "col"),
            P("col"),
            P("row", "col"),
            P("row", "col"),
            P("col"),
            P("col", "row"),
            P("row"),
            P("row"),
            P("row"),
            P("row", "col"),
            P("col"),
            P("col", "row"),
            P("row"),
        ),
        check_vma=False,
    )
```

```python
import functools

import jax
import jax.numpy as jnp
from jax import lax
from jax.experimental import pallas as pl
from jax.experimental.pallas import tpu as pltpu
from jax.sharding import PartitionSpec as P

D = 2048
HEAD_DIM = 64


norm_eps = 1e-05
masked_fill = -1e30


def width_totals(total_one, total_two):
    return lax.psum((total_one, total_two), "row")


def token_gather(values):
    return lax.all_gather(values, "col", axis=0, tiled=True)


def token_sums(partial_rows):
    return lax.psum_scatter(partial_rows, "col", scatter_dimension=0, tiled=True)


def unit_gather(values):
    return lax.all_gather(values, "row", axis=1, tiled=True)


def unit_sums(partial_units):
    return lax.psum_scatter(partial_units, "row", scatter_dimension=1, tiled=True)


def gelu_value(values):
    return jax.nn.gelu(values, approximate=True)


def gelu_slope(values):
    result, pullback = jax.vjp(gelu_value, values)
    return pullback(jnp.ones_like(values))[0]


def active_rows(segment_rows, keep_lengths):
    doc_index = jnp.arange(keep_lengths.shape[-1], dtype=jnp.int32)
    member = (segment_rows[:, :, None] == doc_index).astype(jnp.int32)
    counts = jnp.sum(member, axis=1)
    starts = jnp.cumsum(counts, axis=1) - counts
    first_pos = jnp.sum(member * starts[:, None, :], axis=2)
    keep_here = jnp.sum(member * keep_lengths[:, None, :], axis=2)
    position_in = jnp.arange(segment_rows.shape[1], dtype=jnp.int32)[None, :] - first_pos
    return (position_in < keep_here).reshape(-1)


def norm_forward(values, gain_part, shift_part):
    total_one, total_two = width_totals(jnp.sum(values, axis=1), jnp.sum(values * values, axis=1))
    average = total_one / D
    variance = total_two / D - average * average
    inverse = lax.rsqrt(variance + norm_eps)
    normal = (values - average[:, None]) * inverse[:, None]
    return ((normal * gain_part + shift_part).astype(jnp.bfloat16), normal, inverse)


def norm_backward(grad_rows, normal, inverse, gain_part):
    scaled = grad_rows * gain_part
    total_one, total_two = width_totals(jnp.sum(scaled, axis=1), jnp.sum(scaled * normal, axis=1))
    grad_in = inverse[:, None] * (
        scaled - total_one[:, None] / D - normal * (total_two[:, None] / D)
    )
    return (grad_in, jnp.sum(grad_rows * normal, axis=0), jnp.sum(grad_rows, axis=0))


def allowed_mask(segment_row, offset, block_rows):
    key_pos = jnp.arange(segment_row.shape[0], dtype=jnp.int32)
    query_pos = key_pos[offset : offset + block_rows]
    same_doc = segment_row[None, :] == segment_row[offset : offset + block_rows, None]
    return (key_pos[None, :] <= query_pos[:, None]) & same_doc


def attend_forward(query_seq, key_seq, value_seq, segment_row, score_scale):
    seq_length = query_seq.shape[2]
    block_rows = min(512, seq_length)
    outputs = []
    log_parts = []
    for offset in range(0, seq_length, block_rows):
        query_block = query_seq[:, :, offset : offset + block_rows]
        scores = (
            jnp.einsum("hdq,hdk->hqk", query_block, key_seq, preferred_element_type=jnp.float32)
            * score_scale
        )
        scores = jnp.where(allowed_mask(segment_row, offset, block_rows)[None], scores, masked_fill)
        row_max = jnp.max(scores, axis=2, keepdims=True)
        exp_scores = jnp.exp(scores - row_max)
        row_total = jnp.sum(exp_scores, axis=2, keepdims=True)
        weights = (exp_scores / row_total).astype(jnp.bfloat16)
        outputs.append(
            jnp.einsum("hqk,hdk->hdq", weights, value_seq, preferred_element_type=jnp.float32)
        )
        log_parts.append((row_max + jnp.log(row_total))[:, :, 0])
    return (jnp.concatenate(outputs, axis=2), jnp.concatenate(log_parts, axis=1))


def attend_backward(query_seq, key_seq, value_seq, grad_seq, segment_row, log_sums, score_scale):
    seq_length = query_seq.shape[2]
    block_rows = min(512, seq_length)
    key_grad = jnp.zeros(key_seq.shape, jnp.float32)
    value_grad = jnp.zeros(value_seq.shape, jnp.float32)
    query_grads = []
    for offset in range(0, seq_length, block_rows):
        query_block = query_seq[:, :, offset : offset + block_rows]
        grad_block = grad_seq[:, :, offset : offset + block_rows]
        scores = (
            jnp.einsum("hdq,hdk->hqk", query_block, key_seq, preferred_element_type=jnp.float32)
            * score_scale
        )
        scores = jnp.where(allowed_mask(segment_row, offset, block_rows)[None], scores, masked_fill)
        probs = jnp.exp(scores - log_sums[:, offset : offset + block_rows, None])
        prob_grad = jnp.einsum(
            "hdq,hdk->hqk", grad_block, value_seq, preferred_element_type=jnp.float32
        )
        row_dot = jnp.sum(probs * prob_grad, axis=2, keepdims=True)
        score_grad = (probs * (prob_grad - row_dot)).astype(jnp.bfloat16)
        query_grads.append(
            jnp.einsum("hqk,hdk->hdq", score_grad, key_seq, preferred_element_type=jnp.float32)
            * score_scale
        )
        key_grad = (
            key_grad
            + jnp.einsum(
                "hqk,hdq->hdk", score_grad, query_block, preferred_element_type=jnp.float32
            )
            * score_scale
        )
        value_grad = value_grad + jnp.einsum(
            "hqk,hdq->hdk",
            probs.astype(jnp.bfloat16),
            grad_block,
            preferred_element_type=jnp.float32,
        )
    return (jnp.concatenate(query_grads, axis=2), key_grad, value_grad)


def body_general(
    tokens_in,
    out_grad,
    segment_ids,
    active_lengths,
    norm1_gain,
    norm1_shift,
    query_weight,
    query_bias,
    key_weight,
    value_weight,
    value_bias,
    out_weight,
    out_bias,
    norm2_gain,
    norm2_shift,
    up_weight,
    up_bias,
    down_weight,
    down_bias,
):
    local_rows = tokens_in.shape[0]
    seq_here = segment_ids.shape[0]
    seq_length = segment_ids.shape[1]
    group_rows = seq_here * seq_length
    row_index = lax.axis_index("row")
    col_index = lax.axis_index("col")
    active_all = active_rows(segment_ids, active_lengths)
    active_here = lax.dynamic_slice_in_dim(active_all, col_index * local_rows, local_rows)
    keep_mask = active_here.astype(jnp.float32)[:, None]
    score_scale = HEAD_DIM ** (-0.5)
    rows_in = tokens_in.astype(jnp.float32)
    normed_one, normal_one, inverse_one = norm_forward(rows_in, norm1_gain, norm1_shift)
    gathered_one = token_gather(normed_one)
    stacked_weight = jnp.stack([query_weight, key_weight, value_weight])
    projected = unit_sums(
        jnp.einsum("td,kdh->kht", gathered_one, stacked_weight, preferred_element_type=jnp.float32)
    )
    head_width = projected.shape[1]
    head_count = head_width // HEAD_DIM
    query_part = lax.dynamic_slice_in_dim(query_bias, row_index * head_width, head_width)
    value_part = lax.dynamic_slice_in_dim(value_bias, row_index * head_width, head_width)
    bias_stack = jnp.stack([query_part, jnp.zeros_like(query_part), value_part])
    heads_all = (projected + bias_stack[:, :, None]).astype(jnp.bfloat16)

    def to_seqs(values):
        return jnp.moveaxis(values.reshape(head_count, HEAD_DIM, seq_here, seq_length), 2, 0)

    def from_seqs(values):
        return jnp.moveaxis(values, 0, 2).reshape(head_width, group_rows)

    query_seqs = to_seqs(heads_all[0])
    key_seqs = to_seqs(heads_all[1])
    value_seqs = to_seqs(heads_all[2])
    attended_seqs, log_sums = lax.map(
        lambda seq_items: attend_forward(
            seq_items[0], seq_items[1], seq_items[2], seq_items[3], score_scale
        ),
        (query_seqs, key_seqs, value_seqs, segment_ids),
    )
    attended = from_seqs(attended_seqs).astype(jnp.bfloat16)
    gathered_heads = unit_gather(attended[None])
    attention_rows = (
        token_sums(
            jnp.einsum("kht,hd->td", gathered_heads, out_weight, preferred_element_type=jnp.float32)
        )
        + out_bias
    )
    hidden_one = rows_in + attention_rows
    normed_two, normal_two, inverse_two = norm_forward(hidden_one, norm2_gain, norm2_shift)
    gathered_two = token_gather(normed_two)
    up_part = jnp.einsum("td,df->ft", gathered_two, up_weight, preferred_element_type=jnp.float32)[
        None
    ]
    unit_width = up_part.shape[1] // lax.axis_size("row")
    up_slice = lax.dynamic_slice_in_dim(up_bias, row_index * unit_width, unit_width)
    pre_act = unit_sums(up_part)[0] + up_slice[:, None]
    gathered_act = unit_gather(gelu_value(pre_act).astype(jnp.bfloat16)[None])
    ffn_rows = (
        token_sums(
            jnp.einsum("kft,fd->td", gathered_act, down_weight, preferred_element_type=jnp.float32)
        )
        + down_bias
    )
    layer_out = jnp.where(active_here[:, None], hidden_one + ffn_rows, rows_in)
    grad_rows = out_grad.astype(jnp.float32) * keep_mask
    branch_grad = token_gather(grad_rows.astype(jnp.bfloat16))
    down_grad = jnp.einsum(
        "kft,td->fd", gathered_act, branch_grad, preferred_element_type=jnp.float32
    )
    down_bias_grad = jnp.sum(branch_grad, axis=0, dtype=jnp.float32)
    act_part = jnp.einsum(
        "td,fd->ft", branch_grad, down_weight, preferred_element_type=jnp.float32
    )[None]
    act_grad = unit_sums(act_part)[0]
    pre_grad = (act_grad * gelu_slope(pre_act)).astype(jnp.bfloat16)
    gathered_pre = unit_gather(pre_grad[None])
    up_grad = jnp.einsum(
        "td,kft->df", gathered_two, gathered_pre, preferred_element_type=jnp.float32
    )
    up_bias_grad = jnp.sum(gathered_pre[0], axis=1, dtype=jnp.float32)
    normed_grad_two = token_sums(
        jnp.einsum("kft,df->td", gathered_pre, up_weight, preferred_element_type=jnp.float32)
    )
    back_two, gain_two_grad, shift_two_grad = norm_backward(
        normed_grad_two, normal_two, inverse_two, norm2_gain
    )
    hidden_grad = grad_rows + back_two
    attention_grad = token_gather(hidden_grad.astype(jnp.bfloat16))
    out_weight_grad = jnp.einsum(
        "kht,td->hd", gathered_heads, attention_grad, preferred_element_type=jnp.float32
    )
    out_bias_grad = jnp.sum(attention_grad, axis=0, dtype=jnp.float32)
    head_grad = unit_sums(
        jnp.einsum("td,hd->ht", attention_grad, out_weight, preferred_element_type=jnp.float32)[
            None
        ]
    )[0].astype(jnp.bfloat16)
    query_grads, key_grads, value_grads = lax.map(
        lambda seq_items: attend_backward(
            seq_items[0],
            seq_items[1],
            seq_items[2],
            seq_items[3],
            seq_items[4],
            seq_items[5],
            score_scale,
        ),
        (query_seqs, key_seqs, value_seqs, to_seqs(head_grad), segment_ids, log_sums),
    )
    stacked_grad = jnp.stack(
        [from_seqs(query_grads), from_seqs(key_grads), from_seqs(value_grads)]
    ).astype(jnp.bfloat16)
    gathered_grad = unit_gather(stacked_grad)
    stacked_weight_grad = jnp.einsum(
        "td,kht->kdh", gathered_one, gathered_grad, preferred_element_type=jnp.float32
    )
    query_bias_grad = jnp.sum(gathered_grad[0], axis=1, dtype=jnp.float32)
    value_bias_grad = jnp.sum(gathered_grad[2], axis=1, dtype=jnp.float32)
    normed_grad_one = token_sums(
        jnp.einsum("kht,kdh->td", gathered_grad, stacked_weight, preferred_element_type=jnp.float32)
    )
    back_one, gain_one_grad, shift_one_grad = norm_backward(
        normed_grad_one, normal_one, inverse_one, norm1_gain
    )
    input_grad = out_grad.astype(jnp.float32) * (1.0 - keep_mask) + hidden_grad + back_one
    (
        stacked_weight_grad,
        query_bias_grad,
        value_bias_grad,
        out_weight_grad,
        out_bias_grad,
        down_grad,
        down_bias_grad,
        up_grad,
        up_bias_grad,
    ) = lax.psum(
        (
            stacked_weight_grad,
            query_bias_grad,
            value_bias_grad,
            out_weight_grad,
            out_bias_grad,
            down_grad,
            down_bias_grad,
            up_grad,
            up_bias_grad,
        ),
        "dp",
    )
    gain_one_grad, shift_one_grad, gain_two_grad, shift_two_grad = lax.psum(
        (gain_one_grad, shift_one_grad, gain_two_grad, shift_two_grad), ("dp", "col")
    )
    return (
        layer_out,
        input_grad,
        gain_one_grad,
        shift_one_grad,
        stacked_weight_grad[0],
        query_bias_grad,
        stacked_weight_grad[1],
        stacked_weight_grad[2],
        value_bias_grad,
        out_weight_grad,
        out_bias_grad,
        gain_two_grad,
        shift_two_grad,
        up_grad,
        up_bias_grad,
        down_grad,
        down_bias_grad,
    )


def after(values, *others):
    return lax.optimization_barrier((values, others))[0]


def swap(values):
    return lax.ppermute(values, "row", [(0, 1), (1, 0)])


def step_x(values):
    return lax.ppermute(values, "dp", [(0, 1), (1, 0), (2, 3), (3, 2)])


def step_y(values):
    return lax.ppermute(values, "dp", [(0, 2), (2, 0), (1, 3), (3, 1)])


def step_up(values):
    count = lax.axis_size("col")
    return lax.ppermute(values, "col", [(i, (i + 1) % count) for i in range(count)])


def step_down(values):
    count = lax.axis_size("col")
    return lax.ppermute(values, "col", [(i, (i - 1) % count) for i in range(count)])


class Link:
    def __init__(self):
        self.last = None

    def send(self, step, values):
        if self.last is not None:
            values = after(values, self.last)
        self.last = step(values)
        return self.last


class Plane:
    def __init__(self):
        self.x = Link()
        self.y = Link()

    def near(self, values):
        return self.x.send(step_x, values), self.y.send(step_y, values)

    def far(self, from_x, from_y):
        half = from_x.shape[0] // 2
        far_one = self.y.send(step_y, from_x[:half])
        far_two = self.x.send(step_x, from_y[half:])
        return far_one, far_two

    def gather(self, values):
        from_x, from_y = self.near(values)
        return [values, from_x, from_y, *self.far(from_x, from_y)]

    def sum_early(self, here, to_x, to_y, to_far):
        half = here.shape[0] // 2
        f32 = jnp.float32
        x_top = self.x.send(step_x, to_x[:half])
        y_bottom = self.y.send(step_y, to_y[half:])
        via_x = self.x.send(step_x, to_far[:half])
        via_y = self.y.send(step_y, to_far[half:])
        x_bottom = self.x.send(step_x, add_rounded(to_x[half:], via_y))
        y_top = self.y.send(step_y, add_rounded(to_y[:half], via_x))
        top = here[:half].astype(f32) + x_top.astype(f32) + y_top.astype(f32)
        bottom = here[half:].astype(f32) + x_bottom.astype(f32) + y_bottom.astype(f32)
        return jnp.concatenate([top, bottom], axis=0)

    def sum_pairs(self, parts):
        f32 = jnp.float32
        here, to_x, to_y, to_far = parts
        via_x = self.x.send(step_x, to_far[0])
        via_y = self.y.send(step_y, to_far[1])
        for_x = jnp.concatenate([to_x[0], add_rounded(to_x[1], via_y)], axis=1)
        for_y = jnp.concatenate([add_rounded(to_y[0], via_x), to_y[1]], axis=1)
        from_x = self.x.send(step_x, for_x)
        from_y = self.y.send(step_y, for_y)
        return (
            jnp.concatenate(here, axis=1).astype(f32) + from_x.astype(f32) + from_y.astype(f32)
        ).astype(jnp.bfloat16)


def add_rounded(left, right):
    return (left.astype(jnp.float32) + right.astype(jnp.float32)).astype(jnp.bfloat16)


def ring_gather(link, values):
    held = [values]
    for _ in range(lax.axis_size("col") - 1):
        held.append(link.send(step_up, held[-1]))
    return held


def ring_sum(link, blocks):
    total = blocks[-1]
    for block in blocks[-2::-1]:
        total = add_rounded(link.send(step_down, total), block)
    return total


def butterfly_sum(values):
    count = lax.axis_size("col")
    values = values + step_x(values)
    values = values + step_y(values)
    step = 1
    while step < count:
        values = values + lax.ppermute(values, "col", [(i, i ^ step) for i in range(count)])
        step *= 2
    return values


def picked(stacked, index):
    return lax.dynamic_index_in_dim(stacked, index, 0, keepdims=False)


def exchanged(values, index, axis):
    size = values.shape[axis] // 4
    return jnp.concatenate(
        [
            lax.dynamic_slice_in_dim(values, jnp.bitwise_xor(index, i) * size, size, axis=axis)
            for i in range(4)
        ],
        axis=axis,
    )


def row_norm(values):
    average = jnp.mean(values, axis=1, keepdims=True)
    centered = values - average
    inverse = lax.rsqrt(jnp.mean(centered * centered, axis=1, keepdims=True) + norm_eps)
    return (average, inverse)


def mm(left, right, left_dim, right_dim, dtype=jnp.float32):
    return lax.dot_general(
        left, right, (((left_dim,), (right_dim,)), ((), ())), preferred_element_type=jnp.float32
    ).astype(dtype)


PAIR = 2 * HEAD_DIM
vmem_bytes = 48 * 1024 * 1024


def head_lanes(head, value):
    lane = lax.broadcasted_iota(jnp.int32, (1, PAIR), 1)
    return jnp.where(lane // HEAD_DIM == head, value, 0.0).astype(jnp.bfloat16)


def allowed_keys(first_row, low, high):
    key_pos = lax.broadcasted_iota(jnp.int32, (high, high - low), 0)
    query_pos = lax.broadcasted_iota(jnp.int32, (high, high - low), 1) + low
    return (key_pos >= first_row) & (key_pos <= query_pos)


def local_forward_kernel(size, first_ref, query_ref, key_ref, value_ref, out_ref):
    lane = lax.broadcasted_iota(jnp.int32, (size, PAIR), 1)
    for low in range(0, key_ref.shape[0], size):
        high = low + size
        keys = key_ref[:high, :]
        values = value_ref[:high, :]
        queries = query_ref[low:high, :]
        allowed = allowed_keys(first_ref[:, low:high], low, high)
        results = []
        for head in range(2):
            scores = mm(keys, queries * head_lanes(head, HEAD_DIM ** (-0.5)), 1, 1)
            scores = jnp.where(allowed, scores, masked_fill)
            exp_scores = jnp.exp(scores - jnp.max(scores, axis=0, keepdims=True))
            inverse = 1.0 / jnp.sum(exp_scores, axis=0, keepdims=True)
            results.append(mm((exp_scores * inverse).astype(jnp.bfloat16), values, 0, 0))
        out_ref[low:high, :] = jnp.where(lane < HEAD_DIM, results[0], results[1]).astype(
            jnp.bfloat16
        )


def local_forward(heads, first_row):
    length = heads.shape[0]
    pairs = heads.shape[1] // (3 * PAIR)
    return pl.pallas_call(
        functools.partial(local_forward_kernel, min(256, length)),
        grid=(pairs,),
        in_specs=[
            pl.BlockSpec((1, length), lambda p: (0, 0)),
            pl.BlockSpec((length, PAIR), lambda p: (0, p)),
            pl.BlockSpec((length, PAIR), lambda p: (0, pairs + p)),
            pl.BlockSpec((length, PAIR), lambda p: (0, 2 * pairs + p)),
        ],
        out_specs=pl.BlockSpec((length, PAIR), lambda p: (0, p)),
        out_shape=jax.ShapeDtypeStruct((length, pairs * PAIR), jnp.bfloat16),
        compiler_params=pltpu.CompilerParams(vmem_limit_bytes=vmem_bytes),
        cost_estimate=pl.CostEstimate(
            flops=16 * length * length * pairs * PAIR, bytes_accessed=8 * heads.size, transcendentals=0
        ),
    )(first_row, heads, heads, heads)


def local_backward_kernel(
    size, first_ref, query_ref, grad_ref, key_ref, value_ref, out_ref, key_sum, value_sum
):
    length = key_ref.shape[0]
    pair = pl.program_id(0)
    pairs = out_ref.shape[1] // (3 * PAIR)
    scale = HEAD_DIM ** (-0.5)
    lane = lax.broadcasted_iota(jnp.int32, (size, PAIR), 1)

    def lanes(part):
        return pl.ds(pl.multiple_of((part * pairs + pair) * PAIR, PAIR), PAIR)

    for low in range(length - size, -1, -size):
        high = low + size
        keys = key_ref[:high, :]
        values = value_ref[:high, :]
        queries = query_ref[low:high, :]
        grads = grad_ref[low:high, :]
        allowed = allowed_keys(first_ref[:, low:high], low, high)
        query_grads = []
        for head in range(2):
            scaled = queries * head_lanes(head, scale)
            grad = grads * head_lanes(head, 1.0)
            scores = jnp.where(allowed, mm(keys, scaled, 1, 1), masked_fill)
            exp_scores = jnp.exp(scores - jnp.max(scores, axis=0, keepdims=True))
            probs = exp_scores * (1.0 / jnp.sum(exp_scores, axis=0, keepdims=True))
            prob_grad = mm(values, grad, 1, 1)
            row_dot = jnp.sum(probs * prob_grad, axis=0, keepdims=True)
            score_grad = (probs * (prob_grad - row_dot)).astype(jnp.bfloat16)
            value_part = mm(probs.astype(jnp.bfloat16), grad, 1, 0)
            key_part = mm(score_grad, scaled, 1, 0)
            query_grads.append(mm(score_grad, keys, 0, 0) * scale)
            if head == 0:
                key_add, value_add = key_part, value_part
            else:
                key_add, value_add = key_add + key_part, value_add + value_part
        if high == length:
            key_sum[...] = key_add
            value_sum[...] = value_add
        else:
            key_sum[:high, :] += key_add
            value_sum[:high, :] += value_add
        out_ref[low:high, lanes(0)] = jnp.where(
            lane < HEAD_DIM, query_grads[0], query_grads[1]
        ).astype(jnp.bfloat16)
    out_ref[:, lanes(1)] = key_sum[...].astype(jnp.bfloat16)
    out_ref[:, lanes(2)] = value_sum[...].astype(jnp.bfloat16)


def local_backward(heads, head_grad, first_row):
    length = heads.shape[0]
    pairs = heads.shape[1] // (3 * PAIR)
    return pl.pallas_call(
        functools.partial(local_backward_kernel, min(512, length)),
        grid=(pairs,),
        in_specs=[
            pl.BlockSpec((1, length), lambda p: (0, 0)),
            pl.BlockSpec((length, PAIR), lambda p: (0, p)),
            pl.BlockSpec((length, PAIR), lambda p: (0, p)),
            pl.BlockSpec((length, PAIR), lambda p: (0, pairs + p)),
            pl.BlockSpec((length, PAIR), lambda p: (0, 2 * pairs + p)),
        ],
        out_specs=pl.BlockSpec(heads.shape, lambda p: (0, 0)),
        out_shape=jax.ShapeDtypeStruct(heads.shape, jnp.bfloat16),
        scratch_shapes=[pltpu.VMEM((length, PAIR), jnp.float32)] * 2,
        compiler_params=pltpu.CompilerParams(vmem_limit_bytes=vmem_bytes),
        cost_estimate=pl.CostEstimate(
            flops=32 * length * length * pairs * PAIR, bytes_accessed=8 * heads.size, transcendentals=0
        ),
    )(first_row, heads, head_grad, heads, heads)


gelu_scale = 0.7978845608028654
gelu_cubic = 0.044715


def ffn_kernel(*refs):
    normed_own, normed_sib, grad_own, grad_sib = [r[...] for r in refs[:4]]
    count = (len(refs) - 7) // 2
    own_pieces, sib_pieces = refs[4 : 4 + count], refs[4 + count : 4 + 2 * count]
    bias_ref, out_ref, sum_ref = refs[-3:]
    unit = own_pieces[0].shape[1] // 2
    units = unit * count

    @pl.when(pl.program_id(0) == 0)
    def _():
        sum_ref[...] = jnp.zeros_like(sum_ref)

    for k in range(count):
        own_piece, sib_piece = own_pieces[k], sib_pieces[k]
        span = slice(k * unit, (k + 1) * unit)
        pre = mm(normed_own, own_piece[:, :unit], 1, 0) + mm(normed_sib, sib_piece[:, :unit], 1, 0)
        act_grad = mm(grad_own, own_piece[:, unit:], 1, 0) + mm(grad_sib, sib_piece[:, unit:], 1, 0)
        pre = pre + bias_ref[:, span]
        square = pre * pre
        bent = jnp.tanh(gelu_scale * pre * (1.0 + gelu_cubic * square))
        half = 0.5 * (1.0 + bent)
        slope = half + 0.5 * gelu_scale * pre * (1.0 - bent * bent) * (1.0 + 3.0 * gelu_cubic * square)
        pre_grad = (act_grad * slope).astype(jnp.bfloat16)
        out_ref[:, span] = (pre * half).astype(jnp.bfloat16)
        out_ref[:, units + k * unit : units + (k + 1) * unit] = pre_grad
        sum_ref[:, span] += jnp.sum(pre_grad.astype(jnp.float32), axis=0, keepdims=True)


def ffn_rows_of(normed, grad, own_pieces, sib_pieces, bias):
    tokens, width = normed[0].shape
    count = len(own_pieces)
    unit = sib_pieces[0].shape[1] // 2
    units = unit * count
    size = min(256, tokens)
    rows = pl.BlockSpec((size, width), lambda i: (i, 0))
    piece = pl.BlockSpec((width, 2 * unit), lambda i: (0, 0))
    return pl.pallas_call(
        ffn_kernel,
        grid=(tokens // size,),
        in_specs=[rows] * 4 + [piece] * (2 * count) + [pl.BlockSpec((1, units), lambda i: (0, 0))],
        out_specs=[
            pl.BlockSpec((size, 2 * units), lambda i: (i, 0)),
            pl.BlockSpec((1, units), lambda i: (0, 0)),
        ],
        out_shape=[
            jax.ShapeDtypeStruct((tokens, 2 * units), jnp.bfloat16),
            jax.ShapeDtypeStruct((1, units), jnp.float32),
        ],
        compiler_params=pltpu.CompilerParams(vmem_limit_bytes=vmem_bytes),
        cost_estimate=pl.CostEstimate(
            flops=8 * tokens * width * units,
            bytes_accessed=8 * tokens * width + 8 * width * units + 4 * tokens * units,
            transcendentals=0,
        ),
    )(*normed, *grad, *own_pieces, *sib_pieces, bias)


def unit_products_kernel(offset, own_ref, sib_ref, *refs):
    out_ref = refs[-1]
    unit = refs[0].shape[1] // 4
    total = None
    for k, piece in enumerate(refs[:-1]):
        span = slice(k * unit, (k + 1) * unit)
        for rows, start in ((own_ref, offset * unit), (sib_ref, (offset + 2) * unit)):
            part = mm(rows[:, span], piece[:, start : start + unit], 1, 1)
            total = part if total is None else total + part
    out_ref[...] = total.astype(jnp.bfloat16)


def unit_products(own_rows, sib_rows, pieces, which):
    tokens, twice = own_rows.shape
    width = pieces[0].shape[0]
    units = twice // 2
    size = min(256, tokens)
    rows = pl.BlockSpec((size, units), lambda i: (i, which))
    piece = pl.BlockSpec(pieces[0].shape, lambda i: (0, 0))
    return pl.pallas_call(
        functools.partial(unit_products_kernel, 1 - which),
        grid=(tokens // size,),
        in_specs=[rows] * 2 + [piece] * len(pieces),
        out_specs=pl.BlockSpec((size, width), lambda i: (i, 0)),
        out_shape=jax.ShapeDtypeStruct((tokens, width), jnp.bfloat16),
        compiler_params=pltpu.CompilerParams(vmem_limit_bytes=vmem_bytes),
        cost_estimate=pl.CostEstimate(
            flops=4 * tokens * units * width,
            bytes_accessed=6 * tokens * units + 4 * units * width,
            transcendentals=0,
        ),
    )(own_rows, sib_rows, *pieces)


def weight_products_kernel(count, *refs):
    out_ref = refs[-1]
    normed, grads = refs[:count], refs[count : 2 * count]
    act_own, pre_own, act_sib, pre_sib = [
        refs[(2 + i) * count : (3 + i) * count] for i in range(4)
    ]
    unit = act_own[0].shape[1]
    up = down = None
    for j in range(count):
        pre = jnp.concatenate([pre_own[j][...], pre_sib[j][...]], axis=1)
        act = jnp.concatenate([act_own[j][...], act_sib[j][...]], axis=1)
        up_part = mm(normed[j][...], pre, 0, 0)
        down_part = mm(grads[j][...], act, 0, 0)
        up = up_part if up is None else up + up_part
        down = down_part if down is None else down + down_part
    for i, part in enumerate((up[:, :unit], down[:, :unit], up[:, unit:], down[:, unit:])):
        out_ref[0, :, i * unit : (i + 1) * unit] = part.astype(jnp.bfloat16)


def weight_products(normed, grads, own_rows, sib_rows, unit):
    count = len(normed)
    tokens, width = normed[0].shape
    ring = own_rows[0].shape[1] // (2 * unit)
    size = min(256, width)
    left = [pl.BlockSpec((tokens, size), lambda k, d: (0, d))] * (2 * count)
    act = [pl.BlockSpec((tokens, unit), lambda k, d: (0, k))] * count
    pre = [pl.BlockSpec((tokens, unit), lambda k, d: (0, ring + k))] * count
    return pl.pallas_call(
        functools.partial(weight_products_kernel, count),
        grid=(ring, width // size),
        in_specs=left + act + pre + act + pre,
        out_specs=pl.BlockSpec((1, size, 4 * unit), lambda k, d: (k, d, 0)),
        out_shape=jax.ShapeDtypeStruct((ring, width, 4 * unit), jnp.bfloat16),
        compiler_params=pltpu.CompilerParams(vmem_limit_bytes=vmem_bytes),
        cost_estimate=pl.CostEstimate(
            flops=8 * count * tokens * width * ring * unit,
            bytes_accessed=16 * count * tokens * width,
            transcendentals=0,
        ),
    )(*normed, *grads, *own_rows, *own_rows, *sib_rows, *sib_rows)


def body_local(
    tokens_in,
    out_grad,
    segment_ids,
    active_lengths,
    norm1_gain,
    norm1_shift,
    query_weight,
    query_bias,
    key_weight,
    value_weight,
    value_bias,
    out_weight,
    out_bias,
    norm2_gain,
    norm2_shift,
    up_weight,
    up_bias,
    down_weight,
    down_bias,
):
    f32, bf16 = jnp.float32, jnp.bfloat16
    rows, width = tokens_in.shape
    ring = lax.axis_size("col")
    row_i = lax.axis_index("row")
    plane_i = lax.axis_index("dp")
    col_i = lax.axis_index("col")
    own = query_weight.shape[1] // 2
    block = width // 4
    quarter = up_weight.shape[1] // 4
    unit = quarter // 2
    half_rows = rows // 2
    plane, column = Plane(), Link()
    both_cores = (row_i, 1 - row_i)

    def cut(weight, start, size, axis):
        return lax.dynamic_slice_in_dim(weight, start, size, axis=axis)

    def by_core(weights, size):
        return jnp.concatenate(
            [cut(w, which * size, size, 1) for which in both_cores for w in weights], axis=1
        )

    names = (query_weight, key_weight, value_weight)
    piece = [cut(w, plane_i * block, block, 0) for w in names]
    piece.append(cut(out_weight, plane_i * block, block, 1).T)
    pieces = ring_gather(column, by_core(piece, own))

    active_all = active_rows(segment_ids, active_lengths)
    active_here = lax.dynamic_slice_in_dim(active_all, col_i * rows, rows)
    keep_mask = active_here.astype(f32)[:, None]
    branch_mine = (out_grad.astype(f32) * keep_mask).astype(bf16)
    branch_first = plane.near(branch_mine[:half_rows])

    tokens_sib = swap(tokens_in)
    gains = jnp.stack([norm1_gain, norm1_shift])
    gains_sib = swap(gains)

    segment_row = picked(segment_ids, col_i)
    member = (segment_row[:, None] == jnp.arange(active_lengths.shape[1])).astype(jnp.int32)
    counts = jnp.sum(member, axis=0)
    first_row = jnp.sum(member * (jnp.cumsum(counts) - counts), axis=1)[None, :]

    ff_offset = plane_i * quarter
    query_part = cut(query_bias, row_i * own, own, 0)
    value_part = cut(value_bias, row_i * own, own, 0)
    up_part = cut(up_bias, ff_offset + row_i * unit, unit, 0)
    small = ring_gather(
        Link(), jnp.concatenate([query_part, jnp.zeros_like(query_part), value_part, up_part])
    )
    up_biases = jnp.concatenate([s[3 * own :] for s in small])[None, :]

    here = by_core(names + (out_weight.T,), own)
    here = exchanged(here, plane_i, 0)
    own_rows, other_units = [here[:, : 4 * own]], [here[:, 4 * own :]]
    for piece in pieces[1:]:
        gathered = plane.gather(piece)
        own_rows.append(jnp.concatenate([p[:, : 4 * own] for p in gathered], axis=0))
        other_units.append(jnp.concatenate([p[:, 4 * own :] for p in gathered], axis=0))
    groups = [jnp.concatenate([a, swap(b)], axis=0) for a, b in zip(own_rows, other_units)]

    branch_far = plane.far(*branch_first)
    branch_second = plane.gather(branch_mine[half_rows:])
    branch_first = [branch_mine[:half_rows], *branch_first, jnp.concatenate(branch_far, axis=0)]
    branch_second = branch_second[:3] + [jnp.concatenate(branch_second[3:], axis=0)]
    branch_own = [branch_mine] + [
        jnp.concatenate([a, b], axis=0) for a, b in zip(branch_first[1:], branch_second[1:])
    ]
    branch_sib = [swap(b) for b in branch_own]

    down_part = cut(down_weight, ff_offset, quarter, 0).T
    up_part = cut(up_weight, ff_offset, quarter, 1)
    ff_own = ring_gather(column, by_core((up_part, down_part), unit))
    ff_sib = [swap(p[:, 2 * unit :]) for p in ff_own]

    tokens_own = tokens_in.astype(f32)
    tokens_all = jnp.concatenate([tokens_own, tokens_sib.astype(f32)], axis=1)
    average_one, inverse_one = row_norm(tokens_all)
    normed_one = jnp.concatenate(
        [
            exchanged((((t - average_one) * inverse_one) * g[0] + g[1]).astype(bf16), plane_i, 1)
            for t, g in ((tokens_own, gains), (tokens_sib.astype(f32), gains_sib))
        ],
        axis=1,
    )
    heads, attended = [], []
    attention_rows = None
    for k in range(ring):
        weights = groups[k]
        head = (mm(normed_one, weights[:, : 3 * own], 1, 0) + small[k][: 3 * own]).astype(bf16)
        result = local_forward(head, first_row)
        heads.append(head)
        attended.append(result)
        both = jnp.concatenate([result, swap(result)], axis=1)
        out_both = jnp.concatenate([own_rows[k][:, 3 * own :], other_units[k][:, 3 * own :]], axis=1)
        part = mm(both, out_both, 1, 1)
        attention_rows = part if k == 0 else attention_rows + part
    hidden_one = tokens_own + exchanged(attention_rows, plane_i, 1) + out_bias

    half_mean = jnp.mean(hidden_one, axis=1, keepdims=True)
    centered = hidden_one - half_mean
    half_square = jnp.mean(centered * centered, axis=1, keepdims=True)
    half_stats = jnp.concatenate([half_mean, half_square], axis=1).T
    other_stats = swap(half_stats)
    gap = half_stats[0] - other_stats[0]
    average_two = (0.5 * (half_stats[0] + other_stats[0]))[:, None]
    variance_two = (0.5 * (half_stats[1] + other_stats[1]) + 0.25 * gap * gap)[:, None]
    inverse_two = lax.rsqrt(variance_two + norm_eps)
    normal_two = (hidden_one - average_two) * inverse_two
    normed_two = (normal_two * norm2_gain + norm2_shift).astype(bf16)

    normed_own = plane.gather(normed_two)
    normed_own = normed_own[:3] + [jnp.concatenate(normed_own[3:], axis=0)]
    chips, chip_sibs, up_sums = [], [], []
    for j in range(4):
        normed = (normed_own[j], swap(normed_own[j]))
        if j > 0:
            normed = after(normed, chips[-1])
        chip, up_sum = ffn_rows_of(normed, (branch_own[j], branch_sib[j]), ff_own, ff_sib, up_biases)
        chips.append(chip)
        chip_sibs.append(swap(chip))
        up_sums.append(up_sum)
    grad_parts = [None] * 4
    last = chips[3]
    for j in (1, 2, 3, 0):
        grad_parts[j] = unit_products(after(chips[j], last), chip_sibs[j], ff_own, 1)
        last = grad_parts[j]
    normed_grad_two = plane.sum_early(*grad_parts)
    down_parts = [None] * 4
    for j in (1, 2, 3, 0):
        down_parts[j] = unit_products(after(chips[j], last), chip_sibs[j], ff_own, 0)
        last = down_parts[j]
    ff_grads = weight_products(normed_own, branch_own, [after(chips[0], last)] + chips[1:], chip_sibs, unit)
    ff_sum = ring_sum(column, [ff_grads[k] for k in range(ring)])
    ffn_rows = plane.sum_early(*down_parts) + down_bias
    layer_out = jnp.where(active_here[:, None], hidden_one + ffn_rows, tokens_own)

    def both_sums(one, two):
        sums = jnp.stack([jnp.sum(one, axis=1), jnp.sum(two, axis=1)])
        sums = (sums + swap(sums)) / (2 * width)
        return sums[0][:, None], sums[1][:, None]

    scaled = normed_grad_two * norm2_gain
    mean_one, mean_two = both_sums(scaled, scaled * normal_two)
    hidden_grad = branch_mine.astype(f32) + inverse_two * (scaled - mean_one - normal_two * mean_two)
    attention_grad = hidden_grad.astype(bf16)
    gain_two_grad = jnp.sum(normed_grad_two * normal_two, axis=0)
    shift_two_grad = jnp.sum(normed_grad_two, axis=0)

    grad_blocks = exchanged(attention_grad, plane_i, 1)
    grad_blocks = jnp.concatenate([grad_blocks, swap(grad_blocks)], axis=1)
    reduced = [None] * ring
    normed_grad_one = None
    bias_rows = [None] * ring
    last = grad_blocks
    for k in range(ring - 1, -1, -1):
        weights = groups[k]
        head_grad = mm(after(grad_blocks, last), weights[:, 3 * own :], 1, 0, bf16)
        grads = local_backward(heads[k], head_grad, first_row)
        weight_grads = jnp.concatenate(
            [mm(normed_one, grads, 0, 0, bf16), mm(grad_blocks, attended[k], 0, 0, bf16)], axis=1
        )
        last = weight_grads
        mine = weight_grads[:width]
        arrived = swap(weight_grads[width:])
        reduced[k] = plane.sum_pairs(
            [[m[j * block : (j + 1) * block] for m in (mine, arrived)] for j in range(4)]
        )
        bias_rows[k] = jnp.sum(grads.astype(f32), axis=0)
        part = mm(grads, weights[:, : 3 * own], 1, 1)
        normed_grad_one = part if normed_grad_one is None else normed_grad_one + part
    head_sum = ring_sum(column, reduced)
    head_all = exchanged(jnp.concatenate(plane.gather(head_sum), axis=0), plane_i, 0)

    def by_row(mine, sib, axis):
        return jnp.where(
            row_i == 0,
            jnp.concatenate([mine, sib], axis=axis),
            jnp.concatenate([sib, mine], axis=axis),
        )

    query_weight_grad, key_weight_grad, value_weight_grad, out_weight_grad = [
        by_row(head_all[:, m * own : (m + 1) * own], head_all[:, (4 + m) * own : (5 + m) * own], 1).astype(f32)
        for m in range(4)
    ]
    out_weight_grad = out_weight_grad.T

    ff_all = plane.gather(ff_sum)
    ff_all = jnp.stack(ff_all[:3] + [jnp.concatenate(ff_all[3:], axis=0)])
    up_parts, down_cuts = [], []
    for q in range(4):
        part = picked(ff_all, plane_i ^ q)
        up_parts.append(by_row(part[:, :unit], part[:, 2 * unit : 3 * unit], 1))
        down_cuts.append(by_row(part[:, unit : 2 * unit], part[:, 3 * unit :], 1))
    up_weight_grad = jnp.concatenate(up_parts, axis=1).astype(f32)
    down_weight_grad = jnp.concatenate(down_cuts, axis=1).T.astype(f32)

    normed_grad_one = normed_grad_one[:, :width] + swap(
        normed_grad_one[:, width:].astype(bf16)
    ).astype(f32)
    normed_grad_one = exchanged(normed_grad_one, plane_i, 1)
    normal_own = (tokens_own - average_one) * inverse_one
    scaled = normed_grad_one * norm1_gain
    mean_one, mean_two = both_sums(scaled, scaled * normal_own)
    back_one = inverse_one * (scaled - mean_one - normal_own * mean_two)
    gain_one_grad = jnp.sum(normed_grad_one * normal_own, axis=0)
    shift_one_grad = jnp.sum(normed_grad_one, axis=0)
    input_grad = out_grad.astype(f32) * (1.0 - keep_mask) + hidden_grad + back_one

    def by_column(relative):
        index = jnp.mod(col_i - jnp.arange(ring), ring)
        return jnp.take(relative, index, axis=0)

    row_hot = (jnp.arange(2) == row_i).astype(f32)
    plane_hot = (jnp.arange(4) == plane_i).astype(f32)
    head_bias = by_column(jnp.stack(bias_rows)).reshape(ring, 3, 1, own) * row_hot[:, None]
    up_bias_part = by_column(sum(up_sums).reshape(ring, unit)).reshape(ring, 1, 1, unit)
    up_bias_part = up_bias_part * plane_hot[:, None, None] * row_hot[:, None]
    bias_vector = jnp.concatenate([head_bias.reshape(ring, -1), up_bias_part.reshape(ring, -1)], axis=1)
    bias_vector = bias_vector + swap(bias_vector)
    out_bias_part = jnp.sum(attention_grad.astype(f32), axis=0)
    down_bias_part = jnp.sum(branch_mine.astype(f32), axis=0)
    own_vector = jnp.concatenate(
        [gain_one_grad, shift_one_grad, gain_two_grad, shift_two_grad, out_bias_part, down_bias_part]
    )
    summed = butterfly_sum(jnp.concatenate([bias_vector.reshape(-1), own_vector]))
    bias_here = picked(summed[: bias_vector.size].reshape(ring, -1), col_i)
    own_here = summed[bias_vector.size :].reshape(6, width)
    size = 2 * own
    return (
        layer_out,
        input_grad,
        own_here[0],
        own_here[1],
        query_weight_grad,
        bias_here[:size],
        key_weight_grad,
        value_weight_grad,
        bias_here[2 * size : 3 * size],
        out_weight_grad,
        own_here[4],
        own_here[2],
        own_here[3],
        up_weight_grad,
        bias_here[3 * size :],
        down_weight_grad,
        own_here[5],
    )


def body(tokens_in, out_grad, segment_ids, *rest):
    ring = lax.axis_size("col")
    local = (
        lax.axis_size("dp") == 4
        and lax.axis_size("row") == 2
        and ring & (ring - 1) == 0
        and tokens_in.shape[0] == segment_ids.shape[1]
    )
    chosen = body_local if local else body_general
    return chosen(tokens_in, out_grad, segment_ids, *rest)


def solution(mesh):
    placed = (
        P(("dp", "col"), "row"),
        P(("dp", "col"), "row"),
        P("dp", None),
        P("dp", None),
        P("row"),
        P("row"),
        P("row", "col"),
        P("col"),
        P("row", "col"),
        P("row", "col"),
        P("col"),
        P("col", "row"),
        P("row"),
        P("row"),
        P("row"),
        P("row", "col"),
        P("col"),
        P("col", "row"),
        P("row"),
    )
    return jax.shard_map(
        body,
        mesh=mesh,
        in_specs=placed,
        out_specs=(
            P(("dp", "col"), "row"),
            P(("dp", "col"), "row"),
            P("row"),
            P("row"),
            P("row", "col"),
            P("col"),
            P("row", "col"),
            P("row", "col"),
            P("col"),
            P("col", "row"),
            P("row"),
            P("row"),
            P("row"),
            P("row", "col"),
            P("col"),
            P("col", "row"),
            P("row"),
        ),
        check_vma=False,
    )
```

```python
import functools

import jax
import jax.numpy as jnp
from jax import lax
from jax.experimental import pallas as pl
from jax.experimental.pallas import tpu as pltpu
from jax.sharding import PartitionSpec as P

D = 2048
HEAD_DIM = 64


norm_eps = 1e-05
masked_fill = -1e30


def width_totals(total_one, total_two):
    return lax.psum((total_one, total_two), "row")


def token_gather(values):
    return lax.all_gather(values, "col", axis=0, tiled=True)


def token_sums(partial_rows):
    return lax.psum_scatter(partial_rows, "col", scatter_dimension=0, tiled=True)


def unit_gather(values):
    return lax.all_gather(values, "row", axis=1, tiled=True)


def unit_sums(partial_units):
    return lax.psum_scatter(partial_units, "row", scatter_dimension=1, tiled=True)


def gelu_value(values):
    return jax.nn.gelu(values, approximate=True)


def gelu_slope(values):
    result, pullback = jax.vjp(gelu_value, values)
    return pullback(jnp.ones_like(values))[0]


def active_rows(segment_rows, keep_lengths):
    doc_index = jnp.arange(keep_lengths.shape[-1], dtype=jnp.int32)
    member = (segment_rows[:, :, None] == doc_index).astype(jnp.int32)
    counts = jnp.sum(member, axis=1)
    starts = jnp.cumsum(counts, axis=1) - counts
    first_pos = jnp.sum(member * starts[:, None, :], axis=2)
    keep_here = jnp.sum(member * keep_lengths[:, None, :], axis=2)
    position_in = jnp.arange(segment_rows.shape[1], dtype=jnp.int32)[None, :] - first_pos
    return (position_in < keep_here).reshape(-1)


def norm_forward(values, gain_part, shift_part):
    total_one, total_two = width_totals(jnp.sum(values, axis=1), jnp.sum(values * values, axis=1))
    average = total_one / D
    variance = total_two / D - average * average
    inverse = lax.rsqrt(variance + norm_eps)
    normal = (values - average[:, None]) * inverse[:, None]
    return ((normal * gain_part + shift_part).astype(jnp.bfloat16), normal, inverse)


def norm_backward(grad_rows, normal, inverse, gain_part):
    scaled = grad_rows * gain_part
    total_one, total_two = width_totals(jnp.sum(scaled, axis=1), jnp.sum(scaled * normal, axis=1))
    grad_in = inverse[:, None] * (
        scaled - total_one[:, None] / D - normal * (total_two[:, None] / D)
    )
    return (grad_in, jnp.sum(grad_rows * normal, axis=0), jnp.sum(grad_rows, axis=0))


def allowed_mask(segment_row, offset, block_rows):
    key_pos = jnp.arange(segment_row.shape[0], dtype=jnp.int32)
    query_pos = key_pos[offset : offset + block_rows]
    same_doc = segment_row[None, :] == segment_row[offset : offset + block_rows, None]
    return (key_pos[None, :] <= query_pos[:, None]) & same_doc


def attend_forward(query_seq, key_seq, value_seq, segment_row, score_scale):
    seq_length = query_seq.shape[2]
    block_rows = min(512, seq_length)
    outputs = []
    log_parts = []
    for offset in range(0, seq_length, block_rows):
        query_block = query_seq[:, :, offset : offset + block_rows]
        scores = (
            jnp.einsum("hdq,hdk->hqk", query_block, key_seq, preferred_element_type=jnp.float32)
            * score_scale
        )
        scores = jnp.where(allowed_mask(segment_row, offset, block_rows)[None], scores, masked_fill)
        row_max = jnp.max(scores, axis=2, keepdims=True)
        exp_scores = jnp.exp(scores - row_max)
        row_total = jnp.sum(exp_scores, axis=2, keepdims=True)
        weights = (exp_scores / row_total).astype(jnp.bfloat16)
        outputs.append(
            jnp.einsum("hqk,hdk->hdq", weights, value_seq, preferred_element_type=jnp.float32)
        )
        log_parts.append((row_max + jnp.log(row_total))[:, :, 0])
    return (jnp.concatenate(outputs, axis=2), jnp.concatenate(log_parts, axis=1))


def attend_backward(query_seq, key_seq, value_seq, grad_seq, segment_row, log_sums, score_scale):
    seq_length = query_seq.shape[2]
    block_rows = min(512, seq_length)
    key_grad = jnp.zeros(key_seq.shape, jnp.float32)
    value_grad = jnp.zeros(value_seq.shape, jnp.float32)
    query_grads = []
    for offset in range(0, seq_length, block_rows):
        query_block = query_seq[:, :, offset : offset + block_rows]
        grad_block = grad_seq[:, :, offset : offset + block_rows]
        scores = (
            jnp.einsum("hdq,hdk->hqk", query_block, key_seq, preferred_element_type=jnp.float32)
            * score_scale
        )
        scores = jnp.where(allowed_mask(segment_row, offset, block_rows)[None], scores, masked_fill)
        probs = jnp.exp(scores - log_sums[:, offset : offset + block_rows, None])
        prob_grad = jnp.einsum(
            "hdq,hdk->hqk", grad_block, value_seq, preferred_element_type=jnp.float32
        )
        row_dot = jnp.sum(probs * prob_grad, axis=2, keepdims=True)
        score_grad = (probs * (prob_grad - row_dot)).astype(jnp.bfloat16)
        query_grads.append(
            jnp.einsum("hqk,hdk->hdq", score_grad, key_seq, preferred_element_type=jnp.float32)
            * score_scale
        )
        key_grad = (
            key_grad
            + jnp.einsum(
                "hqk,hdq->hdk", score_grad, query_block, preferred_element_type=jnp.float32
            )
            * score_scale
        )
        value_grad = value_grad + jnp.einsum(
            "hqk,hdq->hdk",
            probs.astype(jnp.bfloat16),
            grad_block,
            preferred_element_type=jnp.float32,
        )
    return (jnp.concatenate(query_grads, axis=2), key_grad, value_grad)


def body_general(
    tokens_in,
    out_grad,
    segment_ids,
    active_lengths,
    norm1_gain,
    norm1_shift,
    query_weight,
    query_bias,
    key_weight,
    value_weight,
    value_bias,
    out_weight,
    out_bias,
    norm2_gain,
    norm2_shift,
    up_weight,
    up_bias,
    down_weight,
    down_bias,
):
    local_rows = tokens_in.shape[0]
    seq_here = segment_ids.shape[0]
    seq_length = segment_ids.shape[1]
    group_rows = seq_here * seq_length
    row_index = lax.axis_index("row")
    col_index = lax.axis_index("col")
    active_all = active_rows(segment_ids, active_lengths)
    active_here = lax.dynamic_slice_in_dim(active_all, col_index * local_rows, local_rows)
    keep_mask = active_here.astype(jnp.float32)[:, None]
    score_scale = HEAD_DIM ** (-0.5)
    rows_in = tokens_in.astype(jnp.float32)
    normed_one, normal_one, inverse_one = norm_forward(rows_in, norm1_gain, norm1_shift)
    gathered_one = token_gather(normed_one)
    stacked_weight = jnp.stack([query_weight, key_weight, value_weight])
    projected = unit_sums(
        jnp.einsum("td,kdh->kht", gathered_one, stacked_weight, preferred_element_type=jnp.float32)
    )
    head_width = projected.shape[1]
    head_count = head_width // HEAD_DIM
    query_part = lax.dynamic_slice_in_dim(query_bias, row_index * head_width, head_width)
    value_part = lax.dynamic_slice_in_dim(value_bias, row_index * head_width, head_width)
    bias_stack = jnp.stack([query_part, jnp.zeros_like(query_part), value_part])
    heads_all = (projected + bias_stack[:, :, None]).astype(jnp.bfloat16)

    def to_seqs(values):
        return jnp.moveaxis(values.reshape(head_count, HEAD_DIM, seq_here, seq_length), 2, 0)

    def from_seqs(values):
        return jnp.moveaxis(values, 0, 2).reshape(head_width, group_rows)

    query_seqs = to_seqs(heads_all[0])
    key_seqs = to_seqs(heads_all[1])
    value_seqs = to_seqs(heads_all[2])
    attended_seqs, log_sums = lax.map(
        lambda seq_items: attend_forward(
            seq_items[0], seq_items[1], seq_items[2], seq_items[3], score_scale
        ),
        (query_seqs, key_seqs, value_seqs, segment_ids),
    )
    attended = from_seqs(attended_seqs).astype(jnp.bfloat16)
    gathered_heads = unit_gather(attended[None])
    attention_rows = (
        token_sums(
            jnp.einsum("kht,hd->td", gathered_heads, out_weight, preferred_element_type=jnp.float32)
        )
        + out_bias
    )
    hidden_one = rows_in + attention_rows
    normed_two, normal_two, inverse_two = norm_forward(hidden_one, norm2_gain, norm2_shift)
    gathered_two = token_gather(normed_two)
    up_part = jnp.einsum("td,df->ft", gathered_two, up_weight, preferred_element_type=jnp.float32)[
        None
    ]
    unit_width = up_part.shape[1] // lax.axis_size("row")
    up_slice = lax.dynamic_slice_in_dim(up_bias, row_index * unit_width, unit_width)
    pre_act = unit_sums(up_part)[0] + up_slice[:, None]
    gathered_act = unit_gather(gelu_value(pre_act).astype(jnp.bfloat16)[None])
    ffn_rows = (
        token_sums(
            jnp.einsum("kft,fd->td", gathered_act, down_weight, preferred_element_type=jnp.float32)
        )
        + down_bias
    )
    layer_out = jnp.where(active_here[:, None], hidden_one + ffn_rows, rows_in)
    grad_rows = out_grad.astype(jnp.float32) * keep_mask
    branch_grad = token_gather(grad_rows.astype(jnp.bfloat16))
    down_grad = jnp.einsum(
        "kft,td->fd", gathered_act, branch_grad, preferred_element_type=jnp.float32
    )
    down_bias_grad = jnp.sum(branch_grad, axis=0, dtype=jnp.float32)
    act_part = jnp.einsum(
        "td,fd->ft", branch_grad, down_weight, preferred_element_type=jnp.float32
    )[None]
    act_grad = unit_sums(act_part)[0]
    pre_grad = (act_grad * gelu_slope(pre_act)).astype(jnp.bfloat16)
    gathered_pre = unit_gather(pre_grad[None])
    up_grad = jnp.einsum(
        "td,kft->df", gathered_two, gathered_pre, preferred_element_type=jnp.float32
    )
    up_bias_grad = jnp.sum(gathered_pre[0], axis=1, dtype=jnp.float32)
    normed_grad_two = token_sums(
        jnp.einsum("kft,df->td", gathered_pre, up_weight, preferred_element_type=jnp.float32)
    )
    back_two, gain_two_grad, shift_two_grad = norm_backward(
        normed_grad_two, normal_two, inverse_two, norm2_gain
    )
    hidden_grad = grad_rows + back_two
    attention_grad = token_gather(hidden_grad.astype(jnp.bfloat16))
    out_weight_grad = jnp.einsum(
        "kht,td->hd", gathered_heads, attention_grad, preferred_element_type=jnp.float32
    )
    out_bias_grad = jnp.sum(attention_grad, axis=0, dtype=jnp.float32)
    head_grad = unit_sums(
        jnp.einsum("td,hd->ht", attention_grad, out_weight, preferred_element_type=jnp.float32)[
            None
        ]
    )[0].astype(jnp.bfloat16)
    query_grads, key_grads, value_grads = lax.map(
        lambda seq_items: attend_backward(
            seq_items[0],
            seq_items[1],
            seq_items[2],
            seq_items[3],
            seq_items[4],
            seq_items[5],
            score_scale,
        ),
        (query_seqs, key_seqs, value_seqs, to_seqs(head_grad), segment_ids, log_sums),
    )
    stacked_grad = jnp.stack(
        [from_seqs(query_grads), from_seqs(key_grads), from_seqs(value_grads)]
    ).astype(jnp.bfloat16)
    gathered_grad = unit_gather(stacked_grad)
    stacked_weight_grad = jnp.einsum(
        "td,kht->kdh", gathered_one, gathered_grad, preferred_element_type=jnp.float32
    )
    query_bias_grad = jnp.sum(gathered_grad[0], axis=1, dtype=jnp.float32)
    value_bias_grad = jnp.sum(gathered_grad[2], axis=1, dtype=jnp.float32)
    normed_grad_one = token_sums(
        jnp.einsum("kht,kdh->td", gathered_grad, stacked_weight, preferred_element_type=jnp.float32)
    )
    back_one, gain_one_grad, shift_one_grad = norm_backward(
        normed_grad_one, normal_one, inverse_one, norm1_gain
    )
    input_grad = out_grad.astype(jnp.float32) * (1.0 - keep_mask) + hidden_grad + back_one
    (
        stacked_weight_grad,
        query_bias_grad,
        value_bias_grad,
        out_weight_grad,
        out_bias_grad,
        down_grad,
        down_bias_grad,
        up_grad,
        up_bias_grad,
    ) = lax.psum(
        (
            stacked_weight_grad,
            query_bias_grad,
            value_bias_grad,
            out_weight_grad,
            out_bias_grad,
            down_grad,
            down_bias_grad,
            up_grad,
            up_bias_grad,
        ),
        "dp",
    )
    gain_one_grad, shift_one_grad, gain_two_grad, shift_two_grad = lax.psum(
        (gain_one_grad, shift_one_grad, gain_two_grad, shift_two_grad), ("dp", "col")
    )
    return (
        layer_out,
        input_grad,
        gain_one_grad,
        shift_one_grad,
        stacked_weight_grad[0],
        query_bias_grad,
        stacked_weight_grad[1],
        stacked_weight_grad[2],
        value_bias_grad,
        out_weight_grad,
        out_bias_grad,
        gain_two_grad,
        shift_two_grad,
        up_grad,
        up_bias_grad,
        down_grad,
        down_bias_grad,
    )


def after(values, *others):
    return lax.optimization_barrier((values, others))[0]


def swap(values):
    return lax.ppermute(values, "row", [(0, 1), (1, 0)])


def step_x(values):
    return lax.ppermute(values, "dp", [(0, 1), (1, 0), (2, 3), (3, 2)])


def step_y(values):
    return lax.ppermute(values, "dp", [(0, 2), (2, 0), (1, 3), (3, 1)])


def step_up(values):
    count = lax.axis_size("col")
    return lax.ppermute(values, "col", [(i, (i + 1) % count) for i in range(count)])


def step_down(values):
    count = lax.axis_size("col")
    return lax.ppermute(values, "col", [(i, (i - 1) % count) for i in range(count)])


class Link:
    def __init__(self):
        self.last = None
        self.sent = None

    def send(self, step, values):
        if self.last is not None:
            values = after(values, self.last)
        self.sent = values
        self.last = step(values)
        return self.last


class Order:
    def __init__(self):
        self.token = None

    def run(self, function, first, *others, past=()):
        earlier = [t for t in (self.token, *past) if t is not None]
        if earlier:
            first = after(first, *earlier)
        result = function(first, *others)
        self.token = jax.tree.leaves(result)[0]
        return result


class Plane:
    def __init__(self):
        self.x = Link()
        self.y = Link()

    def sent(self):
        return (self.x.sent, self.y.sent)

    def near(self, values):
        return self.x.send(step_x, values), self.y.send(step_y, values)

    def far(self, from_x, from_y):
        half = from_x.shape[0] // 2
        far_one = self.y.send(step_y, from_x[:half])
        far_two = self.x.send(step_x, from_y[half:])
        return far_one, far_two

    def gather(self, values):
        from_x, from_y = self.near(values)
        return [values, from_x, from_y, *self.far(from_x, from_y)]

    def add_x(self, part, arrived):
        return self.x.send(step_x, add_rounded(part, arrived))

    def add_y(self, part, arrived):
        return self.y.send(step_y, add_rounded(part, arrived))


def add_rounded(left, right):
    return (left.astype(jnp.float32) + right.astype(jnp.float32)).astype(jnp.bfloat16)


def ring_gather(link, values):
    held = [values]
    for _ in range(lax.axis_size("col") - 1):
        held.append(link.send(step_up, held[-1]))
    return held


def picked(stacked, index):
    return lax.dynamic_index_in_dim(stacked, index, 0, keepdims=False)


def exchanged(values, index, axis):
    size = values.shape[axis] // 4
    return jnp.concatenate(
        [
            lax.dynamic_slice_in_dim(values, jnp.bitwise_xor(index, i) * size, size, axis=axis)
            for i in range(4)
        ],
        axis=axis,
    )


def mm(left, right, left_dim, right_dim, dtype=jnp.float32):
    return lax.dot_general(
        left, right, (((left_dim,), (right_dim,)), ((), ())), preferred_element_type=jnp.float32
    ).astype(dtype)


PAIR = 2 * HEAD_DIM
vmem_bytes = 48 * 1024 * 1024


def head_lanes(head, value):
    lane = lax.broadcasted_iota(jnp.int32, (1, PAIR), 1)
    return jnp.where(lane // HEAD_DIM == head, value, 0.0).astype(jnp.bfloat16)


def allowed_keys(first_row, low, high):
    key_pos = lax.broadcasted_iota(jnp.int32, (high, high - low), 0)
    query_pos = lax.broadcasted_iota(jnp.int32, (high, high - low), 1) + low
    return (key_pos >= first_row) & (key_pos <= query_pos)


def local_forward_kernel(size, first_ref, query_ref, key_ref, value_ref, out_ref):
    lane = lax.broadcasted_iota(jnp.int32, (size, PAIR), 1)
    for low in range(0, key_ref.shape[0], size):
        high = low + size
        keys = key_ref[:high, :]
        values = value_ref[:high, :]
        queries = query_ref[low:high, :]
        allowed = allowed_keys(first_ref[:, low:high], low, high)
        results = []
        for head in range(2):
            scores = mm(keys, queries * head_lanes(head, HEAD_DIM ** (-0.5)), 1, 1)
            scores = jnp.where(allowed, scores, masked_fill)
            exp_scores = jnp.exp(scores - jnp.max(scores, axis=0, keepdims=True))
            inverse = 1.0 / jnp.sum(exp_scores, axis=0, keepdims=True)
            results.append(mm((exp_scores * inverse).astype(jnp.bfloat16), values, 0, 0))
        out_ref[low:high, :] = jnp.where(lane < HEAD_DIM, results[0], results[1]).astype(
            jnp.bfloat16
        )


def local_forward(heads, first_row):
    length = heads.shape[0]
    pairs = heads.shape[1] // (3 * PAIR)
    return pl.pallas_call(
        functools.partial(local_forward_kernel, min(256, length)),
        grid=(pairs,),
        in_specs=[
            pl.BlockSpec((1, length), lambda p: (0, 0)),
            pl.BlockSpec((length, PAIR), lambda p: (0, p)),
            pl.BlockSpec((length, PAIR), lambda p: (0, pairs + p)),
            pl.BlockSpec((length, PAIR), lambda p: (0, 2 * pairs + p)),
        ],
        out_specs=pl.BlockSpec((length, PAIR), lambda p: (0, p)),
        out_shape=jax.ShapeDtypeStruct((length, pairs * PAIR), jnp.bfloat16),
        compiler_params=pltpu.CompilerParams(vmem_limit_bytes=vmem_bytes),
        cost_estimate=pl.CostEstimate(
            flops=16 * length * length * pairs * PAIR, bytes_accessed=8 * heads.size, transcendentals=0
        ),
    )(first_row, heads, heads, heads)


def local_backward_kernel(
    size, first_ref, query_ref, grad_ref, key_ref, value_ref, out_ref, key_sum, value_sum
):
    length = key_ref.shape[0]
    pair = pl.program_id(0)
    pairs = out_ref.shape[1] // (3 * PAIR)
    scale = HEAD_DIM ** (-0.5)
    lane = lax.broadcasted_iota(jnp.int32, (size, PAIR), 1)

    def lanes(part):
        return pl.ds(pl.multiple_of((part * pairs + pair) * PAIR, PAIR), PAIR)

    for low in range(length - size, -1, -size):
        high = low + size
        keys = key_ref[:high, :]
        values = value_ref[:high, :]
        queries = query_ref[low:high, :]
        grads = grad_ref[low:high, :]
        allowed = allowed_keys(first_ref[:, low:high], low, high)
        query_grads = []
        for head in range(2):
            scaled = queries * head_lanes(head, scale)
            grad = grads * head_lanes(head, 1.0)
            scores = jnp.where(allowed, mm(keys, scaled, 1, 1), masked_fill)
            exp_scores = jnp.exp(scores - jnp.max(scores, axis=0, keepdims=True))
            probs = exp_scores * (1.0 / jnp.sum(exp_scores, axis=0, keepdims=True))
            prob_grad = mm(values, grad, 1, 1)
            row_dot = jnp.sum(probs * prob_grad, axis=0, keepdims=True)
            score_grad = (probs * (prob_grad - row_dot)).astype(jnp.bfloat16)
            value_part = mm(probs.astype(jnp.bfloat16), grad, 1, 0)
            key_part = mm(score_grad, scaled, 1, 0)
            query_grads.append(mm(score_grad, keys, 0, 0) * scale)
            if head == 0:
                key_add, value_add = key_part, value_part
            else:
                key_add, value_add = key_add + key_part, value_add + value_part
        if high == length:
            key_sum[...] = key_add
            value_sum[...] = value_add
        else:
            key_sum[:high, :] += key_add
            value_sum[:high, :] += value_add
        out_ref[low:high, lanes(0)] = jnp.where(
            lane < HEAD_DIM, query_grads[0], query_grads[1]
        ).astype(jnp.bfloat16)
    out_ref[:, lanes(1)] = key_sum[...].astype(jnp.bfloat16)
    out_ref[:, lanes(2)] = value_sum[...].astype(jnp.bfloat16)


def local_backward(heads, head_grad, group, first_row):
    length = heads.shape[0]
    pairs = heads.shape[1] // (3 * PAIR)
    return pl.pallas_call(
        functools.partial(local_backward_kernel, min(512, length)),
        grid=(pairs,),
        in_specs=[
            pl.BlockSpec((1, length), lambda p: (0, 0)),
            pl.BlockSpec((length, PAIR), lambda p: (0, p)),
            pl.BlockSpec((length, PAIR), lambda p: (0, group * pairs + p)),
            pl.BlockSpec((length, PAIR), lambda p: (0, pairs + p)),
            pl.BlockSpec((length, PAIR), lambda p: (0, 2 * pairs + p)),
        ],
        out_specs=pl.BlockSpec(heads.shape, lambda p: (0, 0)),
        out_shape=jax.ShapeDtypeStruct(heads.shape, jnp.bfloat16),
        scratch_shapes=[pltpu.VMEM((length, PAIR), jnp.float32)] * 2,
        compiler_params=pltpu.CompilerParams(vmem_limit_bytes=vmem_bytes),
        cost_estimate=pl.CostEstimate(
            flops=32 * length * length * pairs * PAIR, bytes_accessed=8 * heads.size, transcendentals=0
        ),
    )(first_row, heads, head_grad, heads, heads)


gelu_scale = 0.7978845608028654
gelu_cubic = 0.044715


def ffn_kernel(*refs):
    normed_own, normed_sib, grad_own, grad_sib = [r[...] for r in refs[:4]]
    count = (len(refs) - 7) // 2
    own_pieces, sib_pieces = refs[4 : 4 + count], refs[4 + count : 4 + 2 * count]
    bias_ref, out_ref, sum_ref = refs[-3:]
    unit = own_pieces[0].shape[1] // 2
    units = unit * count

    @pl.when(pl.program_id(0) == 0)
    def _():
        sum_ref[...] = jnp.zeros_like(sum_ref)

    for k in range(count):
        own_piece, sib_piece = own_pieces[k], sib_pieces[k]
        span = slice(k * unit, (k + 1) * unit)
        pre = mm(normed_own, own_piece[:, :unit], 1, 0) + mm(normed_sib, sib_piece[:, :unit], 1, 0)
        act_grad = mm(grad_own, own_piece[:, unit:], 1, 0) + mm(grad_sib, sib_piece[:, unit:], 1, 0)
        pre = pre + bias_ref[:, span]
        square = pre * pre
        bent = jnp.tanh(gelu_scale * pre * (1.0 + gelu_cubic * square))
        half = 0.5 * (1.0 + bent)
        slope = half + 0.5 * gelu_scale * pre * (1.0 - bent * bent) * (1.0 + 3.0 * gelu_cubic * square)
        pre_grad = (act_grad * slope).astype(jnp.bfloat16)
        out_ref[:, span] = (pre * half).astype(jnp.bfloat16)
        out_ref[:, units + k * unit : units + (k + 1) * unit] = pre_grad
        sum_ref[:, span] += jnp.sum(pre_grad.astype(jnp.float32), axis=0, keepdims=True)


def ffn_rows_of(normed, grad, own_pieces, sib_pieces, bias):
    tokens, width = normed[0].shape
    count = len(own_pieces)
    unit = sib_pieces[0].shape[1] // 2
    units = unit * count
    size = min(256, tokens)
    rows = pl.BlockSpec((size, width), lambda i: (i, 0))
    piece = pl.BlockSpec((width, 2 * unit), lambda i: (0, 0))
    return pl.pallas_call(
        ffn_kernel,
        grid=(tokens // size,),
        in_specs=[rows] * 4 + [piece] * (2 * count) + [pl.BlockSpec((1, units), lambda i: (0, 0))],
        out_specs=[
            pl.BlockSpec((size, 2 * units), lambda i: (i, 0)),
            pl.BlockSpec((1, units), lambda i: (0, 0)),
        ],
        out_shape=[
            jax.ShapeDtypeStruct((tokens, 2 * units), jnp.bfloat16),
            jax.ShapeDtypeStruct((1, units), jnp.float32),
        ],
        compiler_params=pltpu.CompilerParams(vmem_limit_bytes=vmem_bytes),
        cost_estimate=pl.CostEstimate(
            flops=8 * tokens * width * units,
            bytes_accessed=8 * tokens * width + 8 * width * units + 4 * tokens * units,
            transcendentals=0,
        ),
    )(*normed, *grad, *own_pieces, *sib_pieces, bias)


def unit_products_kernel(count, own_ref, sib_ref, *refs):
    out_ref = refs[-1]
    unit = refs[0].shape[1]
    total = None
    for k in range(count):
        span = slice(k * unit, (k + 1) * unit)
        for rows, piece in ((own_ref, refs[k]), (sib_ref, refs[count + k])):
            part = mm(rows[:, span], piece[...], 1, 1)
            total = part if total is None else total + part
    out_ref[...] = total.astype(jnp.bfloat16)


def unit_products(own_rows, sib_rows, pieces, which):
    tokens, twice = own_rows.shape
    width = pieces[0].shape[0]
    unit = pieces[0].shape[1] // 4
    units = twice // 2
    count = len(pieces)
    size = min(256, tokens)
    rows = pl.BlockSpec((size, units), lambda i: (i, which))
    own_piece = pl.BlockSpec((width, unit), lambda i: (0, 1 - which))
    sib_piece = pl.BlockSpec((width, unit), lambda i: (0, 3 - which))
    return pl.pallas_call(
        functools.partial(unit_products_kernel, count),
        grid=(tokens // size,),
        in_specs=[rows] * 2 + [own_piece] * count + [sib_piece] * count,
        out_specs=pl.BlockSpec((size, width), lambda i: (i, 0)),
        out_shape=jax.ShapeDtypeStruct((tokens, width), jnp.bfloat16),
        compiler_params=pltpu.CompilerParams(vmem_limit_bytes=vmem_bytes),
        cost_estimate=pl.CostEstimate(
            flops=4 * tokens * units * width,
            bytes_accessed=6 * tokens * units + 4 * units * width,
            transcendentals=0,
        ),
    )(own_rows, sib_rows, *pieces, *pieces)


def weight_products_kernel(count, *refs):
    out_ref = refs[-1]
    normed, grads = refs[:count], refs[count : 2 * count]
    act_own, pre_own, act_sib, pre_sib = [
        refs[(2 + i) * count : (3 + i) * count] for i in range(4)
    ]
    unit = act_own[0].shape[1]
    up = down = None
    for j in range(count):
        pre = jnp.concatenate([pre_own[j][...], pre_sib[j][...]], axis=1)
        act = jnp.concatenate([act_own[j][...], act_sib[j][...]], axis=1)
        up_part = mm(normed[j][...], pre, 0, 0)
        down_part = mm(grads[j][...], act, 0, 0)
        up = up_part if up is None else up + up_part
        down = down_part if down is None else down + down_part
    for i, part in enumerate((up[:, :unit], down[:, :unit], up[:, unit:], down[:, unit:])):
        out_ref[:, i * unit : (i + 1) * unit] = part.astype(jnp.bfloat16)


def weight_products(normed, grads, own_rows, sib_rows, unit, k):
    count = len(normed)
    tokens, width = normed[0].shape
    ring = own_rows[0].shape[1] // (2 * unit)
    size = min(256, width)
    left = [pl.BlockSpec((tokens, size), lambda d: (0, d))] * (2 * count)
    act = [pl.BlockSpec((tokens, unit), lambda d: (0, k))] * count
    pre = [pl.BlockSpec((tokens, unit), lambda d: (0, ring + k))] * count
    return pl.pallas_call(
        functools.partial(weight_products_kernel, count),
        grid=(width // size,),
        in_specs=left + act + pre + act + pre,
        out_specs=pl.BlockSpec((size, 4 * unit), lambda d: (d, 0)),
        out_shape=jax.ShapeDtypeStruct((width, 4 * unit), jnp.bfloat16),
        compiler_params=pltpu.CompilerParams(vmem_limit_bytes=vmem_bytes),
        cost_estimate=pl.CostEstimate(
            flops=8 * count * tokens * width * unit,
            bytes_accessed=8 * count * tokens * width,
            transcendentals=0,
        ),
    )(*normed, *grads, *own_rows, *own_rows, *sib_rows, *sib_rows)


def params(**more):
    return pltpu.CompilerParams(vmem_limit_bytes=vmem_bytes, **more)


def cost(flops, nbytes):
    return pl.CostEstimate(flops=flops, bytes_accessed=nbytes, transcendentals=0)


def shape(dims, dtype=jnp.bfloat16):
    return jax.ShapeDtypeStruct(dims, dtype)


def turned(values):
    return values.astype(jnp.float32).T.astype(jnp.bfloat16)


def pack_heads_kernel(index_ref, *refs):
    sources, outs = refs[:8], refs[8:]
    own = sources[0].shape[1]
    for which in range(2):
        parts = [sources[4 * which + i][...] for i in range(3)] + [turned(sources[4 * which + 3][...])]
        for i, part in enumerate(parts):
            if len(outs) == 1:
                at = (4 * which + i) * own
                outs[0][:, at : at + own] = part
            else:
                outs[which][:, i * own : (i + 1) * own] = part


def pack_heads(index, weights, count, split):
    width, units = weights[0].shape
    own, block = units // 2, width // 4

    def feature(which):
        return pl.BlockSpec((block, own), lambda j, s: (s[1] ^ j, s[0] ^ which))

    def turned_block(which):
        return pl.BlockSpec((own, block), lambda j, s: (s[0] ^ which, s[1] ^ j))

    in_specs = []
    for which in range(2):
        in_specs += [feature(which)] * 3 + [turned_block(which)]
    if split:
        out_specs = [pl.BlockSpec((block, 4 * own), lambda j, s: (j, 0))] * 2
        out_shape = [shape((count * block, 4 * own))] * 2
    else:
        out_specs = pl.BlockSpec((block, 8 * own), lambda j, s: (j, 0))
        out_shape = shape((count * block, 8 * own))
    return pl.pallas_call(
        pack_heads_kernel,
        grid_spec=pltpu.PrefetchScalarGridSpec(
            num_scalar_prefetch=1, grid=(count,), in_specs=in_specs, out_specs=out_specs
        ),
        out_shape=out_shape,
        compiler_params=params(),
        cost_estimate=cost(0, 32 * count * block * own),
    )(index, *weights, *weights)


def pack_ff_kernel(index_ref, up_own, down_own, up_sib, down_sib, out_ref):
    unit = up_own.shape[1]
    parts = (up_own[...], turned(down_own[...]), up_sib[...], turned(down_sib[...]))
    for i, part in enumerate(parts):
        out_ref[:, i * unit : (i + 1) * unit] = part


def pack_ff(index, up_weight, down_weight):
    width, units = up_weight.shape
    unit, block = units // 8, width // 4
    in_specs = []
    for which in range(2):
        in_specs += [
            pl.BlockSpec((block, unit), lambda d, s, w=which: (d, 2 * s[1] + (s[0] ^ w))),
            pl.BlockSpec((unit, block), lambda d, s, w=which: (2 * s[1] + (s[0] ^ w), d)),
        ]
    return pl.pallas_call(
        pack_ff_kernel,
        grid_spec=pltpu.PrefetchScalarGridSpec(
            num_scalar_prefetch=1,
            grid=(4,),
            in_specs=in_specs,
            out_specs=pl.BlockSpec((block, 4 * unit), lambda d, s: (d, 0)),
        ),
        out_shape=shape((width, 4 * unit)),
        compiler_params=params(),
        cost_estimate=cost(0, 16 * width * unit),
    )(index, up_weight, down_weight, up_weight, down_weight)


def stack_kernel(*refs):
    pieces, own_ref, sib_ref = refs[:-2], refs[-2], refs[-1]
    half = own_ref.shape[1]
    at = 0
    for piece in pieces:
        end = at + piece.shape[0]
        own_ref[at:end, :] = piece[:, :half]
        sib_ref[at:end, :] = piece[:, half:]
        at = end


def stack_pieces(pieces):
    rows = sum(p.shape[0] for p in pieces)
    half = pieces[0].shape[1] // 2
    return pl.pallas_call(
        stack_kernel,
        out_shape=[shape((rows, half))] * 2,
        compiler_params=params(),
        cost_estimate=cost(0, 8 * rows * half),
    )(*pieces)


def norm_kernel(index_ref, own_ref, sib_ref, vectors_ref, own_out, sib_out, stats_ref):
    own = own_ref[...].astype(jnp.float32)
    sib = sib_ref[...].astype(jnp.float32)
    width = own.shape[1]
    average = (jnp.sum(own, axis=1, keepdims=True) + jnp.sum(sib, axis=1, keepdims=True)) / (2 * width)
    own, sib = own - average, sib - average
    square = jnp.sum(own * own, axis=1, keepdims=True) + jnp.sum(sib * sib, axis=1, keepdims=True)
    inverse = lax.rsqrt(square / (2 * width) + norm_eps)
    block = width // 4
    for half, (values, out) in enumerate(((own, own_out), (sib, sib_out))):
        gain, shift = vectors_ref[2 * half, :][None], vectors_ref[2 * half + 1, :][None]
        rounded = (values * inverse * gain + shift).astype(jnp.bfloat16)
        for i in range(4):
            at = pl.multiple_of((index_ref[1] ^ i) * block, block)
            out[:, pl.ds(at, block)] = rounded[:, i * block : (i + 1) * block]
    lane = lax.broadcasted_iota(jnp.int32, stats_ref.shape, 1)
    stats_ref[...] = jnp.where(lane == 0, average, inverse)


def norm_rows(index, own, sib, vectors):
    tokens, width = own.shape
    size = min(256, tokens)
    rows = pl.BlockSpec((size, width), lambda i, s: (i, 0))
    return pl.pallas_call(
        norm_kernel,
        grid_spec=pltpu.PrefetchScalarGridSpec(
            num_scalar_prefetch=1,
            grid=(tokens // size,),
            in_specs=[rows, rows, pl.BlockSpec((4, width), lambda i, s: (0, 0))],
            out_specs=[rows, rows, pl.BlockSpec((size, 128), lambda i, s: (i, 0))],
        ),
        out_shape=[shape((tokens, width))] * 2 + [shape((tokens, 128), jnp.float32)],
        compiler_params=params(),
        cost_estimate=cost(0, 8 * tokens * width),
    )(index, own, sib, vectors)


def project_kernel(own_ref, sib_ref, own_weight, sib_weight, bias_ref, out_ref):
    total = mm(own_ref[...], own_weight[...], 1, 0) + mm(sib_ref[...], sib_weight[...], 1, 0)
    out_ref[...] = (total + bias_ref[...]).astype(jnp.bfloat16)


def project(own, sib, own_weight, sib_weight, bias):
    tokens, width = own.shape
    units = bias.shape[1]
    size = min(256, tokens)
    rows = pl.BlockSpec((size, width), lambda i: (i, 0))
    weight = pl.BlockSpec((width, units), lambda i: (0, 0))
    return pl.pallas_call(
        project_kernel,
        grid=(tokens // size,),
        in_specs=[rows, rows, weight, weight, pl.BlockSpec((1, units), lambda i: (0, 0))],
        out_specs=pl.BlockSpec((size, units), lambda i: (i, 0)),
        out_shape=shape((tokens, units)),
        compiler_params=params(),
        cost_estimate=cost(4 * tokens * width * units, 4 * tokens * width + 4 * width * units),
    )(own, sib, own_weight, sib_weight, bias)


def out_rows_kernel(count, *refs):
    out_ref = refs[-1]
    total = refs[2 * count][...] if len(refs) > 2 * count + 1 else None
    for i in range(count):
        part = mm(refs[i][...], refs[count + i][...], 1, 1)
        total = part if total is None else total + part
    out_ref[...] = total


def out_rows(attended, weights, before=None):
    count = len(attended)
    tokens, own = attended[0].shape
    width = weights[0].shape[0]
    size = min(256, tokens)
    extra = [] if before is None else [before]
    full = pl.BlockSpec((size, width), lambda i: (i, 0))
    return pl.pallas_call(
        functools.partial(out_rows_kernel, count),
        grid=(tokens // size,),
        in_specs=[pl.BlockSpec((size, own), lambda i: (i, 0))] * count
        + [pl.BlockSpec((width, own), lambda i: (0, 3))] * count
        + [full] * len(extra),
        out_specs=full,
        out_shape=shape((tokens, width), jnp.float32),
        compiler_params=params(),
        cost_estimate=cost(2 * count * tokens * own * width, 4 * tokens * width * (1 + len(extra))),
    )(*attended, *weights, *extra)


def head_grads_kernel(own_ref, sib_ref, *refs):
    out_ref = refs[-1]
    count = (len(refs) - 1) // 2
    own = refs[0].shape[1]
    for k in range(count):
        total = mm(own_ref[...], refs[k][...], 1, 0) + mm(sib_ref[...], refs[count + k][...], 1, 0)
        out_ref[:, k * own : (k + 1) * own] = total.astype(jnp.bfloat16)


def head_grads(own, sib, own_weights, sib_weights):
    tokens, width = own.shape
    count = len(own_weights)
    units = own_weights[0].shape[1] // 4
    size = min(256, tokens)
    rows = pl.BlockSpec((size, width), lambda i: (i, 0))
    return pl.pallas_call(
        head_grads_kernel,
        grid=(tokens // size,),
        in_specs=[rows] * 2 + [pl.BlockSpec((width, units), lambda i: (0, 3))] * (2 * count),
        out_specs=pl.BlockSpec((size, count * units), lambda i: (i, 0)),
        out_shape=shape((tokens, count * units)),
        compiler_params=params(),
        cost_estimate=cost(4 * count * tokens * width * units, 8 * tokens * width),
    )(own, sib, *own_weights, *sib_weights)


def head_products_kernel(*refs):
    normed, grads = refs[:2], refs[2:4]
    heads_ref, attended_ref = refs[4:6]
    outs, sum_ref = refs[6:8], refs[8]
    split = heads_ref.shape[1]
    for i in range(2):
        outs[i][:, :split] = mm(normed[i][...], heads_ref[...], 0, 0).astype(jnp.bfloat16)
        outs[i][:, split:] = mm(grads[i][...], attended_ref[...], 0, 0).astype(jnp.bfloat16)

    @pl.when(pl.program_id(0) == 0)
    def _():
        sum_ref[...] = jnp.sum(heads_ref[...].astype(jnp.float32), axis=0, keepdims=True)


def head_products(normed, grads, head_grad, attended):
    tokens, width = normed[0].shape
    split, own = head_grad.shape[1], attended.shape[1]
    size = min(256, width)
    left = pl.BlockSpec((tokens, size), lambda d: (0, d))
    out = pl.BlockSpec((size, split + own), lambda d: (d, 0))
    return pl.pallas_call(
        head_products_kernel,
        grid=(width // size,),
        in_specs=[left] * 4
        + [pl.BlockSpec((tokens, split), lambda d: (0, 0)), pl.BlockSpec((tokens, own), lambda d: (0, 0))],
        out_specs=[out, out, pl.BlockSpec((1, split), lambda d: (0, 0))],
        out_shape=[shape((width, split + own))] * 2 + [shape((1, split), jnp.float32)],
        compiler_params=params(),
        cost_estimate=cost(4 * tokens * width * (split + own), 12 * tokens * width),
    )(*normed, *grads, head_grad, attended)


def back_rows_kernel(count, *refs):
    own_out, sib_out = refs[-2:]
    own = sib = None
    for k in range(count):
        grads = refs[k][...]
        own_part = mm(grads, refs[count + k][...], 1, 1)
        sib_part = mm(grads, refs[2 * count + k][...], 1, 1)
        own = own_part if own is None else own + own_part
        sib = sib_part if sib is None else sib + sib_part
    own_out[...] = own
    sib_out[...] = sib.astype(jnp.bfloat16)


def back_rows(grads, own_weights, sib_weights):
    count = len(grads)
    tokens, units = grads[0].shape
    width = own_weights[0].shape[0]
    size = min(256, tokens)
    full = pl.BlockSpec((size, width), lambda i: (i, 0))
    return pl.pallas_call(
        functools.partial(back_rows_kernel, count),
        grid=(tokens // size,),
        in_specs=[pl.BlockSpec((size, units), lambda i: (i, 0))] * count
        + [pl.BlockSpec((width, units), lambda i: (0, 0))] * (2 * count),
        out_specs=[full, full],
        out_shape=[shape((tokens, width), jnp.float32), shape((tokens, width))],
        compiler_params=params(),
        cost_estimate=cost(4 * count * tokens * width * units, 4 * count * width * units),
    )(*grads, *own_weights, *sib_weights)


def select_piece(refs, step, use):
    for j in range(3):

        @pl.when(step == j)
        def _():
            use(refs[j][...])

    @pl.when(step == 3)
    def _():
        use(jnp.concatenate([refs[3][...], refs[4][...]], axis=0))


def place_heads_kernel(index_ref, *refs):
    pieces, outs = refs[:5], refs[5:]
    own = pieces[0].shape[1] // 8

    def use(piece):
        for which in range(2):
            at = pl.multiple_of((index_ref[0] ^ which) * own, own)
            for m in range(4):
                part = piece[:, (4 * which + m) * own : (4 * which + m + 1) * own].astype(jnp.float32)
                if m < 3:
                    outs[m][:, pl.ds(at, own)] = part
                else:
                    outs[m][pl.ds(at, own), :] = part.T

    select_piece(pieces, pl.program_id(0), use)


def place_heads(index, pieces):
    block, columns = pieces[0].shape
    units, width = columns // 4, 4 * block
    whole = [pl.BlockSpec(p.shape, lambda j, s: (0, 0)) for p in pieces]
    return pl.pallas_call(
        place_heads_kernel,
        grid_spec=pltpu.PrefetchScalarGridSpec(
            num_scalar_prefetch=1,
            grid=(4,),
            in_specs=whole,
            out_specs=[pl.BlockSpec((block, units), lambda j, s: (s[1] ^ j, 0))] * 3
            + [pl.BlockSpec((units, block), lambda j, s: (0, s[1] ^ j))],
        ),
        out_shape=[shape((width, units), jnp.float32)] * 3 + [shape((units, width), jnp.float32)],
        compiler_params=params(),
        cost_estimate=cost(0, 24 * width * units),
    )(index, *pieces)


def place_ff_kernel(index_ref, *refs):
    pieces, (up_out, down_out) = refs[:5], refs[5:]
    unit = pieces[0].shape[1] // 4

    def use(piece):
        for which in range(2):
            at = pl.multiple_of((index_ref[0] ^ which) * unit, unit)
            start = 2 * which * unit
            up_out[:, pl.ds(at, unit)] = piece[:, start : start + unit].astype(jnp.float32)
            down_out[pl.ds(at, unit), :] = piece[:, start + unit : start + 2 * unit].astype(jnp.float32).T

    select_piece(pieces, pl.program_id(0), use)


def place_ff(index, pieces):
    width, columns = pieces[0].shape
    quarter = columns // 2
    whole = [pl.BlockSpec(p.shape, lambda j, s: (0, 0)) for p in pieces]
    return pl.pallas_call(
        place_ff_kernel,
        grid_spec=pltpu.PrefetchScalarGridSpec(
            num_scalar_prefetch=1,
            grid=(4,),
            in_specs=whole,
            out_specs=[
                pl.BlockSpec((width, quarter), lambda j, s: (0, s[1] ^ j)),
                pl.BlockSpec((quarter, width), lambda j, s: (s[1] ^ j, 0)),
            ],
        ),
        out_shape=[shape((width, 4 * quarter), jnp.float32), shape((4 * quarter, width), jnp.float32)],
        compiler_params=params(),
        cost_estimate=cost(0, 48 * width * quarter),
    )(index, *pieces)


def body_local(
    tokens_in,
    out_grad,
    segment_ids,
    active_lengths,
    norm1_gain,
    norm1_shift,
    query_weight,
    query_bias,
    key_weight,
    value_weight,
    value_bias,
    out_weight,
    out_bias,
    norm2_gain,
    norm2_shift,
    up_weight,
    up_bias,
    down_weight,
    down_bias,
):
    f32, bf16 = jnp.float32, jnp.bfloat16
    rows, width = tokens_in.shape
    ring = lax.axis_size("col")
    row_i = lax.axis_index("row")
    plane_i = lax.axis_index("dp")
    col_i = lax.axis_index("col")
    own = query_weight.shape[1] // 2
    block = width // 4
    quarter = up_weight.shape[1] // 4
    unit = quarter // 2
    half = rows // 2
    plane, column, order = Plane(), Link(), Order()
    index = jnp.stack([row_i, plane_i]).astype(jnp.int32)

    def cut(values, start, size):
        return lax.dynamic_slice_in_dim(values, start, size, axis=0)

    mine = jnp.concatenate(
        [
            cut(query_bias, row_i * own, own),
            jnp.zeros((own,), f32),
            cut(value_bias, row_i * own, own),
            cut(up_bias, plane_i * quarter + row_i * unit, unit),
        ]
    )
    small = [mine] + [
        lax.ppermute(mine, "col", [(i, (i + k) % ring) for i in range(ring)]) for k in range(1, ring)
    ]
    column.last = small[1:]
    up_biases = jnp.concatenate([s[3 * own :] for s in small])[None, :]
    head_biases = [s[None, : 3 * own] for s in small]

    sources = (query_weight, key_weight, value_weight, out_weight)
    piece = order.run(pack_heads, index, sources, 1, False)
    pieces = ring_gather(column, piece)

    active_all = active_rows(segment_ids, active_lengths)
    active_here = cut(active_all, col_i * rows, rows)
    keep_mask = active_here.astype(f32)[:, None]
    branch_mine = (out_grad.astype(f32) * keep_mask).astype(bf16)
    branch_first = plane.near(branch_mine[:half])
    tokens_sib = swap(tokens_in)
    vectors = jnp.stack([norm1_gain, norm1_shift])
    vectors = jnp.concatenate([vectors, swap(vectors)], axis=0)
    segment_row = picked(segment_ids, col_i)
    member = (segment_row[:, None] == jnp.arange(active_lengths.shape[1])).astype(jnp.int32)
    counts = jnp.sum(member, axis=0)
    first_row = jnp.sum(member * (jnp.cumsum(counts) - counts), axis=1)[None, :]

    own_parts, sib_parts = [[part] for part in order.run(pack_heads, index, sources, 4, True)]
    other_rows = [swap(sib_parts[0])]
    ff_piece = order.run(pack_ff, index, up_weight, down_weight)
    ff_own = ring_gather(column, ff_piece)
    *normed_one, stats_one = order.run(norm_rows, index, tokens_in, tokens_sib, vectors)

    heads, attended, attended_sib = [], [], []

    def attend(k):
        head = order.run(
            project, normed_one[0], normed_one[1], own_parts[k], other_rows[k], head_biases[k]
        )
        result = order.run(local_forward, head, first_row)
        heads.append(head)
        attended.append(result)
        attended_sib.append(swap(result))

    for k in range(1, ring):
        near = plane.near(pieces[k])
        attend(k - 1)
        far = plane.far(*after(near, order.token))
        gathered = [pieces[k], *near, *far]
        if k < ring - 1:
            upcoming = pieces[k + 1]
            pieces[k + 1] = after(upcoming, *far)
            past = (pieces[k + 1],)
        else:
            branch_first = after(branch_first, *far)
            past = branch_first
        own_part, sib_part = order.run(stack_pieces, gathered, past=past)
        own_parts.append(own_part)
        sib_parts.append(sib_part)
        other_rows.append(swap(sib_part))
    branch_far = plane.far(*branch_first)
    second_near = plane.near(branch_mine[half:])
    before = None
    if ring > 1:
        before = order.run(
            out_rows,
            attended[: ring - 1] + attended_sib[: ring - 1],
            own_parts[: ring - 1] + sib_parts[: ring - 1],
        )
    attend(ring - 1)
    second_far = plane.far(*second_near)
    attention_rows = order.run(
        out_rows, [attended[-1], attended_sib[-1]], [own_parts[-1], sib_parts[-1]], before
    )
    tokens_own = tokens_in.astype(f32)
    hidden_one = tokens_own + exchanged(attention_rows, plane_i, 1) + out_bias

    half_mean = jnp.mean(hidden_one, axis=1, keepdims=True)
    centered = hidden_one - half_mean
    half_square = jnp.mean(centered * centered, axis=1, keepdims=True)
    half_stats = jnp.concatenate([half_mean, half_square], axis=1).T
    other_stats = swap(half_stats)
    gap = half_stats[0] - other_stats[0]
    average_two = (0.5 * (half_stats[0] + other_stats[0]))[:, None]
    variance_two = (0.5 * (half_stats[1] + other_stats[1]) + 0.25 * gap * gap)[:, None]
    inverse_two = lax.rsqrt(variance_two + norm_eps)
    normal_two = (hidden_one - average_two) * inverse_two
    normed_two = (normal_two * norm2_gain + norm2_shift).astype(bf16)

    normed_own = [normed_two, *plane.near(normed_two)]
    first = [branch_mine[:half], *branch_first, jnp.concatenate(branch_far, axis=0)]
    second = [branch_mine[half:], *second_near, jnp.concatenate(second_far, axis=0)]
    branch_own = [branch_mine] + [jnp.concatenate([first[j], second[j]], axis=0) for j in range(1, 4)]
    branch_sib = [swap(b) for b in branch_own]
    ff_sib = [swap(p[:, 2 * unit :]) for p in ff_own]
    chips, chip_sibs, up_sums = [], [], []
    grad_parts, down_parts = [None] * 4, [None] * 4

    def feed_forward(j):
        chip, up_sum = order.run(
            ffn_rows_of,
            (normed_own[j], swap(normed_own[j])),
            (branch_own[j], branch_sib[j]),
            ff_own,
            ff_sib,
            up_biases,
        )
        chips.append(chip)
        chip_sibs.append(swap(chip))
        up_sums.append(up_sum)

    def products(parts, j, which):
        parts[j] = order.run(unit_products, chips[j], chip_sibs[j], ff_own, which)

    def weight_grads(k):
        return order.run(weight_products, normed_own, branch_own, chips, chip_sibs, unit, k)

    feed_forward(0)
    normed_far = plane.far(normed_own[1], normed_own[2])
    normed_own.append(jnp.concatenate(normed_far, axis=0))
    feed_forward(1)
    feed_forward(2)
    products(grad_parts, 1, 1)
    feed_forward(3)
    products(grad_parts, 2, 1)
    x_top = plane.x.send(step_x, grad_parts[1][:half])
    y_bottom = plane.y.send(step_y, grad_parts[2][half:])
    products(grad_parts, 3, 1)
    via_x = plane.x.send(step_x, grad_parts[3][:half])
    via_y = plane.y.send(step_y, grad_parts[3][half:])
    products(grad_parts, 0, 1)
    products(down_parts, 1, 0)
    products(down_parts, 2, 0)
    products(down_parts, 3, 0)
    via_x, via_y = after((via_x, via_y), order.token)
    x_bottom = plane.add_x(grad_parts[1][half:], via_y)
    y_top = plane.add_y(grad_parts[2][:half], via_x)
    sent = plane.sent()
    ff_grads = [None] * ring
    order.token = (order.token, *sent)
    ff_total = weight_grads(ring - 1)
    ff_came = column.send(step_down, ff_total)
    products(down_parts, 0, 0)
    x_bottom, y_top = after((x_bottom, y_top), order.token)
    normed_grad_two = jnp.concatenate(
        [
            grad_parts[0][:half].astype(f32) + x_top.astype(f32) + y_top.astype(f32),
            grad_parts[0][half:].astype(f32) + x_bottom.astype(f32) + y_bottom.astype(f32),
        ],
        axis=0,
    )
    down_x_top = plane.x.send(step_x, down_parts[1][:half])
    down_y_bottom = plane.y.send(step_y, down_parts[2][half:])

    def both_sums(one, two):
        sums = jnp.stack([jnp.sum(one, axis=1), jnp.sum(two, axis=1)])
        sums = (sums + swap(sums)) / (2 * width)
        return sums[0][:, None], sums[1][:, None]

    scaled = normed_grad_two * norm2_gain
    mean_one, mean_two = both_sums(scaled, scaled * normal_two)
    hidden_grad = branch_mine.astype(f32) + inverse_two * (scaled - mean_one - normal_two * mean_two)
    attention_grad = hidden_grad.astype(bf16)
    gain_two_grad = jnp.sum(normed_grad_two * normal_two, axis=0)
    shift_two_grad = jnp.sum(normed_grad_two, axis=0)
    grad_own = exchanged(attention_grad, plane_i, 1)
    grad_sib = swap(grad_own)
    order.token = (order.token, grad_own)
    for k in range(ring - 2, ring // 2 - 1, -1):
        ff_grads[k] = weight_grads(k)
    via_x = plane.x.send(step_x, down_parts[3][:half])
    via_y = plane.y.send(step_y, down_parts[3][half:])

    head_grad = order.run(
        head_grads, grad_own, grad_sib, own_parts, other_rows
    )
    head_rows, head_sums, bias_rows, swapped = [None] * ring, [None] * ring, [None] * ring, [None] * ring
    stage = 0
    for k in range(ring - 1, -1, -1):
        head_rows[k] = order.run(
            lambda h, g, f, k=k: local_backward(h, g, k, f), heads[k], head_grad, first_row
        )
        mine, other, bias_rows[k] = order.run(
            head_products, normed_one, (grad_own, grad_sib), head_rows[k], attended[k]
        )
        head_sums[k] = mine
        swapped[k] = swap(other)
        if stage == 0:
            ff_came = after(ff_came, order.token)
            ff_total = add_rounded(ff_came, ff_grads[ring - 2])
            ff_came = column.send(step_down, ff_total)
        if stage == 1:
            via_x, via_y = after((via_x, via_y), order.token)
            down_x_bottom = plane.add_x(down_parts[1][half:], via_y)
            down_y_top = plane.add_y(down_parts[2][:half], via_x)
        stage += 1
    for k in range(ring // 2 - 1, -1, -1):
        ff_grads[k] = weight_grads(k)
    for k in range(ring - 3, -1, -1):
        ff_came = after(ff_came, order.token)
        ff_total = add_rounded(ff_came, ff_grads[k])
        if k > 0:
            ff_came = column.send(step_down, ff_total)

    back_own, back_sib = order.run(back_rows, head_rows, own_parts, other_rows)
    normed_grad_one = exchanged(back_own + swap(back_sib).astype(f32), plane_i, 1)
    average_one, inverse_one = stats_one[:, :1], stats_one[:, 1:2]
    normal_own = (tokens_own - average_one) * inverse_one
    scaled = normed_grad_one * norm1_gain
    mean_one, mean_two = both_sums(scaled, scaled * normal_own)
    back_one = inverse_one * (scaled - mean_one - normal_own * mean_two)
    gain_one_grad = jnp.sum(normed_grad_one * normal_own, axis=0)
    shift_one_grad = jnp.sum(normed_grad_one, axis=0)
    input_grad = out_grad.astype(f32) * (1.0 - keep_mask) + hidden_grad + back_one

    def by_column(relative):
        places = jnp.mod(col_i - jnp.arange(ring), ring)
        return jnp.take(relative, places, axis=0)

    row_hot = (jnp.arange(2) == row_i).astype(f32)
    plane_hot = (jnp.arange(4) == plane_i).astype(f32)
    head_bias = by_column(jnp.stack(bias_rows)).reshape(ring, 3, 1, own) * row_hot[:, None]
    up_bias_part = by_column(sum(up_sums).reshape(ring, unit)).reshape(ring, 1, 1, unit)
    up_bias_part = up_bias_part * plane_hot[:, None, None] * row_hot[:, None]
    bias_vector = jnp.concatenate([head_bias.reshape(ring, -1), up_bias_part.reshape(ring, -1)], axis=1)
    bias_vector = bias_vector + swap(bias_vector)
    out_bias_part = jnp.sum(attention_grad.astype(f32), axis=0)
    down_bias_part = jnp.sum(branch_mine.astype(f32), axis=0)
    own_vector = jnp.concatenate(
        [gain_one_grad, shift_one_grad, gain_two_grad, shift_two_grad, out_bias_part, down_bias_part]
    )
    summed = jnp.concatenate([bias_vector.reshape(-1), own_vector])

    def part_of(k, j, which):
        rows_of = slice(j * block, (j + 1) * block)
        return (swapped if which else head_sums)[k][rows_of]

    total = None
    for k in range(ring - 1, -1, -1):
        if k == 0:
            summed = summed + plane.x.send(step_x, summed)
            summed = summed + plane.y.send(step_y, summed)
            step = 1
            while step < ring:
                pairs = [(i, i ^ step) for i in range(ring)]
                summed = summed + column.send(lambda v: lax.ppermute(v, "col", pairs), summed)
                step *= 2
            ff_gathered = plane.gather(ff_total)
        via_x = plane.x.send(step_x, part_of(k, 3, 0))
        via_y = plane.y.send(step_y, part_of(k, 3, 1))
        for_x = jnp.concatenate([part_of(k, 1, 0), add_rounded(part_of(k, 1, 1), via_y)], axis=1)
        for_y = jnp.concatenate([add_rounded(part_of(k, 2, 0), via_x), part_of(k, 2, 1)], axis=1)
        from_x = plane.x.send(step_x, for_x)
        from_y = plane.y.send(step_y, for_y)
        here = jnp.concatenate([part_of(k, 0, 0), part_of(k, 0, 1)], axis=1)
        here = here.astype(f32) + from_x.astype(f32) + from_y.astype(f32)
        if total is not None:
            here = here + total.astype(f32)
        total = here.astype(bf16)
        if k > 0:
            total = column.send(step_down, total)
    up_weight_grad, down_weight_grad = place_ff(index, ff_gathered)
    query_weight_grad, key_weight_grad, value_weight_grad, out_weight_grad = place_heads(
        index, plane.gather(total)
    )

    down_top = down_parts[0][:half].astype(f32) + down_x_top.astype(f32) + down_y_top.astype(f32)
    down_bottom = down_parts[0][half:].astype(f32) + down_x_bottom.astype(f32) + down_y_bottom.astype(f32)
    ffn_rows = jnp.concatenate([down_top, down_bottom], axis=0) + down_bias
    layer_out = jnp.where(active_here[:, None], hidden_one + ffn_rows, tokens_own)

    bias_here = picked(summed[: bias_vector.size].reshape(ring, -1), col_i)
    own_here = summed[bias_vector.size :].reshape(6, width)
    size = 2 * own
    return (
        layer_out,
        input_grad,
        own_here[0],
        own_here[1],
        query_weight_grad,
        bias_here[:size],
        key_weight_grad,
        value_weight_grad,
        bias_here[2 * size : 3 * size],
        out_weight_grad,
        own_here[4],
        own_here[2],
        own_here[3],
        up_weight_grad,
        bias_here[3 * size :],
        down_weight_grad,
        own_here[5],
    )


def body(tokens_in, out_grad, segment_ids, *rest):
    ring = lax.axis_size("col")
    local = (
        lax.axis_size("dp") == 4
        and lax.axis_size("row") == 2
        and ring == 4
        and tokens_in.shape[0] == segment_ids.shape[1]
    )
    chosen = body_local if local else body_general
    return chosen(tokens_in, out_grad, segment_ids, *rest)


def solution(mesh):
    placed = (
        P(("dp", "col"), "row"),
        P(("dp", "col"), "row"),
        P("dp", None),
        P("dp", None),
        P("row"),
        P("row"),
        P("row", "col"),
        P("col"),
        P("row", "col"),
        P("row", "col"),
        P("col"),
        P("col", "row"),
        P("row"),
        P("row"),
        P("row"),
        P("row", "col"),
        P("col"),
        P("col", "row"),
        P("row"),
    )
    return jax.shard_map(
        body,
        mesh=mesh,
        in_specs=placed,
        out_specs=(
            P(("dp", "col"), "row"),
            P(("dp", "col"), "row"),
            P("row"),
            P("row"),
            P("row", "col"),
            P("col"),
            P("row", "col"),
            P("row", "col"),
            P("col"),
            P("col", "row"),
            P("row"),
            P("row"),
            P("row"),
            P("row", "col"),
            P("col"),
            P("col", "row"),
            P("row"),
        ),
        check_vma=False,
    )
```

```python
import functools

import jax
import jax.numpy as jnp
from jax import lax
from jax.experimental import pallas as pl
from jax.experimental.pallas import tpu as pltpu
from jax.sharding import PartitionSpec as P

D = 2048
HEAD_DIM = 64


norm_eps = 1e-05
masked_fill = -1e30


def width_totals(total_one, total_two):
    return lax.psum((total_one, total_two), "row")


def token_gather(values):
    return lax.all_gather(values, "col", axis=0, tiled=True)


def token_sums(partial_rows):
    return lax.psum_scatter(partial_rows, "col", scatter_dimension=0, tiled=True)


def unit_gather(values):
    return lax.all_gather(values, "row", axis=1, tiled=True)


def unit_sums(partial_units):
    return lax.psum_scatter(partial_units, "row", scatter_dimension=1, tiled=True)


def gelu_value(values):
    return jax.nn.gelu(values, approximate=True)


def gelu_slope(values):
    result, pullback = jax.vjp(gelu_value, values)
    return pullback(jnp.ones_like(values))[0]


def active_rows(segment_rows, keep_lengths):
    doc_index = jnp.arange(keep_lengths.shape[-1], dtype=jnp.int32)
    member = (segment_rows[:, :, None] == doc_index).astype(jnp.int32)
    counts = jnp.sum(member, axis=1)
    starts = jnp.cumsum(counts, axis=1) - counts
    first_pos = jnp.sum(member * starts[:, None, :], axis=2)
    keep_here = jnp.sum(member * keep_lengths[:, None, :], axis=2)
    position_in = jnp.arange(segment_rows.shape[1], dtype=jnp.int32)[None, :] - first_pos
    return (position_in < keep_here).reshape(-1)


def norm_forward(values, gain_part, shift_part):
    total_one, total_two = width_totals(jnp.sum(values, axis=1), jnp.sum(values * values, axis=1))
    average = total_one / D
    variance = total_two / D - average * average
    inverse = lax.rsqrt(variance + norm_eps)
    normal = (values - average[:, None]) * inverse[:, None]
    return ((normal * gain_part + shift_part).astype(jnp.bfloat16), normal, inverse)


def norm_backward(grad_rows, normal, inverse, gain_part):
    scaled = grad_rows * gain_part
    total_one, total_two = width_totals(jnp.sum(scaled, axis=1), jnp.sum(scaled * normal, axis=1))
    grad_in = inverse[:, None] * (
        scaled - total_one[:, None] / D - normal * (total_two[:, None] / D)
    )
    return (grad_in, jnp.sum(grad_rows * normal, axis=0), jnp.sum(grad_rows, axis=0))


def allowed_mask(segment_row, offset, block_rows):
    key_pos = jnp.arange(segment_row.shape[0], dtype=jnp.int32)
    query_pos = key_pos[offset : offset + block_rows]
    same_doc = segment_row[None, :] == segment_row[offset : offset + block_rows, None]
    return (key_pos[None, :] <= query_pos[:, None]) & same_doc


def attend_forward(query_seq, key_seq, value_seq, segment_row, score_scale):
    seq_length = query_seq.shape[2]
    block_rows = min(512, seq_length)
    outputs = []
    log_parts = []
    for offset in range(0, seq_length, block_rows):
        query_block = query_seq[:, :, offset : offset + block_rows]
        scores = (
            jnp.einsum("hdq,hdk->hqk", query_block, key_seq, preferred_element_type=jnp.float32)
            * score_scale
        )
        scores = jnp.where(allowed_mask(segment_row, offset, block_rows)[None], scores, masked_fill)
        row_max = jnp.max(scores, axis=2, keepdims=True)
        exp_scores = jnp.exp(scores - row_max)
        row_total = jnp.sum(exp_scores, axis=2, keepdims=True)
        weights = (exp_scores / row_total).astype(jnp.bfloat16)
        outputs.append(
            jnp.einsum("hqk,hdk->hdq", weights, value_seq, preferred_element_type=jnp.float32)
        )
        log_parts.append((row_max + jnp.log(row_total))[:, :, 0])
    return (jnp.concatenate(outputs, axis=2), jnp.concatenate(log_parts, axis=1))


def attend_backward(query_seq, key_seq, value_seq, grad_seq, segment_row, log_sums, score_scale):
    seq_length = query_seq.shape[2]
    block_rows = min(512, seq_length)
    key_grad = jnp.zeros(key_seq.shape, jnp.float32)
    value_grad = jnp.zeros(value_seq.shape, jnp.float32)
    query_grads = []
    for offset in range(0, seq_length, block_rows):
        query_block = query_seq[:, :, offset : offset + block_rows]
        grad_block = grad_seq[:, :, offset : offset + block_rows]
        scores = (
            jnp.einsum("hdq,hdk->hqk", query_block, key_seq, preferred_element_type=jnp.float32)
            * score_scale
        )
        scores = jnp.where(allowed_mask(segment_row, offset, block_rows)[None], scores, masked_fill)
        probs = jnp.exp(scores - log_sums[:, offset : offset + block_rows, None])
        prob_grad = jnp.einsum(
            "hdq,hdk->hqk", grad_block, value_seq, preferred_element_type=jnp.float32
        )
        row_dot = jnp.sum(probs * prob_grad, axis=2, keepdims=True)
        score_grad = (probs * (prob_grad - row_dot)).astype(jnp.bfloat16)
        query_grads.append(
            jnp.einsum("hqk,hdk->hdq", score_grad, key_seq, preferred_element_type=jnp.float32)
            * score_scale
        )
        key_grad = (
            key_grad
            + jnp.einsum(
                "hqk,hdq->hdk", score_grad, query_block, preferred_element_type=jnp.float32
            )
            * score_scale
        )
        value_grad = value_grad + jnp.einsum(
            "hqk,hdq->hdk",
            probs.astype(jnp.bfloat16),
            grad_block,
            preferred_element_type=jnp.float32,
        )
    return (jnp.concatenate(query_grads, axis=2), key_grad, value_grad)


def body_general(
    tokens_in,
    out_grad,
    segment_ids,
    active_lengths,
    norm1_gain,
    norm1_shift,
    query_weight,
    query_bias,
    key_weight,
    value_weight,
    value_bias,
    out_weight,
    out_bias,
    norm2_gain,
    norm2_shift,
    up_weight,
    up_bias,
    down_weight,
    down_bias,
):
    local_rows = tokens_in.shape[0]
    seq_here = segment_ids.shape[0]
    seq_length = segment_ids.shape[1]
    group_rows = seq_here * seq_length
    row_index = lax.axis_index("row")
    col_index = lax.axis_index("col")
    active_all = active_rows(segment_ids, active_lengths)
    active_here = lax.dynamic_slice_in_dim(active_all, col_index * local_rows, local_rows)
    keep_mask = active_here.astype(jnp.float32)[:, None]
    score_scale = HEAD_DIM ** (-0.5)
    rows_in = tokens_in.astype(jnp.float32)
    normed_one, normal_one, inverse_one = norm_forward(rows_in, norm1_gain, norm1_shift)
    gathered_one = token_gather(normed_one)
    stacked_weight = jnp.stack([query_weight, key_weight, value_weight])
    projected = unit_sums(
        jnp.einsum("td,kdh->kht", gathered_one, stacked_weight, preferred_element_type=jnp.float32)
    )
    head_width = projected.shape[1]
    head_count = head_width // HEAD_DIM
    query_part = lax.dynamic_slice_in_dim(query_bias, row_index * head_width, head_width)
    value_part = lax.dynamic_slice_in_dim(value_bias, row_index * head_width, head_width)
    bias_stack = jnp.stack([query_part, jnp.zeros_like(query_part), value_part])
    heads_all = (projected + bias_stack[:, :, None]).astype(jnp.bfloat16)

    def to_seqs(values):
        return jnp.moveaxis(values.reshape(head_count, HEAD_DIM, seq_here, seq_length), 2, 0)

    def from_seqs(values):
        return jnp.moveaxis(values, 0, 2).reshape(head_width, group_rows)

    query_seqs = to_seqs(heads_all[0])
    key_seqs = to_seqs(heads_all[1])
    value_seqs = to_seqs(heads_all[2])
    attended_seqs, log_sums = lax.map(
        lambda seq_items: attend_forward(
            seq_items[0], seq_items[1], seq_items[2], seq_items[3], score_scale
        ),
        (query_seqs, key_seqs, value_seqs, segment_ids),
    )
    attended = from_seqs(attended_seqs).astype(jnp.bfloat16)
    gathered_heads = unit_gather(attended[None])
    attention_rows = (
        token_sums(
            jnp.einsum("kht,hd->td", gathered_heads, out_weight, preferred_element_type=jnp.float32)
        )
        + out_bias
    )
    hidden_one = rows_in + attention_rows
    normed_two, normal_two, inverse_two = norm_forward(hidden_one, norm2_gain, norm2_shift)
    gathered_two = token_gather(normed_two)
    up_part = jnp.einsum("td,df->ft", gathered_two, up_weight, preferred_element_type=jnp.float32)[
        None
    ]
    unit_width = up_part.shape[1] // lax.axis_size("row")
    up_slice = lax.dynamic_slice_in_dim(up_bias, row_index * unit_width, unit_width)
    pre_act = unit_sums(up_part)[0] + up_slice[:, None]
    gathered_act = unit_gather(gelu_value(pre_act).astype(jnp.bfloat16)[None])
    ffn_rows = (
        token_sums(
            jnp.einsum("kft,fd->td", gathered_act, down_weight, preferred_element_type=jnp.float32)
        )
        + down_bias
    )
    layer_out = jnp.where(active_here[:, None], hidden_one + ffn_rows, rows_in)
    grad_rows = out_grad.astype(jnp.float32) * keep_mask
    branch_grad = token_gather(grad_rows.astype(jnp.bfloat16))
    down_grad = jnp.einsum(
        "kft,td->fd", gathered_act, branch_grad, preferred_element_type=jnp.float32
    )
    down_bias_grad = jnp.sum(branch_grad, axis=0, dtype=jnp.float32)
    act_part = jnp.einsum(
        "td,fd->ft", branch_grad, down_weight, preferred_element_type=jnp.float32
    )[None]
    act_grad = unit_sums(act_part)[0]
    pre_grad = (act_grad * gelu_slope(pre_act)).astype(jnp.bfloat16)
    gathered_pre = unit_gather(pre_grad[None])
    up_grad = jnp.einsum(
        "td,kft->df", gathered_two, gathered_pre, preferred_element_type=jnp.float32
    )
    up_bias_grad = jnp.sum(gathered_pre[0], axis=1, dtype=jnp.float32)
    normed_grad_two = token_sums(
        jnp.einsum("kft,df->td", gathered_pre, up_weight, preferred_element_type=jnp.float32)
    )
    back_two, gain_two_grad, shift_two_grad = norm_backward(
        normed_grad_two, normal_two, inverse_two, norm2_gain
    )
    hidden_grad = grad_rows + back_two
    attention_grad = token_gather(hidden_grad.astype(jnp.bfloat16))
    out_weight_grad = jnp.einsum(
        "kht,td->hd", gathered_heads, attention_grad, preferred_element_type=jnp.float32
    )
    out_bias_grad = jnp.sum(attention_grad, axis=0, dtype=jnp.float32)
    head_grad = unit_sums(
        jnp.einsum("td,hd->ht", attention_grad, out_weight, preferred_element_type=jnp.float32)[
            None
        ]
    )[0].astype(jnp.bfloat16)
    query_grads, key_grads, value_grads = lax.map(
        lambda seq_items: attend_backward(
            seq_items[0],
            seq_items[1],
            seq_items[2],
            seq_items[3],
            seq_items[4],
            seq_items[5],
            score_scale,
        ),
        (query_seqs, key_seqs, value_seqs, to_seqs(head_grad), segment_ids, log_sums),
    )
    stacked_grad = jnp.stack(
        [from_seqs(query_grads), from_seqs(key_grads), from_seqs(value_grads)]
    ).astype(jnp.bfloat16)
    gathered_grad = unit_gather(stacked_grad)
    stacked_weight_grad = jnp.einsum(
        "td,kht->kdh", gathered_one, gathered_grad, preferred_element_type=jnp.float32
    )
    query_bias_grad = jnp.sum(gathered_grad[0], axis=1, dtype=jnp.float32)
    value_bias_grad = jnp.sum(gathered_grad[2], axis=1, dtype=jnp.float32)
    normed_grad_one = token_sums(
        jnp.einsum("kht,kdh->td", gathered_grad, stacked_weight, preferred_element_type=jnp.float32)
    )
    back_one, gain_one_grad, shift_one_grad = norm_backward(
        normed_grad_one, normal_one, inverse_one, norm1_gain
    )
    input_grad = out_grad.astype(jnp.float32) * (1.0 - keep_mask) + hidden_grad + back_one
    (
        stacked_weight_grad,
        query_bias_grad,
        value_bias_grad,
        out_weight_grad,
        out_bias_grad,
        down_grad,
        down_bias_grad,
        up_grad,
        up_bias_grad,
    ) = lax.psum(
        (
            stacked_weight_grad,
            query_bias_grad,
            value_bias_grad,
            out_weight_grad,
            out_bias_grad,
            down_grad,
            down_bias_grad,
            up_grad,
            up_bias_grad,
        ),
        "dp",
    )
    gain_one_grad, shift_one_grad, gain_two_grad, shift_two_grad = lax.psum(
        (gain_one_grad, shift_one_grad, gain_two_grad, shift_two_grad), ("dp", "col")
    )
    return (
        layer_out,
        input_grad,
        gain_one_grad,
        shift_one_grad,
        stacked_weight_grad[0],
        query_bias_grad,
        stacked_weight_grad[1],
        stacked_weight_grad[2],
        value_bias_grad,
        out_weight_grad,
        out_bias_grad,
        gain_two_grad,
        shift_two_grad,
        up_grad,
        up_bias_grad,
        down_grad,
        down_bias_grad,
    )


def after(values, *others):
    return lax.optimization_barrier((values, others))[0]


def swap(values):
    return lax.ppermute(values, "row", [(0, 1), (1, 0)])


def step_x(values):
    return lax.ppermute(values, "dp", [(0, 1), (1, 0), (2, 3), (3, 2)])


def step_y(values):
    return lax.ppermute(values, "dp", [(0, 2), (2, 0), (1, 3), (3, 1)])


def step_up(values):
    count = lax.axis_size("col")
    return lax.ppermute(values, "col", [(i, (i + 1) % count) for i in range(count)])


def step_down(values):
    count = lax.axis_size("col")
    return lax.ppermute(values, "col", [(i, (i - 1) % count) for i in range(count)])


class Order:
    def __init__(self):
        self.tokens = []
        self.fresh, self.due = [], []

    def tie(self, values):
        if self.tokens:
            values = after(values, *self.tokens)
        self.tokens.append(values)
        return values

    def swap(self, values, due=True):
        arrived = swap(self.tie(values))
        if due:
            self.fresh.append(arrived)
        return arrived

    def run(self, function, first, *others):
        first = after(first, *self.tokens, *self.due) if self.tokens or self.due else first
        self.due, self.fresh = self.fresh, []
        result = function(first, *others)
        self.tokens = [jax.tree.leaves(result)[0]]
        return result


class Link:
    def __init__(self, order):
        self.order = order
        self.last = None

    def send(self, step, values, free=False):
        if self.last is not None and not free:
            values = after(values, self.last)
        self.last = step(self.order.tie(values))
        return self.last


class Plane:
    def __init__(self, order):
        self.x = Link(order)
        self.y = Link(order)

    def both(self, for_x, for_y, free=False):
        return self.x.send(step_x, for_x, free), self.y.send(step_y, for_y, free)

    def far(self, from_x, from_y):
        half = from_x.shape[0] // 2
        far_two, far_one = self.both(from_y[half:], from_x[:half])
        return far_one, far_two


def add_rounded(left, right):
    return (left.astype(jnp.float32) + right.astype(jnp.float32)).astype(jnp.bfloat16)


def ring_gather(link, values):
    held = [values]
    for _ in range(lax.axis_size("col") - 1):
        held.append(link.send(step_up, held[-1]))
    return held


def picked(stacked, index):
    return lax.dynamic_index_in_dim(stacked, index, 0, keepdims=False)


def mm(left, right, left_dim, right_dim, dtype=jnp.float32):
    return lax.dot_general(
        left, right, (((left_dim,), (right_dim,)), ((), ())), preferred_element_type=jnp.float32
    ).astype(dtype)


PAIR = 2 * HEAD_DIM
vmem_bytes = 48 * 1024 * 1024


def head_lanes(head, value):
    lane = lax.broadcasted_iota(jnp.int32, (1, PAIR), 1)
    return jnp.where(lane // HEAD_DIM == head, value, 0.0).astype(jnp.bfloat16)


def allowed_keys(first_row, low, high):
    key_pos = lax.broadcasted_iota(jnp.int32, (high, high - low), 0)
    query_pos = lax.broadcasted_iota(jnp.int32, (high, high - low), 1) + low
    return (key_pos >= first_row) & (key_pos <= query_pos)


def local_forward_kernel(size, first_ref, query_ref, key_ref, value_ref, out_ref):
    lane = lax.broadcasted_iota(jnp.int32, (size, PAIR), 1)
    for low in range(0, key_ref.shape[0], size):
        high = low + size
        keys = key_ref[:high, :]
        values = value_ref[:high, :]
        queries = query_ref[low:high, :]
        allowed = allowed_keys(first_ref[:, low:high], low, high)
        results = []
        for head in range(2):
            scores = mm(keys, queries * head_lanes(head, HEAD_DIM ** (-0.5)), 1, 1)
            scores = jnp.where(allowed, scores, masked_fill)
            exp_scores = jnp.exp(scores - jnp.max(scores, axis=0, keepdims=True))
            inverse = 1.0 / jnp.sum(exp_scores, axis=0, keepdims=True)
            results.append(mm((exp_scores * inverse).astype(jnp.bfloat16), values, 0, 0))
        out_ref[low:high, :] = jnp.where(lane < HEAD_DIM, results[0], results[1]).astype(
            jnp.bfloat16
        )


def local_forward(heads, first_row):
    length = heads.shape[0]
    pairs = heads.shape[1] // (3 * PAIR)
    return pl.pallas_call(
        functools.partial(local_forward_kernel, min(256, length)),
        grid=(pairs,),
        in_specs=[
            pl.BlockSpec((1, length), lambda p: (0, 0)),
            pl.BlockSpec((length, PAIR), lambda p: (0, p)),
            pl.BlockSpec((length, PAIR), lambda p: (0, pairs + p)),
            pl.BlockSpec((length, PAIR), lambda p: (0, 2 * pairs + p)),
        ],
        out_specs=pl.BlockSpec((length, PAIR), lambda p: (0, p)),
        out_shape=jax.ShapeDtypeStruct((length, pairs * PAIR), jnp.bfloat16),
        compiler_params=pltpu.CompilerParams(vmem_limit_bytes=vmem_bytes),
        cost_estimate=cost(16 * length * length * pairs * PAIR, 8 * heads.size),
    )(first_row, heads, heads, heads)


def local_backward_kernel(
    size, first_ref, query_ref, grad_ref, key_ref, value_ref, out_ref, key_sum, value_sum
):
    length = key_ref.shape[0]
    pair = pl.program_id(0)
    pairs = out_ref.shape[1] // (3 * PAIR)
    scale = HEAD_DIM ** (-0.5)
    lane = lax.broadcasted_iota(jnp.int32, (size, PAIR), 1)

    def lanes(part):
        return pl.ds(pl.multiple_of((part * pairs + pair) * PAIR, PAIR), PAIR)

    for low in range(length - size, -1, -size):
        high = low + size
        keys = key_ref[:high, :]
        values = value_ref[:high, :]
        queries = query_ref[low:high, :]
        grads = grad_ref[low:high, :]
        allowed = allowed_keys(first_ref[:, low:high], low, high)
        query_grads = []
        for head in range(2):
            scaled = queries * head_lanes(head, scale)
            grad = grads * head_lanes(head, 1.0)
            scores = jnp.where(allowed, mm(keys, scaled, 1, 1), masked_fill)
            exp_scores = jnp.exp(scores - jnp.max(scores, axis=0, keepdims=True))
            probs = exp_scores * (1.0 / jnp.sum(exp_scores, axis=0, keepdims=True))
            prob_grad = mm(values, grad, 1, 1)
            row_dot = jnp.sum(probs * prob_grad, axis=0, keepdims=True)
            score_grad = (probs * (prob_grad - row_dot)).astype(jnp.bfloat16)
            value_part = mm(probs.astype(jnp.bfloat16), grad, 1, 0)
            key_part = mm(score_grad, scaled, 1, 0)
            query_grads.append(mm(score_grad, keys, 0, 0) * scale)
            if head == 0:
                key_add, value_add = key_part, value_part
            else:
                key_add, value_add = key_add + key_part, value_add + value_part
        if high == length:
            key_sum[...] = key_add
            value_sum[...] = value_add
        else:
            key_sum[:high, :] += key_add
            value_sum[:high, :] += value_add
        out_ref[low:high, lanes(0)] = jnp.where(
            lane < HEAD_DIM, query_grads[0], query_grads[1]
        ).astype(jnp.bfloat16)
    out_ref[:, lanes(1)] = key_sum[...].astype(jnp.bfloat16)
    out_ref[:, lanes(2)] = value_sum[...].astype(jnp.bfloat16)


def local_backward(heads, head_grad, group, first_row):
    length = heads.shape[0]
    pairs = heads.shape[1] // (3 * PAIR)
    return pl.pallas_call(
        functools.partial(local_backward_kernel, min(512, length)),
        grid=(pairs,),
        in_specs=[
            pl.BlockSpec((1, length), lambda p: (0, 0)),
            pl.BlockSpec((length, PAIR), lambda p: (0, p)),
            pl.BlockSpec((length, PAIR), lambda p: (0, group * pairs + p)),
            pl.BlockSpec((length, PAIR), lambda p: (0, pairs + p)),
            pl.BlockSpec((length, PAIR), lambda p: (0, 2 * pairs + p)),
        ],
        out_specs=pl.BlockSpec(heads.shape, lambda p: (0, 0)),
        out_shape=jax.ShapeDtypeStruct(heads.shape, jnp.bfloat16),
        scratch_shapes=[pltpu.VMEM((length, PAIR), jnp.float32)] * 2,
        compiler_params=pltpu.CompilerParams(vmem_limit_bytes=vmem_bytes),
        cost_estimate=cost(32 * length * length * pairs * PAIR, 8 * heads.size),
    )(first_row, heads, head_grad, heads, heads)


gelu_scale = 0.7978845608028654
gelu_cubic = 0.044715


def ffn_kernel(*refs):
    normed, grads, pieces = [r[...] for r in refs[:2]], [r[...] for r in refs[2:4]], refs[4:6]
    bias_ref, rows_ref, sum_ref, grad_out, down_out, grad_acc, down_acc = refs[6:]
    step = pl.program_id(0)
    width = normed[0].shape[1]
    unit = pieces[0].shape[2] // 4

    def weight(half, units, kind):
        at = (2 * (units ^ half) + kind) * unit
        return pieces[half][0, :, at : at + unit]

    ups, downs = [None] * 2, [None] * 2
    for units in range(2):
        pre = mm(normed[0], weight(0, units, 0), 1, 0) + mm(normed[1], weight(1, units, 0), 1, 0)
        act_grad = mm(grads[0], weight(0, units, 1), 1, 0) + mm(grads[1], weight(1, units, 1), 1, 0)
        span = slice(units * unit, (units + 1) * unit)
        pre = pre + bias_ref[0, :, span]
        square = pre * pre
        bent = jnp.tanh(gelu_scale * pre * (1.0 + gelu_cubic * square))
        half = 0.5 * (1.0 + bent)
        slope = half + 0.5 * gelu_scale * pre * (1.0 - bent * bent) * (1.0 + 3.0 * gelu_cubic * square)
        act = (pre * half).astype(jnp.bfloat16)
        pre_grad = (act_grad * slope).astype(jnp.bfloat16)
        rows_ref[:, span] = act
        rows_ref[:, (2 + units) * unit : (3 + units) * unit] = pre_grad
        sum_ref[0, :, span] = jnp.sum(pre_grad.astype(jnp.float32), axis=0, keepdims=True)
        for half in range(2):
            up = mm(pre_grad, weight(half, units, 0), 1, 1)
            down = mm(act, weight(half, units, 1), 1, 1)
            ups[half] = up if units == 0 else ups[half] + up
            downs[half] = down if units == 0 else downs[half] + down

    for half in range(2):
        at = slice(half * width, (half + 1) * width)

        @pl.when(step == 0)
        def _():
            grad_acc[:, at] = ups[half]
            down_acc[:, at] = downs[half]

        @pl.when(step > 0)
        def _():
            grad_acc[:, at] += ups[half]
            down_acc[:, at] += downs[half]

    @pl.when(step == pl.num_programs(0) - 1)
    def _():
        grad_out[...] = grad_acc[...].astype(jnp.bfloat16)
        down_out[...] = down_acc[...].astype(jnp.bfloat16)


def ffn_rows_of(normed, grads, part, own_pieces, sib_pieces, bias):
    tokens, features = normed.shape
    width = features // 2
    ring, _, columns = own_pieces.shape
    unit = columns // 4

    def halves(at):
        return [pl.BlockSpec((tokens, width), lambda k, h=h: (at, h)) for h in range(2)]

    piece = pl.BlockSpec((1, width, columns), lambda k: (k, 0, 0))
    whole = pl.BlockSpec((tokens, features), lambda k: (0, 0))
    vector = pl.BlockSpec((1, 1, 2 * unit), lambda k: (k, 0, 0))
    return pl.pallas_call(
        ffn_kernel,
        grid=(ring,),
        in_specs=halves(0) + halves(part) + [piece] * 2 + [vector],
        out_specs=[pl.BlockSpec((tokens, columns), lambda k: (0, k)), vector, whole, whole],
        out_shape=[
            shape((tokens, ring * columns)),
            shape((ring, 1, 2 * unit), jnp.float32),
            shape((tokens, features)),
            shape((tokens, features)),
        ],
        scratch_shapes=[pltpu.VMEM((tokens, features), jnp.float32)] * 2,
        compiler_params=params(),
        cost_estimate=cost(16 * tokens * features * ring * unit, 12 * ring * width * columns),
    )(normed, normed, grads, grads, own_pieces, sib_pieces, bias)


def weight_products_kernel(count, mirrored, index_ref, *refs):
    out_ref = refs[-1]
    normed, grads, rows = [refs[i * count : (i + 1) * count] for i in range(3)]
    twice = rows[0].shape[1] // 2
    unit = twice // 2
    up = down = None
    for j in range(count):
        up_part = mm(normed[j][...], rows[j][:, twice:], 0, 0)
        down_part = mm(grads[j][...], rows[j][:, :twice], 0, 0)
        up = up_part if up is None else up + up_part
        down = down_part if down is None else down + down_part
    for i in range(2):
        units = slice((i ^ mirrored) * unit, ((i ^ mirrored) + 1) * unit)
        out_ref[0, :, i * twice : i * twice + unit] = up[:, units].astype(jnp.bfloat16)
        out_ref[0, :, i * twice + unit : (i + 1) * twice] = down[:, units].astype(jnp.bfloat16)


def weight_products(index, normed, grads, rows, half):
    count = len(normed)
    tokens, features = normed[0].shape
    width = features // 2
    ring = 4
    columns = rows[0].shape[1] // ring
    size = min(256, width)
    blocks = width // size
    left = [pl.BlockSpec((tokens, size), lambda k, d, s: (0, half * blocks + d))] * count
    left += [
        pl.BlockSpec((tokens, size), lambda k, d, s, j=j: (j, half * blocks + d)) for j in range(count)
    ]
    right = [pl.BlockSpec((tokens, columns), lambda k, d, s: (0, k))] * count
    return pl.pallas_call(
        functools.partial(weight_products_kernel, count, half),
        grid_spec=pltpu.PrefetchScalarGridSpec(
            num_scalar_prefetch=1,
            grid=(ring, blocks),
            in_specs=left + right,
            out_specs=pl.BlockSpec(
                (1, size, columns),
                lambda k, d, s: (jnp.where(s[2] >= k, s[2] - k, s[2] - k + ring), d, 0),
            ),
        ),
        out_shape=shape((ring, width, columns)),
        compiler_params=params(),
        cost_estimate=cost(
            2 * count * tokens * width * ring * columns, 4 * count * tokens * features * ring
        ),
    )(index, *normed, *([grads] * count), *rows)


def params(**more):
    return pltpu.CompilerParams(vmem_limit_bytes=vmem_bytes, **more)


def cost(flops, nbytes):
    return pl.CostEstimate(flops=20 * flops, bytes_accessed=20 * nbytes, transcendentals=0)


def shape(dims, dtype=jnp.bfloat16):
    return jax.ShapeDtypeStruct(dims, dtype)


def turned(values):
    return values.astype(jnp.float32).T.astype(jnp.bfloat16)


def pack_heads_kernel(index_ref, *refs):
    sources, outs = refs[:8], refs[8:]
    own = sources[0].shape[1]
    for which in range(2):
        for i in range(4):
            part = sources[4 * which + i][...]
            outs[which][:, i * own : (i + 1) * own] = part if i < 3 else turned(part)


def pack_heads(index, weights, count):
    width, units = weights[0].shape
    own, block = units // 2, width // 4

    def feature(which):
        return pl.BlockSpec((block, own), lambda j, s: (s[1] ^ j, s[0] ^ which))

    def turned_block(which):
        return pl.BlockSpec((own, block), lambda j, s: (s[0] ^ which, s[1] ^ j))

    in_specs = []
    for which in range(2):
        in_specs += [feature(which)] * 3 + [turned_block(which)]
    return pl.pallas_call(
        pack_heads_kernel,
        grid_spec=pltpu.PrefetchScalarGridSpec(
            num_scalar_prefetch=1,
            grid=(count,),
            in_specs=in_specs,
            out_specs=[pl.BlockSpec((block, 4 * own), lambda j, s: (j, 0))] * 2,
        ),
        out_shape=[shape((count * block, 4 * own))] * 2,
        compiler_params=params(),
        cost_estimate=cost(0, 32 * count * block * own),
    )(index, *weights, *weights)


def pack_ff_kernel(index_ref, up_own, down_own, up_sib, down_sib, out_ref):
    unit = up_own.shape[1]
    parts = (up_own[...], turned(down_own[...]), up_sib[...], turned(down_sib[...]))
    for i, part in enumerate(parts):
        out_ref[:, i * unit : (i + 1) * unit] = part


def pack_ff(index, up_weight, down_weight):
    width, units = up_weight.shape
    unit, block = units // 8, width // 4
    in_specs = []
    for which in range(2):
        in_specs += [
            pl.BlockSpec((block, unit), lambda d, s, w=which: (d, 2 * s[1] + (s[0] ^ w))),
            pl.BlockSpec((unit, block), lambda d, s, w=which: (2 * s[1] + (s[0] ^ w), d)),
        ]
    return pl.pallas_call(
        pack_ff_kernel,
        grid_spec=pltpu.PrefetchScalarGridSpec(
            num_scalar_prefetch=1,
            grid=(4,),
            in_specs=in_specs,
            out_specs=pl.BlockSpec((block, 4 * unit), lambda d, s: (d, 0)),
        ),
        out_shape=shape((width, 4 * unit)),
        compiler_params=params(),
        cost_estimate=cost(0, 16 * width * unit),
    )(index, up_weight, down_weight, up_weight, down_weight)


def stack_kernel(*refs):
    pieces, outs = refs[:3], refs[-2:]
    block = pieces[0].shape[0] // 2
    for j, piece in enumerate(pieces):
        for i in range(2):
            outs[i][j * block : (j + 1) * block, :] = piece[i * block : (i + 1) * block, :]
    for i in range(2):
        outs[i][3 * block :, :] = refs[3 + i][...]


def stack_pieces(pieces):
    rows, columns = pieces[0].shape
    return pl.pallas_call(
        stack_kernel,
        out_shape=[shape((2 * rows, columns))] * 2,
        compiler_params=params(),
        cost_estimate=cost(0, 16 * rows * columns),
    )(*pieces)


def norm_kernel(index_ref, own_ref, sib_ref, vectors_ref, out_ref, stats_ref):
    own = own_ref[...].astype(jnp.float32)
    sib = sib_ref[...].astype(jnp.float32)
    width = own.shape[1]
    average = (jnp.sum(own, axis=1, keepdims=True) + jnp.sum(sib, axis=1, keepdims=True)) / (2 * width)
    own, sib = own - average, sib - average
    square = jnp.sum(own * own, axis=1, keepdims=True) + jnp.sum(sib * sib, axis=1, keepdims=True)
    inverse = lax.rsqrt(square / (2 * width) + norm_eps)
    block = width // 4
    for half, values in enumerate((own, sib)):
        gain, shift = vectors_ref[2 * half, :][None], vectors_ref[2 * half + 1, :][None]
        rounded = (values * inverse * gain + shift).astype(jnp.bfloat16)
        for i in range(4):
            at = pl.multiple_of(half * width + (index_ref[1] ^ i) * block, block)
            out_ref[:, pl.ds(at, block)] = rounded[:, i * block : (i + 1) * block]
    lane = lax.broadcasted_iota(jnp.int32, stats_ref.shape, 1)
    stats_ref[...] = jnp.where(lane == 0, average, inverse)


def norm_rows(index, own, sib, vectors):
    tokens, width = own.shape
    size = min(256, tokens)
    rows = pl.BlockSpec((size, width), lambda i, s: (i, 0))
    return pl.pallas_call(
        norm_kernel,
        grid_spec=pltpu.PrefetchScalarGridSpec(
            num_scalar_prefetch=1,
            grid=(tokens // size,),
            in_specs=[rows, rows, pl.BlockSpec((4, width), lambda i, s: (0, 0))],
            out_specs=[
                pl.BlockSpec((size, 2 * width), lambda i, s: (i, 0)),
                pl.BlockSpec((size, 128), lambda i, s: (i, 0)),
            ],
        ),
        out_shape=[shape((tokens, 2 * width)), shape((tokens, 128), jnp.float32)],
        compiler_params=params(),
        cost_estimate=cost(0, 8 * tokens * width),
    )(index, own, sib, vectors)


def project_kernel(own_ref, sib_ref, own_weight, sib_weight, bias_ref, out_ref):
    total = mm(own_ref[...], own_weight[...], 1, 0) + mm(sib_ref[...], sib_weight[...], 1, 0)
    out_ref[...] = (total + bias_ref[...]).astype(jnp.bfloat16)


def halves_of(size, width):
    return [pl.BlockSpec((size, width), lambda i, h=h: (i, h)) for h in range(2)]


def project(normed, own_weight, sib_weight, bias):
    tokens, features = normed.shape
    width, units = features // 2, bias.shape[1]
    size = min(256, tokens)
    weight = pl.BlockSpec((width, units), lambda i: (0, 0))
    return pl.pallas_call(
        project_kernel,
        grid=(tokens // size,),
        in_specs=halves_of(size, width)
        + [weight, weight, pl.BlockSpec((1, units), lambda i: (0, 0))],
        out_specs=pl.BlockSpec((size, units), lambda i: (i, 0)),
        out_shape=shape((tokens, units)),
        compiler_params=params(),
        cost_estimate=cost(4 * tokens * width * units, 4 * tokens * width + 4 * width * units),
    )(normed, normed, own_weight, sib_weight, bias)


def sum_rows_kernel(count, *refs):
    out_ref = refs[-1]
    width = refs[count].shape[0]
    for half in range(2):
        at = slice(half * width, (half + 1) * width)
        total = refs[3 * count][:, at] if len(refs) > 3 * count + 1 else None
        for k in range(count):
            part = mm(refs[k][...], refs[(1 + half) * count + k][...], 1, 1)
            total = part if total is None else total + part
        out_ref[:, at] = total


def sum_rows(rows, own_weights, sib_weights, at, before=()):
    count = len(rows)
    tokens, units = rows[0].shape
    width = own_weights[0].shape[0]
    size = min(256, tokens)
    full = pl.BlockSpec((size, 2 * width), lambda i: (i, 0))
    return pl.pallas_call(
        functools.partial(sum_rows_kernel, count),
        grid=(tokens // size,),
        in_specs=[pl.BlockSpec((size, units), lambda i: (i, 0))] * count
        + [pl.BlockSpec((width, units), lambda i: (0, at))] * (2 * count)
        + [full] * len(before),
        out_specs=full,
        out_shape=shape((tokens, 2 * width), jnp.float32),
        compiler_params=params(),
        cost_estimate=cost(4 * count * tokens * units * width, 8 * tokens * width),
    )(*rows, *own_weights, *sib_weights, *before)


def head_grads_kernel(own_ref, sib_ref, *refs):
    out_ref = refs[-1]
    count = (len(refs) - 1) // 2
    own = refs[0].shape[1]
    for k in range(count):
        total = mm(own_ref[...], refs[k][...], 1, 0) + mm(sib_ref[...], refs[count + k][...], 1, 0)
        out_ref[:, k * own : (k + 1) * own] = total.astype(jnp.bfloat16)


def head_grads(grads, own_weights, sib_weights):
    tokens, width = grads.shape[0], grads.shape[1] // 2
    count = len(own_weights)
    units = own_weights[0].shape[1] // 4
    size = min(256, tokens)
    return pl.pallas_call(
        head_grads_kernel,
        grid=(tokens // size,),
        in_specs=halves_of(size, width) + [pl.BlockSpec((width, units), lambda i: (0, 3))] * (2 * count),
        out_specs=pl.BlockSpec((size, count * units), lambda i: (i, 0)),
        out_shape=shape((tokens, count * units)),
        compiler_params=params(),
        cost_estimate=cost(4 * count * tokens * width * units, 8 * tokens * width),
    )(grads, grads, *own_weights, *sib_weights)


def head_products_kernel(*refs):
    normed, grads = refs[:2], refs[2:4]
    heads_ref, attended_ref = refs[4:6]
    outs, sum_ref = refs[6:8], refs[8]
    split = heads_ref.shape[1]
    for i in range(2):
        outs[i][:, :split] = mm(normed[i][...], heads_ref[...], 0, 0).astype(jnp.bfloat16)
        outs[i][:, split:] = mm(grads[i][...], attended_ref[...], 0, 0).astype(jnp.bfloat16)

    @pl.when(pl.program_id(0) == 0)
    def _():
        sum_ref[...] = jnp.sum(heads_ref[...].astype(jnp.float32), axis=0, keepdims=True)


def head_products(normed, grads, head_grad, attended):
    tokens, width = normed.shape[0], normed.shape[1] // 2
    split, own = head_grad.shape[1], attended.shape[1]
    size = min(256, width)
    blocks = width // size
    left = [pl.BlockSpec((tokens, size), lambda d, h=h: (0, h * blocks + d)) for h in range(2)]
    out = pl.BlockSpec((size, split + own), lambda d: (d, 0))
    return pl.pallas_call(
        head_products_kernel,
        grid=(width // size,),
        in_specs=left * 2
        + [pl.BlockSpec((tokens, split), lambda d: (0, 0)), pl.BlockSpec((tokens, own), lambda d: (0, 0))],
        out_specs=[out, out, pl.BlockSpec((1, split), lambda d: (0, 0))],
        out_shape=[shape((width, split + own))] * 2 + [shape((1, split), jnp.float32)],
        compiler_params=params(),
        cost_estimate=cost(4 * tokens * width * (split + own), 12 * tokens * width),
    )(normed, normed, grads, grads, head_grad, attended)


def block_at(half, width, place):
    block = width // 4
    return pl.ds(pl.multiple_of(half * width + place * block, block), block)


def norm_two_kernel(
    index_ref, rows_ref, came_ref, own_ref, sib_ref, vectors_ref, hidden_ref, normed_ref, stats_ref
):
    width = own_ref.shape[1]
    block = width // 4
    for half, tokens_ref in enumerate((own_ref, sib_ref)):
        for i in range(4):
            at = block_at(half, width, index_ref[1] ^ i)
            span = slice(half * width + i * block, half * width + (i + 1) * block)
            hidden_ref[:, span] = (
                tokens_ref[:, i * block : (i + 1) * block].astype(jnp.float32)
                + rows_ref[:, at]
                + came_ref[:, at].astype(jnp.float32)
                + vectors_ref[4:5, span]
            )
    hidden = hidden_ref[...]
    average = jnp.mean(hidden, axis=1, keepdims=True)
    centered = hidden - average
    inverse = lax.rsqrt(jnp.mean(centered * centered, axis=1, keepdims=True) + norm_eps)
    normed_ref[...] = (centered * inverse * vectors_ref[2:3, :] + vectors_ref[3:4, :]).astype(jnp.bfloat16)
    lane = lax.broadcasted_iota(jnp.int32, stats_ref.shape, 1)
    stats_ref[...] = jnp.where(lane == 0, average, inverse)


def my_rows(size, columns, blocks):
    return pl.BlockSpec((size, columns), lambda i, s: (s[0] * blocks + i, 0))


def norm_two(index, rows, came, own, sib, vectors):
    tokens, features = came.shape
    size = tokens // 2
    mine = my_rows(size, features // 2, 2)
    plain = pl.BlockSpec((size, features), lambda i, s: (i, 0))
    return pl.pallas_call(
        norm_two_kernel,
        grid_spec=pltpu.PrefetchScalarGridSpec(
            num_scalar_prefetch=1,
            grid=(2,),
            in_specs=[
                my_rows(size, features, 2),
                plain,
                mine,
                mine,
                pl.BlockSpec(vectors.shape, lambda i, s: (0, 0)),
            ],
            out_specs=[plain, plain, pl.BlockSpec((size, 128), lambda i, s: (i, 0))],
        ),
        out_shape=[
            shape((tokens, features), jnp.float32),
            shape((tokens, features)),
            shape((tokens, 128), jnp.float32),
        ],
        compiler_params=params(),
        cost_estimate=cost(0, 16 * tokens * features),
    )(index, rows, came, own, sib, vectors)


def norm_pull(grads, normal, inverse, gain):
    scaled = grads * gain
    return inverse * (
        scaled
        - jnp.mean(scaled, axis=1, keepdims=True)
        - normal * jnp.mean(scaled * normal, axis=1, keepdims=True)
    )


def add_sums(sums_ref, parts):
    rows = [jnp.sum(p, axis=0, keepdims=True) for p in parts]
    rows += [jnp.zeros_like(rows[0])] * (8 - len(rows))
    total = jnp.concatenate(rows, axis=0)

    @pl.when(pl.program_id(0) == 0)
    def _():
        sums_ref[...] = total

    @pl.when(pl.program_id(0) > 0)
    def _():
        sums_ref[...] += total


def norm_two_back_kernel(index_ref, *refs):
    here, x_top, y_top, x_bottom, y_bottom, hidden_ref, stats_ref, branch_ref, vectors_ref = refs[:9]
    grad_ref, blocks_ref, mirror_ref, sums_ref = refs[9:]
    f32 = jnp.float32
    top = pl.program_id(0) == 0
    from_x = jnp.where(top, x_top[...].astype(f32), x_bottom[...].astype(f32))
    from_y = jnp.where(top, y_top[...].astype(f32), y_bottom[...].astype(f32))
    grads = here[...].astype(f32) + from_x + from_y
    inverse = stats_ref[:, 1:2]
    normal = (hidden_ref[...] - stats_ref[:, :1]) * inverse
    branch = branch_ref[...].astype(f32)
    total = branch + norm_pull(grads, normal, inverse, vectors_ref[2:3, :])
    grad_ref[...] = total
    rounded = total.astype(jnp.bfloat16)
    width = rounded.shape[1] // 2
    block = width // 4
    for half in range(2):
        for i in range(4):
            part = rounded[:, half * width + i * block : half * width + (i + 1) * block]
            place = index_ref[1] ^ i
            blocks_ref[:, block_at(half, width, place)] = part
            mirror_ref[:, block_at(1 - half, width, place)] = part
    add_sums(sums_ref, (grads * normal, grads, rounded.astype(f32), branch))


def norm_two_back(index, parts, hidden, stats, branch, vectors):
    tokens, features = hidden.shape
    size = tokens // 2
    plain = pl.BlockSpec((size, features), lambda i, s: (i, 0))
    once = pl.BlockSpec((size, features), lambda i, s: (0, 0))
    return pl.pallas_call(
        norm_two_back_kernel,
        grid_spec=pltpu.PrefetchScalarGridSpec(
            num_scalar_prefetch=1,
            grid=(2,),
            in_specs=[plain]
            + [once] * 4
            + [
                plain,
                pl.BlockSpec((size, 128), lambda i, s: (i, 0)),
                plain,
                pl.BlockSpec(vectors.shape, lambda i, s: (0, 0)),
            ],
            out_specs=[plain] * 3 + [pl.BlockSpec((8, features), lambda i, s: (0, 0))],
        ),
        out_shape=[
            shape((tokens, features), jnp.float32),
            shape((tokens, features)),
            shape((tokens, features)),
            shape((8, features), jnp.float32),
        ],
        compiler_params=params(),
        cost_estimate=cost(0, 24 * tokens * features),
    )(index, *parts, hidden, stats, branch, vectors)


def norm_one_back_kernel(index_ref, *refs):
    rows_ref, came_ref, own_ref, sib_ref, stats_ref, out_own, out_sib, keep_ref, hidden_ref = refs[:9]
    vectors_ref, own_grad, sib_grad, sums_ref, grads_ref = refs[9:]
    f32 = jnp.float32
    width = own_ref.shape[1]
    block = width // 4
    for half in range(2):
        for i in range(4):
            at = block_at(half, width, index_ref[1] ^ i)
            span = slice(half * width + i * block, half * width + (i + 1) * block)
            grads_ref[:, span] = rows_ref[:, at] + came_ref[:, at].astype(f32)
    grads = grads_ref[...]
    inverse = stats_ref[:, 1:2]
    tokens = jnp.concatenate([own_ref[...], sib_ref[...]], axis=1).astype(f32)
    normal = (tokens - stats_ref[:, :1]) * inverse
    total = hidden_ref[...] + norm_pull(grads, normal, inverse, vectors_ref[0:1, :])
    dropped = 1.0 - keep_ref[...]
    own_grad[...] = out_own[...].astype(f32) * dropped + total[:, :width]
    sib_grad[...] = out_sib[...].astype(f32) * dropped + total[:, width:]
    add_sums(sums_ref, (grads * normal, grads))


def norm_one_back(index, rows, came, own, sib, stats, out_own, out_sib, keep, hidden, vectors):
    tokens, features = came.shape
    size, width = tokens // 2, features // 2
    plain = pl.BlockSpec((size, features), lambda i, s: (i, 0))
    half_wide = pl.BlockSpec((size, width), lambda i, s: (i, 0))
    return pl.pallas_call(
        norm_one_back_kernel,
        grid_spec=pltpu.PrefetchScalarGridSpec(
            num_scalar_prefetch=1,
            grid=(2,),
            in_specs=[
                my_rows(size, features, 2),
                plain,
                my_rows(size, width, 2),
                my_rows(size, width, 2),
                my_rows(size, 128, 2),
                my_rows(size, width, 2),
                half_wide,
                pl.BlockSpec((size, 1), lambda i, s: (i, 0)),
                plain,
                pl.BlockSpec(vectors.shape, lambda i, s: (0, 0)),
            ],
            out_specs=[half_wide, half_wide, pl.BlockSpec((8, features), lambda i, s: (0, 0))],
            scratch_shapes=[pltpu.VMEM((size, features), jnp.float32)],
        ),
        out_shape=[shape((tokens, width), jnp.float32)] * 2 + [shape((8, features), jnp.float32)],
        compiler_params=params(),
        cost_estimate=cost(0, 24 * tokens * features),
    )(index, rows, came, own, sib, stats, out_own, out_sib, keep, hidden, vectors)


def select_piece(refs, step, use):
    for j in range(3):

        @pl.when(step == j)
        def _():
            use(refs[j][...])

    @pl.when(step == 3)
    def _():
        use(jnp.concatenate([refs[3][...], refs[4][...]], axis=0))


def place_heads_kernel(index_ref, *refs):
    pieces, outs = refs[:5], refs[5:]
    own = pieces[0].shape[1] // 8

    def use(piece):
        for which in range(2):
            at = pl.multiple_of((index_ref[0] ^ which) * own, own)
            for m in range(4):
                part = piece[:, (4 * which + m) * own : (4 * which + m + 1) * own].astype(jnp.float32)
                if m < 3:
                    outs[m][:, pl.ds(at, own)] = part
                else:
                    outs[m][pl.ds(at, own), :] = part.T

    select_piece(pieces, pl.program_id(0), use)


def place_heads(index, pieces):
    block, columns = pieces[0].shape
    units, width = columns // 4, 4 * block
    whole = [pl.BlockSpec(p.shape, lambda j, s: (0, 0)) for p in pieces]
    return pl.pallas_call(
        place_heads_kernel,
        grid_spec=pltpu.PrefetchScalarGridSpec(
            num_scalar_prefetch=1,
            grid=(4,),
            in_specs=whole,
            out_specs=[pl.BlockSpec((block, units), lambda j, s: (s[1] ^ j, 0))] * 3
            + [pl.BlockSpec((units, block), lambda j, s: (0, s[1] ^ j))],
        ),
        out_shape=[shape((width, units), jnp.float32)] * 3 + [shape((units, width), jnp.float32)],
        compiler_params=params(),
        cost_estimate=cost(0, 24 * width * units),
    )(index, *pieces)


def place_ff_kernel(index_ref, *refs):
    pieces, (up_out, down_out) = refs[:-2], refs[-2:]
    rows = pieces[0].shape[1]
    unit = pieces[0].shape[2] // 4
    for part, piece_ref in enumerate(pieces):
        span = slice(part * rows, (part + 1) * rows)
        for which in range(2):
            at = pl.multiple_of((index_ref[0] ^ which) * unit, unit)
            start = 2 * which * unit
            up_out[span, pl.ds(at, unit)] = piece_ref[0, :, start : start + unit].astype(jnp.float32)
            down_out[pl.ds(at, unit), span] = (
                piece_ref[0, :, start + unit : start + 2 * unit].astype(jnp.float32).T
            )


def place_ff(index, pieces):
    count, rows, columns = pieces[0].shape
    width, quarter = rows * len(pieces), columns // 2
    return pl.pallas_call(
        place_ff_kernel,
        grid_spec=pltpu.PrefetchScalarGridSpec(
            num_scalar_prefetch=1,
            grid=(count,),
            in_specs=[pl.BlockSpec((1, rows, columns), lambda j, s: (j, 0, 0))] * len(pieces),
            out_specs=[
                pl.BlockSpec((width, quarter), lambda j, s: (0, j)),
                pl.BlockSpec((quarter, width), lambda j, s: (j, 0)),
            ],
        ),
        out_shape=[
            shape((width, count * quarter), jnp.float32),
            shape((count * quarter, width), jnp.float32),
        ],
        compiler_params=params(),
        cost_estimate=cost(0, 48 * width * quarter),
    )(index, *pieces)


def body_local(
    tokens_in,
    out_grad,
    segment_ids,
    active_lengths,
    norm1_gain,
    norm1_shift,
    query_weight,
    query_bias,
    key_weight,
    value_weight,
    value_bias,
    out_weight,
    out_bias,
    norm2_gain,
    norm2_shift,
    up_weight,
    up_bias,
    down_weight,
    down_bias,
):
    f32, bf16 = jnp.float32, jnp.bfloat16
    rows, width = tokens_in.shape
    ring = lax.axis_size("col")
    row_i = lax.axis_index("row")
    plane_i = lax.axis_index("dp")
    col_i = lax.axis_index("col")
    own = query_weight.shape[1] // 2
    block = width // 4
    quarter = up_weight.shape[1] // 4
    unit = quarter // 2
    half = rows // 2
    order = Order()
    plane, column = Plane(order), Link(order)
    index = jnp.stack([row_i, plane_i, col_i]).astype(jnp.int32)

    def cut(values, start, size):
        return lax.dynamic_slice_in_dim(values, start, size, axis=0)

    def mirrored(values):
        return jnp.concatenate([values[:, width:], values[:, :width]], axis=1)

    def my_tokens(values):
        return cut(values, row_i * half, half)

    def other_tokens(values):
        return cut(values, (1 - row_i) * half, half)

    def all_tokens(mine, other):
        return jnp.where(
            row_i == 0, jnp.concatenate([mine, other], axis=0), jnp.concatenate([other, mine], axis=0)
        )

    tokens_sib = order.swap(tokens_in)
    out_grad_sib = swap(other_tokens(out_grad))

    ff_bias = cut(up_bias, plane_i * quarter, quarter).reshape(2, unit)
    mine = jnp.concatenate(
        [
            cut(query_bias, row_i * own, own),
            jnp.zeros((own,), f32),
            cut(value_bias, row_i * own, own),
            picked(ff_bias, row_i),
            picked(ff_bias, 1 - row_i),
        ]
    )
    small = [mine] + [
        lax.ppermute(mine, "col", [(i, (i + k) % ring) for i in range(ring)]) for k in range(1, ring)
    ]

    sources = (query_weight, key_weight, value_weight, out_weight)
    piece = order.run(pack_heads, after(index, mine), sources, 1)
    pieces = [jnp.concatenate([piece[0], swap(piece[1])], axis=0)]
    column.last = small[1:]
    pieces.append(column.send(step_up, pieces[0]))

    active_all = active_rows(segment_ids, active_lengths)
    active_here = my_tokens(cut(active_all, col_i * rows, rows))
    keep_mask = active_here.astype(f32)[:, None]
    out_grads = jnp.concatenate([my_tokens(out_grad), out_grad_sib], axis=1).astype(f32)
    branch_mine = (after(out_grads, *order.tokens) * keep_mask).astype(bf16)
    branch_first = plane.both(branch_mine[: half // 2], branch_mine[: half // 2])
    vectors = jnp.stack([norm1_gain, norm1_shift, norm2_gain, norm2_shift, out_bias, down_bias])
    vectors_sib = swap(vectors)
    vectors_all = jnp.concatenate([vectors, vectors_sib], axis=1)
    here = order.run(pack_heads, index, sources, 4)
    own_parts, other_rows = [here[0]], [order.swap(here[1])]
    ff_piece = order.run(pack_ff, index, up_weight, down_weight)
    ff_own, ff_sib = [ff_piece], []
    normed_one, stats_one = order.run(
        norm_rows,
        index,
        tokens_in,
        tokens_sib,
        jnp.concatenate([vectors[:2], vectors_sib[:2]], axis=0),
    )

    segment_row = picked(segment_ids, col_i)
    member = (segment_row[:, None] == jnp.arange(active_lengths.shape[1])).astype(jnp.int32)
    counts = jnp.sum(member, axis=0)
    first_row = jnp.sum(member * (jnp.cumsum(counts) - counts), axis=1)[None, :]

    heads, attended = [], []

    def attend_project(k):
        heads.append(
            order.run(project, normed_one, own_parts[k], other_rows[k], small[k][None, : 3 * own])
        )

    def attend(k):
        attended.append(order.run(local_forward, heads[k], first_row))

    def stack(k, near, far):
        own_part, other_part = order.run(stack_pieces, [pieces[k], *near, *far])
        own_parts.append(own_part)
        other_rows.append(other_part)

    def next_ff():
        ff_sib.append(order.swap(ff_own[-1]))
        ff_own.append(column.send(step_up, ff_own[-1]))

    attend_project(0)
    pieces.append(column.send(step_up, pieces[1]))
    near = plane.both(pieces[1], pieces[1])
    attend(0)
    far = plane.far(*near)
    pieces.append(column.send(step_up, pieces[2]))
    last_near, last_far = near, far
    near = plane.both(pieces[2], pieces[2])
    stack(1, last_near, last_far)
    attend_project(1)
    attend(1)
    next_ff()
    far = plane.far(*near)
    last_near, last_far = near, far
    near = plane.both(pieces[3], pieces[3])
    stack(2, last_near, last_far)
    attend_project(2)
    attend(2)
    next_ff()
    far = plane.far(*near)
    last_near, last_far = near, far
    branch_far = plane.far(*branch_first)
    stack(3, last_near, last_far)
    before = order.run(sum_rows, attended[:3], own_parts[:3], other_rows[:3], 3)
    second_near = plane.both(branch_mine[half // 2 :], branch_mine[half // 2 :])
    attend_project(3)
    attend(3)
    next_ff()
    order.tokens += second_near
    attention_rows = order.run(sum_rows, attended[3:], own_parts[3:], other_rows[3:], 3, (before,))
    arrived = swap(order.tie(mirrored(other_tokens(attention_rows)).astype(bf16)))
    second_far = plane.far(*second_near)

    hidden_one, normed_two, stats_two = order.run(
        norm_two, index, attention_rows, arrived, tokens_in, tokens_sib, vectors_all
    )

    normed = [normed_two, *plane.both(normed_two, normed_two, True)]
    branch_all = jnp.concatenate(
        [branch_mine]
        + [part for pair in zip(branch_first, second_near) for part in pair]
        + [*branch_far, *second_far],
        axis=0,
    )
    ff_sib.append(order.swap(ff_own[3]))
    ff_own_all, ff_sib_all = jnp.stack(ff_own), jnp.stack(ff_sib)
    ff_biases = jnp.stack([s[None, 3 * own :] for s in small])
    ff_rows, up_sums, grad_parts, down_parts = [], [], [], []

    def feed_forward(j):
        results = order.run(ffn_rows_of, normed[j], branch_all, j, ff_own_all, ff_sib_all, ff_biases)
        for kept, result in zip((ff_rows, up_sums, grad_parts, down_parts), results):
            kept.append(result)

    def plane_total(here, x_top, y_top, x_bottom, y_bottom):
        cut_at = half // 2
        return jnp.concatenate(
            [
                here[:cut_at].astype(f32) + x_top.astype(f32) + y_top.astype(f32),
                here[cut_at:].astype(f32) + x_bottom.astype(f32) + y_bottom.astype(f32),
            ],
            axis=0,
        )

    def top(values):
        return values[: half // 2]

    def bottom(values):
        return values[half // 2 :]

    def second_steps(parts, via_x, via_y):
        via_x, via_y = after((via_x, via_y), *order.tokens)
        return plane.both(add_rounded(bottom(parts[1]), via_y), add_rounded(top(parts[2]), via_x))

    def weight_grads(part):
        return order.run(weight_products, index, normed, branch_all, ff_rows, part)

    feed_forward(0)
    normed_far = plane.far(normed[1], normed[2])
    feed_forward(1)
    feed_forward(2)
    x_top, y_bottom = plane.both(top(grad_parts[1]), bottom(grad_parts[2]))
    normed.append(jnp.concatenate(normed_far, axis=0))
    feed_forward(3)
    via_x, via_y = plane.both(top(grad_parts[3]), bottom(grad_parts[3]))
    ff_other = order.swap(weight_grads(1))
    x_bottom, y_top = second_steps(grad_parts, via_x, via_y)
    ff_mine = weight_grads(0)

    hidden_grad, grad_mine, grad_mirror, sums_two = order.run(
        norm_two_back,
        index,
        (grad_parts[0], x_top, y_top, x_bottom, y_bottom),
        hidden_one,
        stats_two,
        branch_mine,
        vectors_all,
    )
    down_x_top, down_y_bottom = plane.both(top(down_parts[1]), bottom(down_parts[2]))
    grad_other = order.swap(grad_mirror)
    grad_rows = all_tokens(grad_mine, grad_other)

    ff_grads = []
    for part in range(2):
        span = slice(part * width // 2, (part + 1) * width // 2)
        total = order.tie(add_rounded(ff_mine[:, span], ff_other[:, span]))
        total = lax.psum_scatter(total, "col", scatter_dimension=0, tiled=False)
        ff_grads.append(lax.all_gather(total, "dp"))

    head_grad = order.run(head_grads, grad_rows, own_parts, other_rows)
    head_rows, bias_rows, group_parts = [None] * ring, [None] * ring, [None] * ring

    def backward(k):
        head_rows[k] = order.run(
            lambda h, g, f: local_backward(h, g, k, f), heads[k], head_grad, first_row
        )

    def head_weights(k):
        *group_parts[k], bias_rows[k] = order.run(
            head_products, normed_one, grad_rows, head_rows[k], attended[k]
        )

    def part_of(k, j, which):
        return group_parts[k][which][j * block : (j + 1) * block]

    def first_messages(k):
        return plane.both(part_of(k, 3, 0), part_of(k, 3, 1))

    def second_messages(k, via):
        via_x, via_y = after(via, *order.tokens)
        return plane.both(
            jnp.concatenate([part_of(k, 1, 0), add_rounded(part_of(k, 1, 1), via_y)], axis=1),
            jnp.concatenate([add_rounded(part_of(k, 2, 0), via_x), part_of(k, 2, 1)], axis=1),
        )

    def group_total(k, came, total):
        came_x, came_y = after(came, *order.tokens)
        here = jnp.concatenate([part_of(k, 0, 0), part_of(k, 0, 1)], axis=1)
        here = here.astype(f32) + came_x.astype(f32) + came_y.astype(f32)
        if total is not None:
            here = here + total.astype(f32)
        return here.astype(bf16)

    down_via_x, down_via_y = plane.both(top(down_parts[3]), bottom(down_parts[3]))
    backward(3)
    head_weights(3)
    down_x_bottom, down_y_top = second_steps(down_parts, down_via_x, down_via_y)
    backward(2)
    head_weights(2)
    via = first_messages(3)
    backward(1)
    came = second_messages(3, via)
    head_weights(1)
    backward(0)
    total = group_total(3, came, None)
    via = first_messages(2)
    head_weights(0)
    came = second_messages(2, via)
    summed_group = group_total(2, came, None)
    via = first_messages(1)
    back_rows = order.run(sum_rows, head_rows, own_parts, other_rows, 0)
    arrived = order.swap(mirrored(other_tokens(back_rows)).astype(bf16))
    came = second_messages(1, via)
    total = column.send(step_down, total)

    input_mine, input_other, sums_one = order.run(
        norm_one_back,
        index,
        back_rows,
        arrived,
        tokens_in,
        tokens_sib,
        stats_one,
        out_grad,
        out_grad_sib,
        keep_mask,
        hidden_grad,
        vectors_all,
    )
    input_grad = all_tokens(input_mine, swap(input_other))

    def by_column(relative):
        places = jnp.mod(col_i - jnp.arange(ring), ring)
        return jnp.take(relative, places, axis=0)

    row_hot = (jnp.arange(2) == row_i).astype(f32)
    plane_hot = (jnp.arange(4) == plane_i).astype(f32)
    head_bias = by_column(jnp.stack(bias_rows)).reshape(ring, 3, 1, own) * row_hot[:, None]
    up_bias_part = by_column(sum(up_sums).reshape(ring, 2, unit))
    up_bias_part = jnp.where(row_i == 0, up_bias_part, up_bias_part[:, ::-1])
    up_bias_part = up_bias_part[:, None] * plane_hot[:, None, None]
    bias_vector = jnp.concatenate([head_bias.reshape(ring, -1), up_bias_part.reshape(ring, -1)], axis=1)
    feature_sums = jnp.concatenate([sums_one[:2], sums_two[:4]], axis=0)
    summed = jnp.concatenate([bias_vector.reshape(-1), feature_sums[:, :width].reshape(-1)])
    summed = summed + swap(
        jnp.concatenate([bias_vector.reshape(-1), feature_sums[:, width:].reshape(-1)])
    )

    via = first_messages(0)
    total = add_rounded(total, summed_group)
    total = column.send(step_down, total)
    summed_group = group_total(1, came, None)
    came = second_messages(0, via)
    total = add_rounded(total, summed_group)
    total = column.send(step_down, total)
    summed = order.tie(summed)
    summed = summed + plane.x.send(step_x, summed)
    summed = summed + plane.y.send(step_y, summed)
    step = 1
    while step < ring:
        pairs = [(i, i ^ step) for i in range(ring)]
        summed = summed + column.send(lambda v: lax.ppermute(v, "col", pairs), summed)
        step *= 2
    total = group_total(0, came, total)
    total = jnp.concatenate([total[:, : 4 * own], swap(total[:, 4 * own :])], axis=1)
    near = plane.both(total, total)
    up_weight_grad, down_weight_grad = order.run(place_ff, index, ff_grads)
    far = plane.far(*near)
    query_weight_grad, key_weight_grad, value_weight_grad, out_weight_grad = place_heads(
        index, [total, *near, *far]
    )

    tokens_mine = jnp.concatenate([my_tokens(tokens_in), my_tokens(tokens_sib)], axis=1).astype(f32)
    ffn_rows = plane_total(down_parts[0], down_x_top, down_y_top, down_x_bottom, down_y_bottom)
    out_mine = jnp.where(active_here[:, None], hidden_one + ffn_rows + vectors_all[5], tokens_mine)
    layer_out = all_tokens(out_mine[:, :width], swap(out_mine[:, width:]))

    bias_here = picked(summed[: bias_vector.size].reshape(ring, -1), col_i)
    own_here = summed[bias_vector.size :].reshape(6, width)
    size = 2 * own
    return (
        layer_out,
        input_grad,
        own_here[0],
        own_here[1],
        query_weight_grad,
        bias_here[:size],
        key_weight_grad,
        value_weight_grad,
        bias_here[2 * size : 3 * size],
        out_weight_grad,
        own_here[4],
        own_here[2],
        own_here[3],
        up_weight_grad,
        bias_here[3 * size :],
        down_weight_grad,
        own_here[5],
    )


def body(tokens_in, out_grad, segment_ids, *rest):
    ring = lax.axis_size("col")
    local = (
        lax.axis_size("dp") == 4
        and lax.axis_size("row") == 2
        and ring == 4
        and tokens_in.shape[0] == segment_ids.shape[1]
    )
    chosen = body_local if local else body_general
    return chosen(tokens_in, out_grad, segment_ids, *rest)


def solution(mesh):
    placed = (
        P(("dp", "col"), "row"),
        P(("dp", "col"), "row"),
        P("dp", None),
        P("dp", None),
        P("row"),
        P("row"),
        P("row", "col"),
        P("col"),
        P("row", "col"),
        P("row", "col"),
        P("col"),
        P("col", "row"),
        P("row"),
        P("row"),
        P("row"),
        P("row", "col"),
        P("col"),
        P("col", "row"),
        P("row"),
    )
    return jax.shard_map(
        body,
        mesh=mesh,
        in_specs=placed,
        out_specs=(
            P(("dp", "col"), "row"),
            P(("dp", "col"), "row"),
            P("row"),
            P("row"),
            P("row", "col"),
            P("col"),
            P("row", "col"),
            P("row", "col"),
            P("col"),
            P("col", "row"),
            P("row"),
            P("row"),
            P("row"),
            P("row", "col"),
            P("col"),
            P("col", "row"),
            P("row"),
        ),
        check_vma=False,
    )
```

```python
import functools

import jax
import jax.numpy as jnp
from jax import lax
from jax.experimental import pallas as pl
from jax.experimental.pallas import tpu as pltpu
from jax.sharding import PartitionSpec as P

D = 2048
HEAD_DIM = 64


norm_eps = 1e-05
masked_fill = -1e30


def width_totals(total_one, total_two):
    return lax.psum((total_one, total_two), "row")


def token_gather(values):
    return lax.all_gather(values, "col", axis=0, tiled=True)


def token_sums(partial_rows):
    return lax.psum_scatter(partial_rows, "col", scatter_dimension=0, tiled=True)


def unit_gather(values):
    return lax.all_gather(values, "row", axis=1, tiled=True)


def unit_sums(partial_units):
    return lax.psum_scatter(partial_units, "row", scatter_dimension=1, tiled=True)


def gelu_value(values):
    return jax.nn.gelu(values, approximate=True)


def gelu_slope(values):
    result, pullback = jax.vjp(gelu_value, values)
    return pullback(jnp.ones_like(values))[0]


def active_rows(segment_rows, keep_lengths):
    doc_index = jnp.arange(keep_lengths.shape[-1], dtype=jnp.int32)
    member = (segment_rows[:, :, None] == doc_index).astype(jnp.int32)
    counts = jnp.sum(member, axis=1)
    starts = jnp.cumsum(counts, axis=1) - counts
    first_pos = jnp.sum(member * starts[:, None, :], axis=2)
    keep_here = jnp.sum(member * keep_lengths[:, None, :], axis=2)
    position_in = jnp.arange(segment_rows.shape[1], dtype=jnp.int32)[None, :] - first_pos
    return (position_in < keep_here).reshape(-1)


def norm_forward(values, gain_part, shift_part):
    total_one, total_two = width_totals(jnp.sum(values, axis=1), jnp.sum(values * values, axis=1))
    average = total_one / D
    variance = total_two / D - average * average
    inverse = lax.rsqrt(variance + norm_eps)
    normal = (values - average[:, None]) * inverse[:, None]
    return ((normal * gain_part + shift_part).astype(jnp.bfloat16), normal, inverse)


def norm_backward(grad_rows, normal, inverse, gain_part):
    scaled = grad_rows * gain_part
    total_one, total_two = width_totals(jnp.sum(scaled, axis=1), jnp.sum(scaled * normal, axis=1))
    grad_in = inverse[:, None] * (
        scaled - total_one[:, None] / D - normal * (total_two[:, None] / D)
    )
    return (grad_in, jnp.sum(grad_rows * normal, axis=0), jnp.sum(grad_rows, axis=0))


def allowed_mask(segment_row, offset, block_rows):
    key_pos = jnp.arange(segment_row.shape[0], dtype=jnp.int32)
    query_pos = key_pos[offset : offset + block_rows]
    same_doc = segment_row[None, :] == segment_row[offset : offset + block_rows, None]
    return (key_pos[None, :] <= query_pos[:, None]) & same_doc


def attend_forward(query_seq, key_seq, value_seq, segment_row, score_scale):
    seq_length = query_seq.shape[2]
    block_rows = min(512, seq_length)
    outputs = []
    log_parts = []
    for offset in range(0, seq_length, block_rows):
        query_block = query_seq[:, :, offset : offset + block_rows]
        scores = (
            jnp.einsum("hdq,hdk->hqk", query_block, key_seq, preferred_element_type=jnp.float32)
            * score_scale
        )
        scores = jnp.where(allowed_mask(segment_row, offset, block_rows)[None], scores, masked_fill)
        row_max = jnp.max(scores, axis=2, keepdims=True)
        exp_scores = jnp.exp(scores - row_max)
        row_total = jnp.sum(exp_scores, axis=2, keepdims=True)
        weights = (exp_scores / row_total).astype(jnp.bfloat16)
        outputs.append(
            jnp.einsum("hqk,hdk->hdq", weights, value_seq, preferred_element_type=jnp.float32)
        )
        log_parts.append((row_max + jnp.log(row_total))[:, :, 0])
    return (jnp.concatenate(outputs, axis=2), jnp.concatenate(log_parts, axis=1))


def attend_backward(query_seq, key_seq, value_seq, grad_seq, segment_row, log_sums, score_scale):
    seq_length = query_seq.shape[2]
    block_rows = min(512, seq_length)
    key_grad = jnp.zeros(key_seq.shape, jnp.float32)
    value_grad = jnp.zeros(value_seq.shape, jnp.float32)
    query_grads = []
    for offset in range(0, seq_length, block_rows):
        query_block = query_seq[:, :, offset : offset + block_rows]
        grad_block = grad_seq[:, :, offset : offset + block_rows]
        scores = (
            jnp.einsum("hdq,hdk->hqk", query_block, key_seq, preferred_element_type=jnp.float32)
            * score_scale
        )
        scores = jnp.where(allowed_mask(segment_row, offset, block_rows)[None], scores, masked_fill)
        probs = jnp.exp(scores - log_sums[:, offset : offset + block_rows, None])
        prob_grad = jnp.einsum(
            "hdq,hdk->hqk", grad_block, value_seq, preferred_element_type=jnp.float32
        )
        row_dot = jnp.sum(probs * prob_grad, axis=2, keepdims=True)
        score_grad = (probs * (prob_grad - row_dot)).astype(jnp.bfloat16)
        query_grads.append(
            jnp.einsum("hqk,hdk->hdq", score_grad, key_seq, preferred_element_type=jnp.float32)
            * score_scale
        )
        key_grad = (
            key_grad
            + jnp.einsum(
                "hqk,hdq->hdk", score_grad, query_block, preferred_element_type=jnp.float32
            )
            * score_scale
        )
        value_grad = value_grad + jnp.einsum(
            "hqk,hdq->hdk",
            probs.astype(jnp.bfloat16),
            grad_block,
            preferred_element_type=jnp.float32,
        )
    return (jnp.concatenate(query_grads, axis=2), key_grad, value_grad)


def body_general(
    tokens_in,
    out_grad,
    segment_ids,
    active_lengths,
    norm1_gain,
    norm1_shift,
    query_weight,
    query_bias,
    key_weight,
    value_weight,
    value_bias,
    out_weight,
    out_bias,
    norm2_gain,
    norm2_shift,
    up_weight,
    up_bias,
    down_weight,
    down_bias,
):
    local_rows = tokens_in.shape[0]
    seq_here = segment_ids.shape[0]
    seq_length = segment_ids.shape[1]
    group_rows = seq_here * seq_length
    row_index = lax.axis_index("row")
    col_index = lax.axis_index("col")
    active_all = active_rows(segment_ids, active_lengths)
    active_here = lax.dynamic_slice_in_dim(active_all, col_index * local_rows, local_rows)
    keep_mask = active_here.astype(jnp.float32)[:, None]
    score_scale = HEAD_DIM ** (-0.5)
    rows_in = tokens_in.astype(jnp.float32)
    normed_one, normal_one, inverse_one = norm_forward(rows_in, norm1_gain, norm1_shift)
    gathered_one = token_gather(normed_one)
    stacked_weight = jnp.stack([query_weight, key_weight, value_weight])
    projected = unit_sums(
        jnp.einsum("td,kdh->kht", gathered_one, stacked_weight, preferred_element_type=jnp.float32)
    )
    head_width = projected.shape[1]
    head_count = head_width // HEAD_DIM
    query_part = lax.dynamic_slice_in_dim(query_bias, row_index * head_width, head_width)
    value_part = lax.dynamic_slice_in_dim(value_bias, row_index * head_width, head_width)
    bias_stack = jnp.stack([query_part, jnp.zeros_like(query_part), value_part])
    heads_all = (projected + bias_stack[:, :, None]).astype(jnp.bfloat16)

    def to_seqs(values):
        return jnp.moveaxis(values.reshape(head_count, HEAD_DIM, seq_here, seq_length), 2, 0)

    def from_seqs(values):
        return jnp.moveaxis(values, 0, 2).reshape(head_width, group_rows)

    query_seqs = to_seqs(heads_all[0])
    key_seqs = to_seqs(heads_all[1])
    value_seqs = to_seqs(heads_all[2])
    attended_seqs, log_sums = lax.map(
        lambda seq_items: attend_forward(
            seq_items[0], seq_items[1], seq_items[2], seq_items[3], score_scale
        ),
        (query_seqs, key_seqs, value_seqs, segment_ids),
    )
    attended = from_seqs(attended_seqs).astype(jnp.bfloat16)
    gathered_heads = unit_gather(attended[None])
    attention_rows = (
        token_sums(
            jnp.einsum("kht,hd->td", gathered_heads, out_weight, preferred_element_type=jnp.float32)
        )
        + out_bias
    )
    hidden_one = rows_in + attention_rows
    normed_two, normal_two, inverse_two = norm_forward(hidden_one, norm2_gain, norm2_shift)
    gathered_two = token_gather(normed_two)
    up_part = jnp.einsum("td,df->ft", gathered_two, up_weight, preferred_element_type=jnp.float32)[
        None
    ]
    unit_width = up_part.shape[1] // lax.axis_size("row")
    up_slice = lax.dynamic_slice_in_dim(up_bias, row_index * unit_width, unit_width)
    pre_act = unit_sums(up_part)[0] + up_slice[:, None]
    gathered_act = unit_gather(gelu_value(pre_act).astype(jnp.bfloat16)[None])
    ffn_rows = (
        token_sums(
            jnp.einsum("kft,fd->td", gathered_act, down_weight, preferred_element_type=jnp.float32)
        )
        + down_bias
    )
    layer_out = jnp.where(active_here[:, None], hidden_one + ffn_rows, rows_in)
    grad_rows = out_grad.astype(jnp.float32) * keep_mask
    branch_grad = token_gather(grad_rows.astype(jnp.bfloat16))
    down_grad = jnp.einsum(
        "kft,td->fd", gathered_act, branch_grad, preferred_element_type=jnp.float32
    )
    down_bias_grad = jnp.sum(branch_grad, axis=0, dtype=jnp.float32)
    act_part = jnp.einsum(
        "td,fd->ft", branch_grad, down_weight, preferred_element_type=jnp.float32
    )[None]
    act_grad = unit_sums(act_part)[0]
    pre_grad = (act_grad * gelu_slope(pre_act)).astype(jnp.bfloat16)
    gathered_pre = unit_gather(pre_grad[None])
    up_grad = jnp.einsum(
        "td,kft->df", gathered_two, gathered_pre, preferred_element_type=jnp.float32
    )
    up_bias_grad = jnp.sum(gathered_pre[0], axis=1, dtype=jnp.float32)
    normed_grad_two = token_sums(
        jnp.einsum("kft,df->td", gathered_pre, up_weight, preferred_element_type=jnp.float32)
    )
    back_two, gain_two_grad, shift_two_grad = norm_backward(
        normed_grad_two, normal_two, inverse_two, norm2_gain
    )
    hidden_grad = grad_rows + back_two
    attention_grad = token_gather(hidden_grad.astype(jnp.bfloat16))
    out_weight_grad = jnp.einsum(
        "kht,td->hd", gathered_heads, attention_grad, preferred_element_type=jnp.float32
    )
    out_bias_grad = jnp.sum(attention_grad, axis=0, dtype=jnp.float32)
    head_grad = unit_sums(
        jnp.einsum("td,hd->ht", attention_grad, out_weight, preferred_element_type=jnp.float32)[
            None
        ]
    )[0].astype(jnp.bfloat16)
    query_grads, key_grads, value_grads = lax.map(
        lambda seq_items: attend_backward(
            seq_items[0],
            seq_items[1],
            seq_items[2],
            seq_items[3],
            seq_items[4],
            seq_items[5],
            score_scale,
        ),
        (query_seqs, key_seqs, value_seqs, to_seqs(head_grad), segment_ids, log_sums),
    )
    stacked_grad = jnp.stack(
        [from_seqs(query_grads), from_seqs(key_grads), from_seqs(value_grads)]
    ).astype(jnp.bfloat16)
    gathered_grad = unit_gather(stacked_grad)
    stacked_weight_grad = jnp.einsum(
        "td,kht->kdh", gathered_one, gathered_grad, preferred_element_type=jnp.float32
    )
    query_bias_grad = jnp.sum(gathered_grad[0], axis=1, dtype=jnp.float32)
    value_bias_grad = jnp.sum(gathered_grad[2], axis=1, dtype=jnp.float32)
    normed_grad_one = token_sums(
        jnp.einsum("kht,kdh->td", gathered_grad, stacked_weight, preferred_element_type=jnp.float32)
    )
    back_one, gain_one_grad, shift_one_grad = norm_backward(
        normed_grad_one, normal_one, inverse_one, norm1_gain
    )
    input_grad = out_grad.astype(jnp.float32) * (1.0 - keep_mask) + hidden_grad + back_one
    (
        stacked_weight_grad,
        query_bias_grad,
        value_bias_grad,
        out_weight_grad,
        out_bias_grad,
        down_grad,
        down_bias_grad,
        up_grad,
        up_bias_grad,
    ) = lax.psum(
        (
            stacked_weight_grad,
            query_bias_grad,
            value_bias_grad,
            out_weight_grad,
            out_bias_grad,
            down_grad,
            down_bias_grad,
            up_grad,
            up_bias_grad,
        ),
        "dp",
    )
    gain_one_grad, shift_one_grad, gain_two_grad, shift_two_grad = lax.psum(
        (gain_one_grad, shift_one_grad, gain_two_grad, shift_two_grad), ("dp", "col")
    )
    return (
        layer_out,
        input_grad,
        gain_one_grad,
        shift_one_grad,
        stacked_weight_grad[0],
        query_bias_grad,
        stacked_weight_grad[1],
        stacked_weight_grad[2],
        value_bias_grad,
        out_weight_grad,
        out_bias_grad,
        gain_two_grad,
        shift_two_grad,
        up_grad,
        up_bias_grad,
        down_grad,
        down_bias_grad,
    )


def after(values, *others):
    return lax.optimization_barrier((values, others))[0]


def swap(values):
    return lax.ppermute(values, "row", [(0, 1), (1, 0)])


def step_x(values):
    return lax.ppermute(values, "dp", [(0, 1), (1, 0), (2, 3), (3, 2)])


def step_y(values):
    return lax.ppermute(values, "dp", [(0, 2), (2, 0), (1, 3), (3, 1)])


def step_up(values):
    count = lax.axis_size("col")
    return lax.ppermute(values, "col", [(i, (i + 1) % count) for i in range(count)])


def step_down(values):
    count = lax.axis_size("col")
    return lax.ppermute(values, "col", [(i, (i - 1) % count) for i in range(count)])


class Order:
    def __init__(self):
        self.tokens = []
        self.fresh, self.due = [], []

    def tie(self, values):
        if self.tokens:
            values = after(values, *self.tokens)
        self.tokens.append(values)
        return values

    def swap(self, values, due=True):
        arrived = swap(self.tie(values))
        if due:
            self.fresh.append(arrived)
        return arrived

    def run(self, function, first, *others):
        first = after(first, *self.tokens, *self.due) if self.tokens or self.due else first
        self.due, self.fresh = self.fresh, []
        result = function(first, *others)
        self.tokens = [jax.tree.leaves(result)[0]]
        return result


class Link:
    def __init__(self, order):
        self.order = order
        self.last = None

    def send(self, step, values, free=False):
        if self.last is not None and not free:
            values = after(values, self.last)
        self.last = step(self.order.tie(values))
        return self.last


class Plane:
    def __init__(self, order):
        self.x = Link(order)
        self.y = Link(order)

    def both(self, for_x, for_y, free=False):
        return self.x.send(step_x, for_x, free), self.y.send(step_y, for_y, free)

    def far(self, from_x, from_y):
        half = from_x.shape[0] // 2
        far_two, far_one = self.both(from_y[half:], from_x[:half])
        return far_one, far_two


def add_rounded(left, right):
    return (left.astype(jnp.float32) + right.astype(jnp.float32)).astype(jnp.bfloat16)


def ring_gather(link, values):
    held = [values]
    for _ in range(lax.axis_size("col") - 1):
        held.append(link.send(step_up, held[-1]))
    return held


def picked(stacked, index):
    return lax.dynamic_index_in_dim(stacked, index, 0, keepdims=False)


def mm(left, right, left_dim, right_dim, dtype=jnp.float32):
    return lax.dot_general(
        left, right, (((left_dim,), (right_dim,)), ((), ())), preferred_element_type=jnp.float32
    ).astype(dtype)


PAIR = 2 * HEAD_DIM
vmem_bytes = 48 * 1024 * 1024


def head_lanes(head, value):
    lane = lax.broadcasted_iota(jnp.int32, (1, PAIR), 1)
    return jnp.where(lane // HEAD_DIM == head, value, 0.0).astype(jnp.bfloat16)


def allowed_keys(first_row, low, high):
    key_pos = lax.broadcasted_iota(jnp.int32, (high, high - low), 0)
    query_pos = lax.broadcasted_iota(jnp.int32, (high, high - low), 1) + low
    return (key_pos >= first_row) & (key_pos <= query_pos)


def local_forward_kernel(size, first_ref, query_ref, key_ref, value_ref, out_ref):
    lane = lax.broadcasted_iota(jnp.int32, (size, PAIR), 1)
    for low in range(0, key_ref.shape[0], size):
        high = low + size
        keys = key_ref[:high, :]
        values = value_ref[:high, :]
        queries = query_ref[low:high, :]
        allowed = allowed_keys(first_ref[:, low:high], low, high)
        results = []
        for head in range(2):
            scores = mm(keys, queries * head_lanes(head, HEAD_DIM ** (-0.5)), 1, 1)
            scores = jnp.where(allowed, scores, masked_fill)
            exp_scores = jnp.exp(scores - jnp.max(scores, axis=0, keepdims=True))
            inverse = 1.0 / jnp.sum(exp_scores, axis=0, keepdims=True)
            results.append(mm((exp_scores * inverse).astype(jnp.bfloat16), values, 0, 0))
        out_ref[low:high, :] = jnp.where(lane < HEAD_DIM, results[0], results[1]).astype(
            jnp.bfloat16
        )


def local_forward(heads, first_row):
    length = heads.shape[0]
    pairs = heads.shape[1] // (3 * PAIR)
    return pl.pallas_call(
        functools.partial(local_forward_kernel, min(256, length)),
        grid=(pairs,),
        in_specs=[
            pl.BlockSpec((1, length), lambda p: (0, 0)),
            pl.BlockSpec((length, PAIR), lambda p: (0, p)),
            pl.BlockSpec((length, PAIR), lambda p: (0, pairs + p)),
            pl.BlockSpec((length, PAIR), lambda p: (0, 2 * pairs + p)),
        ],
        out_specs=pl.BlockSpec((length, PAIR), lambda p: (0, p)),
        out_shape=jax.ShapeDtypeStruct((length, pairs * PAIR), jnp.bfloat16),
        compiler_params=pltpu.CompilerParams(vmem_limit_bytes=vmem_bytes),
        cost_estimate=cost(16 * length * length * pairs * PAIR, 8 * heads.size),
    )(first_row, heads, heads, heads)


def local_backward_kernel(
    size, first_ref, query_ref, grad_ref, key_ref, value_ref, out_ref, key_sum, value_sum
):
    length = key_ref.shape[0]
    pair = pl.program_id(0)
    pairs = out_ref.shape[1] // (3 * PAIR)
    scale = HEAD_DIM ** (-0.5)
    lane = lax.broadcasted_iota(jnp.int32, (size, PAIR), 1)

    def lanes(part):
        return pl.ds(pl.multiple_of((part * pairs + pair) * PAIR, PAIR), PAIR)

    for low in range(length - size, -1, -size):
        high = low + size
        keys = key_ref[:high, :]
        values = value_ref[:high, :]
        queries = query_ref[low:high, :]
        grads = grad_ref[low:high, :]
        allowed = allowed_keys(first_ref[:, low:high], low, high)
        query_grads = []
        for head in range(2):
            scaled = queries * head_lanes(head, scale)
            grad = grads * head_lanes(head, 1.0)
            scores = jnp.where(allowed, mm(keys, scaled, 1, 1), masked_fill)
            exp_scores = jnp.exp(scores - jnp.max(scores, axis=0, keepdims=True))
            probs = exp_scores * (1.0 / jnp.sum(exp_scores, axis=0, keepdims=True))
            prob_grad = mm(values, grad, 1, 1)
            row_dot = jnp.sum(probs * prob_grad, axis=0, keepdims=True)
            score_grad = (probs * (prob_grad - row_dot)).astype(jnp.bfloat16)
            value_part = mm(probs.astype(jnp.bfloat16), grad, 1, 0)
            key_part = mm(score_grad, scaled, 1, 0)
            query_grads.append(mm(score_grad, keys, 0, 0) * scale)
            if head == 0:
                key_add, value_add = key_part, value_part
            else:
                key_add, value_add = key_add + key_part, value_add + value_part
        if high == length:
            key_sum[...] = key_add
            value_sum[...] = value_add
        else:
            key_sum[:high, :] += key_add
            value_sum[:high, :] += value_add
        out_ref[low:high, lanes(0)] = jnp.where(
            lane < HEAD_DIM, query_grads[0], query_grads[1]
        ).astype(jnp.bfloat16)
    out_ref[:, lanes(1)] = key_sum[...].astype(jnp.bfloat16)
    out_ref[:, lanes(2)] = value_sum[...].astype(jnp.bfloat16)


def local_backward(heads, head_grad, group, first_row):
    length = heads.shape[0]
    pairs = heads.shape[1] // (3 * PAIR)
    return pl.pallas_call(
        functools.partial(local_backward_kernel, min(512, length)),
        grid=(pairs,),
        in_specs=[
            pl.BlockSpec((1, length), lambda p: (0, 0)),
            pl.BlockSpec((length, PAIR), lambda p: (0, p)),
            pl.BlockSpec((length, PAIR), lambda p: (0, group * pairs + p)),
            pl.BlockSpec((length, PAIR), lambda p: (0, pairs + p)),
            pl.BlockSpec((length, PAIR), lambda p: (0, 2 * pairs + p)),
        ],
        out_specs=pl.BlockSpec(heads.shape, lambda p: (0, 0)),
        out_shape=jax.ShapeDtypeStruct(heads.shape, jnp.bfloat16),
        scratch_shapes=[pltpu.VMEM((length, PAIR), jnp.float32)] * 2,
        compiler_params=pltpu.CompilerParams(vmem_limit_bytes=vmem_bytes),
        cost_estimate=cost(32 * length * length * pairs * PAIR, 8 * heads.size),
    )(first_row, heads, head_grad, heads, heads)


gelu_scale = 0.7978845608028654
gelu_cubic = 0.044715


def ffn_kernel(index_ref, *refs):
    normed, grads, pieces = refs[:2], refs[2:4], [r.at[0] for r in refs[4:6]]
    bias_ref, rows_ref, sum_ref, grad_out, down_out, grad_acc, down_acc = refs[6:]
    step = pl.program_id(0)
    width = normed[0].shape[1]
    quarter = pieces[0].shape[1] // 2
    ups, downs = slice(0, quarter), slice(quarter, 2 * quarter)
    pre = mm(normed[0][...], pieces[0][:, ups], 1, 0) + mm(normed[1][...], pieces[1][:, ups], 1, 0)
    pre = pre + bias_ref[0]
    act_grad = mm(grads[0][...], pieces[0][:, downs], 1, 0) + mm(grads[1][...], pieces[1][:, downs], 1, 0)
    square = pre * pre
    bent = jnp.tanh(gelu_scale * pre * (1.0 + gelu_cubic * square))
    half = 0.5 * (1.0 + bent)
    slope = half + 0.5 * gelu_scale * pre * (1.0 - bent * bent) * (1.0 + 3.0 * gelu_cubic * square)
    act = (pre * half).astype(jnp.bfloat16)
    pre_grad = (act_grad * slope).astype(jnp.bfloat16)
    rows_ref[:, :quarter] = act
    rows_ref[:, quarter:] = pre_grad
    sum_ref[0] = jnp.sum(pre_grad.astype(jnp.float32), axis=0, keepdims=True)

    @pl.when(step == 0)
    def _():
        for i in range(2):
            at = slice(i * width, (i + 1) * width)
            grad_acc[:, at] = mm(pre_grad, pieces[i][:, ups], 1, 1)
            down_acc[:, at] = mm(act, pieces[i][:, downs], 1, 1)

    @pl.when(step > 0)
    def _():
        for i in range(2):
            at = slice(i * width, (i + 1) * width)
            grad_acc[:, at] += mm(pre_grad, pieces[i][:, ups], 1, 1)
            down_acc[:, at] += mm(act, pieces[i][:, downs], 1, 1)

    @pl.when(step == pl.num_programs(0) - 1)
    def _():
        grad_out[...] = grad_acc[...].astype(jnp.bfloat16)
        down_out[...] = down_acc[...].astype(jnp.bfloat16)


def ffn_rows_of(index, normed, grads, part, pieces, bias):
    tokens, features = normed.shape
    width = features // 2
    columns = pieces.shape[2]
    ring, quarter = pieces.shape[0] // 2, columns // 2

    def halves(at):
        return [pl.BlockSpec((tokens, width), lambda k, s, h=h: (at, h)) for h in range(2)]

    piece = [
        pl.BlockSpec((1, width, columns), lambda k, s, h=h: ((s[0] ^ h) * ring + k, 0, 0))
        for h in range(2)
    ]
    whole = pl.BlockSpec((tokens, features), lambda k, s: (0, 0))
    vector = pl.BlockSpec((1, 1, quarter), lambda k, s: (k, 0, 0))
    return pl.pallas_call(
        ffn_kernel,
        grid_spec=pltpu.PrefetchScalarGridSpec(
            num_scalar_prefetch=1,
            grid=(ring,),
            in_specs=halves(0) + halves(part) + piece + [vector],
            out_specs=[pl.BlockSpec((tokens, columns), lambda k, s: (0, k)), vector, whole, whole],
            scratch_shapes=[pltpu.VMEM((tokens, features), jnp.float32)] * 2,
        ),
        out_shape=[
            shape((tokens, ring * columns)),
            shape((ring, 1, quarter), jnp.float32),
            shape((tokens, features)),
            shape((tokens, features)),
        ],
        compiler_params=params(),
        cost_estimate=cost(8 * tokens * features * ring * quarter, 12 * ring * width * columns),
    )(index, normed, normed, grads, grads, pieces, pieces, bias)


def weight_products_kernel(count, *refs):
    out_ref = refs[-1]
    normed, grads, rows = [refs[i * count : (i + 1) * count] for i in range(3)]
    quarter = rows[0].shape[1] // 2
    up = down = None
    for j in range(count):
        up_part = mm(normed[j][...], rows[j][:, quarter:], 0, 0)
        down_part = mm(grads[j][...], rows[j][:, :quarter], 0, 0)
        up = up_part if up is None else up + up_part
        down = down_part if down is None else down + down_part
    out_ref[0, :, :quarter] = up.astype(jnp.bfloat16)
    out_ref[0, :, quarter:] = down.astype(jnp.bfloat16)


def weight_products(normed, grads, rows, half):
    count = len(normed)
    tokens, features = normed[0].shape
    width = features // 2
    ring = 4
    columns = rows[0].shape[1] // ring
    size = min(512, width)
    blocks = width // size
    left = [pl.BlockSpec((tokens, size), lambda k, d: (0, half * blocks + d))] * count
    left += [
        pl.BlockSpec((tokens, size), lambda k, d, j=j: (j, half * blocks + d)) for j in range(count)
    ]
    return pl.pallas_call(
        functools.partial(weight_products_kernel, count),
        grid=(ring, blocks),
        in_specs=left + [pl.BlockSpec((tokens, columns), lambda k, d: (0, k))] * count,
        out_specs=pl.BlockSpec((1, size, columns), lambda k, d: (k, d, 0)),
        out_shape=shape((ring, width, columns)),
        compiler_params=params(),
        cost_estimate=cost(
            2 * count * tokens * width * ring * columns, 4 * count * tokens * features * ring
        ),
    )(*normed, *([grads] * count), *rows)


def params(**more):
    return pltpu.CompilerParams(vmem_limit_bytes=vmem_bytes, **more)


def cost(flops, nbytes):
    return pl.CostEstimate(flops=flops // 10, bytes_accessed=nbytes // 10, transcendentals=0)


def shape(dims, dtype=jnp.bfloat16):
    return jax.ShapeDtypeStruct(dims, dtype)


def turned(values):
    return values.astype(jnp.float32).T.astype(jnp.bfloat16)


def pack_heads_kernel(index_ref, *refs):
    sources, outs = refs[:8], refs[8:]
    own = sources[0].shape[1]
    for which in range(2):
        for i in range(4):
            part = sources[4 * which + i][...]
            outs[which][:, i * own : (i + 1) * own] = part if i < 3 else turned(part)


def pack_heads(index, weights, count):
    width, units = weights[0].shape
    own, block = units // 2, width // 4

    def feature(which):
        return pl.BlockSpec((block, own), lambda j, s: (s[1] ^ j, s[0] ^ which))

    def turned_block(which):
        return pl.BlockSpec((own, block), lambda j, s: (s[0] ^ which, s[1] ^ j))

    in_specs = []
    for which in range(2):
        in_specs += [feature(which)] * 3 + [turned_block(which)]
    return pl.pallas_call(
        pack_heads_kernel,
        grid_spec=pltpu.PrefetchScalarGridSpec(
            num_scalar_prefetch=1,
            grid=(count,),
            in_specs=in_specs,
            out_specs=[pl.BlockSpec((block, 4 * own), lambda j, s: (j, 0))] * 2,
        ),
        out_shape=[shape((count * block, 4 * own))] * 2,
        compiler_params=params(),
        cost_estimate=cost(0, 32 * count * block * own),
    )(index, *weights, *weights)


def pack_ff_kernel(index_ref, up_ref, down_ref, out_ref):
    quarter = up_ref.shape[1]
    out_ref[:, :quarter] = up_ref[...]
    out_ref[:, quarter:] = turned(down_ref[...])


def pack_ff(index, up_weight, down_weight):
    width, units = up_weight.shape
    quarter, block = units // 4, width // 4
    return pl.pallas_call(
        pack_ff_kernel,
        grid_spec=pltpu.PrefetchScalarGridSpec(
            num_scalar_prefetch=1,
            grid=(4,),
            in_specs=[
                pl.BlockSpec((block, quarter), lambda d, s: (d, s[1])),
                pl.BlockSpec((quarter, block), lambda d, s: (s[1], d)),
            ],
            out_specs=pl.BlockSpec((block, 2 * quarter), lambda d, s: (d, 0)),
        ),
        out_shape=shape((width, 2 * quarter)),
        compiler_params=params(),
        cost_estimate=cost(0, 8 * width * quarter),
    )(index, up_weight, down_weight)


def stack_kernel(*refs):
    pieces, outs = refs[:3], refs[-2:]
    block = pieces[0].shape[0] // 2
    for j, piece in enumerate(pieces):
        for i in range(2):
            outs[i][j * block : (j + 1) * block, :] = piece[i * block : (i + 1) * block, :]
    for i in range(2):
        outs[i][3 * block :, :] = refs[3 + i][...]


def stack_pieces(pieces):
    rows, columns = pieces[0].shape
    return pl.pallas_call(
        stack_kernel,
        out_shape=[shape((2 * rows, columns))] * 2,
        compiler_params=params(),
        cost_estimate=cost(0, 16 * rows * columns),
    )(*pieces)


def norm_kernel(index_ref, own_ref, sib_ref, vectors_ref, out_ref, stats_ref):
    own = own_ref[...].astype(jnp.float32)
    sib = sib_ref[...].astype(jnp.float32)
    width = own.shape[1]
    average = (jnp.sum(own, axis=1, keepdims=True) + jnp.sum(sib, axis=1, keepdims=True)) / (2 * width)
    own, sib = own - average, sib - average
    square = jnp.sum(own * own, axis=1, keepdims=True) + jnp.sum(sib * sib, axis=1, keepdims=True)
    inverse = lax.rsqrt(square / (2 * width) + norm_eps)
    block = width // 4
    for half, values in enumerate((own, sib)):
        gain, shift = vectors_ref[2 * half, :][None], vectors_ref[2 * half + 1, :][None]
        rounded = (values * inverse * gain + shift).astype(jnp.bfloat16)
        for i in range(4):
            at = pl.multiple_of(half * width + (index_ref[1] ^ i) * block, block)
            out_ref[:, pl.ds(at, block)] = rounded[:, i * block : (i + 1) * block]
    lane = lax.broadcasted_iota(jnp.int32, stats_ref.shape, 1)
    stats_ref[...] = jnp.where(lane == 0, average, inverse)


def norm_rows(index, own, sib, vectors):
    tokens, width = own.shape
    size = min(256, tokens)
    rows = pl.BlockSpec((size, width), lambda i, s: (i, 0))
    return pl.pallas_call(
        norm_kernel,
        grid_spec=pltpu.PrefetchScalarGridSpec(
            num_scalar_prefetch=1,
            grid=(tokens // size,),
            in_specs=[rows, rows, pl.BlockSpec((4, width), lambda i, s: (0, 0))],
            out_specs=[
                pl.BlockSpec((size, 2 * width), lambda i, s: (i, 0)),
                pl.BlockSpec((size, 128), lambda i, s: (i, 0)),
            ],
        ),
        out_shape=[shape((tokens, 2 * width)), shape((tokens, 128), jnp.float32)],
        compiler_params=params(),
        cost_estimate=cost(0, 8 * tokens * width),
    )(index, own, sib, vectors)


def project_kernel(own_ref, sib_ref, own_weight, sib_weight, bias_ref, out_ref):
    total = mm(own_ref[...], own_weight[...], 1, 0) + mm(sib_ref[...], sib_weight[...], 1, 0)
    out_ref[...] = (total + bias_ref[...]).astype(jnp.bfloat16)


def halves_of(size, width):
    return [pl.BlockSpec((size, width), lambda i, h=h: (i, h)) for h in range(2)]


def project(normed, own_weight, sib_weight, bias):
    tokens, features = normed.shape
    width, units = features // 2, bias.shape[1]
    size = min(256, tokens)
    weight = pl.BlockSpec((width, units), lambda i: (0, 0))
    return pl.pallas_call(
        project_kernel,
        grid=(tokens // size,),
        in_specs=halves_of(size, width)
        + [weight, weight, pl.BlockSpec((1, units), lambda i: (0, 0))],
        out_specs=pl.BlockSpec((size, units), lambda i: (i, 0)),
        out_shape=shape((tokens, units)),
        compiler_params=params(),
        cost_estimate=cost(4 * tokens * width * units, 4 * tokens * width + 4 * width * units),
    )(normed, normed, own_weight, sib_weight, bias)


def sum_rows_kernel(count, *refs):
    out_ref = refs[-1]
    width = refs[count].shape[0]
    for half in range(2):
        at = slice(half * width, (half + 1) * width)
        total = refs[3 * count][:, at] if len(refs) > 3 * count + 1 else None
        for k in range(count):
            part = mm(refs[k][...], refs[(1 + half) * count + k][...], 1, 1)
            total = part if total is None else total + part
        out_ref[:, at] = total


def sum_rows(rows, own_weights, sib_weights, at, before=()):
    count = len(rows)
    tokens, units = rows[0].shape
    width = own_weights[0].shape[0]
    size = min(512, tokens)
    full = pl.BlockSpec((size, 2 * width), lambda i: (i, 0))
    return pl.pallas_call(
        functools.partial(sum_rows_kernel, count),
        grid=(tokens // size,),
        in_specs=[pl.BlockSpec((size, units), lambda i: (i, 0))] * count
        + [pl.BlockSpec((width, units), lambda i: (0, at))] * (2 * count)
        + [full] * len(before),
        out_specs=full,
        out_shape=shape((tokens, 2 * width), jnp.float32),
        compiler_params=params(),
        cost_estimate=cost(4 * count * tokens * units * width, 8 * tokens * width),
    )(*rows, *own_weights, *sib_weights, *before)


def head_grads_kernel(own_ref, sib_ref, *refs):
    out_ref = refs[-1]
    count = (len(refs) - 1) // 2
    own = refs[0].shape[1]
    for k in range(count):
        total = mm(own_ref[...], refs[k][...], 1, 0) + mm(sib_ref[...], refs[count + k][...], 1, 0)
        out_ref[:, k * own : (k + 1) * own] = total.astype(jnp.bfloat16)


def head_grads(grads, own_weights, sib_weights):
    tokens, width = grads.shape[0], grads.shape[1] // 2
    count = len(own_weights)
    units = own_weights[0].shape[1] // 4
    size = min(256, tokens)
    return pl.pallas_call(
        head_grads_kernel,
        grid=(tokens // size,),
        in_specs=halves_of(size, width) + [pl.BlockSpec((width, units), lambda i: (0, 3))] * (2 * count),
        out_specs=pl.BlockSpec((size, count * units), lambda i: (i, 0)),
        out_shape=shape((tokens, count * units)),
        compiler_params=params(),
        cost_estimate=cost(4 * count * tokens * width * units, 8 * tokens * width),
    )(grads, grads, *own_weights, *sib_weights)


def head_products_kernel(*refs):
    normed, grads = refs[:2], refs[2:4]
    heads_ref, attended_ref = refs[4:6]
    outs, sum_ref = refs[6:8], refs[8]
    split = heads_ref.shape[1]
    for i in range(2):
        outs[i][:, :split] = mm(normed[i][...], heads_ref[...], 0, 0).astype(jnp.bfloat16)
        outs[i][:, split:] = mm(grads[i][...], attended_ref[...], 0, 0).astype(jnp.bfloat16)

    @pl.when(pl.program_id(0) == 0)
    def _():
        sum_ref[...] = jnp.sum(heads_ref[...].astype(jnp.float32), axis=0, keepdims=True)


def head_products(normed, grads, head_grad, attended):
    tokens, width = normed.shape[0], normed.shape[1] // 2
    split, own = head_grad.shape[1], attended.shape[1]
    size = min(512, width)
    blocks = width // size
    left = [pl.BlockSpec((tokens, size), lambda d, h=h: (0, h * blocks + d)) for h in range(2)]
    out = pl.BlockSpec((size, split + own), lambda d: (d, 0))
    return pl.pallas_call(
        head_products_kernel,
        grid=(width // size,),
        in_specs=left * 2
        + [pl.BlockSpec((tokens, split), lambda d: (0, 0)), pl.BlockSpec((tokens, own), lambda d: (0, 0))],
        out_specs=[out, out, pl.BlockSpec((1, split), lambda d: (0, 0))],
        out_shape=[shape((width, split + own))] * 2 + [shape((1, split), jnp.float32)],
        compiler_params=params(),
        cost_estimate=cost(4 * tokens * width * (split + own), 12 * tokens * width),
    )(normed, normed, grads, grads, head_grad, attended)


def block_at(half, width, place):
    block = width // 4
    return pl.ds(pl.multiple_of(half * width + place * block, block), block)


def norm_two_kernel(
    index_ref, rows_ref, came_ref, own_ref, sib_ref, vectors_ref, hidden_ref, normed_ref, stats_ref
):
    width = own_ref.shape[1]
    block = width // 4
    for half, tokens_ref in enumerate((own_ref, sib_ref)):
        for i in range(4):
            at = block_at(half, width, index_ref[1] ^ i)
            span = slice(half * width + i * block, half * width + (i + 1) * block)
            hidden_ref[:, span] = (
                tokens_ref[:, i * block : (i + 1) * block].astype(jnp.float32)
                + rows_ref[:, at]
                + came_ref[:, at].astype(jnp.float32)
                + vectors_ref[4:5, span]
            )
    hidden = hidden_ref[...]
    average = jnp.mean(hidden, axis=1, keepdims=True)
    centered = hidden - average
    inverse = lax.rsqrt(jnp.mean(centered * centered, axis=1, keepdims=True) + norm_eps)
    normed_ref[...] = (centered * inverse * vectors_ref[2:3, :] + vectors_ref[3:4, :]).astype(jnp.bfloat16)
    lane = lax.broadcasted_iota(jnp.int32, stats_ref.shape, 1)
    stats_ref[...] = jnp.where(lane == 0, average, inverse)


def my_rows(size, columns, blocks):
    return pl.BlockSpec((size, columns), lambda i, s: (s[0] * blocks + i, 0))


def norm_two(index, rows, came, own, sib, vectors):
    tokens, features = came.shape
    size = tokens // 2
    mine = my_rows(size, features // 2, 2)
    plain = pl.BlockSpec((size, features), lambda i, s: (i, 0))
    return pl.pallas_call(
        norm_two_kernel,
        grid_spec=pltpu.PrefetchScalarGridSpec(
            num_scalar_prefetch=1,
            grid=(2,),
            in_specs=[
                my_rows(size, features, 2),
                plain,
                mine,
                mine,
                pl.BlockSpec(vectors.shape, lambda i, s: (0, 0)),
            ],
            out_specs=[plain, plain, pl.BlockSpec((size, 128), lambda i, s: (i, 0))],
        ),
        out_shape=[
            shape((tokens, features), jnp.float32),
            shape((tokens, features)),
            shape((tokens, 128), jnp.float32),
        ],
        compiler_params=params(),
        cost_estimate=cost(0, 16 * tokens * features),
    )(index, rows, came, own, sib, vectors)


def norm_pull(grads, normal, inverse, gain):
    scaled = grads * gain
    return inverse * (
        scaled
        - jnp.mean(scaled, axis=1, keepdims=True)
        - normal * jnp.mean(scaled * normal, axis=1, keepdims=True)
    )


def add_sums(sums_ref, parts):
    rows = [jnp.sum(p, axis=0, keepdims=True) for p in parts]
    rows += [jnp.zeros_like(rows[0])] * (8 - len(rows))
    total = jnp.concatenate(rows, axis=0)

    @pl.when(pl.program_id(0) == 0)
    def _():
        sums_ref[...] = total

    @pl.when(pl.program_id(0) > 0)
    def _():
        sums_ref[...] += total


def norm_two_back_kernel(index_ref, *refs):
    here, x_top, y_top, x_bottom, y_bottom, hidden_ref, stats_ref, branch_ref, vectors_ref = refs[:9]
    grad_ref, blocks_ref, mirror_ref, sums_ref = refs[9:]
    f32 = jnp.float32
    top = pl.program_id(0) == 0
    from_x = jnp.where(top, x_top[...].astype(f32), x_bottom[...].astype(f32))
    from_y = jnp.where(top, y_top[...].astype(f32), y_bottom[...].astype(f32))
    grads = here[...].astype(f32) + from_x + from_y
    inverse = stats_ref[:, 1:2]
    normal = (hidden_ref[...] - stats_ref[:, :1]) * inverse
    branch = branch_ref[...].astype(f32)
    total = branch + norm_pull(grads, normal, inverse, vectors_ref[2:3, :])
    grad_ref[...] = total
    rounded = total.astype(jnp.bfloat16)
    width = rounded.shape[1] // 2
    block = width // 4
    for half in range(2):
        for i in range(4):
            part = rounded[:, half * width + i * block : half * width + (i + 1) * block]
            place = index_ref[1] ^ i
            blocks_ref[:, block_at(half, width, place)] = part
            mirror_ref[:, block_at(1 - half, width, place)] = part
    add_sums(sums_ref, (grads * normal, grads, rounded.astype(f32), branch))


def norm_two_back(index, parts, hidden, stats, branch, vectors):
    tokens, features = hidden.shape
    size = tokens // 2
    plain = pl.BlockSpec((size, features), lambda i, s: (i, 0))
    once = pl.BlockSpec((size, features), lambda i, s: (0, 0))
    return pl.pallas_call(
        norm_two_back_kernel,
        grid_spec=pltpu.PrefetchScalarGridSpec(
            num_scalar_prefetch=1,
            grid=(2,),
            in_specs=[plain]
            + [once] * 4
            + [
                plain,
                pl.BlockSpec((size, 128), lambda i, s: (i, 0)),
                plain,
                pl.BlockSpec(vectors.shape, lambda i, s: (0, 0)),
            ],
            out_specs=[plain] * 3 + [pl.BlockSpec((8, features), lambda i, s: (0, 0))],
        ),
        out_shape=[
            shape((tokens, features), jnp.float32),
            shape((tokens, features)),
            shape((tokens, features)),
            shape((8, features), jnp.float32),
        ],
        compiler_params=params(),
        cost_estimate=cost(0, 24 * tokens * features),
    )(index, *parts, hidden, stats, branch, vectors)


def norm_one_back_kernel(index_ref, *refs):
    rows_ref, came_ref, own_ref, sib_ref, stats_ref, out_own, out_sib, keep_ref, hidden_ref = refs[:9]
    vectors_ref, own_grad, sib_grad, sums_ref, grads_ref = refs[9:]
    f32 = jnp.float32
    width = own_ref.shape[1]
    block = width // 4
    for half in range(2):
        for i in range(4):
            at = block_at(half, width, index_ref[1] ^ i)
            span = slice(half * width + i * block, half * width + (i + 1) * block)
            grads_ref[:, span] = rows_ref[:, at] + came_ref[:, at].astype(f32)
    grads = grads_ref[...]
    inverse = stats_ref[:, 1:2]
    tokens = jnp.concatenate([own_ref[...], sib_ref[...]], axis=1).astype(f32)
    normal = (tokens - stats_ref[:, :1]) * inverse
    total = hidden_ref[...] + norm_pull(grads, normal, inverse, vectors_ref[0:1, :])
    dropped = 1.0 - keep_ref[...]
    own_grad[...] = out_own[...].astype(f32) * dropped + total[:, :width]
    sib_grad[...] = out_sib[...].astype(f32) * dropped + total[:, width:]
    add_sums(sums_ref, (grads * normal, grads))


def norm_one_back(index, rows, came, own, sib, stats, out_own, out_sib, keep, hidden, vectors):
    tokens, features = came.shape
    size, width = tokens // 2, features // 2
    plain = pl.BlockSpec((size, features), lambda i, s: (i, 0))
    half_wide = pl.BlockSpec((size, width), lambda i, s: (i, 0))
    return pl.pallas_call(
        norm_one_back_kernel,
        grid_spec=pltpu.PrefetchScalarGridSpec(
            num_scalar_prefetch=1,
            grid=(2,),
            in_specs=[
                my_rows(size, features, 2),
                plain,
                my_rows(size, width, 2),
                my_rows(size, width, 2),
                my_rows(size, 128, 2),
                my_rows(size, width, 2),
                half_wide,
                pl.BlockSpec((size, 1), lambda i, s: (i, 0)),
                plain,
                pl.BlockSpec(vectors.shape, lambda i, s: (0, 0)),
            ],
            out_specs=[half_wide, half_wide, pl.BlockSpec((8, features), lambda i, s: (0, 0))],
            scratch_shapes=[pltpu.VMEM((size, features), jnp.float32)],
        ),
        out_shape=[shape((tokens, width), jnp.float32)] * 2 + [shape((8, features), jnp.float32)],
        compiler_params=params(),
        cost_estimate=cost(0, 24 * tokens * features),
    )(index, rows, came, own, sib, stats, out_own, out_sib, keep, hidden, vectors)


def select_piece(refs, step, use):
    for j in range(3):

        @pl.when(step == j)
        def _():
            use(refs[j][...])

    @pl.when(step == 3)
    def _():
        use(jnp.concatenate([refs[3][...], refs[4][...]], axis=0))


def place_heads_kernel(index_ref, *refs):
    pieces, outs = refs[:5], refs[5:]
    own = pieces[0].shape[1] // 8

    def use(piece):
        for which in range(2):
            at = pl.multiple_of((index_ref[0] ^ which) * own, own)
            for m in range(4):
                part = piece[:, (4 * which + m) * own : (4 * which + m + 1) * own].astype(jnp.float32)
                if m < 3:
                    outs[m][:, pl.ds(at, own)] = part
                else:
                    outs[m][pl.ds(at, own), :] = part.T

    select_piece(pieces, pl.program_id(0), use)


def place_heads(index, pieces):
    block, columns = pieces[0].shape
    units, width = columns // 4, 4 * block
    whole = [pl.BlockSpec(p.shape, lambda j, s: (0, 0)) for p in pieces]
    return pl.pallas_call(
        place_heads_kernel,
        grid_spec=pltpu.PrefetchScalarGridSpec(
            num_scalar_prefetch=1,
            grid=(4,),
            in_specs=whole,
            out_specs=[pl.BlockSpec((block, units), lambda j, s: (s[1] ^ j, 0))] * 3
            + [pl.BlockSpec((units, block), lambda j, s: (0, s[1] ^ j))],
        ),
        out_shape=[shape((width, units), jnp.float32)] * 3 + [shape((units, width), jnp.float32)],
        compiler_params=params(),
        cost_estimate=cost(0, 24 * width * units),
    )(index, *pieces)


def place_ff_kernel(*refs):
    pieces, (up_out, down_out) = refs[:-2], refs[-2:]
    rows = pieces[0].shape[1]
    quarter = pieces[0].shape[2] // 2
    for part, piece in enumerate(pieces):
        span = slice(part * rows, (part + 1) * rows)
        up_out[span, :] = piece[0, :, :quarter].astype(jnp.float32)
        down_out[:, span] = piece[0, :, quarter:].astype(jnp.float32).T


def place_ff(pieces):
    count, rows, columns = pieces[0].shape
    width, quarter = rows * len(pieces), columns // 2
    return pl.pallas_call(
        place_ff_kernel,
        grid=(count,),
        in_specs=[pl.BlockSpec((1, rows, columns), lambda j: (j, 0, 0))] * len(pieces),
        out_specs=[
            pl.BlockSpec((width, quarter), lambda j: (0, j)),
            pl.BlockSpec((quarter, width), lambda j: (j, 0)),
        ],
        out_shape=[
            shape((width, count * quarter), jnp.float32),
            shape((count * quarter, width), jnp.float32),
        ],
        compiler_params=params(),
        cost_estimate=cost(0, 48 * width * quarter),
    )(*pieces)


def join_kernel(index_ref, mine_ref, first_ref, second_ref, out_ref):
    step = pl.program_id(0)

    @pl.when(step < 2)
    def _():
        out_ref[...] = mine_ref[...]

    @pl.when(step == 2)
    def _():
        out_ref[...] = first_ref[...]

    @pl.when(step == 3)
    def _():
        out_ref[...] = second_ref[...]


def join_tokens(index, mine, first, second):
    tokens, width = mine.shape
    size = tokens // 2
    once = pl.BlockSpec((size, width), lambda i, s: (0, 0))
    return pl.pallas_call(
        join_kernel,
        grid_spec=pltpu.PrefetchScalarGridSpec(
            num_scalar_prefetch=1,
            grid=(4,),
            in_specs=[pl.BlockSpec((size, width), lambda i, s: (jnp.minimum(i, 1), 0)), once, once],
            out_specs=pl.BlockSpec(
                (size, width), lambda i, s: (jnp.where(i < 2, s[0] * 2 + i, (1 - s[0]) * 2 + i - 2), 0)
            ),
        ),
        out_shape=shape((2 * tokens, width), mine.dtype),
        compiler_params=params(),
        cost_estimate=cost(0, 8 * tokens * width),
    )(index, mine, first, second)


def layer_out_kernel(*refs):
    here, x_top, y_top, x_bottom, y_bottom, hidden_ref, own_ref, sib_ref, keep_ref, vectors_ref = refs[1:11]
    own_out, sib_out = refs[11:]
    f32 = jnp.float32
    width = own_ref.shape[1]
    top = pl.program_id(0) == 0
    from_x = jnp.where(top, x_top[...].astype(f32), x_bottom[...].astype(f32))
    from_y = jnp.where(top, y_top[...].astype(f32), y_bottom[...].astype(f32))
    total = hidden_ref[...] + here[...].astype(f32) + from_x + from_y + vectors_ref[5:6, :]
    keep = keep_ref[...] > 0.5
    own_out[...] = jnp.where(keep, total[:, :width], own_ref[...].astype(f32))
    sib_out[...] = jnp.where(keep, total[:, width:], sib_ref[...].astype(f32))


def layer_rows(index, parts, hidden, own, sib, keep, vectors):
    tokens, features = hidden.shape
    size, width = tokens // 2, features // 2
    plain = pl.BlockSpec((size, features), lambda i, s: (i, 0))
    half_wide = pl.BlockSpec((size, width), lambda i, s: (i, 0))
    return pl.pallas_call(
        layer_out_kernel,
        grid_spec=pltpu.PrefetchScalarGridSpec(
            num_scalar_prefetch=1,
            grid=(2,),
            in_specs=[plain]
            + [pl.BlockSpec((size, features), lambda i, s: (0, 0))] * 4
            + [
                plain,
                my_rows(size, width, 2),
                my_rows(size, width, 2),
                pl.BlockSpec((size, 1), lambda i, s: (i, 0)),
                pl.BlockSpec(vectors.shape, lambda i, s: (0, 0)),
            ],
            out_specs=[half_wide, half_wide],
        ),
        out_shape=[shape((tokens, width), jnp.float32)] * 2,
        compiler_params=params(),
        cost_estimate=cost(0, 20 * tokens * features),
    )(index, *parts, hidden, own, sib, keep, vectors)


def body_local(
    tokens_in,
    out_grad,
    segment_ids,
    active_lengths,
    norm1_gain,
    norm1_shift,
    query_weight,
    query_bias,
    key_weight,
    value_weight,
    value_bias,
    out_weight,
    out_bias,
    norm2_gain,
    norm2_shift,
    up_weight,
    up_bias,
    down_weight,
    down_bias,
):
    f32, bf16 = jnp.float32, jnp.bfloat16
    rows, width = tokens_in.shape
    ring = lax.axis_size("col")
    row_i = lax.axis_index("row")
    plane_i = lax.axis_index("dp")
    col_i = lax.axis_index("col")
    own = query_weight.shape[1] // 2
    block = width // 4
    quarter = up_weight.shape[1] // 4
    unit = quarter // 2
    half = rows // 2
    order = Order()
    plane, column = Plane(order), Link(order)
    index = jnp.stack([row_i, plane_i, col_i]).astype(jnp.int32)

    def cut(values, start, size):
        return lax.dynamic_slice_in_dim(values, start, size, axis=0)

    def mirrored(values):
        return jnp.concatenate([values[:, width:], values[:, :width]], axis=1)

    def my_tokens(values):
        return cut(values, row_i * half, half)

    def other_tokens(values):
        return cut(values, (1 - row_i) * half, half)

    tokens_sib = order.swap(tokens_in)
    out_grad_sib = swap(other_tokens(out_grad))

    mine = jnp.concatenate(
        [
            cut(query_bias, row_i * own, own),
            jnp.zeros((own,), f32),
            cut(value_bias, row_i * own, own),
            cut(up_bias, plane_i * quarter, quarter),
        ]
    )
    small = [mine] + [
        lax.ppermute(mine, "col", [(i, (i + k) % ring) for i in range(ring)]) for k in range(1, ring)
    ]

    sources = (query_weight, key_weight, value_weight, out_weight)
    piece = order.run(pack_heads, after(index, mine), sources, 1)
    pieces = [jnp.concatenate([piece[0], swap(piece[1])], axis=0)]
    column.last = small[1:]
    pieces.append(column.send(step_up, pieces[0]))

    active_all = active_rows(segment_ids, active_lengths)
    active_here = my_tokens(cut(active_all, col_i * rows, rows))
    keep_mask = active_here.astype(f32)[:, None]
    out_grads = jnp.concatenate([my_tokens(out_grad), out_grad_sib], axis=1).astype(f32)
    branch_mine = (after(out_grads, *order.tokens) * keep_mask).astype(bf16)
    branch_first = plane.both(branch_mine[: half // 2], branch_mine[: half // 2])
    ff_piece = order.run(pack_ff, index, up_weight, down_weight)
    ff_pieces = lax.all_gather(ff_piece, ("row", "col"))
    vectors = jnp.stack([norm1_gain, norm1_shift, norm2_gain, norm2_shift, out_bias, down_bias])
    vectors_sib = swap(vectors)
    vectors_all = jnp.concatenate([vectors, vectors_sib], axis=1)
    pieces.append(column.send(step_up, pieces[1]))
    near = plane.both(pieces[1], pieces[1])
    here = order.run(pack_heads, index, sources, 4)
    own_parts, other_rows = [here[0]], [order.swap(here[1])]
    normed_one, stats_one = order.run(
        norm_rows,
        index,
        tokens_in,
        tokens_sib,
        jnp.concatenate([vectors[:2], vectors_sib[:2]], axis=0),
    )

    segment_row = picked(segment_ids, col_i)
    member = (segment_row[:, None] == jnp.arange(active_lengths.shape[1])).astype(jnp.int32)
    counts = jnp.sum(member, axis=0)
    first_row = jnp.sum(member * (jnp.cumsum(counts) - counts), axis=1)[None, :]

    heads, attended = [], []

    def attend_project(k):
        heads.append(
            order.run(project, normed_one, own_parts[k], other_rows[k], small[k][None, : 3 * own])
        )

    def attend(k):
        attended.append(order.run(local_forward, heads[k], first_row))

    def stack(k, near, far):
        own_part, other_part = order.run(stack_pieces, [pieces[k], *near, *far])
        own_parts.append(own_part)
        other_rows.append(other_part)

    attend_project(0)
    attend(0)
    far = plane.far(*near)
    pieces.append(column.send(step_up, pieces[2]))
    last_near, last_far = near, far
    near = plane.both(pieces[2], pieces[2])
    stack(1, last_near, last_far)
    attend_project(1)
    attend(1)
    far = plane.far(*near)
    last_near, last_far = near, far
    near = plane.both(pieces[3], pieces[3])
    stack(2, last_near, last_far)
    attend_project(2)
    attend(2)
    far = plane.far(*near)
    last_near, last_far = near, far
    branch_far = plane.far(*branch_first)
    stack(3, last_near, last_far)
    before = order.run(sum_rows, attended[:3], own_parts[:3], other_rows[:3], 3)
    second_near = plane.both(branch_mine[half // 2 :], branch_mine[half // 2 :])
    attend_project(3)
    attend(3)
    second_far = plane.far(*second_near)
    attention_rows = order.run(sum_rows, attended[3:], own_parts[3:], other_rows[3:], 3, (before,))
    arrived = swap(order.tie(mirrored(other_tokens(attention_rows)).astype(bf16)))

    order.tokens.append(ff_pieces)
    hidden_one, normed_two, stats_two = order.run(
        norm_two, index, attention_rows, arrived, tokens_in, tokens_sib, vectors_all
    )

    normed = [normed_two, *plane.both(normed_two, normed_two)]
    branch_all = jnp.concatenate(
        [branch_mine]
        + [part for pair in zip(branch_first, second_near) for part in pair]
        + [*branch_far, *second_far],
        axis=0,
    )
    def by_column(relative):
        places = jnp.mod(col_i - jnp.arange(ring), ring)
        return jnp.take(relative, places, axis=0)

    ff_biases = by_column(jnp.stack([s[None, 3 * own :] for s in small]))
    ff_rows, up_sums, grad_parts, down_parts = [], [], [], []

    def feed_forward(j):
        grads, part = (branch_all, j) if j > 0 else (branch_mine, 0)
        results = order.run(ffn_rows_of, index, normed[j], grads, part, ff_pieces, ff_biases)
        for kept, result in zip((ff_rows, up_sums, grad_parts, down_parts), results):
            kept.append(result)

    def top(values):
        return values[: half // 2]

    def bottom(values):
        return values[half // 2 :]

    def second_steps(parts, via_x, via_y):
        via_x, via_y = after((via_x, via_y), *order.tokens)
        return plane.both(add_rounded(bottom(parts[1]), via_y), add_rounded(top(parts[2]), via_x))

    def weight_grads(part):
        return order.run(weight_products, normed, branch_all, ff_rows, part)

    feed_forward(0)
    normed_far = plane.far(normed[1], normed[2])
    feed_forward(1)
    x_top = plane.x.send(step_x, top(grad_parts[1]))
    feed_forward(2)
    y_bottom = plane.y.send(step_y, bottom(grad_parts[2]))
    normed.append(jnp.concatenate(normed_far, axis=0))
    feed_forward(3)
    via_x, via_y = plane.both(top(grad_parts[3]), bottom(grad_parts[3]))
    ff_mine = weight_grads(0)
    x_bottom, y_top = second_steps(grad_parts, via_x, via_y)
    ff_other = order.swap(weight_grads(1))

    hidden_grad, grad_mine, grad_mirror, sums_two = order.run(
        norm_two_back,
        index,
        (grad_parts[0], x_top, y_top, x_bottom, y_bottom),
        hidden_one,
        stats_two,
        branch_mine,
        vectors_all,
    )
    down_x_top, down_y_bottom = plane.both(top(down_parts[1]), bottom(down_parts[2]))
    grad_others = [order.swap(top(grad_mirror)), order.swap(bottom(grad_mirror))]
    grad_rows = order.run(join_tokens, index, grad_mine, *grad_others)

    ff_grads = []
    for part in range(2):
        span = slice(part * width // 2, (part + 1) * width // 2)
        total = order.tie(add_rounded(ff_mine[:, span], ff_other[:, span]))
        total = lax.psum_scatter(total, "col", scatter_dimension=0, tiled=False)
        ff_grads.append(lax.all_gather(total, "dp"))

    head_grad = order.run(head_grads, grad_rows, own_parts, other_rows)
    head_rows, bias_rows, group_parts = [None] * ring, [None] * ring, [None] * ring

    def backward(k):
        head_rows[k] = order.run(
            lambda h, g, f: local_backward(h, g, k, f), heads[k], head_grad, first_row
        )

    def head_weights(k):
        *group_parts[k], bias_rows[k] = order.run(
            head_products, normed_one, grad_rows, head_rows[k], attended[k]
        )

    def part_of(k, j, which):
        return group_parts[k][which][j * block : (j + 1) * block]

    def first_messages(k):
        return plane.both(part_of(k, 3, 0), part_of(k, 3, 1), True)

    def second_messages(k, via):
        via_x, via_y = after(via, *order.tokens)
        return plane.both(
            jnp.concatenate([part_of(k, 1, 0), add_rounded(part_of(k, 1, 1), via_y)], axis=1),
            jnp.concatenate([add_rounded(part_of(k, 2, 0), via_x), part_of(k, 2, 1)], axis=1),
        )

    def group_total(k, came, total):
        came_x, came_y = after(came, *order.tokens)
        here = jnp.concatenate([part_of(k, 0, 0), part_of(k, 0, 1)], axis=1)
        here = here.astype(f32) + came_x.astype(f32) + came_y.astype(f32)
        if total is not None:
            here = here + total.astype(f32)
        return here.astype(bf16)

    down_via_x, down_via_y = plane.both(top(down_parts[3]), bottom(down_parts[3]))
    def layer_out_rows():
        own_out, sib_out = order.run(
            layer_rows,
            index,
            (down_parts[0], down_x_top, down_y_top, down_x_bottom, down_y_bottom),
            hidden_one,
            tokens_in,
            tokens_sib,
            keep_mask,
            vectors_all,
        )
        return own_out, order.swap(top(sib_out)), order.swap(bottom(sib_out))

    vias, came = [None] * ring, [None] * ring
    backward(3)
    head_weights(3)
    down_x_bottom, down_y_top = second_steps(down_parts, down_via_x, down_via_y)
    vias[3] = first_messages(3)
    backward(2)
    head_weights(2)
    vias[2] = first_messages(2)
    came[3] = second_messages(3, vias[3])
    backward(1)
    head_weights(1)
    vias[1] = first_messages(1)
    came[2] = second_messages(2, vias[2])
    total = column.send(step_down, group_total(3, came[3], None))
    backward(0)
    head_weights(0)
    vias[0] = first_messages(0)
    came[1] = second_messages(1, vias[1])
    total = column.send(step_down, add_rounded(total, group_total(2, came[2], None)))
    back_rows = order.run(sum_rows, head_rows, own_parts, other_rows, 0)
    arrived = order.swap(mirrored(other_tokens(back_rows)).astype(bf16))
    came[0] = second_messages(0, vias[0])
    total = column.send(step_down, add_rounded(total, group_total(1, came[1], None)))
    layer_parts = layer_out_rows()

    input_mine, input_other, sums_one = order.run(
        norm_one_back,
        index,
        back_rows,
        arrived,
        tokens_in,
        tokens_sib,
        stats_one,
        out_grad,
        out_grad_sib,
        keep_mask,
        hidden_grad,
        vectors_all,
    )
    input_others = [order.swap(top(input_other)), order.swap(bottom(input_other))]
    layer_out = order.run(join_tokens, index, *layer_parts)

    row_hot = (jnp.arange(2) == row_i).astype(f32)
    plane_hot = (jnp.arange(4) == plane_i).astype(f32)
    head_bias = by_column(jnp.stack(bias_rows)).reshape(ring, 3, 1, own) * row_hot[:, None]
    up_bias_part = sum(up_sums) * plane_hot[:, None]
    bias_vector = jnp.concatenate([head_bias.reshape(ring, -1), up_bias_part.reshape(ring, -1)], axis=1)
    feature_sums = jnp.concatenate([sums_one[:2], sums_two[:4]], axis=0)
    summed = jnp.concatenate([bias_vector.reshape(-1), feature_sums[:, :width].reshape(-1)])
    summed = summed + swap(
        jnp.concatenate([bias_vector.reshape(-1), feature_sums[:, width:].reshape(-1)])
    )

    summed = order.tie(summed)
    summed = summed + plane.x.send(step_x, summed)
    summed = summed + plane.y.send(step_y, summed)
    total = group_total(0, came[0], total)
    total = jnp.concatenate([total[:, : 4 * own], swap(total[:, 4 * own :])], axis=1)
    near = plane.both(total, total)
    step = 1
    while step < ring:
        pairs = [(i, i ^ step) for i in range(ring)]
        summed = summed + column.send(lambda v: lax.ppermute(v, "col", pairs), summed)
        step *= 2
    input_grad = order.run(join_tokens, index, input_mine, *input_others)
    up_weight_grad, down_weight_grad = order.run(place_ff, ff_grads)
    far = plane.far(*near)
    query_weight_grad, key_weight_grad, value_weight_grad, out_weight_grad = place_heads(
        index, [total, *near, *far]
    )

    bias_here = picked(summed[: bias_vector.size].reshape(ring, -1), col_i)
    own_here = summed[bias_vector.size :].reshape(6, width)
    size = 2 * own
    return (
        layer_out,
        input_grad,
        own_here[0],
        own_here[1],
        query_weight_grad,
        bias_here[:size],
        key_weight_grad,
        value_weight_grad,
        bias_here[2 * size : 3 * size],
        out_weight_grad,
        own_here[4],
        own_here[2],
        own_here[3],
        up_weight_grad,
        bias_here[3 * size :],
        down_weight_grad,
        own_here[5],
    )


def body(tokens_in, out_grad, segment_ids, *rest):
    ring = lax.axis_size("col")
    local = (
        lax.axis_size("dp") == 4
        and lax.axis_size("row") == 2
        and ring == 4
        and tokens_in.shape[0] == segment_ids.shape[1]
    )
    chosen = body_local if local else body_general
    return chosen(tokens_in, out_grad, segment_ids, *rest)


def solution(mesh):
    placed = (
        P(("dp", "col"), "row"),
        P(("dp", "col"), "row"),
        P("dp", None),
        P("dp", None),
        P("row"),
        P("row"),
        P("row", "col"),
        P("col"),
        P("row", "col"),
        P("row", "col"),
        P("col"),
        P("col", "row"),
        P("row"),
        P("row"),
        P("row"),
        P("row", "col"),
        P("col"),
        P("col", "row"),
        P("row"),
    )
    return jax.shard_map(
        body,
        mesh=mesh,
        in_specs=placed,
        out_specs=(
            P(("dp", "col"), "row"),
            P(("dp", "col"), "row"),
            P("row"),
            P("row"),
            P("row", "col"),
            P("col"),
            P("row", "col"),
            P("row", "col"),
            P("col"),
            P("col", "row"),
            P("row"),
            P("row"),
            P("row"),
            P("row", "col"),
            P("col"),
            P("col", "row"),
            P("row"),
        ),
        check_vma=False,
    )
```

```python
import functools

import jax
import jax.numpy as jnp
from jax import lax
from jax.experimental import pallas as pl
from jax.experimental.pallas import tpu as pltpu
from jax.sharding import PartitionSpec as P

D = 2048
HEAD_DIM = 64


norm_eps = 1e-05
masked_fill = -1e30


def width_totals(total_one, total_two):
    return lax.psum((total_one, total_two), "row")


def token_gather(values):
    return lax.all_gather(values, "col", axis=0, tiled=True)


def token_sums(partial_rows):
    return lax.psum_scatter(partial_rows, "col", scatter_dimension=0, tiled=True)


def unit_gather(values):
    return lax.all_gather(values, "row", axis=1, tiled=True)


def unit_sums(partial_units):
    return lax.psum_scatter(partial_units, "row", scatter_dimension=1, tiled=True)


def gelu_value(values):
    return jax.nn.gelu(values, approximate=True)


def gelu_slope(values):
    result, pullback = jax.vjp(gelu_value, values)
    return pullback(jnp.ones_like(values))[0]


def active_rows(segment_rows, keep_lengths):
    doc_index = jnp.arange(keep_lengths.shape[-1], dtype=jnp.int32)
    member = (segment_rows[:, :, None] == doc_index).astype(jnp.int32)
    counts = jnp.sum(member, axis=1)
    starts = jnp.cumsum(counts, axis=1) - counts
    first_pos = jnp.sum(member * starts[:, None, :], axis=2)
    keep_here = jnp.sum(member * keep_lengths[:, None, :], axis=2)
    position_in = jnp.arange(segment_rows.shape[1], dtype=jnp.int32)[None, :] - first_pos
    return (position_in < keep_here).reshape(-1)


def norm_forward(values, gain_part, shift_part):
    total_one, total_two = width_totals(jnp.sum(values, axis=1), jnp.sum(values * values, axis=1))
    average = total_one / D
    variance = total_two / D - average * average
    inverse = lax.rsqrt(variance + norm_eps)
    normal = (values - average[:, None]) * inverse[:, None]
    return ((normal * gain_part + shift_part).astype(jnp.bfloat16), normal, inverse)


def norm_backward(grad_rows, normal, inverse, gain_part):
    scaled = grad_rows * gain_part
    total_one, total_two = width_totals(jnp.sum(scaled, axis=1), jnp.sum(scaled * normal, axis=1))
    grad_in = inverse[:, None] * (
        scaled - total_one[:, None] / D - normal * (total_two[:, None] / D)
    )
    return (grad_in, jnp.sum(grad_rows * normal, axis=0), jnp.sum(grad_rows, axis=0))


def allowed_mask(segment_row, offset, block_rows):
    key_pos = jnp.arange(segment_row.shape[0], dtype=jnp.int32)
    query_pos = key_pos[offset : offset + block_rows]
    same_doc = segment_row[None, :] == segment_row[offset : offset + block_rows, None]
    return (key_pos[None, :] <= query_pos[:, None]) & same_doc


def attend_forward(query_seq, key_seq, value_seq, segment_row, score_scale):
    seq_length = query_seq.shape[2]
    block_rows = min(512, seq_length)
    outputs = []
    log_parts = []
    for offset in range(0, seq_length, block_rows):
        query_block = query_seq[:, :, offset : offset + block_rows]
        scores = (
            jnp.einsum("hdq,hdk->hqk", query_block, key_seq, preferred_element_type=jnp.float32)
            * score_scale
        )
        scores = jnp.where(allowed_mask(segment_row, offset, block_rows)[None], scores, masked_fill)
        row_max = jnp.max(scores, axis=2, keepdims=True)
        exp_scores = jnp.exp(scores - row_max)
        row_total = jnp.sum(exp_scores, axis=2, keepdims=True)
        weights = (exp_scores / row_total).astype(jnp.bfloat16)
        outputs.append(
            jnp.einsum("hqk,hdk->hdq", weights, value_seq, preferred_element_type=jnp.float32)
        )
        log_parts.append((row_max + jnp.log(row_total))[:, :, 0])
    return (jnp.concatenate(outputs, axis=2), jnp.concatenate(log_parts, axis=1))


def attend_backward(query_seq, key_seq, value_seq, grad_seq, segment_row, log_sums, score_scale):
    seq_length = query_seq.shape[2]
    block_rows = min(512, seq_length)
    key_grad = jnp.zeros(key_seq.shape, jnp.float32)
    value_grad = jnp.zeros(value_seq.shape, jnp.float32)
    query_grads = []
    for offset in range(0, seq_length, block_rows):
        query_block = query_seq[:, :, offset : offset + block_rows]
        grad_block = grad_seq[:, :, offset : offset + block_rows]
        scores = (
            jnp.einsum("hdq,hdk->hqk", query_block, key_seq, preferred_element_type=jnp.float32)
            * score_scale
        )
        scores = jnp.where(allowed_mask(segment_row, offset, block_rows)[None], scores, masked_fill)
        probs = jnp.exp(scores - log_sums[:, offset : offset + block_rows, None])
        prob_grad = jnp.einsum(
            "hdq,hdk->hqk", grad_block, value_seq, preferred_element_type=jnp.float32
        )
        row_dot = jnp.sum(probs * prob_grad, axis=2, keepdims=True)
        score_grad = (probs * (prob_grad - row_dot)).astype(jnp.bfloat16)
        query_grads.append(
            jnp.einsum("hqk,hdk->hdq", score_grad, key_seq, preferred_element_type=jnp.float32)
            * score_scale
        )
        key_grad = (
            key_grad
            + jnp.einsum(
                "hqk,hdq->hdk", score_grad, query_block, preferred_element_type=jnp.float32
            )
            * score_scale
        )
        value_grad = value_grad + jnp.einsum(
            "hqk,hdq->hdk",
            probs.astype(jnp.bfloat16),
            grad_block,
            preferred_element_type=jnp.float32,
        )
    return (jnp.concatenate(query_grads, axis=2), key_grad, value_grad)


def body_general(
    tokens_in,
    out_grad,
    segment_ids,
    active_lengths,
    norm1_gain,
    norm1_shift,
    query_weight,
    query_bias,
    key_weight,
    value_weight,
    value_bias,
    out_weight,
    out_bias,
    norm2_gain,
    norm2_shift,
    up_weight,
    up_bias,
    down_weight,
    down_bias,
):
    local_rows = tokens_in.shape[0]
    seq_here = segment_ids.shape[0]
    seq_length = segment_ids.shape[1]
    group_rows = seq_here * seq_length
    row_index = lax.axis_index("row")
    col_index = lax.axis_index("col")
    active_all = active_rows(segment_ids, active_lengths)
    active_here = lax.dynamic_slice_in_dim(active_all, col_index * local_rows, local_rows)
    keep_mask = active_here.astype(jnp.float32)[:, None]
    score_scale = HEAD_DIM ** (-0.5)
    rows_in = tokens_in.astype(jnp.float32)
    normed_one, normal_one, inverse_one = norm_forward(rows_in, norm1_gain, norm1_shift)
    gathered_one = token_gather(normed_one)
    stacked_weight = jnp.stack([query_weight, key_weight, value_weight])
    projected = unit_sums(
        jnp.einsum("td,kdh->kht", gathered_one, stacked_weight, preferred_element_type=jnp.float32)
    )
    head_width = projected.shape[1]
    head_count = head_width // HEAD_DIM
    query_part = lax.dynamic_slice_in_dim(query_bias, row_index * head_width, head_width)
    value_part = lax.dynamic_slice_in_dim(value_bias, row_index * head_width, head_width)
    bias_stack = jnp.stack([query_part, jnp.zeros_like(query_part), value_part])
    heads_all = (projected + bias_stack[:, :, None]).astype(jnp.bfloat16)

    def to_seqs(values):
        return jnp.moveaxis(values.reshape(head_count, HEAD_DIM, seq_here, seq_length), 2, 0)

    def from_seqs(values):
        return jnp.moveaxis(values, 0, 2).reshape(head_width, group_rows)

    query_seqs = to_seqs(heads_all[0])
    key_seqs = to_seqs(heads_all[1])
    value_seqs = to_seqs(heads_all[2])
    attended_seqs, log_sums = lax.map(
        lambda seq_items: attend_forward(
            seq_items[0], seq_items[1], seq_items[2], seq_items[3], score_scale
        ),
        (query_seqs, key_seqs, value_seqs, segment_ids),
    )
    attended = from_seqs(attended_seqs).astype(jnp.bfloat16)
    gathered_heads = unit_gather(attended[None])
    attention_rows = (
        token_sums(
            jnp.einsum("kht,hd->td", gathered_heads, out_weight, preferred_element_type=jnp.float32)
        )
        + out_bias
    )
    hidden_one = rows_in + attention_rows
    normed_two, normal_two, inverse_two = norm_forward(hidden_one, norm2_gain, norm2_shift)
    gathered_two = token_gather(normed_two)
    up_part = jnp.einsum("td,df->ft", gathered_two, up_weight, preferred_element_type=jnp.float32)[
        None
    ]
    unit_width = up_part.shape[1] // lax.axis_size("row")
    up_slice = lax.dynamic_slice_in_dim(up_bias, row_index * unit_width, unit_width)
    pre_act = unit_sums(up_part)[0] + up_slice[:, None]
    gathered_act = unit_gather(gelu_value(pre_act).astype(jnp.bfloat16)[None])
    ffn_rows = (
        token_sums(
            jnp.einsum("kft,fd->td", gathered_act, down_weight, preferred_element_type=jnp.float32)
        )
        + down_bias
    )
    layer_out = jnp.where(active_here[:, None], hidden_one + ffn_rows, rows_in)
    grad_rows = out_grad.astype(jnp.float32) * keep_mask
    branch_grad = token_gather(grad_rows.astype(jnp.bfloat16))
    down_grad = jnp.einsum(
        "kft,td->fd", gathered_act, branch_grad, preferred_element_type=jnp.float32
    )
    down_bias_grad = jnp.sum(branch_grad, axis=0, dtype=jnp.float32)
    act_part = jnp.einsum(
        "td,fd->ft", branch_grad, down_weight, preferred_element_type=jnp.float32
    )[None]
    act_grad = unit_sums(act_part)[0]
    pre_grad = (act_grad * gelu_slope(pre_act)).astype(jnp.bfloat16)
    gathered_pre = unit_gather(pre_grad[None])
    up_grad = jnp.einsum(
        "td,kft->df", gathered_two, gathered_pre, preferred_element_type=jnp.float32
    )
    up_bias_grad = jnp.sum(gathered_pre[0], axis=1, dtype=jnp.float32)
    normed_grad_two = token_sums(
        jnp.einsum("kft,df->td", gathered_pre, up_weight, preferred_element_type=jnp.float32)
    )
    back_two, gain_two_grad, shift_two_grad = norm_backward(
        normed_grad_two, normal_two, inverse_two, norm2_gain
    )
    hidden_grad = grad_rows + back_two
    attention_grad = token_gather(hidden_grad.astype(jnp.bfloat16))
    out_weight_grad = jnp.einsum(
        "kht,td->hd", gathered_heads, attention_grad, preferred_element_type=jnp.float32
    )
    out_bias_grad = jnp.sum(attention_grad, axis=0, dtype=jnp.float32)
    head_grad = unit_sums(
        jnp.einsum("td,hd->ht", attention_grad, out_weight, preferred_element_type=jnp.float32)[
            None
        ]
    )[0].astype(jnp.bfloat16)
    query_grads, key_grads, value_grads = lax.map(
        lambda seq_items: attend_backward(
            seq_items[0],
            seq_items[1],
            seq_items[2],
            seq_items[3],
            seq_items[4],
            seq_items[5],
            score_scale,
        ),
        (query_seqs, key_seqs, value_seqs, to_seqs(head_grad), segment_ids, log_sums),
    )
    stacked_grad = jnp.stack(
        [from_seqs(query_grads), from_seqs(key_grads), from_seqs(value_grads)]
    ).astype(jnp.bfloat16)
    gathered_grad = unit_gather(stacked_grad)
    stacked_weight_grad = jnp.einsum(
        "td,kht->kdh", gathered_one, gathered_grad, preferred_element_type=jnp.float32
    )
    query_bias_grad = jnp.sum(gathered_grad[0], axis=1, dtype=jnp.float32)
    value_bias_grad = jnp.sum(gathered_grad[2], axis=1, dtype=jnp.float32)
    normed_grad_one = token_sums(
        jnp.einsum("kht,kdh->td", gathered_grad, stacked_weight, preferred_element_type=jnp.float32)
    )
    back_one, gain_one_grad, shift_one_grad = norm_backward(
        normed_grad_one, normal_one, inverse_one, norm1_gain
    )
    input_grad = out_grad.astype(jnp.float32) * (1.0 - keep_mask) + hidden_grad + back_one
    (
        stacked_weight_grad,
        query_bias_grad,
        value_bias_grad,
        out_weight_grad,
        out_bias_grad,
        down_grad,
        down_bias_grad,
        up_grad,
        up_bias_grad,
    ) = lax.psum(
        (
            stacked_weight_grad,
            query_bias_grad,
            value_bias_grad,
            out_weight_grad,
            out_bias_grad,
            down_grad,
            down_bias_grad,
            up_grad,
            up_bias_grad,
        ),
        "dp",
    )
    gain_one_grad, shift_one_grad, gain_two_grad, shift_two_grad = lax.psum(
        (gain_one_grad, shift_one_grad, gain_two_grad, shift_two_grad), ("dp", "col")
    )
    return (
        layer_out,
        input_grad,
        gain_one_grad,
        shift_one_grad,
        stacked_weight_grad[0],
        query_bias_grad,
        stacked_weight_grad[1],
        stacked_weight_grad[2],
        value_bias_grad,
        out_weight_grad,
        out_bias_grad,
        gain_two_grad,
        shift_two_grad,
        up_grad,
        up_bias_grad,
        down_grad,
        down_bias_grad,
    )


def after(values, *others):
    return lax.optimization_barrier((values, others))[0]


def swap(values):
    return lax.ppermute(values, "row", [(0, 1), (1, 0)])


def step_x(values):
    return lax.ppermute(values, "dp", [(0, 1), (1, 0), (2, 3), (3, 2)])


def step_y(values):
    return lax.ppermute(values, "dp", [(0, 2), (2, 0), (1, 3), (3, 1)])


def step_up(values):
    count = lax.axis_size("col")
    return lax.ppermute(values, "col", [(i, (i + 1) % count) for i in range(count)])


def step_down(values):
    count = lax.axis_size("col")
    return lax.ppermute(values, "col", [(i, (i - 1) % count) for i in range(count)])


class Order:
    def __init__(self):
        self.tokens = []
        self.fresh, self.due = [], []

    def tie(self, values):
        if self.tokens:
            values = after(values, *self.tokens)
        self.tokens.append(values)
        return values

    def swap(self, values, due=True):
        arrived = swap(self.tie(values))
        if due:
            self.fresh.append(arrived)
        return arrived

    def run(self, function, first, *others):
        first = after(first, *self.tokens, *self.due) if self.tokens or self.due else first
        self.due, self.fresh = self.fresh, []
        result = function(first, *others)
        self.tokens = [jax.tree.leaves(result)[0]]
        return result


class Link:
    def __init__(self, order):
        self.order = order
        self.last = None

    def send(self, step, values, free=False):
        if self.last is not None and not free:
            values = after(values, self.last)
        self.last = step(self.order.tie(values))
        return self.last


class Plane:
    def __init__(self, order):
        self.x = Link(order)
        self.y = Link(order)

    def both(self, for_x, for_y, free=False):
        return self.x.send(step_x, for_x, free), self.y.send(step_y, for_y, free)

    def far(self, from_x, from_y):
        half = from_x.shape[0] // 2
        far_two, far_one = self.both(from_y[half:], from_x[:half])
        return far_one, far_two


def add_rounded(left, right):
    return (left.astype(jnp.float32) + right.astype(jnp.float32)).astype(jnp.bfloat16)


def ring_gather(link, values):
    held = [values]
    for _ in range(lax.axis_size("col") - 1):
        held.append(link.send(step_up, held[-1]))
    return held


def picked(stacked, index):
    return lax.dynamic_index_in_dim(stacked, index, 0, keepdims=False)


def mm(left, right, left_dim, right_dim, dtype=jnp.float32):
    return lax.dot_general(
        left, right, (((left_dim,), (right_dim,)), ((), ())), preferred_element_type=jnp.float32
    ).astype(dtype)


PAIR = 2 * HEAD_DIM
vmem_bytes = 48 * 1024 * 1024


def head_lanes(head, value):
    lane = lax.broadcasted_iota(jnp.int32, (1, PAIR), 1)
    return jnp.where(lane // HEAD_DIM == head, value, 0.0).astype(jnp.bfloat16)


def allowed_keys(first_row, low, high):
    key_pos = lax.broadcasted_iota(jnp.int32, (high, high - low), 0)
    query_pos = lax.broadcasted_iota(jnp.int32, (high, high - low), 1) + low
    return (key_pos >= first_row) & (key_pos <= query_pos)


def local_forward_kernel(size, first_ref, query_ref, key_ref, value_ref, out_ref):
    lane = lax.broadcasted_iota(jnp.int32, (size, PAIR), 1)
    for low in range(0, key_ref.shape[0], size):
        high = low + size
        keys = key_ref[:high, :]
        values = value_ref[:high, :]
        queries = query_ref[low:high, :]
        allowed = allowed_keys(first_ref[:, low:high], low, high)
        results = []
        for head in range(2):
            scores = mm(keys, queries * head_lanes(head, HEAD_DIM ** (-0.5)), 1, 1)
            scores = jnp.where(allowed, scores, masked_fill)
            exp_scores = jnp.exp(scores - jnp.max(scores, axis=0, keepdims=True))
            inverse = 1.0 / jnp.sum(exp_scores, axis=0, keepdims=True)
            results.append(mm((exp_scores * inverse).astype(jnp.bfloat16), values, 0, 0))
        out_ref[low:high, :] = jnp.where(lane < HEAD_DIM, results[0], results[1]).astype(
            jnp.bfloat16
        )


def local_forward(heads, first_row):
    length = heads.shape[0]
    pairs = heads.shape[1] // (3 * PAIR)
    return pl.pallas_call(
        functools.partial(local_forward_kernel, min(256, length)),
        grid=(pairs,),
        in_specs=[
            pl.BlockSpec((1, length), lambda p: (0, 0)),
            pl.BlockSpec((length, PAIR), lambda p: (0, p)),
            pl.BlockSpec((length, PAIR), lambda p: (0, pairs + p)),
            pl.BlockSpec((length, PAIR), lambda p: (0, 2 * pairs + p)),
        ],
        out_specs=pl.BlockSpec((length, PAIR), lambda p: (0, p)),
        out_shape=jax.ShapeDtypeStruct((length, pairs * PAIR), jnp.bfloat16),
        compiler_params=pltpu.CompilerParams(vmem_limit_bytes=vmem_bytes),
        cost_estimate=cost(16 * length * length * pairs * PAIR, 8 * heads.size),
    )(first_row, heads, heads, heads)


def local_backward_kernel(
    size, first_ref, query_ref, grad_ref, key_ref, value_ref, out_ref, key_sum, value_sum
):
    length = key_ref.shape[0]
    pair = pl.program_id(0)
    pairs = out_ref.shape[1] // (3 * PAIR)
    scale = HEAD_DIM ** (-0.5)
    lane = lax.broadcasted_iota(jnp.int32, (size, PAIR), 1)

    def lanes(part):
        return pl.ds(pl.multiple_of((part * pairs + pair) * PAIR, PAIR), PAIR)

    for low in range(length - size, -1, -size):
        high = low + size
        keys = key_ref[:high, :]
        values = value_ref[:high, :]
        queries = query_ref[low:high, :]
        grads = grad_ref[low:high, :]
        allowed = allowed_keys(first_ref[:, low:high], low, high)
        query_grads = []
        for head in range(2):
            scaled = queries * head_lanes(head, scale)
            grad = grads * head_lanes(head, 1.0)
            scores = jnp.where(allowed, mm(keys, scaled, 1, 1), masked_fill)
            exp_scores = jnp.exp(scores - jnp.max(scores, axis=0, keepdims=True))
            probs = exp_scores * (1.0 / jnp.sum(exp_scores, axis=0, keepdims=True))
            prob_grad = mm(values, grad, 1, 1)
            row_dot = jnp.sum(probs * prob_grad, axis=0, keepdims=True)
            score_grad = (probs * (prob_grad - row_dot)).astype(jnp.bfloat16)
            value_part = mm(probs.astype(jnp.bfloat16), grad, 1, 0)
            key_part = mm(score_grad, scaled, 1, 0)
            query_grads.append(mm(score_grad, keys, 0, 0) * scale)
            if head == 0:
                key_add, value_add = key_part, value_part
            else:
                key_add, value_add = key_add + key_part, value_add + value_part
        if high == length:
            key_sum[...] = key_add
            value_sum[...] = value_add
        else:
            key_sum[:high, :] += key_add
            value_sum[:high, :] += value_add
        out_ref[low:high, lanes(0)] = jnp.where(
            lane < HEAD_DIM, query_grads[0], query_grads[1]
        ).astype(jnp.bfloat16)
    out_ref[:, lanes(1)] = key_sum[...].astype(jnp.bfloat16)
    out_ref[:, lanes(2)] = value_sum[...].astype(jnp.bfloat16)


def local_backward(heads, head_grad, group, first_row):
    length = heads.shape[0]
    pairs = heads.shape[1] // (3 * PAIR)
    return pl.pallas_call(
        functools.partial(local_backward_kernel, min(512, length)),
        grid=(pairs,),
        in_specs=[
            pl.BlockSpec((1, length), lambda p: (0, 0)),
            pl.BlockSpec((length, PAIR), lambda p: (0, p)),
            pl.BlockSpec((length, PAIR), lambda p: (0, group * pairs + p)),
            pl.BlockSpec((length, PAIR), lambda p: (0, pairs + p)),
            pl.BlockSpec((length, PAIR), lambda p: (0, 2 * pairs + p)),
        ],
        out_specs=pl.BlockSpec(heads.shape, lambda p: (0, 0)),
        out_shape=jax.ShapeDtypeStruct(heads.shape, jnp.bfloat16),
        scratch_shapes=[pltpu.VMEM((length, PAIR), jnp.float32)] * 2,
        compiler_params=pltpu.CompilerParams(vmem_limit_bytes=vmem_bytes),
        cost_estimate=cost(32 * length * length * pairs * PAIR, 8 * heads.size),
    )(first_row, heads, head_grad, heads, heads)


gelu_scale = 0.7978845608028654
gelu_cubic = 0.044715


def ffn_kernel(index_ref, *refs):
    normed, grads, pieces = refs[:2], refs[2:4], [r.at[0] for r in refs[4:6]]
    bias_ref, rows_ref, sum_ref, grad_out, down_out, grad_acc, down_acc = refs[6:]
    step = pl.program_id(0)
    width = normed[0].shape[1]
    quarter = pieces[0].shape[1] // 2
    ups, downs = slice(0, quarter), slice(quarter, 2 * quarter)
    pre = mm(normed[0][...], pieces[0][:, ups], 1, 0) + mm(normed[1][...], pieces[1][:, ups], 1, 0)
    pre = pre + bias_ref[0]
    act_grad = mm(grads[0][...], pieces[0][:, downs], 1, 0) + mm(grads[1][...], pieces[1][:, downs], 1, 0)
    square = pre * pre
    bent = jnp.tanh(gelu_scale * pre * (1.0 + gelu_cubic * square))
    half = 0.5 * (1.0 + bent)
    slope = half + 0.5 * gelu_scale * pre * (1.0 - bent * bent) * (1.0 + 3.0 * gelu_cubic * square)
    act = (pre * half).astype(jnp.bfloat16)
    pre_grad = (act_grad * slope).astype(jnp.bfloat16)
    rows_ref[:, :quarter] = act
    rows_ref[:, quarter:] = pre_grad
    sum_ref[0] = jnp.sum(pre_grad.astype(jnp.float32), axis=0, keepdims=True)

    @pl.when(step == 0)
    def _():
        for i in range(2):
            at = slice(i * width, (i + 1) * width)
            grad_acc[:, at] = mm(pre_grad, pieces[i][:, ups], 1, 1)
            down_acc[:, at] = mm(act, pieces[i][:, downs], 1, 1)

    @pl.when(step > 0)
    def _():
        for i in range(2):
            at = slice(i * width, (i + 1) * width)
            grad_acc[:, at] += mm(pre_grad, pieces[i][:, ups], 1, 1)
            down_acc[:, at] += mm(act, pieces[i][:, downs], 1, 1)

    @pl.when(step == pl.num_programs(0) - 1)
    def _():
        grad_out[...] = grad_acc[...].astype(jnp.bfloat16)
        down_out[...] = down_acc[...].astype(jnp.bfloat16)


def ffn_rows_of(index, normed, grads, part, pieces, bias):
    tokens, features = normed.shape
    width = features // 2
    columns = pieces.shape[2]
    ring, quarter = pieces.shape[0] // 2, columns // 2

    def halves(at):
        return [pl.BlockSpec((tokens, width), lambda k, s, h=h: (at, h)) for h in range(2)]

    piece = [
        pl.BlockSpec((1, width, columns), lambda k, s, h=h: ((s[0] ^ h) * ring + k, 0, 0))
        for h in range(2)
    ]
    whole = pl.BlockSpec((tokens, features), lambda k, s: (0, 0))
    vector = pl.BlockSpec((1, 1, quarter), lambda k, s: (k, 0, 0))
    return pl.pallas_call(
        ffn_kernel,
        grid_spec=pltpu.PrefetchScalarGridSpec(
            num_scalar_prefetch=1,
            grid=(ring,),
            in_specs=halves(0) + halves(part) + piece + [vector],
            out_specs=[pl.BlockSpec((tokens, columns), lambda k, s: (0, k)), vector, whole, whole],
            scratch_shapes=[pltpu.VMEM((tokens, features), jnp.float32)] * 2,
        ),
        out_shape=[
            shape((tokens, ring * columns)),
            shape((ring, 1, quarter), jnp.float32),
            shape((tokens, features)),
            shape((tokens, features)),
        ],
        compiler_params=params(),
        cost_estimate=cost(8 * tokens * features * ring * quarter, 12 * ring * width * columns),
    )(index, normed, normed, grads, grads, pieces, pieces, bias)


def weight_products_kernel(count, *refs):
    out_ref = refs[-1]
    normed, grads, rows = [refs[i * count : (i + 1) * count] for i in range(3)]
    quarter = rows[0].shape[1] // 2
    up = down = None
    for j in range(count):
        up_part = mm(normed[j][...], rows[j][:, quarter:], 0, 0)
        down_part = mm(grads[j][...], rows[j][:, :quarter], 0, 0)
        up = up_part if up is None else up + up_part
        down = down_part if down is None else down + down_part
    out_ref[0, :, :quarter] = up.astype(jnp.bfloat16)
    out_ref[0, :, quarter:] = down.astype(jnp.bfloat16)


def weight_products(normed, grads, rows, half):
    count = len(normed)
    tokens, features = normed[0].shape
    width = features // 2
    ring = 4
    columns = rows[0].shape[1] // ring
    size = min(512, width)
    blocks = width // size
    left = [pl.BlockSpec((tokens, size), lambda k, d: (0, half * blocks + d))] * count
    left += [
        pl.BlockSpec((tokens, size), lambda k, d, j=j: (j, half * blocks + d)) for j in range(count)
    ]
    return pl.pallas_call(
        functools.partial(weight_products_kernel, count),
        grid=(ring, blocks),
        in_specs=left + [pl.BlockSpec((tokens, columns), lambda k, d: (0, k))] * count,
        out_specs=pl.BlockSpec((1, size, columns), lambda k, d: (k, d, 0)),
        out_shape=shape((ring, width, columns)),
        compiler_params=params(),
        cost_estimate=cost(
            2 * count * tokens * width * ring * columns, 4 * count * tokens * features * ring
        ),
    )(*normed, *([grads] * count), *rows)


def params(**more):
    return pltpu.CompilerParams(vmem_limit_bytes=vmem_bytes, **more)


def cost(flops, nbytes):
    return pl.CostEstimate(flops=flops // 10, bytes_accessed=nbytes // 10, transcendentals=0)


def shape(dims, dtype=jnp.bfloat16):
    return jax.ShapeDtypeStruct(dims, dtype)


def turned(values):
    return values.astype(jnp.float32).T.astype(jnp.bfloat16)


def pack_heads_kernel(index_ref, *refs):
    sources, outs = refs[:8], refs[8:]
    own = sources[0].shape[1]
    for which in range(2):
        for i in range(4):
            part = sources[4 * which + i][...]
            outs[which][:, i * own : (i + 1) * own] = part if i < 3 else turned(part)


def pack_heads(index, weights, count):
    width, units = weights[0].shape
    own, block = units // 2, width // 4

    def feature(which):
        return pl.BlockSpec((block, own), lambda j, s: (s[1] ^ j, s[0] ^ which))

    def turned_block(which):
        return pl.BlockSpec((own, block), lambda j, s: (s[0] ^ which, s[1] ^ j))

    in_specs = []
    for which in range(2):
        in_specs += [feature(which)] * 3 + [turned_block(which)]
    return pl.pallas_call(
        pack_heads_kernel,
        grid_spec=pltpu.PrefetchScalarGridSpec(
            num_scalar_prefetch=1,
            grid=(count,),
            in_specs=in_specs,
            out_specs=[pl.BlockSpec((block, 4 * own), lambda j, s: (j, 0))] * 2,
        ),
        out_shape=[shape((count * block, 4 * own))] * 2,
        compiler_params=params(),
        cost_estimate=cost(0, 32 * count * block * own),
    )(index, *weights, *weights)


def pack_ff_kernel(index_ref, up_ref, down_ref, out_ref):
    quarter = up_ref.shape[1]
    out_ref[:, :quarter] = up_ref[...]
    out_ref[:, quarter:] = turned(down_ref[...])


def pack_ff(index, up_weight, down_weight):
    width, units = up_weight.shape
    quarter, block = units // 4, width // 4
    return pl.pallas_call(
        pack_ff_kernel,
        grid_spec=pltpu.PrefetchScalarGridSpec(
            num_scalar_prefetch=1,
            grid=(4,),
            in_specs=[
                pl.BlockSpec((block, quarter), lambda d, s: (d, s[1])),
                pl.BlockSpec((quarter, block), lambda d, s: (s[1], d)),
            ],
            out_specs=pl.BlockSpec((block, 2 * quarter), lambda d, s: (d, 0)),
        ),
        out_shape=shape((width, 2 * quarter)),
        compiler_params=params(),
        cost_estimate=cost(0, 8 * width * quarter),
    )(index, up_weight, down_weight)


def stack_kernel(*refs):
    pieces, outs = refs[:3], refs[-2:]
    block = pieces[0].shape[0] // 2
    for j, piece in enumerate(pieces):
        for i in range(2):
            outs[i][j * block : (j + 1) * block, :] = piece[i * block : (i + 1) * block, :]
    for i in range(2):
        outs[i][3 * block :, :] = refs[3 + i][...]


def stack_pieces(pieces):
    rows, columns = pieces[0].shape
    return pl.pallas_call(
        stack_kernel,
        out_shape=[shape((2 * rows, columns))] * 2,
        compiler_params=params(),
        cost_estimate=cost(0, 16 * rows * columns),
    )(*pieces)


def norm_kernel(index_ref, own_ref, sib_ref, vectors_ref, out_ref, stats_ref):
    own = own_ref[...].astype(jnp.float32)
    sib = sib_ref[...].astype(jnp.float32)
    width = own.shape[1]
    average = (jnp.sum(own, axis=1, keepdims=True) + jnp.sum(sib, axis=1, keepdims=True)) / (2 * width)
    own, sib = own - average, sib - average
    square = jnp.sum(own * own, axis=1, keepdims=True) + jnp.sum(sib * sib, axis=1, keepdims=True)
    inverse = lax.rsqrt(square / (2 * width) + norm_eps)
    block = width // 4
    for half, values in enumerate((own, sib)):
        gain, shift = vectors_ref[2 * half, :][None], vectors_ref[2 * half + 1, :][None]
        rounded = (values * inverse * gain + shift).astype(jnp.bfloat16)
        for i in range(4):
            at = pl.multiple_of(half * width + (index_ref[1] ^ i) * block, block)
            out_ref[:, pl.ds(at, block)] = rounded[:, i * block : (i + 1) * block]
    lane = lax.broadcasted_iota(jnp.int32, stats_ref.shape, 1)
    stats_ref[...] = jnp.where(lane == 0, average, inverse)


def norm_rows(index, own, sib, vectors):
    tokens, width = own.shape
    size = min(256, tokens)
    rows = pl.BlockSpec((size, width), lambda i, s: (i, 0))
    return pl.pallas_call(
        norm_kernel,
        grid_spec=pltpu.PrefetchScalarGridSpec(
            num_scalar_prefetch=1,
            grid=(tokens // size,),
            in_specs=[rows, rows, pl.BlockSpec((4, width), lambda i, s: (0, 0))],
            out_specs=[
                pl.BlockSpec((size, 2 * width), lambda i, s: (i, 0)),
                pl.BlockSpec((size, 128), lambda i, s: (i, 0)),
            ],
        ),
        out_shape=[shape((tokens, 2 * width)), shape((tokens, 128), jnp.float32)],
        compiler_params=params(),
        cost_estimate=cost(0, 8 * tokens * width),
    )(index, own, sib, vectors)


def project_kernel(own_ref, sib_ref, own_weight, sib_weight, bias_ref, out_ref):
    total = mm(own_ref[...], own_weight[...], 1, 0) + mm(sib_ref[...], sib_weight[...], 1, 0)
    out_ref[...] = (total + bias_ref[...]).astype(jnp.bfloat16)


def halves_of(size, width):
    return [pl.BlockSpec((size, width), lambda i, h=h: (i, h)) for h in range(2)]


def project(normed, own_weight, sib_weight, bias):
    tokens, features = normed.shape
    width, units = features // 2, bias.shape[1]
    size = min(256, tokens)
    weight = pl.BlockSpec((width, units), lambda i: (0, 0))
    return pl.pallas_call(
        project_kernel,
        grid=(tokens // size,),
        in_specs=halves_of(size, width)
        + [weight, weight, pl.BlockSpec((1, units), lambda i: (0, 0))],
        out_specs=pl.BlockSpec((size, units), lambda i: (i, 0)),
        out_shape=shape((tokens, units)),
        compiler_params=params(),
        cost_estimate=cost(4 * tokens * width * units, 4 * tokens * width + 4 * width * units),
    )(normed, normed, own_weight, sib_weight, bias)


def sum_rows_kernel(count, *refs):
    out_ref = refs[-1]
    width = refs[count].shape[0]
    for half in range(2):
        at = slice(half * width, (half + 1) * width)
        total = refs[3 * count][:, at] if len(refs) > 3 * count + 1 else None
        for k in range(count):
            part = mm(refs[k][...], refs[(1 + half) * count + k][...], 1, 1)
            total = part if total is None else total + part
        out_ref[:, at] = total


def sum_rows(rows, own_weights, sib_weights, at, before=()):
    count = len(rows)
    tokens, units = rows[0].shape
    width = own_weights[0].shape[0]
    size = min(512, tokens)
    full = pl.BlockSpec((size, 2 * width), lambda i: (i, 0))
    return pl.pallas_call(
        functools.partial(sum_rows_kernel, count),
        grid=(tokens // size,),
        in_specs=[pl.BlockSpec((size, units), lambda i: (i, 0))] * count
        + [pl.BlockSpec((width, units), lambda i: (0, at))] * (2 * count)
        + [full] * len(before),
        out_specs=full,
        out_shape=shape((tokens, 2 * width), jnp.float32),
        compiler_params=params(),
        cost_estimate=cost(4 * count * tokens * units * width, 8 * tokens * width),
    )(*rows, *own_weights, *sib_weights, *before)


def head_grads_kernel(own_ref, sib_ref, *refs):
    out_ref = refs[-1]
    count = (len(refs) - 1) // 2
    own = refs[0].shape[1]
    for k in range(count):
        total = mm(own_ref[...], refs[k][...], 1, 0) + mm(sib_ref[...], refs[count + k][...], 1, 0)
        out_ref[:, k * own : (k + 1) * own] = total.astype(jnp.bfloat16)


def head_grads(grads, own_weights, sib_weights):
    tokens, width = grads.shape[0], grads.shape[1] // 2
    count = len(own_weights)
    units = own_weights[0].shape[1] // 4
    size = min(256, tokens)
    return pl.pallas_call(
        head_grads_kernel,
        grid=(tokens // size,),
        in_specs=halves_of(size, width) + [pl.BlockSpec((width, units), lambda i: (0, 3))] * (2 * count),
        out_specs=pl.BlockSpec((size, count * units), lambda i: (i, 0)),
        out_shape=shape((tokens, count * units)),
        compiler_params=params(),
        cost_estimate=cost(4 * count * tokens * width * units, 8 * tokens * width),
    )(grads, grads, *own_weights, *sib_weights)


def head_products_kernel(*refs):
    normed, grads = refs[:2], refs[2:4]
    heads_ref, attended_ref = refs[4:6]
    outs, sum_ref = refs[6:8], refs[8]
    split = heads_ref.shape[1]
    for i in range(2):
        outs[i][:, :split] = mm(normed[i][...], heads_ref[...], 0, 0).astype(jnp.bfloat16)
        outs[i][:, split:] = mm(grads[i][...], attended_ref[...], 0, 0).astype(jnp.bfloat16)

    @pl.when(pl.program_id(0) == 0)
    def _():
        sum_ref[...] = jnp.sum(heads_ref[...].astype(jnp.float32), axis=0, keepdims=True)


def head_products(normed, grads, head_grad, attended):
    tokens, width = normed.shape[0], normed.shape[1] // 2
    split, own = head_grad.shape[1], attended.shape[1]
    size = min(512, width)
    blocks = width // size
    left = [pl.BlockSpec((tokens, size), lambda d, h=h: (0, h * blocks + d)) for h in range(2)]
    out = pl.BlockSpec((size, split + own), lambda d: (d, 0))
    return pl.pallas_call(
        head_products_kernel,
        grid=(width // size,),
        in_specs=left * 2
        + [pl.BlockSpec((tokens, split), lambda d: (0, 0)), pl.BlockSpec((tokens, own), lambda d: (0, 0))],
        out_specs=[out, out, pl.BlockSpec((1, split), lambda d: (0, 0))],
        out_shape=[shape((width, split + own))] * 2 + [shape((1, split), jnp.float32)],
        compiler_params=params(),
        cost_estimate=cost(4 * tokens * width * (split + own), 12 * tokens * width),
    )(normed, normed, grads, grads, head_grad, attended)


def block_at(half, width, place):
    block = width // 4
    return pl.ds(pl.multiple_of(half * width + place * block, block), block)


def norm_two_kernel(
    index_ref, rows_ref, came_ref, own_ref, sib_ref, vectors_ref, hidden_ref, normed_ref, stats_ref
):
    width = own_ref.shape[1]
    block = width // 4
    for half, tokens_ref in enumerate((own_ref, sib_ref)):
        for i in range(4):
            at = block_at(half, width, index_ref[1] ^ i)
            span = slice(half * width + i * block, half * width + (i + 1) * block)
            hidden_ref[:, span] = (
                tokens_ref[:, i * block : (i + 1) * block].astype(jnp.float32)
                + rows_ref[:, at]
                + came_ref[:, at].astype(jnp.float32)
                + vectors_ref[4:5, span]
            )
    hidden = hidden_ref[...]
    average = jnp.mean(hidden, axis=1, keepdims=True)
    centered = hidden - average
    inverse = lax.rsqrt(jnp.mean(centered * centered, axis=1, keepdims=True) + norm_eps)
    normed_ref[...] = (centered * inverse * vectors_ref[2:3, :] + vectors_ref[3:4, :]).astype(jnp.bfloat16)
    lane = lax.broadcasted_iota(jnp.int32, stats_ref.shape, 1)
    stats_ref[...] = jnp.where(lane == 0, average, inverse)


def my_rows(size, columns, blocks):
    return pl.BlockSpec((size, columns), lambda i, s: (s[0] * blocks + i, 0))


def norm_two(index, rows, came, own, sib, vectors):
    tokens, features = came.shape
    size = tokens // 2
    mine = my_rows(size, features // 2, 2)
    plain = pl.BlockSpec((size, features), lambda i, s: (i, 0))
    return pl.pallas_call(
        norm_two_kernel,
        grid_spec=pltpu.PrefetchScalarGridSpec(
            num_scalar_prefetch=1,
            grid=(2,),
            in_specs=[
                my_rows(size, features, 2),
                plain,
                mine,
                mine,
                pl.BlockSpec(vectors.shape, lambda i, s: (0, 0)),
            ],
            out_specs=[plain, plain, pl.BlockSpec((size, 128), lambda i, s: (i, 0))],
        ),
        out_shape=[
            shape((tokens, features), jnp.float32),
            shape((tokens, features)),
            shape((tokens, 128), jnp.float32),
        ],
        compiler_params=params(),
        cost_estimate=cost(0, 16 * tokens * features),
    )(index, rows, came, own, sib, vectors)


def norm_pull(grads, normal, inverse, gain):
    scaled = grads * gain
    return inverse * (
        scaled
        - jnp.mean(scaled, axis=1, keepdims=True)
        - normal * jnp.mean(scaled * normal, axis=1, keepdims=True)
    )


def add_sums(sums_ref, parts):
    rows = [jnp.sum(p, axis=0, keepdims=True) for p in parts]
    rows += [jnp.zeros_like(rows[0])] * (8 - len(rows))
    total = jnp.concatenate(rows, axis=0)

    @pl.when(pl.program_id(0) == 0)
    def _():
        sums_ref[...] = total

    @pl.when(pl.program_id(0) > 0)
    def _():
        sums_ref[...] += total


def norm_two_back_kernel(index_ref, *refs):
    here, x_top, y_top, x_bottom, y_bottom, hidden_ref, stats_ref, branch_ref, vectors_ref = refs[:9]
    grad_ref, blocks_ref, mirror_ref, sums_ref = refs[9:]
    f32 = jnp.float32
    top = pl.program_id(0) == 0
    from_x = jnp.where(top, x_top[...].astype(f32), x_bottom[...].astype(f32))
    from_y = jnp.where(top, y_top[...].astype(f32), y_bottom[...].astype(f32))
    grads = here[...].astype(f32) + from_x + from_y
    inverse = stats_ref[:, 1:2]
    normal = (hidden_ref[...] - stats_ref[:, :1]) * inverse
    branch = branch_ref[...].astype(f32)
    total = branch + norm_pull(grads, normal, inverse, vectors_ref[2:3, :])
    grad_ref[...] = total
    rounded = total.astype(jnp.bfloat16)
    width = rounded.shape[1] // 2
    block = width // 4
    for half in range(2):
        for i in range(4):
            part = rounded[:, half * width + i * block : half * width + (i + 1) * block]
            place = index_ref[1] ^ i
            blocks_ref[:, block_at(half, width, place)] = part
            mirror_ref[:, block_at(1 - half, width, place)] = part
    add_sums(sums_ref, (grads * normal, grads, rounded.astype(f32), branch))


def norm_two_back(index, parts, hidden, stats, branch, vectors):
    tokens, features = hidden.shape
    size = tokens // 2
    plain = pl.BlockSpec((size, features), lambda i, s: (i, 0))
    once = pl.BlockSpec((size, features), lambda i, s: (0, 0))
    return pl.pallas_call(
        norm_two_back_kernel,
        grid_spec=pltpu.PrefetchScalarGridSpec(
            num_scalar_prefetch=1,
            grid=(2,),
            in_specs=[plain]
            + [once] * 4
            + [
                plain,
                pl.BlockSpec((size, 128), lambda i, s: (i, 0)),
                plain,
                pl.BlockSpec(vectors.shape, lambda i, s: (0, 0)),
            ],
            out_specs=[plain] * 3 + [pl.BlockSpec((8, features), lambda i, s: (0, 0))],
        ),
        out_shape=[
            shape((tokens, features), jnp.float32),
            shape((tokens, features)),
            shape((tokens, features)),
            shape((8, features), jnp.float32),
        ],
        compiler_params=params(),
        cost_estimate=cost(0, 24 * tokens * features),
    )(index, *parts, hidden, stats, branch, vectors)


def norm_one_back_kernel(index_ref, *refs):
    rows_ref, came_ref, own_ref, sib_ref, stats_ref, out_own, out_sib, keep_ref, hidden_ref = refs[:9]
    vectors_ref, own_grad, sib_grad, sums_ref, grads_ref = refs[9:]
    f32 = jnp.float32
    width = own_ref.shape[1]
    block = width // 4
    for half in range(2):
        for i in range(4):
            at = block_at(half, width, index_ref[1] ^ i)
            span = slice(half * width + i * block, half * width + (i + 1) * block)
            grads_ref[:, span] = rows_ref[:, at] + came_ref[:, at].astype(f32)
    grads = grads_ref[...]
    inverse = stats_ref[:, 1:2]
    tokens = jnp.concatenate([own_ref[...], sib_ref[...]], axis=1).astype(f32)
    normal = (tokens - stats_ref[:, :1]) * inverse
    total = hidden_ref[...] + norm_pull(grads, normal, inverse, vectors_ref[0:1, :])
    dropped = 1.0 - keep_ref[...]
    own_grad[...] = out_own[...].astype(f32) * dropped + total[:, :width]
    sib_grad[...] = out_sib[...].astype(f32) * dropped + total[:, width:]
    add_sums(sums_ref, (grads * normal, grads))


def norm_one_back(index, rows, came, own, sib, stats, out_own, out_sib, keep, hidden, vectors):
    tokens, features = came.shape
    size, width = tokens // 2, features // 2
    plain = pl.BlockSpec((size, features), lambda i, s: (i, 0))
    half_wide = pl.BlockSpec((size, width), lambda i, s: (i, 0))
    return pl.pallas_call(
        norm_one_back_kernel,
        grid_spec=pltpu.PrefetchScalarGridSpec(
            num_scalar_prefetch=1,
            grid=(2,),
            in_specs=[
                my_rows(size, features, 2),
                plain,
                my_rows(size, width, 2),
                my_rows(size, width, 2),
                my_rows(size, 128, 2),
                my_rows(size, width, 2),
                half_wide,
                pl.BlockSpec((size, 1), lambda i, s: (i, 0)),
                plain,
                pl.BlockSpec(vectors.shape, lambda i, s: (0, 0)),
            ],
            out_specs=[half_wide, half_wide, pl.BlockSpec((8, features), lambda i, s: (0, 0))],
            scratch_shapes=[pltpu.VMEM((size, features), jnp.float32)],
        ),
        out_shape=[shape((tokens, width), jnp.float32)] * 2 + [shape((8, features), jnp.float32)],
        compiler_params=params(),
        cost_estimate=cost(0, 24 * tokens * features),
    )(index, rows, came, own, sib, stats, out_own, out_sib, keep, hidden, vectors)


def select_piece(refs, step, use):
    for j in range(3):

        @pl.when(step == j)
        def _():
            use(refs[j][...])

    @pl.when(step == 3)
    def _():
        use(jnp.concatenate([refs[3][...], refs[4][...]], axis=0))


def place_heads_kernel(index_ref, *refs):
    pieces, outs = refs[:5], refs[5:]
    own = pieces[0].shape[1] // 8

    def use(piece):
        for which in range(2):
            at = pl.multiple_of((index_ref[0] ^ which) * own, own)
            for m in range(4):
                part = piece[:, (4 * which + m) * own : (4 * which + m + 1) * own].astype(jnp.float32)
                if m < 3:
                    outs[m][:, pl.ds(at, own)] = part
                else:
                    outs[m][pl.ds(at, own), :] = part.T

    select_piece(pieces, pl.program_id(0), use)


def place_heads(index, pieces):
    block, columns = pieces[0].shape
    units, width = columns // 4, 4 * block
    whole = [pl.BlockSpec(p.shape, lambda j, s: (0, 0)) for p in pieces]
    return pl.pallas_call(
        place_heads_kernel,
        grid_spec=pltpu.PrefetchScalarGridSpec(
            num_scalar_prefetch=1,
            grid=(4,),
            in_specs=whole,
            out_specs=[pl.BlockSpec((block, units), lambda j, s: (s[1] ^ j, 0))] * 3
            + [pl.BlockSpec((units, block), lambda j, s: (0, s[1] ^ j))],
        ),
        out_shape=[shape((width, units), jnp.float32)] * 3 + [shape((units, width), jnp.float32)],
        compiler_params=params(),
        cost_estimate=cost(0, 24 * width * units),
    )(index, *pieces)


def place_ff_kernel(*refs):
    pieces, (up_out, down_out) = refs[:-2], refs[-2:]
    rows = pieces[0].shape[1]
    quarter = pieces[0].shape[2] // 2
    for part, piece in enumerate(pieces):
        span = slice(part * rows, (part + 1) * rows)
        up_out[span, :] = piece[0, :, :quarter].astype(jnp.float32)
        down_out[:, span] = piece[0, :, quarter:].astype(jnp.float32).T


def place_ff(pieces):
    count, rows, columns = pieces[0].shape
    width, quarter = rows * len(pieces), columns // 2
    return pl.pallas_call(
        place_ff_kernel,
        grid=(count,),
        in_specs=[pl.BlockSpec((1, rows, columns), lambda j: (j, 0, 0))] * len(pieces),
        out_specs=[
            pl.BlockSpec((width, quarter), lambda j: (0, j)),
            pl.BlockSpec((quarter, width), lambda j: (j, 0)),
        ],
        out_shape=[
            shape((width, count * quarter), jnp.float32),
            shape((count * quarter, width), jnp.float32),
        ],
        compiler_params=params(),
        cost_estimate=cost(0, 48 * width * quarter),
    )(*pieces)


def join_kernel(index_ref, mine_ref, first_ref, second_ref, out_ref):
    step = pl.program_id(0)

    @pl.when(step < 2)
    def _():
        out_ref[...] = mine_ref[...]

    @pl.when(step == 2)
    def _():
        out_ref[...] = first_ref[...]

    @pl.when(step == 3)
    def _():
        out_ref[...] = second_ref[...]


def join_tokens(index, mine, first, second):
    tokens, width = mine.shape
    size = tokens // 2
    once = pl.BlockSpec((size, width), lambda i, s: (0, 0))
    return pl.pallas_call(
        join_kernel,
        grid_spec=pltpu.PrefetchScalarGridSpec(
            num_scalar_prefetch=1,
            grid=(4,),
            in_specs=[pl.BlockSpec((size, width), lambda i, s: (jnp.minimum(i, 1), 0)), once, once],
            out_specs=pl.BlockSpec(
                (size, width), lambda i, s: (jnp.where(i < 2, s[0] * 2 + i, (1 - s[0]) * 2 + i - 2), 0)
            ),
        ),
        out_shape=shape((2 * tokens, width), mine.dtype),
        compiler_params=params(),
        cost_estimate=cost(0, 8 * tokens * width),
    )(index, mine, first, second)


def layer_out_kernel(*refs):
    here, x_top, y_top, x_bottom, y_bottom, hidden_ref, own_ref, sib_ref, keep_ref, vectors_ref = refs[1:11]
    own_out, sib_out = refs[11:]
    f32 = jnp.float32
    width = own_ref.shape[1]
    top = pl.program_id(0) == 0
    from_x = jnp.where(top, x_top[...].astype(f32), x_bottom[...].astype(f32))
    from_y = jnp.where(top, y_top[...].astype(f32), y_bottom[...].astype(f32))
    total = hidden_ref[...] + here[...].astype(f32) + from_x + from_y + vectors_ref[5:6, :]
    keep = keep_ref[...] > 0.5
    own_out[...] = jnp.where(keep, total[:, :width], own_ref[...].astype(f32))
    sib_out[...] = jnp.where(keep, total[:, width:], sib_ref[...].astype(f32))


def layer_rows(index, parts, hidden, own, sib, keep, vectors):
    tokens, features = hidden.shape
    size, width = tokens // 2, features // 2
    plain = pl.BlockSpec((size, features), lambda i, s: (i, 0))
    half_wide = pl.BlockSpec((size, width), lambda i, s: (i, 0))
    return pl.pallas_call(
        layer_out_kernel,
        grid_spec=pltpu.PrefetchScalarGridSpec(
            num_scalar_prefetch=1,
            grid=(2,),
            in_specs=[plain]
            + [pl.BlockSpec((size, features), lambda i, s: (0, 0))] * 4
            + [
                plain,
                my_rows(size, width, 2),
                my_rows(size, width, 2),
                pl.BlockSpec((size, 1), lambda i, s: (i, 0)),
                pl.BlockSpec(vectors.shape, lambda i, s: (0, 0)),
            ],
            out_specs=[half_wide, half_wide],
        ),
        out_shape=[shape((tokens, width), jnp.float32)] * 2,
        compiler_params=params(),
        cost_estimate=cost(0, 20 * tokens * features),
    )(index, *parts, hidden, own, sib, keep, vectors)


def body_local(
    tokens_in,
    out_grad,
    segment_ids,
    active_lengths,
    norm1_gain,
    norm1_shift,
    query_weight,
    query_bias,
    key_weight,
    value_weight,
    value_bias,
    out_weight,
    out_bias,
    norm2_gain,
    norm2_shift,
    up_weight,
    up_bias,
    down_weight,
    down_bias,
):
    f32, bf16 = jnp.float32, jnp.bfloat16
    rows, width = tokens_in.shape
    ring = lax.axis_size("col")
    row_i = lax.axis_index("row")
    plane_i = lax.axis_index("dp")
    col_i = lax.axis_index("col")
    own = query_weight.shape[1] // 2
    block = width // 4
    quarter = up_weight.shape[1] // 4
    unit = quarter // 2
    half = rows // 2
    order = Order()
    plane, column = Plane(order), Link(order)
    index = jnp.stack([row_i, plane_i, col_i]).astype(jnp.int32)

    def cut(values, start, size):
        return lax.dynamic_slice_in_dim(values, start, size, axis=0)

    def mirrored(values):
        return jnp.concatenate([values[:, width:], values[:, :width]], axis=1)

    def my_tokens(values):
        return cut(values, row_i * half, half)

    def other_tokens(values):
        return cut(values, (1 - row_i) * half, half)

    tokens_sib = order.swap(tokens_in)
    out_grad_sib = swap(other_tokens(out_grad))

    mine = jnp.concatenate(
        [
            cut(query_bias, row_i * own, own),
            jnp.zeros((own,), f32),
            cut(value_bias, row_i * own, own),
            cut(up_bias, plane_i * quarter, quarter),
        ]
    )
    small = [mine] + [
        lax.ppermute(mine, "col", [(i, (i + k) % ring) for i in range(ring)]) for k in range(1, ring)
    ]

    sources = (query_weight, key_weight, value_weight, out_weight)
    piece = order.run(pack_heads, after(index, mine), sources, 1)
    pieces = [jnp.concatenate([piece[0], swap(piece[1])], axis=0)]
    column.last = small[1:]
    pieces.append(column.send(step_up, pieces[0]))

    active_all = active_rows(segment_ids, active_lengths)
    active_here = my_tokens(cut(active_all, col_i * rows, rows))
    keep_mask = active_here.astype(f32)[:, None]
    out_grads = jnp.concatenate([my_tokens(out_grad), out_grad_sib], axis=1).astype(f32)
    branch_mine = (after(out_grads, *order.tokens) * keep_mask).astype(bf16)
    branch_first = plane.both(branch_mine[: half // 2], branch_mine[: half // 2])
    ff_piece = order.run(pack_ff, index, up_weight, down_weight)
    ff_pieces = lax.all_gather(ff_piece, ("row", "col"))
    vectors = jnp.stack([norm1_gain, norm1_shift, norm2_gain, norm2_shift, out_bias, down_bias])
    vectors_sib = swap(vectors)
    vectors_all = jnp.concatenate([vectors, vectors_sib], axis=1)
    pieces.append(column.send(step_up, pieces[1]))
    near = plane.both(pieces[1], pieces[1])
    here = order.run(pack_heads, index, sources, 4)
    own_parts, other_rows = [here[0]], [order.swap(here[1])]
    normed_one, stats_one = order.run(
        norm_rows,
        index,
        tokens_in,
        tokens_sib,
        jnp.concatenate([vectors[:2], vectors_sib[:2]], axis=0),
    )

    segment_row = picked(segment_ids, col_i)
    member = (segment_row[:, None] == jnp.arange(active_lengths.shape[1])).astype(jnp.int32)
    counts = jnp.sum(member, axis=0)
    first_row = jnp.sum(member * (jnp.cumsum(counts) - counts), axis=1)[None, :]

    heads, attended = [], []

    def attend_project(k):
        heads.append(
            order.run(project, normed_one, own_parts[k], other_rows[k], small[k][None, : 3 * own])
        )

    def attend(k):
        attended.append(order.run(local_forward, heads[k], first_row))

    def stack(k, near, far):
        own_part, other_part = order.run(stack_pieces, [pieces[k], *near, *far])
        own_parts.append(own_part)
        other_rows.append(other_part)

    attend_project(0)
    attend(0)
    far = plane.far(*near)
    pieces.append(column.send(step_up, pieces[2]))
    last_near, last_far = near, far
    near = plane.both(pieces[2], pieces[2])
    stack(1, last_near, last_far)
    attend_project(1)
    attend(1)
    far = plane.far(*near)
    last_near, last_far = near, far
    near = plane.both(pieces[3], pieces[3])
    stack(2, last_near, last_far)
    attend_project(2)
    attend(2)
    far = plane.far(*near)
    last_near, last_far = near, far
    branch_far = plane.far(*branch_first)
    stack(3, last_near, last_far)
    before = order.run(sum_rows, attended[:3], own_parts[:3], other_rows[:3], 3)
    second_near = plane.both(branch_mine[half // 2 :], branch_mine[half // 2 :])
    attend_project(3)
    attend(3)
    second_far = plane.far(*second_near)
    attention_rows = order.run(sum_rows, attended[3:], own_parts[3:], other_rows[3:], 3, (before,))
    arrived = swap(order.tie(mirrored(other_tokens(attention_rows)).astype(bf16)))

    order.tokens.append(ff_pieces)
    hidden_one, normed_two, stats_two = order.run(
        norm_two, index, attention_rows, arrived, tokens_in, tokens_sib, vectors_all
    )

    normed = [normed_two, *plane.both(normed_two, normed_two)]
    branch_all = jnp.concatenate(
        [branch_mine]
        + [part for pair in zip(branch_first, second_near) for part in pair]
        + [*branch_far, *second_far],
        axis=0,
    )
    def by_column(relative):
        places = jnp.mod(col_i - jnp.arange(ring), ring)
        return jnp.take(relative, places, axis=0)

    ff_biases = by_column(jnp.stack([s[None, 3 * own :] for s in small]))
    ff_rows, up_sums, grad_parts, down_parts = [], [], [], []

    def feed_forward(j):
        grads, part = (branch_all, j) if j > 0 else (branch_mine, 0)
        results = order.run(ffn_rows_of, index, normed[j], grads, part, ff_pieces, ff_biases)
        for kept, result in zip((ff_rows, up_sums, grad_parts, down_parts), results):
            kept.append(result)

    def top(values):
        return values[: half // 2]

    def bottom(values):
        return values[half // 2 :]

    def second_steps(parts, via_x, via_y):
        via_x, via_y = after((via_x, via_y), *order.tokens)
        return plane.both(add_rounded(bottom(parts[1]), via_y), add_rounded(top(parts[2]), via_x))

    def weight_grads(part):
        return order.run(weight_products, normed, branch_all, ff_rows, part)

    feed_forward(0)
    normed_far = plane.far(normed[1], normed[2])
    feed_forward(1)
    x_top = plane.x.send(step_x, top(grad_parts[1]))
    feed_forward(2)
    y_bottom = plane.y.send(step_y, bottom(grad_parts[2]))
    normed.append(jnp.concatenate(normed_far, axis=0))
    feed_forward(3)
    via_x, via_y = plane.both(top(grad_parts[3]), bottom(grad_parts[3]))
    ff_mine = weight_grads(0)
    x_bottom, y_top = second_steps(grad_parts, via_x, via_y)
    ff_other = order.swap(weight_grads(1))

    hidden_grad, grad_mine, grad_mirror, sums_two = order.run(
        norm_two_back,
        index,
        (grad_parts[0], x_top, y_top, x_bottom, y_bottom),
        hidden_one,
        stats_two,
        branch_mine,
        vectors_all,
    )
    down_x_top, down_y_bottom = plane.both(top(down_parts[1]), bottom(down_parts[2]))
    grad_others = [order.swap(top(grad_mirror)), order.swap(bottom(grad_mirror))]
    grad_rows = order.run(join_tokens, index, grad_mine, *grad_others)

    ff_grads = []
    for part in range(2):
        span = slice(part * width // 2, (part + 1) * width // 2)
        total = order.tie(add_rounded(ff_mine[:, span], ff_other[:, span]))
        total = lax.psum_scatter(total, "col", scatter_dimension=0, tiled=False)
        ff_grads.append(lax.all_gather(total, "dp"))

    down_via_x, down_via_y = plane.both(top(down_parts[3]), bottom(down_parts[3]), True)
    head_grad = order.run(head_grads, grad_rows, own_parts, other_rows)
    head_rows, bias_rows, group_parts = [None] * ring, [None] * ring, [None] * ring

    def backward(k):
        head_rows[k] = order.run(
            lambda h, g, f: local_backward(h, g, k, f), heads[k], head_grad, first_row
        )

    def head_weights(k):
        *group_parts[k], bias_rows[k] = order.run(
            head_products, normed_one, grad_rows, head_rows[k], attended[k]
        )

    def part_of(k, j, which):
        return group_parts[k][which][j * block : (j + 1) * block]

    def first_messages(k):
        return plane.both(part_of(k, 3, 0), part_of(k, 3, 1), True)

    def second_messages(k, via):
        via_x, via_y = after(via, *order.tokens)
        return plane.both(
            jnp.concatenate([part_of(k, 1, 0), add_rounded(part_of(k, 1, 1), via_y)], axis=1),
            jnp.concatenate([add_rounded(part_of(k, 2, 0), via_x), part_of(k, 2, 1)], axis=1),
        )

    def group_total(k, came, total):
        came_x, came_y = after(came, *order.tokens)
        here = jnp.concatenate([part_of(k, 0, 0), part_of(k, 0, 1)], axis=1)
        here = here.astype(f32) + came_x.astype(f32) + came_y.astype(f32)
        if total is not None:
            here = here + total.astype(f32)
        return here.astype(bf16)

    def layer_out_rows():
        own_out, sib_out = order.run(
            layer_rows,
            index,
            (down_parts[0], down_x_top, down_y_top, down_x_bottom, down_y_bottom),
            hidden_one,
            tokens_in,
            tokens_sib,
            keep_mask,
            vectors_all,
        )
        return own_out, order.swap(top(sib_out)), order.swap(bottom(sib_out))

    vias, came = [None] * ring, [None] * ring
    backward(3)
    head_weights(3)
    down_x_bottom, down_y_top = second_steps(down_parts, down_via_x, down_via_y)
    vias[3] = first_messages(3)
    backward(2)
    head_weights(2)
    vias[2] = first_messages(2)
    came[3] = second_messages(3, vias[3])
    backward(1)
    head_weights(1)
    vias[1] = first_messages(1)
    came[2] = second_messages(2, vias[2])
    backward(0)
    head_weights(0)
    total = column.send(step_down, group_total(3, came[3], None))
    vias[0] = first_messages(0)
    came[1] = second_messages(1, vias[1])
    total = column.send(step_down, add_rounded(total, group_total(2, came[2], None)))
    back_rows = order.run(sum_rows, head_rows, own_parts, other_rows, 0)
    arrived = order.swap(mirrored(other_tokens(back_rows)).astype(bf16))
    came[0] = second_messages(0, vias[0])
    total = column.send(step_down, add_rounded(total, group_total(1, came[1], None)))
    layer_parts = layer_out_rows()

    input_mine, input_other, sums_one = order.run(
        norm_one_back,
        index,
        back_rows,
        arrived,
        tokens_in,
        tokens_sib,
        stats_one,
        out_grad,
        out_grad_sib,
        keep_mask,
        hidden_grad,
        vectors_all,
    )
    input_others = [order.swap(top(input_other)), order.swap(bottom(input_other))]
    layer_out = order.run(join_tokens, index, *layer_parts)

    row_hot = (jnp.arange(2) == row_i).astype(f32)
    plane_hot = (jnp.arange(4) == plane_i).astype(f32)
    head_bias = by_column(jnp.stack(bias_rows)).reshape(ring, 3, 1, own) * row_hot[:, None]
    up_bias_part = sum(up_sums) * plane_hot[:, None]
    bias_vector = jnp.concatenate([head_bias.reshape(ring, -1), up_bias_part.reshape(ring, -1)], axis=1)
    feature_sums = jnp.concatenate([sums_one[:2], sums_two[:4]], axis=0)
    summed = jnp.concatenate([bias_vector.reshape(-1), feature_sums[:, :width].reshape(-1)])
    summed = summed + swap(
        jnp.concatenate([bias_vector.reshape(-1), feature_sums[:, width:].reshape(-1)])
    )

    summed = order.tie(summed)
    summed = summed + plane.x.send(step_x, summed)
    summed = summed + plane.y.send(step_y, summed)
    total = group_total(0, came[0], total)
    total = jnp.concatenate([total[:, : 4 * own], swap(total[:, 4 * own :])], axis=1)
    near = plane.both(total, total)
    step = 1
    while step < ring:
        pairs = [(i, i ^ step) for i in range(ring)]
        summed = summed + column.send(lambda v: lax.ppermute(v, "col", pairs), summed)
        step *= 2
    input_grad = order.run(join_tokens, index, input_mine, *input_others)
    up_weight_grad, down_weight_grad = order.run(place_ff, ff_grads)
    far = plane.far(*near)
    query_weight_grad, key_weight_grad, value_weight_grad, out_weight_grad = place_heads(
        index, [total, *near, *far]
    )

    bias_here = picked(summed[: bias_vector.size].reshape(ring, -1), col_i)
    own_here = summed[bias_vector.size :].reshape(6, width)
    size = 2 * own
    return (
        layer_out,
        input_grad,
        own_here[0],
        own_here[1],
        query_weight_grad,
        bias_here[:size],
        key_weight_grad,
        value_weight_grad,
        bias_here[2 * size : 3 * size],
        out_weight_grad,
        own_here[4],
        own_here[2],
        own_here[3],
        up_weight_grad,
        bias_here[3 * size :],
        down_weight_grad,
        own_here[5],
    )


def body(tokens_in, out_grad, segment_ids, *rest):
    ring = lax.axis_size("col")
    local = (
        lax.axis_size("dp") == 4
        and lax.axis_size("row") == 2
        and ring == 4
        and tokens_in.shape[0] == segment_ids.shape[1]
    )
    chosen = body_local if local else body_general
    return chosen(tokens_in, out_grad, segment_ids, *rest)


def solution(mesh):
    placed = (
        P(("dp", "col"), "row"),
        P(("dp", "col"), "row"),
        P("dp", None),
        P("dp", None),
        P("row"),
        P("row"),
        P("row", "col"),
        P("col"),
        P("row", "col"),
        P("row", "col"),
        P("col"),
        P("col", "row"),
        P("row"),
        P("row"),
        P("row"),
        P("row", "col"),
        P("col"),
        P("col", "row"),
        P("row"),
    )
    return jax.shard_map(
        body,
        mesh=mesh,
        in_specs=placed,
        out_specs=(
            P(("dp", "col"), "row"),
            P(("dp", "col"), "row"),
            P("row"),
            P("row"),
            P("row", "col"),
            P("col"),
            P("row", "col"),
            P("row", "col"),
            P("col"),
            P("col", "row"),
            P("row"),
            P("row"),
            P("row"),
            P("row", "col"),
            P("col"),
            P("col", "row"),
            P("row"),
        ),
        check_vma=False,
    )
```

```python
import functools

import jax
import jax.numpy as jnp
from jax import lax
from jax.experimental import pallas as pl
from jax.experimental.pallas import tpu as pltpu
from jax.sharding import PartitionSpec as P

D = 2048
HEAD_DIM = 64


norm_eps = 1e-05
masked_fill = -1e30


def width_totals(total_one, total_two):
    return lax.psum((total_one, total_two), "row")


def token_gather(values):
    return lax.all_gather(values, "col", axis=0, tiled=True)


def token_sums(partial_rows):
    return lax.psum_scatter(partial_rows, "col", scatter_dimension=0, tiled=True)


def unit_gather(values):
    return lax.all_gather(values, "row", axis=1, tiled=True)


def unit_sums(partial_units):
    return lax.psum_scatter(partial_units, "row", scatter_dimension=1, tiled=True)


def gelu_value(values):
    return jax.nn.gelu(values, approximate=True)


def gelu_slope(values):
    result, pullback = jax.vjp(gelu_value, values)
    return pullback(jnp.ones_like(values))[0]


def active_rows(segment_rows, keep_lengths):
    doc_index = jnp.arange(keep_lengths.shape[-1], dtype=jnp.int32)
    member = (segment_rows[:, :, None] == doc_index).astype(jnp.int32)
    counts = jnp.sum(member, axis=1)
    starts = jnp.cumsum(counts, axis=1) - counts
    first_pos = jnp.sum(member * starts[:, None, :], axis=2)
    keep_here = jnp.sum(member * keep_lengths[:, None, :], axis=2)
    position_in = jnp.arange(segment_rows.shape[1], dtype=jnp.int32)[None, :] - first_pos
    return (position_in < keep_here).reshape(-1)


def norm_forward(values, gain_part, shift_part):
    total_one, total_two = width_totals(jnp.sum(values, axis=1), jnp.sum(values * values, axis=1))
    average = total_one / D
    variance = total_two / D - average * average
    inverse = lax.rsqrt(variance + norm_eps)
    normal = (values - average[:, None]) * inverse[:, None]
    return ((normal * gain_part + shift_part).astype(jnp.bfloat16), normal, inverse)


def norm_backward(grad_rows, normal, inverse, gain_part):
    scaled = grad_rows * gain_part
    total_one, total_two = width_totals(jnp.sum(scaled, axis=1), jnp.sum(scaled * normal, axis=1))
    grad_in = inverse[:, None] * (
        scaled - total_one[:, None] / D - normal * (total_two[:, None] / D)
    )
    return (grad_in, jnp.sum(grad_rows * normal, axis=0), jnp.sum(grad_rows, axis=0))


def allowed_mask(segment_row, offset, block_rows):
    key_pos = jnp.arange(segment_row.shape[0], dtype=jnp.int32)
    query_pos = key_pos[offset : offset + block_rows]
    same_doc = segment_row[None, :] == segment_row[offset : offset + block_rows, None]
    return (key_pos[None, :] <= query_pos[:, None]) & same_doc


def attend_forward(query_seq, key_seq, value_seq, segment_row, score_scale):
    seq_length = query_seq.shape[2]
    block_rows = min(512, seq_length)
    outputs = []
    log_parts = []
    for offset in range(0, seq_length, block_rows):
        query_block = query_seq[:, :, offset : offset + block_rows]
        scores = (
            jnp.einsum("hdq,hdk->hqk", query_block, key_seq, preferred_element_type=jnp.float32)
            * score_scale
        )
        scores = jnp.where(allowed_mask(segment_row, offset, block_rows)[None], scores, masked_fill)
        row_max = jnp.max(scores, axis=2, keepdims=True)
        exp_scores = jnp.exp(scores - row_max)
        row_total = jnp.sum(exp_scores, axis=2, keepdims=True)
        weights = (exp_scores / row_total).astype(jnp.bfloat16)
        outputs.append(
            jnp.einsum("hqk,hdk->hdq", weights, value_seq, preferred_element_type=jnp.float32)
        )
        log_parts.append((row_max + jnp.log(row_total))[:, :, 0])
    return (jnp.concatenate(outputs, axis=2), jnp.concatenate(log_parts, axis=1))


def attend_backward(query_seq, key_seq, value_seq, grad_seq, segment_row, log_sums, score_scale):
    seq_length = query_seq.shape[2]
    block_rows = min(512, seq_length)
    key_grad = jnp.zeros(key_seq.shape, jnp.float32)
    value_grad = jnp.zeros(value_seq.shape, jnp.float32)
    query_grads = []
    for offset in range(0, seq_length, block_rows):
        query_block = query_seq[:, :, offset : offset + block_rows]
        grad_block = grad_seq[:, :, offset : offset + block_rows]
        scores = (
            jnp.einsum("hdq,hdk->hqk", query_block, key_seq, preferred_element_type=jnp.float32)
            * score_scale
        )
        scores = jnp.where(allowed_mask(segment_row, offset, block_rows)[None], scores, masked_fill)
        probs = jnp.exp(scores - log_sums[:, offset : offset + block_rows, None])
        prob_grad = jnp.einsum(
            "hdq,hdk->hqk", grad_block, value_seq, preferred_element_type=jnp.float32
        )
        row_dot = jnp.sum(probs * prob_grad, axis=2, keepdims=True)
        score_grad = (probs * (prob_grad - row_dot)).astype(jnp.bfloat16)
        query_grads.append(
            jnp.einsum("hqk,hdk->hdq", score_grad, key_seq, preferred_element_type=jnp.float32)
            * score_scale
        )
        key_grad = (
            key_grad
            + jnp.einsum(
                "hqk,hdq->hdk", score_grad, query_block, preferred_element_type=jnp.float32
            )
            * score_scale
        )
        value_grad = value_grad + jnp.einsum(
            "hqk,hdq->hdk",
            probs.astype(jnp.bfloat16),
            grad_block,
            preferred_element_type=jnp.float32,
        )
    return (jnp.concatenate(query_grads, axis=2), key_grad, value_grad)


def body_general(
    tokens_in,
    out_grad,
    segment_ids,
    active_lengths,
    norm1_gain,
    norm1_shift,
    query_weight,
    query_bias,
    key_weight,
    value_weight,
    value_bias,
    out_weight,
    out_bias,
    norm2_gain,
    norm2_shift,
    up_weight,
    up_bias,
    down_weight,
    down_bias,
):
    local_rows = tokens_in.shape[0]
    seq_here = segment_ids.shape[0]
    seq_length = segment_ids.shape[1]
    group_rows = seq_here * seq_length
    row_index = lax.axis_index("row")
    col_index = lax.axis_index("col")
    active_all = active_rows(segment_ids, active_lengths)
    active_here = lax.dynamic_slice_in_dim(active_all, col_index * local_rows, local_rows)
    keep_mask = active_here.astype(jnp.float32)[:, None]
    score_scale = HEAD_DIM ** (-0.5)
    rows_in = tokens_in.astype(jnp.float32)
    normed_one, normal_one, inverse_one = norm_forward(rows_in, norm1_gain, norm1_shift)
    gathered_one = token_gather(normed_one)
    stacked_weight = jnp.stack([query_weight, key_weight, value_weight])
    projected = unit_sums(
        jnp.einsum("td,kdh->kht", gathered_one, stacked_weight, preferred_element_type=jnp.float32)
    )
    head_width = projected.shape[1]
    head_count = head_width // HEAD_DIM
    query_part = lax.dynamic_slice_in_dim(query_bias, row_index * head_width, head_width)
    value_part = lax.dynamic_slice_in_dim(value_bias, row_index * head_width, head_width)
    bias_stack = jnp.stack([query_part, jnp.zeros_like(query_part), value_part])
    heads_all = (projected + bias_stack[:, :, None]).astype(jnp.bfloat16)

    def to_seqs(values):
        return jnp.moveaxis(values.reshape(head_count, HEAD_DIM, seq_here, seq_length), 2, 0)

    def from_seqs(values):
        return jnp.moveaxis(values, 0, 2).reshape(head_width, group_rows)

    query_seqs = to_seqs(heads_all[0])
    key_seqs = to_seqs(heads_all[1])
    value_seqs = to_seqs(heads_all[2])
    attended_seqs, log_sums = lax.map(
        lambda seq_items: attend_forward(
            seq_items[0], seq_items[1], seq_items[2], seq_items[3], score_scale
        ),
        (query_seqs, key_seqs, value_seqs, segment_ids),
    )
    attended = from_seqs(attended_seqs).astype(jnp.bfloat16)
    gathered_heads = unit_gather(attended[None])
    attention_rows = (
        token_sums(
            jnp.einsum("kht,hd->td", gathered_heads, out_weight, preferred_element_type=jnp.float32)
        )
        + out_bias
    )
    hidden_one = rows_in + attention_rows
    normed_two, normal_two, inverse_two = norm_forward(hidden_one, norm2_gain, norm2_shift)
    gathered_two = token_gather(normed_two)
    up_part = jnp.einsum("td,df->ft", gathered_two, up_weight, preferred_element_type=jnp.float32)[
        None
    ]
    unit_width = up_part.shape[1] // lax.axis_size("row")
    up_slice = lax.dynamic_slice_in_dim(up_bias, row_index * unit_width, unit_width)
    pre_act = unit_sums(up_part)[0] + up_slice[:, None]
    gathered_act = unit_gather(gelu_value(pre_act).astype(jnp.bfloat16)[None])
    ffn_rows = (
        token_sums(
            jnp.einsum("kft,fd->td", gathered_act, down_weight, preferred_element_type=jnp.float32)
        )
        + down_bias
    )
    layer_out = jnp.where(active_here[:, None], hidden_one + ffn_rows, rows_in)
    grad_rows = out_grad.astype(jnp.float32) * keep_mask
    branch_grad = token_gather(grad_rows.astype(jnp.bfloat16))
    down_grad = jnp.einsum(
        "kft,td->fd", gathered_act, branch_grad, preferred_element_type=jnp.float32
    )
    down_bias_grad = jnp.sum(branch_grad, axis=0, dtype=jnp.float32)
    act_part = jnp.einsum(
        "td,fd->ft", branch_grad, down_weight, preferred_element_type=jnp.float32
    )[None]
    act_grad = unit_sums(act_part)[0]
    pre_grad = (act_grad * gelu_slope(pre_act)).astype(jnp.bfloat16)
    gathered_pre = unit_gather(pre_grad[None])
    up_grad = jnp.einsum(
        "td,kft->df", gathered_two, gathered_pre, preferred_element_type=jnp.float32
    )
    up_bias_grad = jnp.sum(gathered_pre[0], axis=1, dtype=jnp.float32)
    normed_grad_two = token_sums(
        jnp.einsum("kft,df->td", gathered_pre, up_weight, preferred_element_type=jnp.float32)
    )
    back_two, gain_two_grad, shift_two_grad = norm_backward(
        normed_grad_two, normal_two, inverse_two, norm2_gain
    )
    hidden_grad = grad_rows + back_two
    attention_grad = token_gather(hidden_grad.astype(jnp.bfloat16))
    out_weight_grad = jnp.einsum(
        "kht,td->hd", gathered_heads, attention_grad, preferred_element_type=jnp.float32
    )
    out_bias_grad = jnp.sum(attention_grad, axis=0, dtype=jnp.float32)
    head_grad = unit_sums(
        jnp.einsum("td,hd->ht", attention_grad, out_weight, preferred_element_type=jnp.float32)[
            None
        ]
    )[0].astype(jnp.bfloat16)
    query_grads, key_grads, value_grads = lax.map(
        lambda seq_items: attend_backward(
            seq_items[0],
            seq_items[1],
            seq_items[2],
            seq_items[3],
            seq_items[4],
            seq_items[5],
            score_scale,
        ),
        (query_seqs, key_seqs, value_seqs, to_seqs(head_grad), segment_ids, log_sums),
    )
    stacked_grad = jnp.stack(
        [from_seqs(query_grads), from_seqs(key_grads), from_seqs(value_grads)]
    ).astype(jnp.bfloat16)
    gathered_grad = unit_gather(stacked_grad)
    stacked_weight_grad = jnp.einsum(
        "td,kht->kdh", gathered_one, gathered_grad, preferred_element_type=jnp.float32
    )
    query_bias_grad = jnp.sum(gathered_grad[0], axis=1, dtype=jnp.float32)
    value_bias_grad = jnp.sum(gathered_grad[2], axis=1, dtype=jnp.float32)
    normed_grad_one = token_sums(
        jnp.einsum("kht,kdh->td", gathered_grad, stacked_weight, preferred_element_type=jnp.float32)
    )
    back_one, gain_one_grad, shift_one_grad = norm_backward(
        normed_grad_one, normal_one, inverse_one, norm1_gain
    )
    input_grad = out_grad.astype(jnp.float32) * (1.0 - keep_mask) + hidden_grad + back_one
    (
        stacked_weight_grad,
        query_bias_grad,
        value_bias_grad,
        out_weight_grad,
        out_bias_grad,
        down_grad,
        down_bias_grad,
        up_grad,
        up_bias_grad,
    ) = lax.psum(
        (
            stacked_weight_grad,
            query_bias_grad,
            value_bias_grad,
            out_weight_grad,
            out_bias_grad,
            down_grad,
            down_bias_grad,
            up_grad,
            up_bias_grad,
        ),
        "dp",
    )
    gain_one_grad, shift_one_grad, gain_two_grad, shift_two_grad = lax.psum(
        (gain_one_grad, shift_one_grad, gain_two_grad, shift_two_grad), ("dp", "col")
    )
    return (
        layer_out,
        input_grad,
        gain_one_grad,
        shift_one_grad,
        stacked_weight_grad[0],
        query_bias_grad,
        stacked_weight_grad[1],
        stacked_weight_grad[2],
        value_bias_grad,
        out_weight_grad,
        out_bias_grad,
        gain_two_grad,
        shift_two_grad,
        up_grad,
        up_bias_grad,
        down_grad,
        down_bias_grad,
    )


def after(values, *others):
    return lax.optimization_barrier((values, others))[0]


def swap(values):
    return lax.ppermute(values, "row", [(0, 1), (1, 0)])


def step_x(values):
    return lax.ppermute(values, "dp", [(0, 1), (1, 0), (2, 3), (3, 2)])


def step_y(values):
    return lax.ppermute(values, "dp", [(0, 2), (2, 0), (1, 3), (3, 1)])


def step_up(values):
    count = lax.axis_size("col")
    return lax.ppermute(values, "col", [(i, (i + 1) % count) for i in range(count)])


def step_down(values):
    count = lax.axis_size("col")
    return lax.ppermute(values, "col", [(i, (i - 1) % count) for i in range(count)])


class Order:
    def __init__(self):
        self.tokens = []
        self.fresh, self.due = [], []

    def tie(self, values):
        if self.tokens:
            values = after(values, *self.tokens)
        self.tokens.append(values)
        return values

    def swap(self, values, due=True):
        arrived = swap(self.tie(values))
        if due:
            self.fresh.append(arrived)
        return arrived

    def run(self, function, first, *others):
        first = after(first, *self.tokens, *self.due) if self.tokens or self.due else first
        self.due, self.fresh = self.fresh, []
        result = function(first, *others)
        self.tokens = [jax.tree.leaves(result)[0]]
        return result


class Link:
    def __init__(self, order):
        self.order = order
        self.last = None

    def send(self, step, values, free=False):
        if self.last is not None and not free:
            values = after(values, self.last)
        self.last = step(self.order.tie(values))
        return self.last


class Plane:
    def __init__(self, order):
        self.x = Link(order)
        self.y = Link(order)

    def both(self, for_x, for_y, free=False):
        return self.x.send(step_x, for_x, free), self.y.send(step_y, for_y, free)

    def far(self, from_x, from_y):
        half = from_x.shape[0] // 2
        far_two, far_one = self.both(from_y[half:], from_x[:half])
        return far_one, far_two


def add_rounded(left, right):
    return (left.astype(jnp.float32) + right.astype(jnp.float32)).astype(jnp.bfloat16)


def ring_gather(link, values):
    held = [values]
    for _ in range(lax.axis_size("col") - 1):
        held.append(link.send(step_up, held[-1]))
    return held


def picked(stacked, index):
    return lax.dynamic_index_in_dim(stacked, index, 0, keepdims=False)


def mm(left, right, left_dim, right_dim, dtype=jnp.float32):
    return lax.dot_general(
        left, right, (((left_dim,), (right_dim,)), ((), ())), preferred_element_type=jnp.float32
    ).astype(dtype)


PAIR = 2 * HEAD_DIM
vmem_bytes = 48 * 1024 * 1024


def head_lanes(head, value):
    lane = lax.broadcasted_iota(jnp.int32, (1, PAIR), 1)
    return jnp.where(lane // HEAD_DIM == head, value, 0.0).astype(jnp.bfloat16)


def allowed_keys(first_row, low, high):
    key_pos = lax.broadcasted_iota(jnp.int32, (high, high - low), 0)
    query_pos = lax.broadcasted_iota(jnp.int32, (high, high - low), 1) + low
    return (key_pos >= first_row) & (key_pos <= query_pos)


def local_forward_kernel(size, first_ref, query_ref, key_ref, value_ref, out_ref):
    lane = lax.broadcasted_iota(jnp.int32, (size, PAIR), 1)
    for low in range(0, key_ref.shape[0], size):
        high = low + size
        keys = key_ref[:high, :]
        values = value_ref[:high, :]
        queries = query_ref[low:high, :]
        allowed = allowed_keys(first_ref[:, low:high], low, high)
        results = []
        for head in range(2):
            scores = mm(keys, queries * head_lanes(head, HEAD_DIM ** (-0.5)), 1, 1)
            scores = jnp.where(allowed, scores, masked_fill)
            exp_scores = jnp.exp(scores - jnp.max(scores, axis=0, keepdims=True))
            inverse = 1.0 / jnp.sum(exp_scores, axis=0, keepdims=True)
            results.append(mm((exp_scores * inverse).astype(jnp.bfloat16), values, 0, 0))
        out_ref[low:high, :] = jnp.where(lane < HEAD_DIM, results[0], results[1]).astype(
            jnp.bfloat16
        )


def local_forward(heads, first_row):
    length = heads.shape[0]
    pairs = heads.shape[1] // (3 * PAIR)
    return pl.pallas_call(
        functools.partial(local_forward_kernel, min(256, length)),
        grid=(pairs,),
        in_specs=[
            pl.BlockSpec((1, length), lambda p: (0, 0)),
            pl.BlockSpec((length, PAIR), lambda p: (0, p)),
            pl.BlockSpec((length, PAIR), lambda p: (0, pairs + p)),
            pl.BlockSpec((length, PAIR), lambda p: (0, 2 * pairs + p)),
        ],
        out_specs=pl.BlockSpec((length, PAIR), lambda p: (0, p)),
        out_shape=jax.ShapeDtypeStruct((length, pairs * PAIR), jnp.bfloat16),
        compiler_params=pltpu.CompilerParams(vmem_limit_bytes=vmem_bytes),
        cost_estimate=cost(16 * length * length * pairs * PAIR, 8 * heads.size),
    )(first_row, heads, heads, heads)


def local_backward_kernel(
    size, first_ref, query_ref, grad_ref, key_ref, value_ref, out_ref, key_sum, value_sum
):
    length = key_ref.shape[0]
    pair = pl.program_id(0)
    pairs = out_ref.shape[1] // (3 * PAIR)
    scale = HEAD_DIM ** (-0.5)
    lane = lax.broadcasted_iota(jnp.int32, (size, PAIR), 1)

    def lanes(part):
        return pl.ds(pl.multiple_of((part * pairs + pair) * PAIR, PAIR), PAIR)

    for low in range(length - size, -1, -size):
        high = low + size
        keys = key_ref[:high, :]
        values = value_ref[:high, :]
        queries = query_ref[low:high, :]
        grads = grad_ref[low:high, :]
        allowed = allowed_keys(first_ref[:, low:high], low, high)
        query_grads = []
        for head in range(2):
            scaled = queries * head_lanes(head, scale)
            grad = grads * head_lanes(head, 1.0)
            scores = jnp.where(allowed, mm(keys, scaled, 1, 1), masked_fill)
            exp_scores = jnp.exp(scores - jnp.max(scores, axis=0, keepdims=True))
            probs = exp_scores * (1.0 / jnp.sum(exp_scores, axis=0, keepdims=True))
            prob_grad = mm(values, grad, 1, 1)
            row_dot = jnp.sum(probs * prob_grad, axis=0, keepdims=True)
            score_grad = (probs * (prob_grad - row_dot)).astype(jnp.bfloat16)
            value_part = mm(probs.astype(jnp.bfloat16), grad, 1, 0)
            key_part = mm(score_grad, scaled, 1, 0)
            query_grads.append(mm(score_grad, keys, 0, 0) * scale)
            if head == 0:
                key_add, value_add = key_part, value_part
            else:
                key_add, value_add = key_add + key_part, value_add + value_part
        if high == length:
            key_sum[...] = key_add
            value_sum[...] = value_add
        else:
            key_sum[:high, :] += key_add
            value_sum[:high, :] += value_add
        out_ref[low:high, lanes(0)] = jnp.where(
            lane < HEAD_DIM, query_grads[0], query_grads[1]
        ).astype(jnp.bfloat16)
    out_ref[:, lanes(1)] = key_sum[...].astype(jnp.bfloat16)
    out_ref[:, lanes(2)] = value_sum[...].astype(jnp.bfloat16)


def local_backward(heads, head_grad, group, first_row):
    length = heads.shape[0]
    pairs = heads.shape[1] // (3 * PAIR)
    return pl.pallas_call(
        functools.partial(local_backward_kernel, min(512, length)),
        grid=(pairs,),
        in_specs=[
            pl.BlockSpec((1, length), lambda p: (0, 0)),
            pl.BlockSpec((length, PAIR), lambda p: (0, p)),
            pl.BlockSpec((length, PAIR), lambda p: (0, group * pairs + p)),
            pl.BlockSpec((length, PAIR), lambda p: (0, pairs + p)),
            pl.BlockSpec((length, PAIR), lambda p: (0, 2 * pairs + p)),
        ],
        out_specs=pl.BlockSpec(heads.shape, lambda p: (0, 0)),
        out_shape=jax.ShapeDtypeStruct(heads.shape, jnp.bfloat16),
        scratch_shapes=[pltpu.VMEM((length, PAIR), jnp.float32)] * 2,
        compiler_params=pltpu.CompilerParams(vmem_limit_bytes=vmem_bytes),
        cost_estimate=cost(32 * length * length * pairs * PAIR, 8 * heads.size),
    )(first_row, heads, head_grad, heads, heads)


gelu_scale = 0.7978845608028654
gelu_cubic = 0.044715


def ffn_kernel(index_ref, *refs):
    normed, grads, pieces = refs[:2], refs[2:4], [r.at[0] for r in refs[4:6]]
    bias_ref, rows_ref, sum_ref, grad_out, down_out, grad_acc, down_acc = refs[6:]
    step = pl.program_id(0)
    width = normed[0].shape[1]
    quarter = pieces[0].shape[1] // 2
    ups, downs = slice(0, quarter), slice(quarter, 2 * quarter)
    pre = mm(normed[0][...], pieces[0][:, ups], 1, 0) + mm(normed[1][...], pieces[1][:, ups], 1, 0)
    pre = pre + bias_ref[0]
    act_grad = mm(grads[0][...], pieces[0][:, downs], 1, 0) + mm(grads[1][...], pieces[1][:, downs], 1, 0)
    square = pre * pre
    bent = jnp.tanh(gelu_scale * pre * (1.0 + gelu_cubic * square))
    half = 0.5 * (1.0 + bent)
    slope = half + 0.5 * gelu_scale * pre * (1.0 - bent * bent) * (1.0 + 3.0 * gelu_cubic * square)
    act = (pre * half).astype(jnp.bfloat16)
    pre_grad = (act_grad * slope).astype(jnp.bfloat16)
    rows_ref[:, :quarter] = act
    rows_ref[:, quarter:] = pre_grad
    sum_ref[0] = jnp.sum(pre_grad.astype(jnp.float32), axis=0, keepdims=True)

    @pl.when(step == 0)
    def _():
        for i in range(2):
            at = slice(i * width, (i + 1) * width)
            grad_acc[:, at] = mm(pre_grad, pieces[i][:, ups], 1, 1)
            down_acc[:, at] = mm(act, pieces[i][:, downs], 1, 1)

    @pl.when(step > 0)
    def _():
        for i in range(2):
            at = slice(i * width, (i + 1) * width)
            grad_acc[:, at] += mm(pre_grad, pieces[i][:, ups], 1, 1)
            down_acc[:, at] += mm(act, pieces[i][:, downs], 1, 1)

    @pl.when(step == pl.num_programs(0) - 1)
    def _():
        grad_out[...] = grad_acc[...].astype(jnp.bfloat16)
        down_out[...] = down_acc[...].astype(jnp.bfloat16)


def ffn_rows_of(index, normed, grads, part, pieces, bias):
    tokens, features = normed.shape
    width = features // 2
    columns = pieces.shape[2]
    ring, quarter = pieces.shape[0] // 2, columns // 2

    def halves(at):
        return [pl.BlockSpec((tokens, width), lambda k, s, h=h: (at, h)) for h in range(2)]

    piece = [
        pl.BlockSpec((1, width, columns), lambda k, s, h=h: ((s[0] ^ h) * ring + k, 0, 0))
        for h in range(2)
    ]
    whole = pl.BlockSpec((tokens, features), lambda k, s: (0, 0))
    vector = pl.BlockSpec((1, 1, quarter), lambda k, s: (k, 0, 0))
    return pl.pallas_call(
        ffn_kernel,
        grid_spec=pltpu.PrefetchScalarGridSpec(
            num_scalar_prefetch=1,
            grid=(ring,),
            in_specs=halves(0) + halves(part) + piece + [vector],
            out_specs=[pl.BlockSpec((tokens, columns), lambda k, s: (0, k)), vector, whole, whole],
            scratch_shapes=[pltpu.VMEM((tokens, features), jnp.float32)] * 2,
        ),
        out_shape=[
            shape((tokens, ring * columns)),
            shape((ring, 1, quarter), jnp.float32),
            shape((tokens, features)),
            shape((tokens, features)),
        ],
        compiler_params=params(),
        cost_estimate=cost(8 * tokens * features * ring * quarter, 12 * ring * width * columns),
    )(index, normed, normed, grads, grads, pieces, pieces, bias)


def weight_products_kernel(count, *refs):
    out_ref = refs[-1]
    normed, grads, rows = [refs[i * count : (i + 1) * count] for i in range(3)]
    quarter = rows[0].shape[1] // 2
    up = down = None
    for j in range(count):
        up_part = mm(normed[j][...], rows[j][:, quarter:], 0, 0)
        down_part = mm(grads[j][...], rows[j][:, :quarter], 0, 0)
        up = up_part if up is None else up + up_part
        down = down_part if down is None else down + down_part
    out_ref[0, :, :quarter] = up.astype(jnp.bfloat16)
    out_ref[0, :, quarter:] = down.astype(jnp.bfloat16)


def weight_products(normed, grads, rows, half):
    count = len(normed)
    tokens, features = normed[0].shape
    width = features // 2
    ring = 4
    columns = rows[0].shape[1] // ring
    size = min(512, width)
    blocks = width // size
    left = [pl.BlockSpec((tokens, size), lambda k, d: (0, half * blocks + d))] * count
    left += [
        pl.BlockSpec((tokens, size), lambda k, d, j=j: (j, half * blocks + d)) for j in range(count)
    ]
    return pl.pallas_call(
        functools.partial(weight_products_kernel, count),
        grid=(ring, blocks),
        in_specs=left + [pl.BlockSpec((tokens, columns), lambda k, d: (0, k))] * count,
        out_specs=pl.BlockSpec((1, size, columns), lambda k, d: (k, d, 0)),
        out_shape=shape((ring, width, columns)),
        compiler_params=params(),
        cost_estimate=cost(
            2 * count * tokens * width * ring * columns, 4 * count * tokens * features * ring
        ),
    )(*normed, *([grads] * count), *rows)


def params(**more):
    return pltpu.CompilerParams(vmem_limit_bytes=vmem_bytes, **more)


def cost(flops, nbytes):
    return pl.CostEstimate(flops=flops // 10, bytes_accessed=nbytes // 10, transcendentals=0)


def shape(dims, dtype=jnp.bfloat16):
    return jax.ShapeDtypeStruct(dims, dtype)


def turned(values):
    return values.astype(jnp.float32).T.astype(jnp.bfloat16)


def pack_heads_kernel(index_ref, *refs):
    sources, outs = refs[:8], refs[8:]
    own = sources[0].shape[1]
    for which in range(2):
        for i in range(4):
            part = sources[4 * which + i][...]
            outs[which][:, i * own : (i + 1) * own] = part if i < 3 else turned(part)


def pack_heads(index, weights, count):
    width, units = weights[0].shape
    own, block = units // 2, width // 4

    def feature(which):
        return pl.BlockSpec((block, own), lambda j, s: (s[1] ^ j, s[0] ^ which))

    def turned_block(which):
        return pl.BlockSpec((own, block), lambda j, s: (s[0] ^ which, s[1] ^ j))

    in_specs = []
    for which in range(2):
        in_specs += [feature(which)] * 3 + [turned_block(which)]
    return pl.pallas_call(
        pack_heads_kernel,
        grid_spec=pltpu.PrefetchScalarGridSpec(
            num_scalar_prefetch=1,
            grid=(count,),
            in_specs=in_specs,
            out_specs=[pl.BlockSpec((block, 4 * own), lambda j, s: (j, 0))] * 2,
        ),
        out_shape=[shape((count * block, 4 * own))] * 2,
        compiler_params=params(),
        cost_estimate=cost(0, 32 * count * block * own),
    )(index, *weights, *weights)


def pack_ff_kernel(index_ref, up_ref, down_ref, out_ref):
    quarter = up_ref.shape[1]
    out_ref[:, :quarter] = up_ref[...]
    out_ref[:, quarter:] = turned(down_ref[...])


def pack_ff(index, up_weight, down_weight):
    width, units = up_weight.shape
    quarter, block = units // 4, width // 4
    return pl.pallas_call(
        pack_ff_kernel,
        grid_spec=pltpu.PrefetchScalarGridSpec(
            num_scalar_prefetch=1,
            grid=(4,),
            in_specs=[
                pl.BlockSpec((block, quarter), lambda d, s: (d, s[1])),
                pl.BlockSpec((quarter, block), lambda d, s: (s[1], d)),
            ],
            out_specs=pl.BlockSpec((block, 2 * quarter), lambda d, s: (d, 0)),
        ),
        out_shape=shape((width, 2 * quarter)),
        compiler_params=params(),
        cost_estimate=cost(0, 8 * width * quarter),
    )(index, up_weight, down_weight)


def stack_kernel(*refs):
    pieces, outs = refs[:3], refs[-2:]
    block = pieces[0].shape[0] // 2
    for j, piece in enumerate(pieces):
        for i in range(2):
            outs[i][j * block : (j + 1) * block, :] = piece[i * block : (i + 1) * block, :]
    for i in range(2):
        outs[i][3 * block :, :] = refs[3 + i][...]


def stack_pieces(pieces):
    rows, columns = pieces[0].shape
    return pl.pallas_call(
        stack_kernel,
        out_shape=[shape((2 * rows, columns))] * 2,
        compiler_params=params(),
        cost_estimate=cost(0, 16 * rows * columns),
    )(*pieces)


def norm_kernel(index_ref, own_ref, sib_ref, vectors_ref, out_ref, stats_ref):
    own = own_ref[...].astype(jnp.float32)
    sib = sib_ref[...].astype(jnp.float32)
    width = own.shape[1]
    average = (jnp.sum(own, axis=1, keepdims=True) + jnp.sum(sib, axis=1, keepdims=True)) / (2 * width)
    own, sib = own - average, sib - average
    square = jnp.sum(own * own, axis=1, keepdims=True) + jnp.sum(sib * sib, axis=1, keepdims=True)
    inverse = lax.rsqrt(square / (2 * width) + norm_eps)
    block = width // 4
    for half, values in enumerate((own, sib)):
        gain, shift = vectors_ref[2 * half, :][None], vectors_ref[2 * half + 1, :][None]
        rounded = (values * inverse * gain + shift).astype(jnp.bfloat16)
        for i in range(4):
            at = pl.multiple_of(half * width + (index_ref[1] ^ i) * block, block)
            out_ref[:, pl.ds(at, block)] = rounded[:, i * block : (i + 1) * block]
    lane = lax.broadcasted_iota(jnp.int32, stats_ref.shape, 1)
    stats_ref[...] = jnp.where(lane == 0, average, inverse)


def norm_rows(index, own, sib, vectors):
    tokens, width = own.shape
    size = min(256, tokens)
    rows = pl.BlockSpec((size, width), lambda i, s: (i, 0))
    return pl.pallas_call(
        norm_kernel,
        grid_spec=pltpu.PrefetchScalarGridSpec(
            num_scalar_prefetch=1,
            grid=(tokens // size,),
            in_specs=[rows, rows, pl.BlockSpec((4, width), lambda i, s: (0, 0))],
            out_specs=[
                pl.BlockSpec((size, 2 * width), lambda i, s: (i, 0)),
                pl.BlockSpec((size, 128), lambda i, s: (i, 0)),
            ],
        ),
        out_shape=[shape((tokens, 2 * width)), shape((tokens, 128), jnp.float32)],
        compiler_params=params(),
        cost_estimate=cost(0, 8 * tokens * width),
    )(index, own, sib, vectors)


def project_kernel(own_ref, sib_ref, own_weight, sib_weight, bias_ref, out_ref):
    total = mm(own_ref[...], own_weight[...], 1, 0) + mm(sib_ref[...], sib_weight[...], 1, 0)
    out_ref[...] = (total + bias_ref[...]).astype(jnp.bfloat16)


def halves_of(size, width):
    return [pl.BlockSpec((size, width), lambda i, h=h: (i, h)) for h in range(2)]


def project(normed, own_weight, sib_weight, bias):
    tokens, features = normed.shape
    width, units = features // 2, bias.shape[1]
    size = min(256, tokens)
    weight = pl.BlockSpec((width, units), lambda i: (0, 0))
    return pl.pallas_call(
        project_kernel,
        grid=(tokens // size,),
        in_specs=halves_of(size, width)
        + [weight, weight, pl.BlockSpec((1, units), lambda i: (0, 0))],
        out_specs=pl.BlockSpec((size, units), lambda i: (i, 0)),
        out_shape=shape((tokens, units)),
        compiler_params=params(),
        cost_estimate=cost(4 * tokens * width * units, 4 * tokens * width + 4 * width * units),
    )(normed, normed, own_weight, sib_weight, bias)


def sum_rows_kernel(count, *refs):
    out_ref = refs[-1]
    width = refs[count].shape[0]
    for half in range(2):
        at = slice(half * width, (half + 1) * width)
        total = refs[3 * count][:, at] if len(refs) > 3 * count + 1 else None
        for k in range(count):
            part = mm(refs[k][...], refs[(1 + half) * count + k][...], 1, 1)
            total = part if total is None else total + part
        out_ref[:, at] = total


def sum_rows(rows, own_weights, sib_weights, at, before=()):
    count = len(rows)
    tokens, units = rows[0].shape
    width = own_weights[0].shape[0]
    size = min(512, tokens)
    full = pl.BlockSpec((size, 2 * width), lambda i: (i, 0))
    return pl.pallas_call(
        functools.partial(sum_rows_kernel, count),
        grid=(tokens // size,),
        in_specs=[pl.BlockSpec((size, units), lambda i: (i, 0))] * count
        + [pl.BlockSpec((width, units), lambda i: (0, at))] * (2 * count)
        + [full] * len(before),
        out_specs=full,
        out_shape=shape((tokens, 2 * width), jnp.float32),
        compiler_params=params(),
        cost_estimate=cost(4 * count * tokens * units * width, 8 * tokens * width),
    )(*rows, *own_weights, *sib_weights, *before)


def head_grads_kernel(own_ref, sib_ref, *refs):
    out_ref = refs[-1]
    count = (len(refs) - 1) // 2
    own = refs[0].shape[1]
    for k in range(count):
        total = mm(own_ref[...], refs[k][...], 1, 0) + mm(sib_ref[...], refs[count + k][...], 1, 0)
        out_ref[:, k * own : (k + 1) * own] = total.astype(jnp.bfloat16)


def head_grads(grads, own_weights, sib_weights):
    tokens, width = grads.shape[0], grads.shape[1] // 2
    count = len(own_weights)
    units = own_weights[0].shape[1] // 4
    size = min(256, tokens)
    return pl.pallas_call(
        head_grads_kernel,
        grid=(tokens // size,),
        in_specs=halves_of(size, width) + [pl.BlockSpec((width, units), lambda i: (0, 3))] * (2 * count),
        out_specs=pl.BlockSpec((size, count * units), lambda i: (i, 0)),
        out_shape=shape((tokens, count * units)),
        compiler_params=params(),
        cost_estimate=cost(4 * count * tokens * width * units, 8 * tokens * width),
    )(grads, grads, *own_weights, *sib_weights)


def head_products_kernel(*refs):
    normed, grads = refs[:2], refs[2:4]
    heads_ref, attended_ref = refs[4:6]
    outs, sum_ref = refs[6:8], refs[8]
    split = heads_ref.shape[1]
    for i in range(2):
        outs[i][:, :split] = mm(normed[i][...], heads_ref[...], 0, 0).astype(jnp.bfloat16)
        outs[i][:, split:] = mm(grads[i][...], attended_ref[...], 0, 0).astype(jnp.bfloat16)

    @pl.when(pl.program_id(0) == 0)
    def _():
        sum_ref[...] = jnp.sum(heads_ref[...].astype(jnp.float32), axis=0, keepdims=True)


def head_products(normed, grads, head_grad, attended):
    tokens, width = normed.shape[0], normed.shape[1] // 2
    split, own = head_grad.shape[1], attended.shape[1]
    size = min(512, width)
    blocks = width // size
    left = [pl.BlockSpec((tokens, size), lambda d, h=h: (0, h * blocks + d)) for h in range(2)]
    out = pl.BlockSpec((size, split + own), lambda d: (d, 0))
    return pl.pallas_call(
        head_products_kernel,
        grid=(width // size,),
        in_specs=left * 2
        + [pl.BlockSpec((tokens, split), lambda d: (0, 0)), pl.BlockSpec((tokens, own), lambda d: (0, 0))],
        out_specs=[out, out, pl.BlockSpec((1, split), lambda d: (0, 0))],
        out_shape=[shape((width, split + own))] * 2 + [shape((1, split), jnp.float32)],
        compiler_params=params(),
        cost_estimate=cost(4 * tokens * width * (split + own), 12 * tokens * width),
    )(normed, normed, grads, grads, head_grad, attended)


def block_at(half, width, place):
    block = width // 4
    return pl.ds(pl.multiple_of(half * width + place * block, block), block)


def norm_two_kernel(
    index_ref, rows_ref, came_ref, own_ref, sib_ref, vectors_ref, hidden_ref, normed_ref, stats_ref
):
    width = own_ref.shape[1]
    block = width // 4
    for half, tokens_ref in enumerate((own_ref, sib_ref)):
        for i in range(4):
            at = block_at(half, width, index_ref[1] ^ i)
            span = slice(half * width + i * block, half * width + (i + 1) * block)
            hidden_ref[:, span] = (
                tokens_ref[:, i * block : (i + 1) * block].astype(jnp.float32)
                + rows_ref[:, at]
                + came_ref[:, at].astype(jnp.float32)
                + vectors_ref[4:5, span]
            )
    hidden = hidden_ref[...]
    average = jnp.mean(hidden, axis=1, keepdims=True)
    centered = hidden - average
    inverse = lax.rsqrt(jnp.mean(centered * centered, axis=1, keepdims=True) + norm_eps)
    normed_ref[...] = (centered * inverse * vectors_ref[2:3, :] + vectors_ref[3:4, :]).astype(jnp.bfloat16)
    lane = lax.broadcasted_iota(jnp.int32, stats_ref.shape, 1)
    stats_ref[...] = jnp.where(lane == 0, average, inverse)


def my_rows(size, columns, blocks):
    return pl.BlockSpec((size, columns), lambda i, s: (s[0] * blocks + i, 0))


def norm_two(index, rows, came, own, sib, vectors):
    tokens, features = came.shape
    size = tokens // 2
    mine = my_rows(size, features // 2, 2)
    plain = pl.BlockSpec((size, features), lambda i, s: (i, 0))
    return pl.pallas_call(
        norm_two_kernel,
        grid_spec=pltpu.PrefetchScalarGridSpec(
            num_scalar_prefetch=1,
            grid=(2,),
            in_specs=[
                my_rows(size, features, 2),
                plain,
                mine,
                mine,
                pl.BlockSpec(vectors.shape, lambda i, s: (0, 0)),
            ],
            out_specs=[plain, plain, pl.BlockSpec((size, 128), lambda i, s: (i, 0))],
        ),
        out_shape=[
            shape((tokens, features), jnp.float32),
            shape((tokens, features)),
            shape((tokens, 128), jnp.float32),
        ],
        compiler_params=params(),
        cost_estimate=cost(0, 16 * tokens * features),
    )(index, rows, came, own, sib, vectors)


def norm_pull(grads, normal, inverse, gain):
    scaled = grads * gain
    return inverse * (
        scaled
        - jnp.mean(scaled, axis=1, keepdims=True)
        - normal * jnp.mean(scaled * normal, axis=1, keepdims=True)
    )


def add_sums(sums_ref, parts):
    rows = [jnp.sum(p, axis=0, keepdims=True) for p in parts]
    rows += [jnp.zeros_like(rows[0])] * (8 - len(rows))
    total = jnp.concatenate(rows, axis=0)

    @pl.when(pl.program_id(0) == 0)
    def _():
        sums_ref[...] = total

    @pl.when(pl.program_id(0) > 0)
    def _():
        sums_ref[...] += total


def norm_two_back_kernel(index_ref, *refs):
    here, x_top, y_top, x_bottom, y_bottom, hidden_ref, stats_ref, branch_ref, vectors_ref = refs[:9]
    grad_ref, blocks_ref, mirror_ref, sums_ref = refs[9:]
    f32 = jnp.float32
    top = pl.program_id(0) == 0
    from_x = jnp.where(top, x_top[...].astype(f32), x_bottom[...].astype(f32))
    from_y = jnp.where(top, y_top[...].astype(f32), y_bottom[...].astype(f32))
    grads = here[...].astype(f32) + from_x + from_y
    inverse = stats_ref[:, 1:2]
    normal = (hidden_ref[...] - stats_ref[:, :1]) * inverse
    branch = branch_ref[...].astype(f32)
    total = branch + norm_pull(grads, normal, inverse, vectors_ref[2:3, :])
    grad_ref[...] = total
    rounded = total.astype(jnp.bfloat16)
    width = rounded.shape[1] // 2
    block = width // 4
    for half in range(2):
        for i in range(4):
            part = rounded[:, half * width + i * block : half * width + (i + 1) * block]
            place = index_ref[1] ^ i
            blocks_ref[:, block_at(half, width, place)] = part
            mirror_ref[:, block_at(1 - half, width, place)] = part
    add_sums(sums_ref, (grads * normal, grads, rounded.astype(f32), branch))


def norm_two_back(index, parts, hidden, stats, branch, vectors):
    tokens, features = hidden.shape
    size = tokens // 2
    plain = pl.BlockSpec((size, features), lambda i, s: (i, 0))
    once = pl.BlockSpec((size, features), lambda i, s: (0, 0))
    return pl.pallas_call(
        norm_two_back_kernel,
        grid_spec=pltpu.PrefetchScalarGridSpec(
            num_scalar_prefetch=1,
            grid=(2,),
            in_specs=[plain]
            + [once] * 4
            + [
                plain,
                pl.BlockSpec((size, 128), lambda i, s: (i, 0)),
                plain,
                pl.BlockSpec(vectors.shape, lambda i, s: (0, 0)),
            ],
            out_specs=[plain] * 3 + [pl.BlockSpec((8, features), lambda i, s: (0, 0))],
        ),
        out_shape=[
            shape((tokens, features), jnp.float32),
            shape((tokens, features)),
            shape((tokens, features)),
            shape((8, features), jnp.float32),
        ],
        compiler_params=params(),
        cost_estimate=cost(0, 24 * tokens * features),
    )(index, *parts, hidden, stats, branch, vectors)


def norm_one_back_kernel(index_ref, *refs):
    rows_ref, came_ref, own_ref, sib_ref, stats_ref, out_own, out_sib, keep_ref, hidden_ref = refs[:9]
    vectors_ref, own_grad, sib_grad, sums_ref, grads_ref = refs[9:]
    f32 = jnp.float32
    width = own_ref.shape[1]
    block = width // 4
    for half in range(2):
        for i in range(4):
            at = block_at(half, width, index_ref[1] ^ i)
            span = slice(half * width + i * block, half * width + (i + 1) * block)
            grads_ref[:, span] = rows_ref[:, at] + came_ref[:, at].astype(f32)
    grads = grads_ref[...]
    inverse = stats_ref[:, 1:2]
    tokens = jnp.concatenate([own_ref[...], sib_ref[...]], axis=1).astype(f32)
    normal = (tokens - stats_ref[:, :1]) * inverse
    total = hidden_ref[...] + norm_pull(grads, normal, inverse, vectors_ref[0:1, :])
    dropped = 1.0 - keep_ref[...]
    own_grad[...] = out_own[...].astype(f32) * dropped + total[:, :width]
    sib_grad[...] = out_sib[...].astype(f32) * dropped + total[:, width:]
    add_sums(sums_ref, (grads * normal, grads))


def norm_one_back(index, rows, came, own, sib, stats, out_own, out_sib, keep, hidden, vectors):
    tokens, features = came.shape
    size, width = tokens // 2, features // 2
    plain = pl.BlockSpec((size, features), lambda i, s: (i, 0))
    half_wide = pl.BlockSpec((size, width), lambda i, s: (i, 0))
    return pl.pallas_call(
        norm_one_back_kernel,
        grid_spec=pltpu.PrefetchScalarGridSpec(
            num_scalar_prefetch=1,
            grid=(2,),
            in_specs=[
                my_rows(size, features, 2),
                plain,
                my_rows(size, width, 2),
                my_rows(size, width, 2),
                my_rows(size, 128, 2),
                my_rows(size, width, 2),
                half_wide,
                pl.BlockSpec((size, 1), lambda i, s: (i, 0)),
                plain,
                pl.BlockSpec(vectors.shape, lambda i, s: (0, 0)),
            ],
            out_specs=[half_wide, half_wide, pl.BlockSpec((8, features), lambda i, s: (0, 0))],
            scratch_shapes=[pltpu.VMEM((size, features), jnp.float32)],
        ),
        out_shape=[shape((tokens, width), jnp.float32)] * 2 + [shape((8, features), jnp.float32)],
        compiler_params=params(),
        cost_estimate=cost(0, 24 * tokens * features),
    )(index, rows, came, own, sib, stats, out_own, out_sib, keep, hidden, vectors)


def select_piece(refs, step, use):
    for j in range(3):

        @pl.when(step == j)
        def _():
            use(refs[j][...])

    @pl.when(step == 3)
    def _():
        use(jnp.concatenate([refs[3][...], refs[4][...]], axis=0))


def place_heads_kernel(index_ref, *refs):
    pieces, outs = refs[:5], refs[5:]
    own = pieces[0].shape[1] // 8

    def use(piece):
        for which in range(2):
            at = pl.multiple_of((index_ref[0] ^ which) * own, own)
            for m in range(4):
                part = piece[:, (4 * which + m) * own : (4 * which + m + 1) * own].astype(jnp.float32)
                if m < 3:
                    outs[m][:, pl.ds(at, own)] = part
                else:
                    outs[m][pl.ds(at, own), :] = part.T

    select_piece(pieces, pl.program_id(0), use)


def place_heads(index, pieces):
    block, columns = pieces[0].shape
    units, width = columns // 4, 4 * block
    whole = [pl.BlockSpec(p.shape, lambda j, s: (0, 0)) for p in pieces]
    return pl.pallas_call(
        place_heads_kernel,
        grid_spec=pltpu.PrefetchScalarGridSpec(
            num_scalar_prefetch=1,
            grid=(4,),
            in_specs=whole,
            out_specs=[pl.BlockSpec((block, units), lambda j, s: (s[1] ^ j, 0))] * 3
            + [pl.BlockSpec((units, block), lambda j, s: (0, s[1] ^ j))],
        ),
        out_shape=[shape((width, units), jnp.float32)] * 3 + [shape((units, width), jnp.float32)],
        compiler_params=params(),
        cost_estimate=cost(0, 24 * width * units),
    )(index, *pieces)


def place_ff_kernel(*refs):
    pieces, (up_out, down_out) = refs[:-2], refs[-2:]
    rows = pieces[0].shape[1]
    quarter = pieces[0].shape[2] // 2
    for part, piece in enumerate(pieces):
        span = slice(part * rows, (part + 1) * rows)
        up_out[span, :] = piece[0, :, :quarter].astype(jnp.float32)
        down_out[:, span] = piece[0, :, quarter:].astype(jnp.float32).T


def place_ff(pieces):
    count, rows, columns = pieces[0].shape
    width, quarter = rows * len(pieces), columns // 2
    return pl.pallas_call(
        place_ff_kernel,
        grid=(count,),
        in_specs=[pl.BlockSpec((1, rows, columns), lambda j: (j, 0, 0))] * len(pieces),
        out_specs=[
            pl.BlockSpec((width, quarter), lambda j: (0, j)),
            pl.BlockSpec((quarter, width), lambda j: (j, 0)),
        ],
        out_shape=[
            shape((width, count * quarter), jnp.float32),
            shape((count * quarter, width), jnp.float32),
        ],
        compiler_params=params(),
        cost_estimate=cost(0, 48 * width * quarter),
    )(*pieces)


def join_kernel(index_ref, mine_ref, first_ref, second_ref, out_ref):
    step = pl.program_id(0)

    @pl.when(step < 2)
    def _():
        out_ref[...] = mine_ref[...]

    @pl.when(step == 2)
    def _():
        out_ref[...] = first_ref[...]

    @pl.when(step == 3)
    def _():
        out_ref[...] = second_ref[...]


def join_tokens(index, mine, first, second):
    tokens, width = mine.shape
    size = tokens // 2
    once = pl.BlockSpec((size, width), lambda i, s: (0, 0))
    return pl.pallas_call(
        join_kernel,
        grid_spec=pltpu.PrefetchScalarGridSpec(
            num_scalar_prefetch=1,
            grid=(4,),
            in_specs=[pl.BlockSpec((size, width), lambda i, s: (jnp.minimum(i, 1), 0)), once, once],
            out_specs=pl.BlockSpec(
                (size, width), lambda i, s: (jnp.where(i < 2, s[0] * 2 + i, (1 - s[0]) * 2 + i - 2), 0)
            ),
        ),
        out_shape=shape((2 * tokens, width), mine.dtype),
        compiler_params=params(),
        cost_estimate=cost(0, 8 * tokens * width),
    )(index, mine, first, second)


def layer_out_kernel(*refs):
    here, x_top, y_top, x_bottom, y_bottom, hidden_ref, own_ref, sib_ref, keep_ref, vectors_ref = refs[1:11]
    own_out, sib_out = refs[11:]
    f32 = jnp.float32
    width = own_ref.shape[1]
    top = pl.program_id(0) == 0
    from_x = jnp.where(top, x_top[...].astype(f32), x_bottom[...].astype(f32))
    from_y = jnp.where(top, y_top[...].astype(f32), y_bottom[...].astype(f32))
    total = hidden_ref[...] + here[...].astype(f32) + from_x + from_y + vectors_ref[5:6, :]
    keep = keep_ref[...] > 0.5
    own_out[...] = jnp.where(keep, total[:, :width], own_ref[...].astype(f32))
    sib_out[...] = jnp.where(keep, total[:, width:], sib_ref[...].astype(f32))


def layer_rows(index, parts, hidden, own, sib, keep, vectors):
    tokens, features = hidden.shape
    size, width = tokens // 2, features // 2
    plain = pl.BlockSpec((size, features), lambda i, s: (i, 0))
    half_wide = pl.BlockSpec((size, width), lambda i, s: (i, 0))
    return pl.pallas_call(
        layer_out_kernel,
        grid_spec=pltpu.PrefetchScalarGridSpec(
            num_scalar_prefetch=1,
            grid=(2,),
            in_specs=[plain]
            + [pl.BlockSpec((size, features), lambda i, s: (0, 0))] * 4
            + [
                plain,
                my_rows(size, width, 2),
                my_rows(size, width, 2),
                pl.BlockSpec((size, 1), lambda i, s: (i, 0)),
                pl.BlockSpec(vectors.shape, lambda i, s: (0, 0)),
            ],
            out_specs=[half_wide, half_wide],
        ),
        out_shape=[shape((tokens, width), jnp.float32)] * 2,
        compiler_params=params(),
        cost_estimate=cost(0, 20 * tokens * features),
    )(index, *parts, hidden, own, sib, keep, vectors)


def body_local(
    tokens_in,
    out_grad,
    segment_ids,
    active_lengths,
    norm1_gain,
    norm1_shift,
    query_weight,
    query_bias,
    key_weight,
    value_weight,
    value_bias,
    out_weight,
    out_bias,
    norm2_gain,
    norm2_shift,
    up_weight,
    up_bias,
    down_weight,
    down_bias,
):
    f32, bf16 = jnp.float32, jnp.bfloat16
    rows, width = tokens_in.shape
    ring = lax.axis_size("col")
    row_i = lax.axis_index("row")
    plane_i = lax.axis_index("dp")
    col_i = lax.axis_index("col")
    own = query_weight.shape[1] // 2
    block = width // 4
    quarter = up_weight.shape[1] // 4
    unit = quarter // 2
    half = rows // 2
    order = Order()
    plane, column = Plane(order), Link(order)
    index = jnp.stack([row_i, plane_i, col_i]).astype(jnp.int32)

    def cut(values, start, size):
        return lax.dynamic_slice_in_dim(values, start, size, axis=0)

    def mirrored(values):
        return jnp.concatenate([values[:, width:], values[:, :width]], axis=1)

    def my_tokens(values):
        return cut(values, row_i * half, half)

    def other_tokens(values):
        return cut(values, (1 - row_i) * half, half)

    tokens_sib = order.swap(tokens_in)
    out_grad_sib = swap(other_tokens(out_grad))

    mine = jnp.concatenate(
        [
            cut(query_bias, row_i * own, own),
            jnp.zeros((own,), f32),
            cut(value_bias, row_i * own, own),
            cut(up_bias, plane_i * quarter, quarter),
        ]
    )
    small = [mine] + [
        lax.ppermute(mine, "col", [(i, (i + k) % ring) for i in range(ring)]) for k in range(1, ring)
    ]

    sources = (query_weight, key_weight, value_weight, out_weight)
    piece = order.run(pack_heads, after(index, mine), sources, 1)
    pieces = [jnp.concatenate([piece[0], swap(piece[1])], axis=0)]
    column.last = small[1:]
    pieces.append(column.send(step_up, pieces[0]))

    active_all = active_rows(segment_ids, active_lengths)
    active_here = my_tokens(cut(active_all, col_i * rows, rows))
    keep_mask = active_here.astype(f32)[:, None]
    out_grads = jnp.concatenate([my_tokens(out_grad), out_grad_sib], axis=1).astype(f32)
    branch_mine = (after(out_grads, *order.tokens) * keep_mask).astype(bf16)
    branch_first = plane.both(branch_mine[: half // 2], branch_mine[: half // 2])
    ff_piece = order.run(pack_ff, index, up_weight, down_weight)
    ff_pieces = lax.all_gather(ff_piece, ("row", "col"))
    vectors = jnp.stack([norm1_gain, norm1_shift, norm2_gain, norm2_shift, out_bias, down_bias])
    vectors_sib = swap(vectors)
    vectors_all = jnp.concatenate([vectors, vectors_sib], axis=1)
    pieces.append(column.send(step_up, pieces[1]))
    near = plane.both(pieces[1], pieces[1])
    here = order.run(pack_heads, index, sources, 4)
    own_parts, other_rows = [here[0]], [order.swap(here[1])]
    normed_one, stats_one = order.run(
        norm_rows,
        index,
        tokens_in,
        tokens_sib,
        jnp.concatenate([vectors[:2], vectors_sib[:2]], axis=0),
    )

    segment_row = picked(segment_ids, col_i)
    member = (segment_row[:, None] == jnp.arange(active_lengths.shape[1])).astype(jnp.int32)
    counts = jnp.sum(member, axis=0)
    first_row = jnp.sum(member * (jnp.cumsum(counts) - counts), axis=1)[None, :]

    heads, attended = [], []

    def attend_project(k):
        heads.append(
            order.run(project, normed_one, own_parts[k], other_rows[k], small[k][None, : 3 * own])
        )

    def attend(k):
        attended.append(order.run(local_forward, heads[k], first_row))

    def stack(k, near, far):
        own_part, other_part = order.run(stack_pieces, [pieces[k], *near, *far])
        own_parts.append(own_part)
        other_rows.append(other_part)

    attend_project(0)
    attend(0)
    far = plane.far(*near)
    pieces.append(column.send(step_up, pieces[2]))
    last_near, last_far = near, far
    near = plane.both(pieces[2], pieces[2])
    stack(1, last_near, last_far)
    attend_project(1)
    attend(1)
    far = plane.far(*near)
    last_near, last_far = near, far
    near = plane.both(pieces[3], pieces[3])
    stack(2, last_near, last_far)
    attend_project(2)
    attend(2)
    far = plane.far(*near)
    last_near, last_far = near, far
    branch_far = plane.far(*branch_first)
    stack(3, last_near, last_far)
    before = order.run(sum_rows, attended[:3], own_parts[:3], other_rows[:3], 3)
    second_near = plane.both(branch_mine[half // 2 :], branch_mine[half // 2 :])
    attend_project(3)
    attend(3)
    second_far = plane.far(*second_near)
    attention_rows = order.run(sum_rows, attended[3:], own_parts[3:], other_rows[3:], 3, (before,))
    arrived = swap(order.tie(mirrored(other_tokens(attention_rows)).astype(bf16)))

    order.tokens.append(ff_pieces)
    hidden_one, normed_two, stats_two = order.run(
        norm_two, index, attention_rows, arrived, tokens_in, tokens_sib, vectors_all
    )

    normed = [normed_two, *plane.both(normed_two, normed_two)]
    branch_all = jnp.concatenate(
        [branch_mine]
        + [part for pair in zip(branch_first, second_near) for part in pair]
        + [*branch_far, *second_far],
        axis=0,
    )
    def by_column(relative):
        places = jnp.mod(col_i - jnp.arange(ring), ring)
        return jnp.take(relative, places, axis=0)

    ff_biases = by_column(jnp.stack([s[None, 3 * own :] for s in small]))
    ff_rows, up_sums, grad_parts, down_parts = [], [], [], []

    def feed_forward(j):
        grads, part = (branch_all, j) if j > 0 else (branch_mine, 0)
        results = order.run(ffn_rows_of, index, normed[j], grads, part, ff_pieces, ff_biases)
        for kept, result in zip((ff_rows, up_sums, grad_parts, down_parts), results):
            kept.append(result)

    def top(values):
        return values[: half // 2]

    def bottom(values):
        return values[half // 2 :]

    def second_steps(parts, via_x, via_y):
        via_x, via_y = after((via_x, via_y), *order.tokens)
        return plane.both(add_rounded(bottom(parts[1]), via_y), add_rounded(top(parts[2]), via_x))

    def weight_grads(part):
        return order.run(weight_products, normed, branch_all, ff_rows, part)

    feed_forward(0)
    normed_far = plane.far(normed[1], normed[2])
    feed_forward(1)
    x_top = plane.x.send(step_x, top(grad_parts[1]))
    feed_forward(2)
    y_bottom = plane.y.send(step_y, bottom(grad_parts[2]))
    normed.append(jnp.concatenate(normed_far, axis=0))
    feed_forward(3)
    via_x, via_y = plane.both(top(grad_parts[3]), bottom(grad_parts[3]))
    ff_mine = weight_grads(0)
    x_bottom, y_top = second_steps(grad_parts, via_x, via_y)
    ff_other = order.swap(weight_grads(1))

    hidden_grad, grad_mine, grad_mirror, sums_two = order.run(
        norm_two_back,
        index,
        (grad_parts[0], x_top, y_top, x_bottom, y_bottom),
        hidden_one,
        stats_two,
        branch_mine,
        vectors_all,
    )
    down_x_top, down_y_bottom = plane.both(top(down_parts[1]), bottom(down_parts[2]))
    grad_others = [order.swap(top(grad_mirror)), order.swap(bottom(grad_mirror))]
    grad_rows = order.run(join_tokens, index, grad_mine, *grad_others)

    ff_grads = []
    for part in range(2):
        span = slice(part * width // 2, (part + 1) * width // 2)
        total = order.tie(add_rounded(ff_mine[:, span], ff_other[:, span]))
        total = lax.psum_scatter(total, "col", scatter_dimension=0, tiled=False)
        ff_grads.append(lax.all_gather(total, "dp"))

    down_via_x, down_via_y = plane.both(top(down_parts[3]), bottom(down_parts[3]), True)
    head_grad = order.run(head_grads, grad_rows, own_parts, other_rows)
    head_rows, bias_rows, group_parts = [None] * ring, [None] * ring, [None] * ring

    def backward(k):
        head_rows[k] = order.run(
            lambda h, g, f: local_backward(h, g, k, f), heads[k], head_grad, first_row
        )

    def head_weights(k):
        *group_parts[k], bias_rows[k] = order.run(
            head_products, normed_one, grad_rows, head_rows[k], attended[k]
        )

    def part_of(k, j, which):
        return group_parts[k][which][j * block : (j + 1) * block]

    def first_messages(k):
        return plane.both(part_of(k, 3, 0), part_of(k, 3, 1), True)

    def second_messages(k, via):
        via_x, via_y = after(via, *order.tokens)
        return plane.both(
            jnp.concatenate([part_of(k, 1, 0), add_rounded(part_of(k, 1, 1), via_y)], axis=1),
            jnp.concatenate([add_rounded(part_of(k, 2, 0), via_x), part_of(k, 2, 1)], axis=1),
            k == 0,
        )

    def group_total(k, came, total):
        came_x, came_y = after(came, *order.tokens)
        here = jnp.concatenate([part_of(k, 0, 0), part_of(k, 0, 1)], axis=1)
        here = here.astype(f32) + came_x.astype(f32) + came_y.astype(f32)
        if total is not None:
            here = here + total.astype(f32)
        return here.astype(bf16)

    def layer_out_rows():
        own_out, sib_out = order.run(
            layer_rows,
            index,
            (down_parts[0], down_x_top, down_y_top, down_x_bottom, down_y_bottom),
            hidden_one,
            tokens_in,
            tokens_sib,
            keep_mask,
            vectors_all,
        )
        return own_out, order.swap(top(sib_out)), order.swap(bottom(sib_out))

    vias, came = [None] * ring, [None] * ring
    backward(3)
    head_weights(3)
    down_x_bottom, down_y_top = second_steps(down_parts, down_via_x, down_via_y)
    vias[3] = first_messages(3)
    backward(2)
    head_weights(2)
    vias[2] = first_messages(2)
    came[3] = second_messages(3, vias[3])
    order.tokens += [down_x_bottom, down_y_top]
    backward(1)
    head_weights(1)
    vias[1] = first_messages(1)
    came[2] = second_messages(2, vias[2])
    backward(0)
    order.tokens += came[3]
    head_weights(0)
    vias[0] = first_messages(0)
    came[1] = second_messages(1, vias[1])
    total = column.send(step_down, group_total(3, came[3], None))
    order.tokens += came[2]
    back_rows = order.run(sum_rows, head_rows, own_parts, other_rows, 0)
    came[0] = second_messages(0, vias[0])
    arrived = order.swap(mirrored(other_tokens(back_rows)).astype(bf16))
    total = column.send(step_down, add_rounded(total, group_total(2, came[2], None)))
    layer_parts = layer_out_rows()

    input_mine, input_other, sums_one = order.run(
        norm_one_back,
        index,
        back_rows,
        arrived,
        tokens_in,
        tokens_sib,
        stats_one,
        out_grad,
        out_grad_sib,
        keep_mask,
        hidden_grad,
        vectors_all,
    )
    input_others = [order.swap(top(input_other)), order.swap(bottom(input_other))]
    total = column.send(step_down, add_rounded(total, group_total(1, came[1], None)))
    layer_out = order.run(join_tokens, index, *layer_parts)

    row_hot = (jnp.arange(2) == row_i).astype(f32)
    plane_hot = (jnp.arange(4) == plane_i).astype(f32)
    head_bias = by_column(jnp.stack(bias_rows)).reshape(ring, 3, 1, own) * row_hot[:, None]
    up_bias_part = sum(up_sums) * plane_hot[:, None]
    bias_vector = jnp.concatenate([head_bias.reshape(ring, -1), up_bias_part.reshape(ring, -1)], axis=1)
    feature_sums = jnp.concatenate([sums_one[:2], sums_two[:4]], axis=0)
    summed = jnp.concatenate([bias_vector.reshape(-1), feature_sums[:, :width].reshape(-1)])
    summed = summed + swap(
        jnp.concatenate([bias_vector.reshape(-1), feature_sums[:, width:].reshape(-1)])
    )

    summed = order.tie(summed)
    summed = summed + plane.x.send(step_x, summed)
    summed = summed + plane.y.send(step_y, summed)
    total = group_total(0, came[0], total)
    total = jnp.concatenate([total[:, : 4 * own], swap(total[:, 4 * own :])], axis=1)
    near = plane.both(total, total)
    step = 1
    while step < ring:
        pairs = [(i, i ^ step) for i in range(ring)]
        summed = summed + column.send(lambda v: lax.ppermute(v, "col", pairs), summed)
        step *= 2
    input_grad = order.run(join_tokens, index, input_mine, *input_others)
    up_weight_grad, down_weight_grad = order.run(place_ff, ff_grads)
    far = plane.far(*near)
    query_weight_grad, key_weight_grad, value_weight_grad, out_weight_grad = place_heads(
        index, [total, *near, *far]
    )

    bias_here = picked(summed[: bias_vector.size].reshape(ring, -1), col_i)
    own_here = summed[bias_vector.size :].reshape(6, width)
    size = 2 * own
    return (
        layer_out,
        input_grad,
        own_here[0],
        own_here[1],
        query_weight_grad,
        bias_here[:size],
        key_weight_grad,
        value_weight_grad,
        bias_here[2 * size : 3 * size],
        out_weight_grad,
        own_here[4],
        own_here[2],
        own_here[3],
        up_weight_grad,
        bias_here[3 * size :],
        down_weight_grad,
        own_here[5],
    )


def body(tokens_in, out_grad, segment_ids, *rest):
    ring = lax.axis_size("col")
    local = (
        lax.axis_size("dp") == 4
        and lax.axis_size("row") == 2
        and ring == 4
        and tokens_in.shape[0] == segment_ids.shape[1]
    )
    chosen = body_local if local else body_general
    return chosen(tokens_in, out_grad, segment_ids, *rest)


def solution(mesh):
    placed = (
        P(("dp", "col"), "row"),
        P(("dp", "col"), "row"),
        P("dp", None),
        P("dp", None),
        P("row"),
        P("row"),
        P("row", "col"),
        P("col"),
        P("row", "col"),
        P("row", "col"),
        P("col"),
        P("col", "row"),
        P("row"),
        P("row"),
        P("row"),
        P("row", "col"),
        P("col"),
        P("col", "row"),
        P("row"),
    )
    return jax.shard_map(
        body,
        mesh=mesh,
        in_specs=placed,
        out_specs=(
            P(("dp", "col"), "row"),
            P(("dp", "col"), "row"),
            P("row"),
            P("row"),
            P("row", "col"),
            P("col"),
            P("row", "col"),
            P("row", "col"),
            P("col"),
            P("col", "row"),
            P("row"),
            P("row"),
            P("row"),
            P("row", "col"),
            P("col"),
            P("col", "row"),
            P("row"),
        ),
        check_vma=False,
    )
```

```python
import functools

import jax
import jax.numpy as jnp
from jax import lax
from jax.experimental import pallas as pl
from jax.experimental.pallas import tpu as pltpu
from jax.sharding import PartitionSpec as P

D = 2048
HEAD_DIM = 64


norm_eps = 1e-05
masked_fill = -1e30


def width_totals(total_one, total_two):
    return lax.psum((total_one, total_two), "row")


def token_gather(values):
    return lax.all_gather(values, "col", axis=0, tiled=True)


def token_sums(partial_rows):
    return lax.psum_scatter(partial_rows, "col", scatter_dimension=0, tiled=True)


def unit_gather(values):
    return lax.all_gather(values, "row", axis=1, tiled=True)


def unit_sums(partial_units):
    return lax.psum_scatter(partial_units, "row", scatter_dimension=1, tiled=True)


def gelu_value(values):
    return jax.nn.gelu(values, approximate=True)


def gelu_slope(values):
    result, pullback = jax.vjp(gelu_value, values)
    return pullback(jnp.ones_like(values))[0]


def active_rows(segment_rows, keep_lengths):
    doc_index = jnp.arange(keep_lengths.shape[-1], dtype=jnp.int32)
    member = (segment_rows[:, :, None] == doc_index).astype(jnp.int32)
    counts = jnp.sum(member, axis=1)
    starts = jnp.cumsum(counts, axis=1) - counts
    first_pos = jnp.sum(member * starts[:, None, :], axis=2)
    keep_here = jnp.sum(member * keep_lengths[:, None, :], axis=2)
    position_in = jnp.arange(segment_rows.shape[1], dtype=jnp.int32)[None, :] - first_pos
    return (position_in < keep_here).reshape(-1)


def norm_forward(values, gain_part, shift_part):
    total_one, total_two = width_totals(jnp.sum(values, axis=1), jnp.sum(values * values, axis=1))
    average = total_one / D
    variance = total_two / D - average * average
    inverse = lax.rsqrt(variance + norm_eps)
    normal = (values - average[:, None]) * inverse[:, None]
    return ((normal * gain_part + shift_part).astype(jnp.bfloat16), normal, inverse)


def norm_backward(grad_rows, normal, inverse, gain_part):
    scaled = grad_rows * gain_part
    total_one, total_two = width_totals(jnp.sum(scaled, axis=1), jnp.sum(scaled * normal, axis=1))
    grad_in = inverse[:, None] * (
        scaled - total_one[:, None] / D - normal * (total_two[:, None] / D)
    )
    return (grad_in, jnp.sum(grad_rows * normal, axis=0), jnp.sum(grad_rows, axis=0))


def allowed_mask(segment_row, offset, block_rows):
    key_pos = jnp.arange(segment_row.shape[0], dtype=jnp.int32)
    query_pos = key_pos[offset : offset + block_rows]
    same_doc = segment_row[None, :] == segment_row[offset : offset + block_rows, None]
    return (key_pos[None, :] <= query_pos[:, None]) & same_doc


def attend_forward(query_seq, key_seq, value_seq, segment_row, score_scale):
    seq_length = query_seq.shape[2]
    block_rows = min(512, seq_length)
    outputs = []
    log_parts = []
    for offset in range(0, seq_length, block_rows):
        query_block = query_seq[:, :, offset : offset + block_rows]
        scores = (
            jnp.einsum("hdq,hdk->hqk", query_block, key_seq, preferred_element_type=jnp.float32)
            * score_scale
        )
        scores = jnp.where(allowed_mask(segment_row, offset, block_rows)[None], scores, masked_fill)
        row_max = jnp.max(scores, axis=2, keepdims=True)
        exp_scores = jnp.exp(scores - row_max)
        row_total = jnp.sum(exp_scores, axis=2, keepdims=True)
        weights = (exp_scores / row_total).astype(jnp.bfloat16)
        outputs.append(
            jnp.einsum("hqk,hdk->hdq", weights, value_seq, preferred_element_type=jnp.float32)
        )
        log_parts.append((row_max + jnp.log(row_total))[:, :, 0])
    return (jnp.concatenate(outputs, axis=2), jnp.concatenate(log_parts, axis=1))


def attend_backward(query_seq, key_seq, value_seq, grad_seq, segment_row, log_sums, score_scale):
    seq_length = query_seq.shape[2]
    block_rows = min(512, seq_length)
    key_grad = jnp.zeros(key_seq.shape, jnp.float32)
    value_grad = jnp.zeros(value_seq.shape, jnp.float32)
    query_grads = []
    for offset in range(0, seq_length, block_rows):
        query_block = query_seq[:, :, offset : offset + block_rows]
        grad_block = grad_seq[:, :, offset : offset + block_rows]
        scores = (
            jnp.einsum("hdq,hdk->hqk", query_block, key_seq, preferred_element_type=jnp.float32)
            * score_scale
        )
        scores = jnp.where(allowed_mask(segment_row, offset, block_rows)[None], scores, masked_fill)
        probs = jnp.exp(scores - log_sums[:, offset : offset + block_rows, None])
        prob_grad = jnp.einsum(
            "hdq,hdk->hqk", grad_block, value_seq, preferred_element_type=jnp.float32
        )
        row_dot = jnp.sum(probs * prob_grad, axis=2, keepdims=True)
        score_grad = (probs * (prob_grad - row_dot)).astype(jnp.bfloat16)
        query_grads.append(
            jnp.einsum("hqk,hdk->hdq", score_grad, key_seq, preferred_element_type=jnp.float32)
            * score_scale
        )
        key_grad = (
            key_grad
            + jnp.einsum(
                "hqk,hdq->hdk", score_grad, query_block, preferred_element_type=jnp.float32
            )
            * score_scale
        )
        value_grad = value_grad + jnp.einsum(
            "hqk,hdq->hdk",
            probs.astype(jnp.bfloat16),
            grad_block,
            preferred_element_type=jnp.float32,
        )
    return (jnp.concatenate(query_grads, axis=2), key_grad, value_grad)


def body_general(
    tokens_in,
    out_grad,
    segment_ids,
    active_lengths,
    norm1_gain,
    norm1_shift,
    query_weight,
    query_bias,
    key_weight,
    value_weight,
    value_bias,
    out_weight,
    out_bias,
    norm2_gain,
    norm2_shift,
    up_weight,
    up_bias,
    down_weight,
    down_bias,
):
    local_rows = tokens_in.shape[0]
    seq_here = segment_ids.shape[0]
    seq_length = segment_ids.shape[1]
    group_rows = seq_here * seq_length
    row_index = lax.axis_index("row")
    col_index = lax.axis_index("col")
    active_all = active_rows(segment_ids, active_lengths)
    active_here = lax.dynamic_slice_in_dim(active_all, col_index * local_rows, local_rows)
    keep_mask = active_here.astype(jnp.float32)[:, None]
    score_scale = HEAD_DIM ** (-0.5)
    rows_in = tokens_in.astype(jnp.float32)
    normed_one, normal_one, inverse_one = norm_forward(rows_in, norm1_gain, norm1_shift)
    gathered_one = token_gather(normed_one)
    stacked_weight = jnp.stack([query_weight, key_weight, value_weight])
    projected = unit_sums(
        jnp.einsum("td,kdh->kht", gathered_one, stacked_weight, preferred_element_type=jnp.float32)
    )
    head_width = projected.shape[1]
    head_count = head_width // HEAD_DIM
    query_part = lax.dynamic_slice_in_dim(query_bias, row_index * head_width, head_width)
    value_part = lax.dynamic_slice_in_dim(value_bias, row_index * head_width, head_width)
    bias_stack = jnp.stack([query_part, jnp.zeros_like(query_part), value_part])
    heads_all = (projected + bias_stack[:, :, None]).astype(jnp.bfloat16)

    def to_seqs(values):
        return jnp.moveaxis(values.reshape(head_count, HEAD_DIM, seq_here, seq_length), 2, 0)

    def from_seqs(values):
        return jnp.moveaxis(values, 0, 2).reshape(head_width, group_rows)

    query_seqs = to_seqs(heads_all[0])
    key_seqs = to_seqs(heads_all[1])
    value_seqs = to_seqs(heads_all[2])
    attended_seqs, log_sums = lax.map(
        lambda seq_items: attend_forward(
            seq_items[0], seq_items[1], seq_items[2], seq_items[3], score_scale
        ),
        (query_seqs, key_seqs, value_seqs, segment_ids),
    )
    attended = from_seqs(attended_seqs).astype(jnp.bfloat16)
    gathered_heads = unit_gather(attended[None])
    attention_rows = (
        token_sums(
            jnp.einsum("kht,hd->td", gathered_heads, out_weight, preferred_element_type=jnp.float32)
        )
        + out_bias
    )
    hidden_one = rows_in + attention_rows
    normed_two, normal_two, inverse_two = norm_forward(hidden_one, norm2_gain, norm2_shift)
    gathered_two = token_gather(normed_two)
    up_part = jnp.einsum("td,df->ft", gathered_two, up_weight, preferred_element_type=jnp.float32)[
        None
    ]
    unit_width = up_part.shape[1] // lax.axis_size("row")
    up_slice = lax.dynamic_slice_in_dim(up_bias, row_index * unit_width, unit_width)
    pre_act = unit_sums(up_part)[0] + up_slice[:, None]
    gathered_act = unit_gather(gelu_value(pre_act).astype(jnp.bfloat16)[None])
    ffn_rows = (
        token_sums(
            jnp.einsum("kft,fd->td", gathered_act, down_weight, preferred_element_type=jnp.float32)
        )
        + down_bias
    )
    layer_out = jnp.where(active_here[:, None], hidden_one + ffn_rows, rows_in)
    grad_rows = out_grad.astype(jnp.float32) * keep_mask
    branch_grad = token_gather(grad_rows.astype(jnp.bfloat16))
    down_grad = jnp.einsum(
        "kft,td->fd", gathered_act, branch_grad, preferred_element_type=jnp.float32
    )
    down_bias_grad = jnp.sum(branch_grad, axis=0, dtype=jnp.float32)
    act_part = jnp.einsum(
        "td,fd->ft", branch_grad, down_weight, preferred_element_type=jnp.float32
    )[None]
    act_grad = unit_sums(act_part)[0]
    pre_grad = (act_grad * gelu_slope(pre_act)).astype(jnp.bfloat16)
    gathered_pre = unit_gather(pre_grad[None])
    up_grad = jnp.einsum(
        "td,kft->df", gathered_two, gathered_pre, preferred_element_type=jnp.float32
    )
    up_bias_grad = jnp.sum(gathered_pre[0], axis=1, dtype=jnp.float32)
    normed_grad_two = token_sums(
        jnp.einsum("kft,df->td", gathered_pre, up_weight, preferred_element_type=jnp.float32)
    )
    back_two, gain_two_grad, shift_two_grad = norm_backward(
        normed_grad_two, normal_two, inverse_two, norm2_gain
    )
    hidden_grad = grad_rows + back_two
    attention_grad = token_gather(hidden_grad.astype(jnp.bfloat16))
    out_weight_grad = jnp.einsum(
        "kht,td->hd", gathered_heads, attention_grad, preferred_element_type=jnp.float32
    )
    out_bias_grad = jnp.sum(attention_grad, axis=0, dtype=jnp.float32)
    head_grad = unit_sums(
        jnp.einsum("td,hd->ht", attention_grad, out_weight, preferred_element_type=jnp.float32)[
            None
        ]
    )[0].astype(jnp.bfloat16)
    query_grads, key_grads, value_grads = lax.map(
        lambda seq_items: attend_backward(
            seq_items[0],
            seq_items[1],
            seq_items[2],
            seq_items[3],
            seq_items[4],
            seq_items[5],
            score_scale,
        ),
        (query_seqs, key_seqs, value_seqs, to_seqs(head_grad), segment_ids, log_sums),
    )
    stacked_grad = jnp.stack(
        [from_seqs(query_grads), from_seqs(key_grads), from_seqs(value_grads)]
    ).astype(jnp.bfloat16)
    gathered_grad = unit_gather(stacked_grad)
    stacked_weight_grad = jnp.einsum(
        "td,kht->kdh", gathered_one, gathered_grad, preferred_element_type=jnp.float32
    )
    query_bias_grad = jnp.sum(gathered_grad[0], axis=1, dtype=jnp.float32)
    value_bias_grad = jnp.sum(gathered_grad[2], axis=1, dtype=jnp.float32)
    normed_grad_one = token_sums(
        jnp.einsum("kht,kdh->td", gathered_grad, stacked_weight, preferred_element_type=jnp.float32)
    )
    back_one, gain_one_grad, shift_one_grad = norm_backward(
        normed_grad_one, normal_one, inverse_one, norm1_gain
    )
    input_grad = out_grad.astype(jnp.float32) * (1.0 - keep_mask) + hidden_grad + back_one
    (
        stacked_weight_grad,
        query_bias_grad,
        value_bias_grad,
        out_weight_grad,
        out_bias_grad,
        down_grad,
        down_bias_grad,
        up_grad,
        up_bias_grad,
    ) = lax.psum(
        (
            stacked_weight_grad,
            query_bias_grad,
            value_bias_grad,
            out_weight_grad,
            out_bias_grad,
            down_grad,
            down_bias_grad,
            up_grad,
            up_bias_grad,
        ),
        "dp",
    )
    gain_one_grad, shift_one_grad, gain_two_grad, shift_two_grad = lax.psum(
        (gain_one_grad, shift_one_grad, gain_two_grad, shift_two_grad), ("dp", "col")
    )
    return (
        layer_out,
        input_grad,
        gain_one_grad,
        shift_one_grad,
        stacked_weight_grad[0],
        query_bias_grad,
        stacked_weight_grad[1],
        stacked_weight_grad[2],
        value_bias_grad,
        out_weight_grad,
        out_bias_grad,
        gain_two_grad,
        shift_two_grad,
        up_grad,
        up_bias_grad,
        down_grad,
        down_bias_grad,
    )


def after(values, *others):
    return lax.optimization_barrier((values, others))[0]


def swap(values):
    return lax.ppermute(values, "row", [(0, 1), (1, 0)])


def step_x(values):
    return lax.ppermute(values, "dp", [(0, 1), (1, 0), (2, 3), (3, 2)])


def step_y(values):
    return lax.ppermute(values, "dp", [(0, 2), (2, 0), (1, 3), (3, 1)])


def step_up(values):
    count = lax.axis_size("col")
    return lax.ppermute(values, "col", [(i, (i + 1) % count) for i in range(count)])


def step_down(values):
    count = lax.axis_size("col")
    return lax.ppermute(values, "col", [(i, (i - 1) % count) for i in range(count)])


class Order:
    def __init__(self):
        self.tokens = []
        self.fresh, self.due = [], []

    def tie(self, values):
        if self.tokens:
            values = after(values, *self.tokens)
        self.tokens.append(values)
        return values

    def swap(self, values, due=True):
        arrived = swap(self.tie(values))
        if due:
            self.fresh.append(arrived)
        return arrived

    def run(self, function, first, *others):
        first = after(first, *self.tokens, *self.due) if self.tokens or self.due else first
        self.due, self.fresh = self.fresh, []
        result = function(first, *others)
        self.tokens = [jax.tree.leaves(result)[0]]
        return result


class Link:
    def __init__(self, order):
        self.order = order
        self.last = None

    def send(self, step, values, free=False):
        if self.last is not None and not free:
            values = after(values, self.last)
        self.last = step(self.order.tie(values))
        return self.last


class Plane:
    def __init__(self, order):
        self.x = Link(order)
        self.y = Link(order)

    def both(self, for_x, for_y, free=False):
        return self.x.send(step_x, for_x, free), self.y.send(step_y, for_y, free)

    def far(self, from_x, from_y):
        half = from_x.shape[0] // 2
        far_two, far_one = self.both(from_y[half:], from_x[:half])
        return far_one, far_two


def add_rounded(left, right):
    return (left.astype(jnp.float32) + right.astype(jnp.float32)).astype(jnp.bfloat16)


def ring_gather(link, values):
    held = [values]
    for _ in range(lax.axis_size("col") - 1):
        held.append(link.send(step_up, held[-1]))
    return held


def picked(stacked, index):
    return lax.dynamic_index_in_dim(stacked, index, 0, keepdims=False)


def mm(left, right, left_dim, right_dim, dtype=jnp.float32):
    return lax.dot_general(
        left, right, (((left_dim,), (right_dim,)), ((), ())), preferred_element_type=jnp.float32
    ).astype(dtype)


PAIR = 2 * HEAD_DIM
vmem_bytes = 48 * 1024 * 1024


def head_lanes(head, value):
    lane = lax.broadcasted_iota(jnp.int32, (1, PAIR), 1)
    return jnp.where(lane // HEAD_DIM == head, value, 0.0).astype(jnp.bfloat16)


def allowed_keys(first_row, low, high):
    key_pos = lax.broadcasted_iota(jnp.int32, (high, high - low), 0)
    query_pos = lax.broadcasted_iota(jnp.int32, (high, high - low), 1) + low
    return (key_pos >= first_row) & (key_pos <= query_pos)


def local_forward_kernel(size, first_ref, query_ref, key_ref, value_ref, out_ref):
    lane = lax.broadcasted_iota(jnp.int32, (size, PAIR), 1)
    for low in range(0, key_ref.shape[0], size):
        high = low + size
        keys = key_ref[:high, :]
        values = value_ref[:high, :]
        queries = query_ref[low:high, :]
        allowed = allowed_keys(first_ref[:, low:high], low, high)
        results = []
        for head in range(2):
            scores = mm(keys, queries * head_lanes(head, HEAD_DIM ** (-0.5)), 1, 1)
            scores = jnp.where(allowed, scores, masked_fill)
            exp_scores = jnp.exp(scores - jnp.max(scores, axis=0, keepdims=True))
            inverse = 1.0 / jnp.sum(exp_scores, axis=0, keepdims=True)
            results.append(mm((exp_scores * inverse).astype(jnp.bfloat16), values, 0, 0))
        out_ref[low:high, :] = jnp.where(lane < HEAD_DIM, results[0], results[1]).astype(
            jnp.bfloat16
        )


def local_forward(heads, first_row):
    length = heads.shape[0]
    pairs = heads.shape[1] // (3 * PAIR)
    return pl.pallas_call(
        functools.partial(local_forward_kernel, min(256, length)),
        grid=(pairs,),
        in_specs=[
            pl.BlockSpec((1, length), lambda p: (0, 0)),
            pl.BlockSpec((length, PAIR), lambda p: (0, p)),
            pl.BlockSpec((length, PAIR), lambda p: (0, pairs + p)),
            pl.BlockSpec((length, PAIR), lambda p: (0, 2 * pairs + p)),
        ],
        out_specs=pl.BlockSpec((length, PAIR), lambda p: (0, p)),
        out_shape=jax.ShapeDtypeStruct((length, pairs * PAIR), jnp.bfloat16),
        compiler_params=pltpu.CompilerParams(vmem_limit_bytes=vmem_bytes),
        cost_estimate=cost(16 * length * length * pairs * PAIR, 8 * heads.size),
    )(first_row, heads, heads, heads)


def local_backward_kernel(
    size, first_ref, query_ref, grad_ref, key_ref, value_ref, out_ref, key_sum, value_sum
):
    length = key_ref.shape[0]
    pair = pl.program_id(0)
    pairs = out_ref.shape[1] // (3 * PAIR)
    scale = HEAD_DIM ** (-0.5)
    lane = lax.broadcasted_iota(jnp.int32, (size, PAIR), 1)

    def lanes(part):
        return pl.ds(pl.multiple_of((part * pairs + pair) * PAIR, PAIR), PAIR)

    for low in range(length - size, -1, -size):
        high = low + size
        keys = key_ref[:high, :]
        values = value_ref[:high, :]
        queries = query_ref[low:high, :]
        grads = grad_ref[low:high, :]
        allowed = allowed_keys(first_ref[:, low:high], low, high)
        query_grads = []
        for head in range(2):
            scaled = queries * head_lanes(head, scale)
            grad = grads * head_lanes(head, 1.0)
            scores = jnp.where(allowed, mm(keys, scaled, 1, 1), masked_fill)
            exp_scores = jnp.exp(scores - jnp.max(scores, axis=0, keepdims=True))
            probs = exp_scores * (1.0 / jnp.sum(exp_scores, axis=0, keepdims=True))
            prob_grad = mm(values, grad, 1, 1)
            row_dot = jnp.sum(probs * prob_grad, axis=0, keepdims=True)
            score_grad = (probs * (prob_grad - row_dot)).astype(jnp.bfloat16)
            value_part = mm(probs.astype(jnp.bfloat16), grad, 1, 0)
            key_part = mm(score_grad, scaled, 1, 0)
            query_grads.append(mm(score_grad, keys, 0, 0) * scale)
            if head == 0:
                key_add, value_add = key_part, value_part
            else:
                key_add, value_add = key_add + key_part, value_add + value_part
        if high == length:
            key_sum[...] = key_add
            value_sum[...] = value_add
        else:
            key_sum[:high, :] += key_add
            value_sum[:high, :] += value_add
        out_ref[low:high, lanes(0)] = jnp.where(
            lane < HEAD_DIM, query_grads[0], query_grads[1]
        ).astype(jnp.bfloat16)
    out_ref[:, lanes(1)] = key_sum[...].astype(jnp.bfloat16)
    out_ref[:, lanes(2)] = value_sum[...].astype(jnp.bfloat16)


def local_backward(heads, head_grad, group, first_row):
    length = heads.shape[0]
    pairs = heads.shape[1] // (3 * PAIR)
    return pl.pallas_call(
        functools.partial(local_backward_kernel, min(512, length)),
        grid=(pairs,),
        in_specs=[
            pl.BlockSpec((1, length), lambda p: (0, 0)),
            pl.BlockSpec((length, PAIR), lambda p: (0, p)),
            pl.BlockSpec((length, PAIR), lambda p: (0, group * pairs + p)),
            pl.BlockSpec((length, PAIR), lambda p: (0, pairs + p)),
            pl.BlockSpec((length, PAIR), lambda p: (0, 2 * pairs + p)),
        ],
        out_specs=pl.BlockSpec(heads.shape, lambda p: (0, 0)),
        out_shape=jax.ShapeDtypeStruct(heads.shape, jnp.bfloat16),
        scratch_shapes=[pltpu.VMEM((length, PAIR), jnp.float32)] * 2,
        compiler_params=pltpu.CompilerParams(vmem_limit_bytes=vmem_bytes),
        cost_estimate=cost(32 * length * length * pairs * PAIR, 8 * heads.size),
    )(first_row, heads, head_grad, heads, heads)


gelu_scale = 0.7978845608028654
gelu_cubic = 0.044715


def ffn_kernel(index_ref, *refs):
    normed, grads, pieces = refs[:2], refs[2:4], [r.at[0] for r in refs[4:6]]
    bias_ref, rows_ref, sum_ref, grad_out, down_out, grad_acc, down_acc = refs[6:]
    step = pl.program_id(0)
    width = normed[0].shape[1]
    quarter = pieces[0].shape[1] // 2
    ups, downs = slice(0, quarter), slice(quarter, 2 * quarter)
    pre = mm(normed[0][...], pieces[0][:, ups], 1, 0) + mm(normed[1][...], pieces[1][:, ups], 1, 0)
    pre = pre + bias_ref[0]
    act_grad = mm(grads[0][...], pieces[0][:, downs], 1, 0) + mm(grads[1][...], pieces[1][:, downs], 1, 0)
    square = pre * pre
    bent = jnp.tanh(gelu_scale * pre * (1.0 + gelu_cubic * square))
    half = 0.5 * (1.0 + bent)
    slope = half + 0.5 * gelu_scale * pre * (1.0 - bent * bent) * (1.0 + 3.0 * gelu_cubic * square)
    act = (pre * half).astype(jnp.bfloat16)
    pre_grad = (act_grad * slope).astype(jnp.bfloat16)
    rows_ref[:, :quarter] = act
    rows_ref[:, quarter:] = pre_grad
    sum_ref[0] = jnp.sum(pre_grad.astype(jnp.float32), axis=0, keepdims=True)

    @pl.when(step == 0)
    def _():
        for i in range(2):
            at = slice(i * width, (i + 1) * width)
            grad_acc[:, at] = mm(pre_grad, pieces[i][:, ups], 1, 1)
            down_acc[:, at] = mm(act, pieces[i][:, downs], 1, 1)

    @pl.when(step > 0)
    def _():
        for i in range(2):
            at = slice(i * width, (i + 1) * width)
            grad_acc[:, at] += mm(pre_grad, pieces[i][:, ups], 1, 1)
            down_acc[:, at] += mm(act, pieces[i][:, downs], 1, 1)

    @pl.when(step == pl.num_programs(0) - 1)
    def _():
        grad_out[...] = grad_acc[...].astype(jnp.bfloat16)
        down_out[...] = down_acc[...].astype(jnp.bfloat16)


def ffn_rows_of(index, normed, grads, part, pieces, bias):
    tokens, features = normed.shape
    width = features // 2
    columns = pieces.shape[2]
    ring, quarter = pieces.shape[0] // 2, columns // 2

    def halves(at):
        return [pl.BlockSpec((tokens, width), lambda k, s, h=h: (at, h)) for h in range(2)]

    piece = [
        pl.BlockSpec((1, width, columns), lambda k, s, h=h: ((s[0] ^ h) * ring + k, 0, 0))
        for h in range(2)
    ]
    whole = pl.BlockSpec((tokens, features), lambda k, s: (0, 0))
    vector = pl.BlockSpec((1, 1, quarter), lambda k, s: (k, 0, 0))
    return pl.pallas_call(
        ffn_kernel,
        grid_spec=pltpu.PrefetchScalarGridSpec(
            num_scalar_prefetch=1,
            grid=(ring,),
            in_specs=halves(0) + halves(part) + piece + [vector],
            out_specs=[pl.BlockSpec((tokens, columns), lambda k, s: (0, k)), vector, whole, whole],
            scratch_shapes=[pltpu.VMEM((tokens, features), jnp.float32)] * 2,
        ),
        out_shape=[
            shape((tokens, ring * columns)),
            shape((ring, 1, quarter), jnp.float32),
            shape((tokens, features)),
            shape((tokens, features)),
        ],
        compiler_params=params(),
        cost_estimate=cost(8 * tokens * features * ring * quarter, 12 * ring * width * columns),
    )(index, normed, normed, grads, grads, pieces, pieces, bias)


def weight_products_kernel(count, *refs):
    out_ref = refs[-1]
    normed, grads, rows = [refs[i * count : (i + 1) * count] for i in range(3)]
    quarter = rows[0].shape[1] // 2
    up = down = None
    for j in range(count):
        up_part = mm(normed[j][...], rows[j][:, quarter:], 0, 0)
        down_part = mm(grads[j][...], rows[j][:, :quarter], 0, 0)
        up = up_part if up is None else up + up_part
        down = down_part if down is None else down + down_part
    out_ref[0, :, :quarter] = up.astype(jnp.bfloat16)
    out_ref[0, :, quarter:] = down.astype(jnp.bfloat16)


def weight_products(normed, grads, rows, half):
    count = len(normed)
    tokens, features = normed[0].shape
    width = features // 2
    ring = 4
    columns = rows[0].shape[1] // ring
    size = min(512, width)
    blocks = width // size
    left = [pl.BlockSpec((tokens, size), lambda k, d: (0, half * blocks + d))] * count
    left += [
        pl.BlockSpec((tokens, size), lambda k, d, j=j: (j, half * blocks + d)) for j in range(count)
    ]
    return pl.pallas_call(
        functools.partial(weight_products_kernel, count),
        grid=(ring, blocks),
        in_specs=left + [pl.BlockSpec((tokens, columns), lambda k, d: (0, k))] * count,
        out_specs=pl.BlockSpec((1, size, columns), lambda k, d: (k, d, 0)),
        out_shape=shape((ring, width, columns)),
        compiler_params=params(),
        cost_estimate=cost(
            2 * count * tokens * width * ring * columns, 4 * count * tokens * features * ring
        ),
    )(*normed, *([grads] * count), *rows)


def params(**more):
    return pltpu.CompilerParams(vmem_limit_bytes=vmem_bytes, **more)


def cost(flops, nbytes):
    return pl.CostEstimate(flops=flops // 10, bytes_accessed=nbytes // 10, transcendentals=0)


def shape(dims, dtype=jnp.bfloat16):
    return jax.ShapeDtypeStruct(dims, dtype)


def turned(values):
    return values.astype(jnp.float32).T.astype(jnp.bfloat16)


def pack_heads_kernel(index_ref, *refs):
    sources, outs = refs[:8], refs[8:]
    own = sources[0].shape[1]
    for which in range(2):
        for i in range(4):
            part = sources[4 * which + i][...]
            outs[which][:, i * own : (i + 1) * own] = part if i < 3 else turned(part)


def pack_heads(index, weights, count):
    width, units = weights[0].shape
    own, block = units // 2, width // 4

    def feature(which):
        return pl.BlockSpec((block, own), lambda j, s: (s[1] ^ j, s[0] ^ which))

    def turned_block(which):
        return pl.BlockSpec((own, block), lambda j, s: (s[0] ^ which, s[1] ^ j))

    in_specs = []
    for which in range(2):
        in_specs += [feature(which)] * 3 + [turned_block(which)]
    return pl.pallas_call(
        pack_heads_kernel,
        grid_spec=pltpu.PrefetchScalarGridSpec(
            num_scalar_prefetch=1,
            grid=(count,),
            in_specs=in_specs,
            out_specs=[pl.BlockSpec((block, 4 * own), lambda j, s: (j, 0))] * 2,
        ),
        out_shape=[shape((count * block, 4 * own))] * 2,
        compiler_params=params(),
        cost_estimate=cost(0, 32 * count * block * own),
    )(index, *weights, *weights)


def pack_ff_kernel(index_ref, up_ref, down_ref, out_ref):
    quarter = up_ref.shape[1]
    out_ref[:, :quarter] = up_ref[...]
    out_ref[:, quarter:] = turned(down_ref[...])


def pack_ff(index, up_weight, down_weight):
    width, units = up_weight.shape
    quarter, block = units // 4, width // 4
    return pl.pallas_call(
        pack_ff_kernel,
        grid_spec=pltpu.PrefetchScalarGridSpec(
            num_scalar_prefetch=1,
            grid=(4,),
            in_specs=[
                pl.BlockSpec((block, quarter), lambda d, s: (d, s[1])),
                pl.BlockSpec((quarter, block), lambda d, s: (s[1], d)),
            ],
            out_specs=pl.BlockSpec((block, 2 * quarter), lambda d, s: (d, 0)),
        ),
        out_shape=shape((width, 2 * quarter)),
        compiler_params=params(),
        cost_estimate=cost(0, 8 * width * quarter),
    )(index, up_weight, down_weight)


def stack_kernel(*refs):
    pieces, outs = refs[:3], refs[-2:]
    block = pieces[0].shape[0] // 2
    for j, piece in enumerate(pieces):
        for i in range(2):
            outs[i][j * block : (j + 1) * block, :] = piece[i * block : (i + 1) * block, :]
    for i in range(2):
        outs[i][3 * block :, :] = refs[3 + i][...]


def stack_pieces(pieces):
    rows, columns = pieces[0].shape
    return pl.pallas_call(
        stack_kernel,
        out_shape=[shape((2 * rows, columns))] * 2,
        compiler_params=params(),
        cost_estimate=cost(0, 16 * rows * columns),
    )(*pieces)


def norm_kernel(index_ref, own_ref, sib_ref, vectors_ref, out_ref, stats_ref):
    own = own_ref[...].astype(jnp.float32)
    sib = sib_ref[...].astype(jnp.float32)
    width = own.shape[1]
    average = (jnp.sum(own, axis=1, keepdims=True) + jnp.sum(sib, axis=1, keepdims=True)) / (2 * width)
    own, sib = own - average, sib - average
    square = jnp.sum(own * own, axis=1, keepdims=True) + jnp.sum(sib * sib, axis=1, keepdims=True)
    inverse = lax.rsqrt(square / (2 * width) + norm_eps)
    block = width // 4
    for half, values in enumerate((own, sib)):
        gain, shift = vectors_ref[2 * half, :][None], vectors_ref[2 * half + 1, :][None]
        rounded = (values * inverse * gain + shift).astype(jnp.bfloat16)
        for i in range(4):
            at = pl.multiple_of(half * width + (index_ref[1] ^ i) * block, block)
            out_ref[:, pl.ds(at, block)] = rounded[:, i * block : (i + 1) * block]
    lane = lax.broadcasted_iota(jnp.int32, stats_ref.shape, 1)
    stats_ref[...] = jnp.where(lane == 0, average, inverse)


def norm_rows(index, own, sib, vectors):
    tokens, width = own.shape
    size = min(256, tokens)
    rows = pl.BlockSpec((size, width), lambda i, s: (i, 0))
    return pl.pallas_call(
        norm_kernel,
        grid_spec=pltpu.PrefetchScalarGridSpec(
            num_scalar_prefetch=1,
            grid=(tokens // size,),
            in_specs=[rows, rows, pl.BlockSpec((4, width), lambda i, s: (0, 0))],
            out_specs=[
                pl.BlockSpec((size, 2 * width), lambda i, s: (i, 0)),
                pl.BlockSpec((size, 128), lambda i, s: (i, 0)),
            ],
        ),
        out_shape=[shape((tokens, 2 * width)), shape((tokens, 128), jnp.float32)],
        compiler_params=params(),
        cost_estimate=cost(0, 8 * tokens * width),
    )(index, own, sib, vectors)


def project_kernel(own_ref, sib_ref, own_weight, sib_weight, bias_ref, out_ref):
    total = mm(own_ref[...], own_weight[...], 1, 0) + mm(sib_ref[...], sib_weight[...], 1, 0)
    out_ref[...] = (total + bias_ref[...]).astype(jnp.bfloat16)


def halves_of(size, width):
    return [pl.BlockSpec((size, width), lambda i, h=h: (i, h)) for h in range(2)]


def project(normed, own_weight, sib_weight, bias):
    tokens, features = normed.shape
    width, units = features // 2, bias.shape[1]
    size = min(256, tokens)
    weight = pl.BlockSpec((width, units), lambda i: (0, 0))
    return pl.pallas_call(
        project_kernel,
        grid=(tokens // size,),
        in_specs=halves_of(size, width)
        + [weight, weight, pl.BlockSpec((1, units), lambda i: (0, 0))],
        out_specs=pl.BlockSpec((size, units), lambda i: (i, 0)),
        out_shape=shape((tokens, units)),
        compiler_params=params(),
        cost_estimate=cost(4 * tokens * width * units, 4 * tokens * width + 4 * width * units),
    )(normed, normed, own_weight, sib_weight, bias)


def sum_rows_kernel(count, *refs):
    out_ref = refs[-1]
    width = refs[count].shape[0]
    for half in range(2):
        at = slice(half * width, (half + 1) * width)
        total = refs[3 * count][:, at] if len(refs) > 3 * count + 1 else None
        for k in range(count):
            part = mm(refs[k][...], refs[(1 + half) * count + k][...], 1, 1)
            total = part if total is None else total + part
        out_ref[:, at] = total


def sum_rows(rows, own_weights, sib_weights, at, before=()):
    count = len(rows)
    tokens, units = rows[0].shape
    width = own_weights[0].shape[0]
    size = min(512, tokens)
    full = pl.BlockSpec((size, 2 * width), lambda i: (i, 0))
    return pl.pallas_call(
        functools.partial(sum_rows_kernel, count),
        grid=(tokens // size,),
        in_specs=[pl.BlockSpec((size, units), lambda i: (i, 0))] * count
        + [pl.BlockSpec((width, units), lambda i: (0, at))] * (2 * count)
        + [full] * len(before),
        out_specs=full,
        out_shape=shape((tokens, 2 * width), jnp.float32),
        compiler_params=params(),
        cost_estimate=cost(4 * count * tokens * units * width, 8 * tokens * width),
    )(*rows, *own_weights, *sib_weights, *before)


def head_grads_kernel(own_ref, sib_ref, *refs):
    out_ref = refs[-1]
    count = (len(refs) - 1) // 2
    own = refs[0].shape[1]
    for k in range(count):
        total = mm(own_ref[...], refs[k][...], 1, 0) + mm(sib_ref[...], refs[count + k][...], 1, 0)
        out_ref[:, k * own : (k + 1) * own] = total.astype(jnp.bfloat16)


def head_grads(grads, own_weights, sib_weights):
    tokens, width = grads.shape[0], grads.shape[1] // 2
    count = len(own_weights)
    units = own_weights[0].shape[1] // 4
    size = min(256, tokens)
    return pl.pallas_call(
        head_grads_kernel,
        grid=(tokens // size,),
        in_specs=halves_of(size, width) + [pl.BlockSpec((width, units), lambda i: (0, 3))] * (2 * count),
        out_specs=pl.BlockSpec((size, count * units), lambda i: (i, 0)),
        out_shape=shape((tokens, count * units)),
        compiler_params=params(),
        cost_estimate=cost(4 * count * tokens * width * units, 8 * tokens * width),
    )(grads, grads, *own_weights, *sib_weights)


def head_products_kernel(*refs):
    normed, grads = refs[:2], refs[2:4]
    heads_ref, attended_ref = refs[4:6]
    outs, sum_ref = refs[6:8], refs[8]
    split = heads_ref.shape[1]
    for i in range(2):
        outs[i][:, :split] = mm(normed[i][...], heads_ref[...], 0, 0).astype(jnp.bfloat16)
        outs[i][:, split:] = mm(grads[i][...], attended_ref[...], 0, 0).astype(jnp.bfloat16)

    @pl.when(pl.program_id(0) == 0)
    def _():
        sum_ref[...] = jnp.sum(heads_ref[...].astype(jnp.float32), axis=0, keepdims=True)


def head_products(normed, grads, head_grad, attended):
    tokens, width = normed.shape[0], normed.shape[1] // 2
    split, own = head_grad.shape[1], attended.shape[1]
    size = min(512, width)
    blocks = width // size
    left = [pl.BlockSpec((tokens, size), lambda d, h=h: (0, h * blocks + d)) for h in range(2)]
    out = pl.BlockSpec((size, split + own), lambda d: (d, 0))
    return pl.pallas_call(
        head_products_kernel,
        grid=(width // size,),
        in_specs=left * 2
        + [pl.BlockSpec((tokens, split), lambda d: (0, 0)), pl.BlockSpec((tokens, own), lambda d: (0, 0))],
        out_specs=[out, out, pl.BlockSpec((1, split), lambda d: (0, 0))],
        out_shape=[shape((width, split + own))] * 2 + [shape((1, split), jnp.float32)],
        compiler_params=params(),
        cost_estimate=cost(4 * tokens * width * (split + own), 12 * tokens * width),
    )(normed, normed, grads, grads, head_grad, attended)


def block_at(half, width, place):
    block = width // 4
    return pl.ds(pl.multiple_of(half * width + place * block, block), block)


def norm_two_kernel(
    index_ref, rows_ref, came_ref, own_ref, sib_ref, vectors_ref, hidden_ref, normed_ref, stats_ref
):
    width = own_ref.shape[1]
    block = width // 4
    for half, tokens_ref in enumerate((own_ref, sib_ref)):
        for i in range(4):
            at = block_at(half, width, index_ref[1] ^ i)
            span = slice(half * width + i * block, half * width + (i + 1) * block)
            hidden_ref[:, span] = (
                tokens_ref[:, i * block : (i + 1) * block].astype(jnp.float32)
                + rows_ref[:, at]
                + came_ref[:, at].astype(jnp.float32)
                + vectors_ref[4:5, span]
            )
    hidden = hidden_ref[...]
    average = jnp.mean(hidden, axis=1, keepdims=True)
    centered = hidden - average
    inverse = lax.rsqrt(jnp.mean(centered * centered, axis=1, keepdims=True) + norm_eps)
    normed_ref[...] = (centered * inverse * vectors_ref[2:3, :] + vectors_ref[3:4, :]).astype(jnp.bfloat16)
    lane = lax.broadcasted_iota(jnp.int32, stats_ref.shape, 1)
    stats_ref[...] = jnp.where(lane == 0, average, inverse)


def my_rows(size, columns, blocks):
    return pl.BlockSpec((size, columns), lambda i, s: (s[0] * blocks + i, 0))


def norm_two(index, rows, came, own, sib, vectors):
    tokens, features = came.shape
    size = tokens // 2
    mine = my_rows(size, features // 2, 2)
    plain = pl.BlockSpec((size, features), lambda i, s: (i, 0))
    return pl.pallas_call(
        norm_two_kernel,
        grid_spec=pltpu.PrefetchScalarGridSpec(
            num_scalar_prefetch=1,
            grid=(2,),
            in_specs=[
                my_rows(size, features, 2),
                plain,
                mine,
                mine,
                pl.BlockSpec(vectors.shape, lambda i, s: (0, 0)),
            ],
            out_specs=[plain, plain, pl.BlockSpec((size, 128), lambda i, s: (i, 0))],
        ),
        out_shape=[
            shape((tokens, features), jnp.float32),
            shape((tokens, features)),
            shape((tokens, 128), jnp.float32),
        ],
        compiler_params=params(),
        cost_estimate=cost(0, 16 * tokens * features),
    )(index, rows, came, own, sib, vectors)


def norm_pull(grads, normal, inverse, gain):
    scaled = grads * gain
    return inverse * (
        scaled
        - jnp.mean(scaled, axis=1, keepdims=True)
        - normal * jnp.mean(scaled * normal, axis=1, keepdims=True)
    )


def add_sums(sums_ref, parts):
    rows = [jnp.sum(p, axis=0, keepdims=True) for p in parts]
    rows += [jnp.zeros_like(rows[0])] * (8 - len(rows))
    total = jnp.concatenate(rows, axis=0)

    @pl.when(pl.program_id(0) == 0)
    def _():
        sums_ref[...] = total

    @pl.when(pl.program_id(0) > 0)
    def _():
        sums_ref[...] += total


def norm_two_back_kernel(index_ref, *refs):
    here, x_top, y_top, x_bottom, y_bottom, hidden_ref, stats_ref, branch_ref, vectors_ref = refs[:9]
    grad_ref, blocks_ref, mirror_ref, sums_ref = refs[9:]
    f32 = jnp.float32
    top = pl.program_id(0) == 0
    from_x = jnp.where(top, x_top[...].astype(f32), x_bottom[...].astype(f32))
    from_y = jnp.where(top, y_top[...].astype(f32), y_bottom[...].astype(f32))
    grads = here[...].astype(f32) + from_x + from_y
    inverse = stats_ref[:, 1:2]
    normal = (hidden_ref[...] - stats_ref[:, :1]) * inverse
    branch = branch_ref[...].astype(f32)
    total = branch + norm_pull(grads, normal, inverse, vectors_ref[2:3, :])
    grad_ref[...] = total
    rounded = total.astype(jnp.bfloat16)
    width = rounded.shape[1] // 2
    block = width // 4
    for half in range(2):
        for i in range(4):
            part = rounded[:, half * width + i * block : half * width + (i + 1) * block]
            place = index_ref[1] ^ i
            blocks_ref[:, block_at(half, width, place)] = part
            mirror_ref[:, block_at(1 - half, width, place)] = part
    add_sums(sums_ref, (grads * normal, grads, rounded.astype(f32), branch))


def norm_two_back(index, parts, hidden, stats, branch, vectors):
    tokens, features = hidden.shape
    size = tokens // 2
    plain = pl.BlockSpec((size, features), lambda i, s: (i, 0))
    once = pl.BlockSpec((size, features), lambda i, s: (0, 0))
    return pl.pallas_call(
        norm_two_back_kernel,
        grid_spec=pltpu.PrefetchScalarGridSpec(
            num_scalar_prefetch=1,
            grid=(2,),
            in_specs=[plain]
            + [once] * 4
            + [
                plain,
                pl.BlockSpec((size, 128), lambda i, s: (i, 0)),
                plain,
                pl.BlockSpec(vectors.shape, lambda i, s: (0, 0)),
            ],
            out_specs=[plain] * 3 + [pl.BlockSpec((8, features), lambda i, s: (0, 0))],
        ),
        out_shape=[
            shape((tokens, features), jnp.float32),
            shape((tokens, features)),
            shape((tokens, features)),
            shape((8, features), jnp.float32),
        ],
        compiler_params=params(),
        cost_estimate=cost(0, 24 * tokens * features),
    )(index, *parts, hidden, stats, branch, vectors)


def norm_one_back_kernel(index_ref, *refs):
    rows_ref, came_ref, own_ref, sib_ref, stats_ref, out_own, out_sib, keep_ref, hidden_ref = refs[:9]
    vectors_ref, own_grad, sib_grad, sums_ref, grads_ref = refs[9:]
    f32 = jnp.float32
    width = own_ref.shape[1]
    block = width // 4
    for half in range(2):
        for i in range(4):
            at = block_at(half, width, index_ref[1] ^ i)
            span = slice(half * width + i * block, half * width + (i + 1) * block)
            grads_ref[:, span] = rows_ref[:, at] + came_ref[:, at].astype(f32)
    grads = grads_ref[...]
    inverse = stats_ref[:, 1:2]
    tokens = jnp.concatenate([own_ref[...], sib_ref[...]], axis=1).astype(f32)
    normal = (tokens - stats_ref[:, :1]) * inverse
    total = hidden_ref[...] + norm_pull(grads, normal, inverse, vectors_ref[0:1, :])
    dropped = 1.0 - keep_ref[...]
    own_grad[...] = out_own[...].astype(f32) * dropped + total[:, :width]
    sib_grad[...] = out_sib[...].astype(f32) * dropped + total[:, width:]
    add_sums(sums_ref, (grads * normal, grads))


def norm_one_back(index, rows, came, own, sib, stats, out_own, out_sib, keep, hidden, vectors):
    tokens, features = came.shape
    size, width = tokens // 2, features // 2
    plain = pl.BlockSpec((size, features), lambda i, s: (i, 0))
    half_wide = pl.BlockSpec((size, width), lambda i, s: (i, 0))
    return pl.pallas_call(
        norm_one_back_kernel,
        grid_spec=pltpu.PrefetchScalarGridSpec(
            num_scalar_prefetch=1,
            grid=(2,),
            in_specs=[
                my_rows(size, features, 2),
                plain,
                my_rows(size, width, 2),
                my_rows(size, width, 2),
                my_rows(size, 128, 2),
                my_rows(size, width, 2),
                half_wide,
                pl.BlockSpec((size, 1), lambda i, s: (i, 0)),
                plain,
                pl.BlockSpec(vectors.shape, lambda i, s: (0, 0)),
            ],
            out_specs=[half_wide, half_wide, pl.BlockSpec((8, features), lambda i, s: (0, 0))],
            scratch_shapes=[pltpu.VMEM((size, features), jnp.float32)],
        ),
        out_shape=[shape((tokens, width), jnp.float32)] * 2 + [shape((8, features), jnp.float32)],
        compiler_params=params(),
        cost_estimate=cost(0, 24 * tokens * features),
    )(index, rows, came, own, sib, stats, out_own, out_sib, keep, hidden, vectors)


def select_piece(refs, step, use):
    for j in range(3):

        @pl.when(step == j)
        def _():
            use(refs[j][...])

    @pl.when(step == 3)
    def _():
        use(jnp.concatenate([refs[3][...], refs[4][...]], axis=0))


def place_heads_kernel(index_ref, *refs):
    pieces, outs = refs[:5], refs[5:]
    own = pieces[0].shape[1] // 8

    def use(piece):
        for which in range(2):
            at = pl.multiple_of((index_ref[0] ^ which) * own, own)
            for m in range(4):
                part = piece[:, (4 * which + m) * own : (4 * which + m + 1) * own].astype(jnp.float32)
                if m < 3:
                    outs[m][:, pl.ds(at, own)] = part
                else:
                    outs[m][pl.ds(at, own), :] = part.T

    select_piece(pieces, pl.program_id(0), use)


def place_heads(index, pieces):
    block, columns = pieces[0].shape
    units, width = columns // 4, 4 * block
    whole = [pl.BlockSpec(p.shape, lambda j, s: (0, 0)) for p in pieces]
    return pl.pallas_call(
        place_heads_kernel,
        grid_spec=pltpu.PrefetchScalarGridSpec(
            num_scalar_prefetch=1,
            grid=(4,),
            in_specs=whole,
            out_specs=[pl.BlockSpec((block, units), lambda j, s: (s[1] ^ j, 0))] * 3
            + [pl.BlockSpec((units, block), lambda j, s: (0, s[1] ^ j))],
        ),
        out_shape=[shape((width, units), jnp.float32)] * 3 + [shape((units, width), jnp.float32)],
        compiler_params=params(),
        cost_estimate=cost(0, 24 * width * units),
    )(index, *pieces)


def place_ff_kernel(*refs):
    pieces, (up_out, down_out) = refs[:-2], refs[-2:]
    rows = pieces[0].shape[1]
    quarter = pieces[0].shape[2] // 2
    for part, piece in enumerate(pieces):
        span = slice(part * rows, (part + 1) * rows)
        up_out[span, :] = piece[0, :, :quarter].astype(jnp.float32)
        down_out[:, span] = piece[0, :, quarter:].astype(jnp.float32).T


def place_ff(pieces):
    count, rows, columns = pieces[0].shape
    width, quarter = rows * len(pieces), columns // 2
    return pl.pallas_call(
        place_ff_kernel,
        grid=(count,),
        in_specs=[pl.BlockSpec((1, rows, columns), lambda j: (j, 0, 0))] * len(pieces),
        out_specs=[
            pl.BlockSpec((width, quarter), lambda j: (0, j)),
            pl.BlockSpec((quarter, width), lambda j: (j, 0)),
        ],
        out_shape=[
            shape((width, count * quarter), jnp.float32),
            shape((count * quarter, width), jnp.float32),
        ],
        compiler_params=params(),
        cost_estimate=cost(0, 48 * width * quarter),
    )(*pieces)


def join_kernel(index_ref, mine_ref, first_ref, second_ref, out_ref):
    step = pl.program_id(0)

    @pl.when(step < 2)
    def _():
        out_ref[...] = mine_ref[...]

    @pl.when(step == 2)
    def _():
        out_ref[...] = first_ref[...]

    @pl.when(step == 3)
    def _():
        out_ref[...] = second_ref[...]


def join_tokens(index, mine, first, second):
    tokens, width = mine.shape
    size = tokens // 2
    once = pl.BlockSpec((size, width), lambda i, s: (0, 0))
    return pl.pallas_call(
        join_kernel,
        grid_spec=pltpu.PrefetchScalarGridSpec(
            num_scalar_prefetch=1,
            grid=(4,),
            in_specs=[pl.BlockSpec((size, width), lambda i, s: (jnp.minimum(i, 1), 0)), once, once],
            out_specs=pl.BlockSpec(
                (size, width), lambda i, s: (jnp.where(i < 2, s[0] * 2 + i, (1 - s[0]) * 2 + i - 2), 0)
            ),
        ),
        out_shape=shape((2 * tokens, width), mine.dtype),
        compiler_params=params(),
        cost_estimate=cost(0, 8 * tokens * width),
    )(index, mine, first, second)


def layer_out_kernel(*refs):
    here, x_top, y_top, x_bottom, y_bottom, hidden_ref, own_ref, sib_ref, keep_ref, vectors_ref = refs[1:11]
    own_out, sib_out = refs[11:]
    f32 = jnp.float32
    width = own_ref.shape[1]
    top = pl.program_id(0) == 0
    from_x = jnp.where(top, x_top[...].astype(f32), x_bottom[...].astype(f32))
    from_y = jnp.where(top, y_top[...].astype(f32), y_bottom[...].astype(f32))
    total = hidden_ref[...] + here[...].astype(f32) + from_x + from_y + vectors_ref[5:6, :]
    keep = keep_ref[...] > 0.5
    own_out[...] = jnp.where(keep, total[:, :width], own_ref[...].astype(f32))
    sib_out[...] = jnp.where(keep, total[:, width:], sib_ref[...].astype(f32))


def layer_rows(index, parts, hidden, own, sib, keep, vectors):
    tokens, features = hidden.shape
    size, width = tokens // 2, features // 2
    plain = pl.BlockSpec((size, features), lambda i, s: (i, 0))
    half_wide = pl.BlockSpec((size, width), lambda i, s: (i, 0))
    return pl.pallas_call(
        layer_out_kernel,
        grid_spec=pltpu.PrefetchScalarGridSpec(
            num_scalar_prefetch=1,
            grid=(2,),
            in_specs=[plain]
            + [pl.BlockSpec((size, features), lambda i, s: (0, 0))] * 4
            + [
                plain,
                my_rows(size, width, 2),
                my_rows(size, width, 2),
                pl.BlockSpec((size, 1), lambda i, s: (i, 0)),
                pl.BlockSpec(vectors.shape, lambda i, s: (0, 0)),
            ],
            out_specs=[half_wide, half_wide],
        ),
        out_shape=[shape((tokens, width), jnp.float32)] * 2,
        compiler_params=params(),
        cost_estimate=cost(0, 20 * tokens * features),
    )(index, *parts, hidden, own, sib, keep, vectors)


def body_local(
    tokens_in,
    out_grad,
    segment_ids,
    active_lengths,
    norm1_gain,
    norm1_shift,
    query_weight,
    query_bias,
    key_weight,
    value_weight,
    value_bias,
    out_weight,
    out_bias,
    norm2_gain,
    norm2_shift,
    up_weight,
    up_bias,
    down_weight,
    down_bias,
):
    f32, bf16 = jnp.float32, jnp.bfloat16
    rows, width = tokens_in.shape
    ring = lax.axis_size("col")
    row_i = lax.axis_index("row")
    plane_i = lax.axis_index("dp")
    col_i = lax.axis_index("col")
    own = query_weight.shape[1] // 2
    block = width // 4
    quarter = up_weight.shape[1] // 4
    unit = quarter // 2
    half = rows // 2
    order = Order()
    plane, column = Plane(order), Link(order)
    index = jnp.stack([row_i, plane_i, col_i]).astype(jnp.int32)

    def cut(values, start, size):
        return lax.dynamic_slice_in_dim(values, start, size, axis=0)

    def mirrored(values):
        return jnp.concatenate([values[:, width:], values[:, :width]], axis=1)

    def my_tokens(values):
        return cut(values, row_i * half, half)

    def other_tokens(values):
        return cut(values, (1 - row_i) * half, half)

    tokens_sib = order.swap(tokens_in)
    out_grad_sib = swap(other_tokens(out_grad))

    mine = jnp.concatenate(
        [
            cut(query_bias, row_i * own, own),
            jnp.zeros((own,), f32),
            cut(value_bias, row_i * own, own),
            cut(up_bias, plane_i * quarter, quarter),
        ]
    )
    small = [mine] + [
        lax.ppermute(mine, "col", [(i, (i + k) % ring) for i in range(ring)]) for k in range(1, ring)
    ]

    sources = (query_weight, key_weight, value_weight, out_weight)
    piece = order.run(pack_heads, after(index, mine), sources, 1)
    pieces = [jnp.concatenate([piece[0], swap(piece[1])], axis=0)]
    column.last = small[1:]
    pieces.append(column.send(step_up, pieces[0]))

    active_all = active_rows(segment_ids, active_lengths)
    active_here = my_tokens(cut(active_all, col_i * rows, rows))
    keep_mask = active_here.astype(f32)[:, None]
    out_grads = jnp.concatenate([my_tokens(out_grad), out_grad_sib], axis=1).astype(f32)
    branch_mine = (after(out_grads, *order.tokens) * keep_mask).astype(bf16)
    branch_first = plane.both(branch_mine[: half // 2], branch_mine[: half // 2])
    ff_piece = order.run(pack_ff, index, up_weight, down_weight)
    ff_pieces = lax.all_gather(ff_piece, ("row", "col"))
    vectors = jnp.stack([norm1_gain, norm1_shift, norm2_gain, norm2_shift, out_bias, down_bias])
    vectors_sib = swap(vectors)
    vectors_all = jnp.concatenate([vectors, vectors_sib], axis=1)
    pieces.append(column.send(step_up, pieces[1]))
    near = plane.both(pieces[1], pieces[1])
    here = order.run(pack_heads, index, sources, 4)
    own_parts, other_rows = [here[0]], [order.swap(here[1])]
    normed_one, stats_one = order.run(
        norm_rows,
        index,
        tokens_in,
        tokens_sib,
        jnp.concatenate([vectors[:2], vectors_sib[:2]], axis=0),
    )

    segment_row = picked(segment_ids, col_i)
    member = (segment_row[:, None] == jnp.arange(active_lengths.shape[1])).astype(jnp.int32)
    counts = jnp.sum(member, axis=0)
    first_row = jnp.sum(member * (jnp.cumsum(counts) - counts), axis=1)[None, :]

    heads, attended = [], []

    def attend_project(k):
        heads.append(
            order.run(project, normed_one, own_parts[k], other_rows[k], small[k][None, : 3 * own])
        )

    def attend(k):
        attended.append(order.run(local_forward, heads[k], first_row))

    def stack(k, near, far):
        own_part, other_part = order.run(stack_pieces, [pieces[k], *near, *far])
        own_parts.append(own_part)
        other_rows.append(other_part)

    attend_project(0)
    attend(0)
    far = plane.far(*near)
    pieces.append(column.send(step_up, pieces[2]))
    last_near, last_far = near, far
    near = plane.both(pieces[2], pieces[2])
    stack(1, last_near, last_far)
    attend_project(1)
    attend(1)
    far = plane.far(*near)
    last_near, last_far = near, far
    near = plane.both(pieces[3], pieces[3])
    stack(2, last_near, last_far)
    attend_project(2)
    attend(2)
    far = plane.far(*near)
    last_near, last_far = near, far
    branch_far = plane.far(*branch_first)
    stack(3, last_near, last_far)
    before = order.run(sum_rows, attended[:3], own_parts[:3], other_rows[:3], 3)
    second_near = plane.both(branch_mine[half // 2 :], branch_mine[half // 2 :])
    attend_project(3)
    attend(3)
    second_far = plane.far(*second_near)
    attention_rows = order.run(sum_rows, attended[3:], own_parts[3:], other_rows[3:], 3, (before,))
    arrived = swap(order.tie(mirrored(other_tokens(attention_rows)).astype(bf16)))

    order.tokens.append(ff_pieces)
    hidden_one, normed_two, stats_two = order.run(
        norm_two, index, attention_rows, arrived, tokens_in, tokens_sib, vectors_all
    )

    normed = [normed_two, *plane.both(normed_two, normed_two)]
    branch_all = jnp.concatenate(
        [branch_mine]
        + [part for pair in zip(branch_first, second_near) for part in pair]
        + [*branch_far, *second_far],
        axis=0,
    )
    def by_column(relative):
        places = jnp.mod(col_i - jnp.arange(ring), ring)
        return jnp.take(relative, places, axis=0)

    ff_biases = by_column(jnp.stack([s[None, 3 * own :] for s in small]))
    ff_rows, up_sums, grad_parts, down_parts = [], [], [], []

    def feed_forward(j):
        grads, part = (branch_all, j) if j > 0 else (branch_mine, 0)
        results = order.run(ffn_rows_of, index, normed[j], grads, part, ff_pieces, ff_biases)
        for kept, result in zip((ff_rows, up_sums, grad_parts, down_parts), results):
            kept.append(result)

    def top(values):
        return values[: half // 2]

    def bottom(values):
        return values[half // 2 :]

    def second_steps(parts, via_x, via_y):
        via_x, via_y = after((via_x, via_y), *order.tokens)
        return plane.both(add_rounded(bottom(parts[1]), via_y), add_rounded(top(parts[2]), via_x))

    def weight_grads(part):
        return order.run(weight_products, normed, branch_all, ff_rows, part)

    feed_forward(0)
    normed_far = plane.far(normed[1], normed[2])
    feed_forward(1)
    x_top = plane.x.send(step_x, top(grad_parts[1]))
    feed_forward(2)
    y_bottom = plane.y.send(step_y, bottom(grad_parts[2]))
    normed.append(jnp.concatenate(normed_far, axis=0))
    feed_forward(3)
    via_x, via_y = plane.both(top(grad_parts[3]), bottom(grad_parts[3]))
    ff_mine = weight_grads(0)
    x_bottom, y_top = second_steps(grad_parts, via_x, via_y)
    ff_other = order.swap(weight_grads(1))

    hidden_grad, grad_mine, grad_mirror, sums_two = order.run(
        norm_two_back,
        index,
        (grad_parts[0], x_top, y_top, x_bottom, y_bottom),
        hidden_one,
        stats_two,
        branch_mine,
        vectors_all,
    )
    down_x_top, down_y_bottom = plane.both(top(down_parts[1]), bottom(down_parts[2]))
    grad_others = [order.swap(top(grad_mirror)), order.swap(bottom(grad_mirror))]
    grad_rows = order.run(join_tokens, index, grad_mine, *grad_others)

    ff_grads = []
    for part in range(2):
        span = slice(part * width // 2, (part + 1) * width // 2)
        total = order.tie(add_rounded(ff_mine[:, span], ff_other[:, span]))
        ff_grads.append(lax.psum_scatter(total, "col", scatter_dimension=0, tiled=False))

    down_via_x, down_via_y = plane.both(top(down_parts[3]), bottom(down_parts[3]), True)
    head_grad = order.run(head_grads, grad_rows, own_parts, other_rows)
    head_rows, bias_rows, group_parts = [None] * ring, [None] * ring, [None] * ring

    def backward(k):
        head_rows[k] = order.run(
            lambda h, g, f: local_backward(h, g, k, f), heads[k], head_grad, first_row
        )

    def head_weights(k):
        *group_parts[k], bias_rows[k] = order.run(
            head_products, normed_one, grad_rows, head_rows[k], attended[k]
        )

    def part_of(k, j, which):
        return group_parts[k][which][j * block : (j + 1) * block]

    def first_messages(k):
        return plane.both(part_of(k, 3, 0), part_of(k, 3, 1), True)

    def second_messages(k, via):
        via_x, via_y = after(via, *order.tokens)
        return plane.both(
            jnp.concatenate([part_of(k, 1, 0), add_rounded(part_of(k, 1, 1), via_y)], axis=1),
            jnp.concatenate([add_rounded(part_of(k, 2, 0), via_x), part_of(k, 2, 1)], axis=1),
            k == 0,
        )

    def group_total(k, came, total):
        came_x, came_y = after(came, *order.tokens)
        here = jnp.concatenate([part_of(k, 0, 0), part_of(k, 0, 1)], axis=1)
        here = here.astype(f32) + came_x.astype(f32) + came_y.astype(f32)
        if total is not None:
            here = here + total.astype(f32)
        return here.astype(bf16)

    def layer_out_rows():
        own_out, sib_out = order.run(
            layer_rows,
            index,
            (down_parts[0], down_x_top, down_y_top, down_x_bottom, down_y_bottom),
            hidden_one,
            tokens_in,
            tokens_sib,
            keep_mask,
            vectors_all,
        )
        return own_out, order.swap(top(sib_out)), order.swap(bottom(sib_out))

    vias, came = [None] * ring, [None] * ring
    backward(3)
    head_weights(3)
    down_x_bottom, down_y_top = second_steps(down_parts, down_via_x, down_via_y)
    vias[3] = first_messages(3)
    backward(2)
    head_weights(2)
    vias[2] = first_messages(2)
    came[3] = second_messages(3, vias[3])
    order.tokens += [down_x_bottom, down_y_top]
    backward(1)
    head_weights(1)
    vias[1] = first_messages(1)
    came[2] = second_messages(2, vias[2])
    backward(0)
    order.tokens += came[3]
    head_weights(0)
    vias[0] = first_messages(0)
    came[1] = second_messages(1, vias[1])
    ff_grads = [lax.all_gather(after(g, *order.tokens), "dp") for g in ff_grads]
    total = column.send(step_down, group_total(3, came[3], None))
    order.tokens += came[2]
    back_rows = order.run(sum_rows, head_rows, own_parts, other_rows, 0)
    came[0] = second_messages(0, vias[0])
    arrived = order.swap(mirrored(other_tokens(back_rows)).astype(bf16))
    total = column.send(step_down, add_rounded(total, group_total(2, came[2], None)))
    layer_parts = layer_out_rows()

    input_mine, input_other, sums_one = order.run(
        norm_one_back,
        index,
        back_rows,
        arrived,
        tokens_in,
        tokens_sib,
        stats_one,
        out_grad,
        out_grad_sib,
        keep_mask,
        hidden_grad,
        vectors_all,
    )
    input_others = [order.swap(top(input_other)), order.swap(bottom(input_other))]
    total = column.send(step_down, add_rounded(total, group_total(1, came[1], None)))
    layer_out = order.run(join_tokens, index, *layer_parts)

    row_hot = (jnp.arange(2) == row_i).astype(f32)
    plane_hot = (jnp.arange(4) == plane_i).astype(f32)
    head_bias = by_column(jnp.stack(bias_rows)).reshape(ring, 3, 1, own) * row_hot[:, None]
    up_bias_part = sum(up_sums) * plane_hot[:, None]
    bias_vector = jnp.concatenate([head_bias.reshape(ring, -1), up_bias_part.reshape(ring, -1)], axis=1)
    feature_sums = jnp.concatenate([sums_one[:2], sums_two[:4]], axis=0)
    summed = jnp.concatenate([bias_vector.reshape(-1), feature_sums[:, :width].reshape(-1)])
    summed = summed + swap(
        jnp.concatenate([bias_vector.reshape(-1), feature_sums[:, width:].reshape(-1)])
    )

    summed = order.tie(summed)
    summed = summed + plane.x.send(step_x, summed)
    summed = summed + plane.y.send(step_y, summed)
    total = group_total(0, came[0], total)
    total = jnp.concatenate([total[:, : 4 * own], swap(total[:, 4 * own :])], axis=1)
    near = plane.both(total, total)
    step = 1
    while step < ring:
        pairs = [(i, i ^ step) for i in range(ring)]
        summed = summed + column.send(lambda v: lax.ppermute(v, "col", pairs), summed)
        step *= 2
    input_grad = order.run(join_tokens, index, input_mine, *input_others)
    far = plane.far(*near)
    up_weight_grad, down_weight_grad = order.run(place_ff, ff_grads)
    query_weight_grad, key_weight_grad, value_weight_grad, out_weight_grad = order.run(
        place_heads, index, [total, *near, *far]
    )

    bias_here = picked(summed[: bias_vector.size].reshape(ring, -1), col_i)
    own_here = summed[bias_vector.size :].reshape(6, width)
    size = 2 * own
    return (
        layer_out,
        input_grad,
        own_here[0],
        own_here[1],
        query_weight_grad,
        bias_here[:size],
        key_weight_grad,
        value_weight_grad,
        bias_here[2 * size : 3 * size],
        out_weight_grad,
        own_here[4],
        own_here[2],
        own_here[3],
        up_weight_grad,
        bias_here[3 * size :],
        down_weight_grad,
        own_here[5],
    )


def body(tokens_in, out_grad, segment_ids, *rest):
    ring = lax.axis_size("col")
    local = (
        lax.axis_size("dp") == 4
        and lax.axis_size("row") == 2
        and ring == 4
        and tokens_in.shape[0] == segment_ids.shape[1]
    )
    chosen = body_local if local else body_general
    return chosen(tokens_in, out_grad, segment_ids, *rest)


def solution(mesh):
    placed = (
        P(("dp", "col"), "row"),
        P(("dp", "col"), "row"),
        P("dp", None),
        P("dp", None),
        P("row"),
        P("row"),
        P("row", "col"),
        P("col"),
        P("row", "col"),
        P("row", "col"),
        P("col"),
        P("col", "row"),
        P("row"),
        P("row"),
        P("row"),
        P("row", "col"),
        P("col"),
        P("col", "row"),
        P("row"),
    )
    return jax.shard_map(
        body,
        mesh=mesh,
        in_specs=placed,
        out_specs=(
            P(("dp", "col"), "row"),
            P(("dp", "col"), "row"),
            P("row"),
            P("row"),
            P("row", "col"),
            P("col"),
            P("row", "col"),
            P("row", "col"),
            P("col"),
            P("col", "row"),
            P("row"),
            P("row"),
            P("row"),
            P("row", "col"),
            P("col"),
            P("col", "row"),
            P("row"),
        ),
        check_vma=False,
    )
```

```python
import functools

import jax
import jax.numpy as jnp
from jax import lax
from jax.experimental import pallas as pl
from jax.experimental.pallas import tpu as pltpu
from jax.sharding import PartitionSpec as P

D = 2048
HEAD_DIM = 64


norm_eps = 1e-05
masked_fill = -1e30


def width_totals(total_one, total_two):
    return lax.psum((total_one, total_two), "row")


def token_gather(values):
    return lax.all_gather(values, "col", axis=0, tiled=True)


def token_sums(partial_rows):
    return lax.psum_scatter(partial_rows, "col", scatter_dimension=0, tiled=True)


def unit_gather(values):
    return lax.all_gather(values, "row", axis=1, tiled=True)


def unit_sums(partial_units):
    return lax.psum_scatter(partial_units, "row", scatter_dimension=1, tiled=True)


def gelu_value(values):
    return jax.nn.gelu(values, approximate=True)


def gelu_slope(values):
    result, pullback = jax.vjp(gelu_value, values)
    return pullback(jnp.ones_like(values))[0]


def active_rows(segment_rows, keep_lengths):
    doc_index = jnp.arange(keep_lengths.shape[-1], dtype=jnp.int32)
    member = (segment_rows[:, :, None] == doc_index).astype(jnp.int32)
    counts = jnp.sum(member, axis=1)
    starts = jnp.cumsum(counts, axis=1) - counts
    first_pos = jnp.sum(member * starts[:, None, :], axis=2)
    keep_here = jnp.sum(member * keep_lengths[:, None, :], axis=2)
    position_in = jnp.arange(segment_rows.shape[1], dtype=jnp.int32)[None, :] - first_pos
    return (position_in < keep_here).reshape(-1)


def norm_forward(values, gain_part, shift_part):
    total_one, total_two = width_totals(jnp.sum(values, axis=1), jnp.sum(values * values, axis=1))
    average = total_one / D
    variance = total_two / D - average * average
    inverse = lax.rsqrt(variance + norm_eps)
    normal = (values - average[:, None]) * inverse[:, None]
    return ((normal * gain_part + shift_part).astype(jnp.bfloat16), normal, inverse)


def norm_backward(grad_rows, normal, inverse, gain_part):
    scaled = grad_rows * gain_part
    total_one, total_two = width_totals(jnp.sum(scaled, axis=1), jnp.sum(scaled * normal, axis=1))
    grad_in = inverse[:, None] * (
        scaled - total_one[:, None] / D - normal * (total_two[:, None] / D)
    )
    return (grad_in, jnp.sum(grad_rows * normal, axis=0), jnp.sum(grad_rows, axis=0))


def allowed_mask(segment_row, offset, block_rows):
    key_pos = jnp.arange(segment_row.shape[0], dtype=jnp.int32)
    query_pos = key_pos[offset : offset + block_rows]
    same_doc = segment_row[None, :] == segment_row[offset : offset + block_rows, None]
    return (key_pos[None, :] <= query_pos[:, None]) & same_doc


def attend_forward(query_seq, key_seq, value_seq, segment_row, score_scale):
    seq_length = query_seq.shape[2]
    block_rows = min(512, seq_length)
    outputs = []
    log_parts = []
    for offset in range(0, seq_length, block_rows):
        query_block = query_seq[:, :, offset : offset + block_rows]
        scores = (
            jnp.einsum("hdq,hdk->hqk", query_block, key_seq, preferred_element_type=jnp.float32)
            * score_scale
        )
        scores = jnp.where(allowed_mask(segment_row, offset, block_rows)[None], scores, masked_fill)
        row_max = jnp.max(scores, axis=2, keepdims=True)
        exp_scores = jnp.exp(scores - row_max)
        row_total = jnp.sum(exp_scores, axis=2, keepdims=True)
        weights = (exp_scores / row_total).astype(jnp.bfloat16)
        outputs.append(
            jnp.einsum("hqk,hdk->hdq", weights, value_seq, preferred_element_type=jnp.float32)
        )
        log_parts.append((row_max + jnp.log(row_total))[:, :, 0])
    return (jnp.concatenate(outputs, axis=2), jnp.concatenate(log_parts, axis=1))


def attend_backward(query_seq, key_seq, value_seq, grad_seq, segment_row, log_sums, score_scale):
    seq_length = query_seq.shape[2]
    block_rows = min(512, seq_length)
    key_grad = jnp.zeros(key_seq.shape, jnp.float32)
    value_grad = jnp.zeros(value_seq.shape, jnp.float32)
    query_grads = []
    for offset in range(0, seq_length, block_rows):
        query_block = query_seq[:, :, offset : offset + block_rows]
        grad_block = grad_seq[:, :, offset : offset + block_rows]
        scores = (
            jnp.einsum("hdq,hdk->hqk", query_block, key_seq, preferred_element_type=jnp.float32)
            * score_scale
        )
        scores = jnp.where(allowed_mask(segment_row, offset, block_rows)[None], scores, masked_fill)
        probs = jnp.exp(scores - log_sums[:, offset : offset + block_rows, None])
        prob_grad = jnp.einsum(
            "hdq,hdk->hqk", grad_block, value_seq, preferred_element_type=jnp.float32
        )
        row_dot = jnp.sum(probs * prob_grad, axis=2, keepdims=True)
        score_grad = (probs * (prob_grad - row_dot)).astype(jnp.bfloat16)
        query_grads.append(
            jnp.einsum("hqk,hdk->hdq", score_grad, key_seq, preferred_element_type=jnp.float32)
            * score_scale
        )
        key_grad = (
            key_grad
            + jnp.einsum(
                "hqk,hdq->hdk", score_grad, query_block, preferred_element_type=jnp.float32
            )
            * score_scale
        )
        value_grad = value_grad + jnp.einsum(
            "hqk,hdq->hdk",
            probs.astype(jnp.bfloat16),
            grad_block,
            preferred_element_type=jnp.float32,
        )
    return (jnp.concatenate(query_grads, axis=2), key_grad, value_grad)


def body_general(
    tokens_in,
    out_grad,
    segment_ids,
    active_lengths,
    norm1_gain,
    norm1_shift,
    query_weight,
    query_bias,
    key_weight,
    value_weight,
    value_bias,
    out_weight,
    out_bias,
    norm2_gain,
    norm2_shift,
    up_weight,
    up_bias,
    down_weight,
    down_bias,
):
    local_rows = tokens_in.shape[0]
    seq_here = segment_ids.shape[0]
    seq_length = segment_ids.shape[1]
    group_rows = seq_here * seq_length
    row_index = lax.axis_index("row")
    col_index = lax.axis_index("col")
    active_all = active_rows(segment_ids, active_lengths)
    active_here = lax.dynamic_slice_in_dim(active_all, col_index * local_rows, local_rows)
    keep_mask = active_here.astype(jnp.float32)[:, None]
    score_scale = HEAD_DIM ** (-0.5)
    rows_in = tokens_in.astype(jnp.float32)
    normed_one, normal_one, inverse_one = norm_forward(rows_in, norm1_gain, norm1_shift)
    gathered_one = token_gather(normed_one)
    stacked_weight = jnp.stack([query_weight, key_weight, value_weight])
    projected = unit_sums(
        jnp.einsum("td,kdh->kht", gathered_one, stacked_weight, preferred_element_type=jnp.float32)
    )
    head_width = projected.shape[1]
    head_count = head_width // HEAD_DIM
    query_part = lax.dynamic_slice_in_dim(query_bias, row_index * head_width, head_width)
    value_part = lax.dynamic_slice_in_dim(value_bias, row_index * head_width, head_width)
    bias_stack = jnp.stack([query_part, jnp.zeros_like(query_part), value_part])
    heads_all = (projected + bias_stack[:, :, None]).astype(jnp.bfloat16)

    def to_seqs(values):
        return jnp.moveaxis(values.reshape(head_count, HEAD_DIM, seq_here, seq_length), 2, 0)

    def from_seqs(values):
        return jnp.moveaxis(values, 0, 2).reshape(head_width, group_rows)

    query_seqs = to_seqs(heads_all[0])
    key_seqs = to_seqs(heads_all[1])
    value_seqs = to_seqs(heads_all[2])
    attended_seqs, log_sums = lax.map(
        lambda seq_items: attend_forward(
            seq_items[0], seq_items[1], seq_items[2], seq_items[3], score_scale
        ),
        (query_seqs, key_seqs, value_seqs, segment_ids),
    )
    attended = from_seqs(attended_seqs).astype(jnp.bfloat16)
    gathered_heads = unit_gather(attended[None])
    attention_rows = (
        token_sums(
            jnp.einsum("kht,hd->td", gathered_heads, out_weight, preferred_element_type=jnp.float32)
        )
        + out_bias
    )
    hidden_one = rows_in + attention_rows
    normed_two, normal_two, inverse_two = norm_forward(hidden_one, norm2_gain, norm2_shift)
    gathered_two = token_gather(normed_two)
    up_part = jnp.einsum("td,df->ft", gathered_two, up_weight, preferred_element_type=jnp.float32)[
        None
    ]
    unit_width = up_part.shape[1] // lax.axis_size("row")
    up_slice = lax.dynamic_slice_in_dim(up_bias, row_index * unit_width, unit_width)
    pre_act = unit_sums(up_part)[0] + up_slice[:, None]
    gathered_act = unit_gather(gelu_value(pre_act).astype(jnp.bfloat16)[None])
    ffn_rows = (
        token_sums(
            jnp.einsum("kft,fd->td", gathered_act, down_weight, preferred_element_type=jnp.float32)
        )
        + down_bias
    )
    layer_out = jnp.where(active_here[:, None], hidden_one + ffn_rows, rows_in)
    grad_rows = out_grad.astype(jnp.float32) * keep_mask
    branch_grad = token_gather(grad_rows.astype(jnp.bfloat16))
    down_grad = jnp.einsum(
        "kft,td->fd", gathered_act, branch_grad, preferred_element_type=jnp.float32
    )
    down_bias_grad = jnp.sum(branch_grad, axis=0, dtype=jnp.float32)
    act_part = jnp.einsum(
        "td,fd->ft", branch_grad, down_weight, preferred_element_type=jnp.float32
    )[None]
    act_grad = unit_sums(act_part)[0]
    pre_grad = (act_grad * gelu_slope(pre_act)).astype(jnp.bfloat16)
    gathered_pre = unit_gather(pre_grad[None])
    up_grad = jnp.einsum(
        "td,kft->df", gathered_two, gathered_pre, preferred_element_type=jnp.float32
    )
    up_bias_grad = jnp.sum(gathered_pre[0], axis=1, dtype=jnp.float32)
    normed_grad_two = token_sums(
        jnp.einsum("kft,df->td", gathered_pre, up_weight, preferred_element_type=jnp.float32)
    )
    back_two, gain_two_grad, shift_two_grad = norm_backward(
        normed_grad_two, normal_two, inverse_two, norm2_gain
    )
    hidden_grad = grad_rows + back_two
    attention_grad = token_gather(hidden_grad.astype(jnp.bfloat16))
    out_weight_grad = jnp.einsum(
        "kht,td->hd", gathered_heads, attention_grad, preferred_element_type=jnp.float32
    )
    out_bias_grad = jnp.sum(attention_grad, axis=0, dtype=jnp.float32)
    head_grad = unit_sums(
        jnp.einsum("td,hd->ht", attention_grad, out_weight, preferred_element_type=jnp.float32)[
            None
        ]
    )[0].astype(jnp.bfloat16)
    query_grads, key_grads, value_grads = lax.map(
        lambda seq_items: attend_backward(
            seq_items[0],
            seq_items[1],
            seq_items[2],
            seq_items[3],
            seq_items[4],
            seq_items[5],
            score_scale,
        ),
        (query_seqs, key_seqs, value_seqs, to_seqs(head_grad), segment_ids, log_sums),
    )
    stacked_grad = jnp.stack(
        [from_seqs(query_grads), from_seqs(key_grads), from_seqs(value_grads)]
    ).astype(jnp.bfloat16)
    gathered_grad = unit_gather(stacked_grad)
    stacked_weight_grad = jnp.einsum(
        "td,kht->kdh", gathered_one, gathered_grad, preferred_element_type=jnp.float32
    )
    query_bias_grad = jnp.sum(gathered_grad[0], axis=1, dtype=jnp.float32)
    value_bias_grad = jnp.sum(gathered_grad[2], axis=1, dtype=jnp.float32)
    normed_grad_one = token_sums(
        jnp.einsum("kht,kdh->td", gathered_grad, stacked_weight, preferred_element_type=jnp.float32)
    )
    back_one, gain_one_grad, shift_one_grad = norm_backward(
        normed_grad_one, normal_one, inverse_one, norm1_gain
    )
    input_grad = out_grad.astype(jnp.float32) * (1.0 - keep_mask) + hidden_grad + back_one
    (
        stacked_weight_grad,
        query_bias_grad,
        value_bias_grad,
        out_weight_grad,
        out_bias_grad,
        down_grad,
        down_bias_grad,
        up_grad,
        up_bias_grad,
    ) = lax.psum(
        (
            stacked_weight_grad,
            query_bias_grad,
            value_bias_grad,
            out_weight_grad,
            out_bias_grad,
            down_grad,
            down_bias_grad,
            up_grad,
            up_bias_grad,
        ),
        "dp",
    )
    gain_one_grad, shift_one_grad, gain_two_grad, shift_two_grad = lax.psum(
        (gain_one_grad, shift_one_grad, gain_two_grad, shift_two_grad), ("dp", "col")
    )
    return (
        layer_out,
        input_grad,
        gain_one_grad,
        shift_one_grad,
        stacked_weight_grad[0],
        query_bias_grad,
        stacked_weight_grad[1],
        stacked_weight_grad[2],
        value_bias_grad,
        out_weight_grad,
        out_bias_grad,
        gain_two_grad,
        shift_two_grad,
        up_grad,
        up_bias_grad,
        down_grad,
        down_bias_grad,
    )


def after(values, *others):
    return lax.optimization_barrier((values, others))[0]


def swap(values):
    return lax.ppermute(values, "row", [(0, 1), (1, 0)])


def step_x(values):
    return lax.ppermute(values, "dp", [(0, 1), (1, 0), (2, 3), (3, 2)])


def step_y(values):
    return lax.ppermute(values, "dp", [(0, 2), (2, 0), (1, 3), (3, 1)])


def step_up(values):
    count = lax.axis_size("col")
    return lax.ppermute(values, "col", [(i, (i + 1) % count) for i in range(count)])


def step_down(values):
    count = lax.axis_size("col")
    return lax.ppermute(values, "col", [(i, (i - 1) % count) for i in range(count)])


class Order:
    def __init__(self):
        self.tokens = []
        self.fresh, self.due = [], []

    def tie(self, values):
        if self.tokens:
            values = after(values, *self.tokens)
        self.tokens.append(values)
        return values

    def swap(self, values, due=True):
        arrived = swap(self.tie(values))
        if due:
            self.fresh.append(arrived)
        return arrived

    def run(self, function, first, *others):
        first = after(first, *self.tokens, *self.due) if self.tokens or self.due else first
        self.due, self.fresh = self.fresh, []
        result = function(first, *others)
        self.tokens = [jax.tree.leaves(result)[0]]
        return result


class Link:
    def __init__(self, order):
        self.order = order
        self.last = None

    def send(self, step, values, free=False):
        if self.last is not None and not free:
            values = after(values, self.last)
        self.last = step(self.order.tie(values))
        return self.last


class Plane:
    def __init__(self, order):
        self.x = Link(order)
        self.y = Link(order)

    def both(self, for_x, for_y, free=False):
        return self.x.send(step_x, for_x, free), self.y.send(step_y, for_y, free)

    def far(self, from_x, from_y):
        half = from_x.shape[0] // 2
        far_two, far_one = self.both(from_y[half:], from_x[:half])
        return far_one, far_two


def add_rounded(left, right):
    return (left.astype(jnp.float32) + right.astype(jnp.float32)).astype(jnp.bfloat16)


def ring_gather(link, values):
    held = [values]
    for _ in range(lax.axis_size("col") - 1):
        held.append(link.send(step_up, held[-1]))
    return held


def picked(stacked, index):
    return lax.dynamic_index_in_dim(stacked, index, 0, keepdims=False)


def mm(left, right, left_dim, right_dim, dtype=jnp.float32):
    return lax.dot_general(
        left, right, (((left_dim,), (right_dim,)), ((), ())), preferred_element_type=jnp.float32
    ).astype(dtype)


PAIR = 2 * HEAD_DIM
vmem_bytes = 48 * 1024 * 1024


def head_lanes(head, value):
    lane = lax.broadcasted_iota(jnp.int32, (1, PAIR), 1)
    return jnp.where(lane // HEAD_DIM == head, value, 0.0).astype(jnp.bfloat16)


def allowed_keys(first_row, low, high):
    key_pos = lax.broadcasted_iota(jnp.int32, (high, high - low), 0)
    query_pos = lax.broadcasted_iota(jnp.int32, (high, high - low), 1) + low
    return (key_pos >= first_row) & (key_pos <= query_pos)


def local_forward_kernel(size, first_ref, query_ref, key_ref, value_ref, out_ref):
    lane = lax.broadcasted_iota(jnp.int32, (size, PAIR), 1)
    for low in range(0, key_ref.shape[0], size):
        high = low + size
        keys = key_ref[:high, :]
        values = value_ref[:high, :]
        queries = query_ref[low:high, :]
        allowed = allowed_keys(first_ref[:, low:high], low, high)
        results = []
        for head in range(2):
            scores = mm(keys, queries * head_lanes(head, HEAD_DIM ** (-0.5)), 1, 1)
            scores = jnp.where(allowed, scores, masked_fill)
            exp_scores = jnp.exp(scores - jnp.max(scores, axis=0, keepdims=True))
            inverse = 1.0 / jnp.sum(exp_scores, axis=0, keepdims=True)
            results.append(mm((exp_scores * inverse).astype(jnp.bfloat16), values, 0, 0))
        out_ref[low:high, :] = jnp.where(lane < HEAD_DIM, results[0], results[1]).astype(
            jnp.bfloat16
        )


def local_forward(heads, first_row):
    length = heads.shape[0]
    pairs = heads.shape[1] // (3 * PAIR)
    return pl.pallas_call(
        functools.partial(local_forward_kernel, min(256, length)),
        grid=(pairs,),
        in_specs=[
            pl.BlockSpec((1, length), lambda p: (0, 0)),
            pl.BlockSpec((length, PAIR), lambda p: (0, p)),
            pl.BlockSpec((length, PAIR), lambda p: (0, pairs + p)),
            pl.BlockSpec((length, PAIR), lambda p: (0, 2 * pairs + p)),
        ],
        out_specs=pl.BlockSpec((length, PAIR), lambda p: (0, p)),
        out_shape=jax.ShapeDtypeStruct((length, pairs * PAIR), jnp.bfloat16),
        compiler_params=pltpu.CompilerParams(vmem_limit_bytes=vmem_bytes),
        cost_estimate=cost(16 * length * length * pairs * PAIR, 8 * heads.size),
    )(first_row, heads, heads, heads)


def local_backward_kernel(
    size, first_ref, query_ref, grad_ref, key_ref, value_ref, out_ref, key_sum, value_sum
):
    length = key_ref.shape[0]
    pair = pl.program_id(0)
    pairs = out_ref.shape[1] // (3 * PAIR)
    scale = HEAD_DIM ** (-0.5)
    lane = lax.broadcasted_iota(jnp.int32, (size, PAIR), 1)

    def lanes(part):
        return pl.ds(pl.multiple_of((part * pairs + pair) * PAIR, PAIR), PAIR)

    for low in range(length - size, -1, -size):
        high = low + size
        keys = key_ref[:high, :]
        values = value_ref[:high, :]
        queries = query_ref[low:high, :]
        grads = grad_ref[low:high, :]
        allowed = allowed_keys(first_ref[:, low:high], low, high)
        query_grads = []
        for head in range(2):
            scaled = queries * head_lanes(head, scale)
            grad = grads * head_lanes(head, 1.0)
            scores = jnp.where(allowed, mm(keys, scaled, 1, 1), masked_fill)
            exp_scores = jnp.exp(scores - jnp.max(scores, axis=0, keepdims=True))
            probs = exp_scores * (1.0 / jnp.sum(exp_scores, axis=0, keepdims=True))
            prob_grad = mm(values, grad, 1, 1)
            row_dot = jnp.sum(probs * prob_grad, axis=0, keepdims=True)
            score_grad = (probs * (prob_grad - row_dot)).astype(jnp.bfloat16)
            value_part = mm(probs.astype(jnp.bfloat16), grad, 1, 0)
            key_part = mm(score_grad, scaled, 1, 0)
            query_grads.append(mm(score_grad, keys, 0, 0) * scale)
            if head == 0:
                key_add, value_add = key_part, value_part
            else:
                key_add, value_add = key_add + key_part, value_add + value_part
        if high == length:
            key_sum[...] = key_add
            value_sum[...] = value_add
        else:
            key_sum[:high, :] += key_add
            value_sum[:high, :] += value_add
        out_ref[low:high, lanes(0)] = jnp.where(
            lane < HEAD_DIM, query_grads[0], query_grads[1]
        ).astype(jnp.bfloat16)
    out_ref[:, lanes(1)] = key_sum[...].astype(jnp.bfloat16)
    out_ref[:, lanes(2)] = value_sum[...].astype(jnp.bfloat16)


def local_backward(heads, head_grad, group, first_row):
    length = heads.shape[0]
    pairs = heads.shape[1] // (3 * PAIR)
    return pl.pallas_call(
        functools.partial(local_backward_kernel, min(512, length)),
        grid=(pairs,),
        in_specs=[
            pl.BlockSpec((1, length), lambda p: (0, 0)),
            pl.BlockSpec((length, PAIR), lambda p: (0, p)),
            pl.BlockSpec((length, PAIR), lambda p: (0, group * pairs + p)),
            pl.BlockSpec((length, PAIR), lambda p: (0, pairs + p)),
            pl.BlockSpec((length, PAIR), lambda p: (0, 2 * pairs + p)),
        ],
        out_specs=pl.BlockSpec(heads.shape, lambda p: (0, 0)),
        out_shape=jax.ShapeDtypeStruct(heads.shape, jnp.bfloat16),
        scratch_shapes=[pltpu.VMEM((length, PAIR), jnp.float32)] * 2,
        compiler_params=pltpu.CompilerParams(vmem_limit_bytes=vmem_bytes),
        cost_estimate=cost(32 * length * length * pairs * PAIR, 8 * heads.size),
    )(first_row, heads, head_grad, heads, heads)


gelu_scale = 0.7978845608028654
gelu_cubic = 0.044715


def ffn_kernel(index_ref, *refs):
    normed, grads, pieces = refs[:2], refs[2:4], [r.at[0] for r in refs[4:6]]
    bias_ref, rows_ref, sum_ref, grad_out, down_out, grad_acc, down_acc = refs[6:]
    step = pl.program_id(0)
    width = normed[0].shape[1]
    quarter = pieces[0].shape[1] // 2
    ups, downs = slice(0, quarter), slice(quarter, 2 * quarter)
    pre = mm(normed[0][...], pieces[0][:, ups], 1, 0) + mm(normed[1][...], pieces[1][:, ups], 1, 0)
    pre = pre + bias_ref[0]
    act_grad = mm(grads[0][...], pieces[0][:, downs], 1, 0) + mm(grads[1][...], pieces[1][:, downs], 1, 0)
    square = pre * pre
    bent = jnp.tanh(gelu_scale * pre * (1.0 + gelu_cubic * square))
    half = 0.5 * (1.0 + bent)
    slope = half + 0.5 * gelu_scale * pre * (1.0 - bent * bent) * (1.0 + 3.0 * gelu_cubic * square)
    act = (pre * half).astype(jnp.bfloat16)
    pre_grad = (act_grad * slope).astype(jnp.bfloat16)
    rows_ref[:, :quarter] = act
    rows_ref[:, quarter:] = pre_grad
    sum_ref[0] = jnp.sum(pre_grad.astype(jnp.float32), axis=0, keepdims=True)

    @pl.when(step == 0)
    def _():
        for i in range(2):
            at = slice(i * width, (i + 1) * width)
            grad_acc[:, at] = mm(pre_grad, pieces[i][:, ups], 1, 1)
            down_acc[:, at] = mm(act, pieces[i][:, downs], 1, 1)

    @pl.when(step > 0)
    def _():
        for i in range(2):
            at = slice(i * width, (i + 1) * width)
            grad_acc[:, at] += mm(pre_grad, pieces[i][:, ups], 1, 1)
            down_acc[:, at] += mm(act, pieces[i][:, downs], 1, 1)

    @pl.when(step == pl.num_programs(0) - 1)
    def _():
        grad_out[...] = grad_acc[...].astype(jnp.bfloat16)
        down_out[...] = down_acc[...].astype(jnp.bfloat16)


def ffn_rows_of(index, normed, grads, part, pieces, bias):
    tokens, features = normed.shape
    width = features // 2
    columns = pieces.shape[2]
    ring, quarter = pieces.shape[0] // 2, columns // 2

    def halves(at):
        return [pl.BlockSpec((tokens, width), lambda k, s, h=h: (at, h)) for h in range(2)]

    piece = [
        pl.BlockSpec((1, width, columns), lambda k, s, h=h: ((s[0] ^ h) * ring + k, 0, 0))
        for h in range(2)
    ]
    whole = pl.BlockSpec((tokens, features), lambda k, s: (0, 0))
    vector = pl.BlockSpec((1, 1, quarter), lambda k, s: (k, 0, 0))
    return pl.pallas_call(
        ffn_kernel,
        grid_spec=pltpu.PrefetchScalarGridSpec(
            num_scalar_prefetch=1,
            grid=(ring,),
            in_specs=halves(0) + halves(part) + piece + [vector],
            out_specs=[pl.BlockSpec((tokens, columns), lambda k, s: (0, k)), vector, whole, whole],
            scratch_shapes=[pltpu.VMEM((tokens, features), jnp.float32)] * 2,
        ),
        out_shape=[
            shape((tokens, ring * columns)),
            shape((ring, 1, quarter), jnp.float32),
            shape((tokens, features)),
            shape((tokens, features)),
        ],
        compiler_params=params(),
        cost_estimate=cost(8 * tokens * features * ring * quarter, 12 * ring * width * columns),
    )(index, normed, normed, grads, grads, pieces, pieces, bias)


def weight_products_kernel(count, *refs):
    out_ref = refs[-1]
    normed, grads, rows = [refs[i * count : (i + 1) * count] for i in range(3)]
    quarter = rows[0].shape[1] // 2
    up = down = None
    for j in range(count):
        up_part = mm(normed[j][...], rows[j][:, quarter:], 0, 0)
        down_part = mm(grads[j][...], rows[j][:, :quarter], 0, 0)
        up = up_part if up is None else up + up_part
        down = down_part if down is None else down + down_part
    out_ref[0, :, :quarter] = up.astype(jnp.bfloat16)
    out_ref[0, :, quarter:] = down.astype(jnp.bfloat16)


def weight_products(normed, grads, rows, half):
    count = len(normed)
    tokens, features = normed[0].shape
    width = features // 2
    ring = 4
    columns = rows[0].shape[1] // ring
    size = min(512, width)
    blocks = width // size
    left = [pl.BlockSpec((tokens, size), lambda k, d: (0, half * blocks + d))] * count
    left += [
        pl.BlockSpec((tokens, size), lambda k, d, j=j: (j, half * blocks + d)) for j in range(count)
    ]
    return pl.pallas_call(
        functools.partial(weight_products_kernel, count),
        grid=(ring, blocks),
        in_specs=left + [pl.BlockSpec((tokens, columns), lambda k, d: (0, k))] * count,
        out_specs=pl.BlockSpec((1, size, columns), lambda k, d: (k, d, 0)),
        out_shape=shape((ring, width, columns)),
        compiler_params=params(),
        cost_estimate=cost(
            2 * count * tokens * width * ring * columns, 4 * count * tokens * features * ring
        ),
    )(*normed, *([grads] * count), *rows)


def params(**more):
    return pltpu.CompilerParams(vmem_limit_bytes=vmem_bytes, **more)


def cost(flops, nbytes):
    return pl.CostEstimate(flops=flops // 10, bytes_accessed=nbytes // 10, transcendentals=0)


def shape(dims, dtype=jnp.bfloat16):
    return jax.ShapeDtypeStruct(dims, dtype)


def turned(values):
    return values.astype(jnp.float32).T.astype(jnp.bfloat16)


def pack_heads_kernel(index_ref, *refs):
    sources, outs = refs[:8], refs[8:]
    own = sources[0].shape[1]
    for which in range(2):
        for i in range(4):
            part = sources[4 * which + i][...]
            outs[which][:, i * own : (i + 1) * own] = part if i < 3 else turned(part)


def pack_heads(index, weights, count):
    width, units = weights[0].shape
    own, block = units // 2, width // 4

    def feature(which):
        return pl.BlockSpec((block, own), lambda j, s: (s[1] ^ j, s[0] ^ which))

    def turned_block(which):
        return pl.BlockSpec((own, block), lambda j, s: (s[0] ^ which, s[1] ^ j))

    in_specs = []
    for which in range(2):
        in_specs += [feature(which)] * 3 + [turned_block(which)]
    return pl.pallas_call(
        pack_heads_kernel,
        grid_spec=pltpu.PrefetchScalarGridSpec(
            num_scalar_prefetch=1,
            grid=(count,),
            in_specs=in_specs,
            out_specs=[pl.BlockSpec((block, 4 * own), lambda j, s: (j, 0))] * 2,
        ),
        out_shape=[shape((count * block, 4 * own))] * 2,
        compiler_params=params(),
        cost_estimate=cost(0, 32 * count * block * own),
    )(index, *weights, *weights)


def pack_ff_kernel(index_ref, up_ref, down_ref, out_ref):
    quarter = up_ref.shape[1]
    out_ref[:, :quarter] = up_ref[...]
    out_ref[:, quarter:] = turned(down_ref[...])


def pack_ff(index, up_weight, down_weight):
    width, units = up_weight.shape
    quarter, block = units // 4, width // 4
    return pl.pallas_call(
        pack_ff_kernel,
        grid_spec=pltpu.PrefetchScalarGridSpec(
            num_scalar_prefetch=1,
            grid=(4,),
            in_specs=[
                pl.BlockSpec((block, quarter), lambda d, s: (d, s[1])),
                pl.BlockSpec((quarter, block), lambda d, s: (s[1], d)),
            ],
            out_specs=pl.BlockSpec((block, 2 * quarter), lambda d, s: (d, 0)),
        ),
        out_shape=shape((width, 2 * quarter)),
        compiler_params=params(),
        cost_estimate=cost(0, 8 * width * quarter),
    )(index, up_weight, down_weight)


def stack_kernel(*refs):
    pieces, outs = refs[:3], refs[-2:]
    block = pieces[0].shape[0] // 2
    for j, piece in enumerate(pieces):
        for i in range(2):
            outs[i][j * block : (j + 1) * block, :] = piece[i * block : (i + 1) * block, :]
    for i in range(2):
        outs[i][3 * block :, :] = refs[3 + i][...]


def stack_pieces(pieces):
    rows, columns = pieces[0].shape
    return pl.pallas_call(
        stack_kernel,
        out_shape=[shape((2 * rows, columns))] * 2,
        compiler_params=params(),
        cost_estimate=cost(0, 16 * rows * columns),
    )(*pieces)


def norm_kernel(index_ref, own_ref, sib_ref, vectors_ref, out_ref, stats_ref):
    own = own_ref[...].astype(jnp.float32)
    sib = sib_ref[...].astype(jnp.float32)
    width = own.shape[1]
    average = (jnp.sum(own, axis=1, keepdims=True) + jnp.sum(sib, axis=1, keepdims=True)) / (2 * width)
    own, sib = own - average, sib - average
    square = jnp.sum(own * own, axis=1, keepdims=True) + jnp.sum(sib * sib, axis=1, keepdims=True)
    inverse = lax.rsqrt(square / (2 * width) + norm_eps)
    block = width // 4
    for half, values in enumerate((own, sib)):
        gain, shift = vectors_ref[2 * half, :][None], vectors_ref[2 * half + 1, :][None]
        rounded = (values * inverse * gain + shift).astype(jnp.bfloat16)
        for i in range(4):
            at = pl.multiple_of(half * width + (index_ref[1] ^ i) * block, block)
            out_ref[:, pl.ds(at, block)] = rounded[:, i * block : (i + 1) * block]
    lane = lax.broadcasted_iota(jnp.int32, stats_ref.shape, 1)
    stats_ref[...] = jnp.where(lane == 0, average, inverse)


def norm_rows(index, own, sib, vectors):
    tokens, width = own.shape
    size = min(256, tokens)
    rows = pl.BlockSpec((size, width), lambda i, s: (i, 0))
    return pl.pallas_call(
        norm_kernel,
        grid_spec=pltpu.PrefetchScalarGridSpec(
            num_scalar_prefetch=1,
            grid=(tokens // size,),
            in_specs=[rows, rows, pl.BlockSpec((4, width), lambda i, s: (0, 0))],
            out_specs=[
                pl.BlockSpec((size, 2 * width), lambda i, s: (i, 0)),
                pl.BlockSpec((size, 128), lambda i, s: (i, 0)),
            ],
        ),
        out_shape=[shape((tokens, 2 * width)), shape((tokens, 128), jnp.float32)],
        compiler_params=params(),
        cost_estimate=cost(0, 8 * tokens * width),
    )(index, own, sib, vectors)


def project_kernel(own_ref, sib_ref, own_weight, sib_weight, bias_ref, out_ref):
    total = mm(own_ref[...], own_weight[...], 1, 0) + mm(sib_ref[...], sib_weight[...], 1, 0)
    out_ref[...] = (total + bias_ref[...]).astype(jnp.bfloat16)


def halves_of(size, width):
    return [pl.BlockSpec((size, width), lambda i, h=h: (i, h)) for h in range(2)]


def project(normed, own_weight, sib_weight, bias):
    tokens, features = normed.shape
    width, units = features // 2, bias.shape[1]
    size = min(256, tokens)
    weight = pl.BlockSpec((width, units), lambda i: (0, 0))
    return pl.pallas_call(
        project_kernel,
        grid=(tokens // size,),
        in_specs=halves_of(size, width)
        + [weight, weight, pl.BlockSpec((1, units), lambda i: (0, 0))],
        out_specs=pl.BlockSpec((size, units), lambda i: (i, 0)),
        out_shape=shape((tokens, units)),
        compiler_params=params(),
        cost_estimate=cost(4 * tokens * width * units, 4 * tokens * width + 4 * width * units),
    )(normed, normed, own_weight, sib_weight, bias)


def sum_rows_kernel(count, *refs):
    out_ref = refs[-1]
    width = refs[count].shape[0]
    for half in range(2):
        at = slice(half * width, (half + 1) * width)
        total = refs[3 * count][:, at] if len(refs) > 3 * count + 1 else None
        for k in range(count):
            part = mm(refs[k][...], refs[(1 + half) * count + k][...], 1, 1)
            total = part if total is None else total + part
        out_ref[:, at] = total


def sum_rows(rows, own_weights, sib_weights, at, before=()):
    count = len(rows)
    tokens, units = rows[0].shape
    width = own_weights[0].shape[0]
    size = min(512, tokens)
    full = pl.BlockSpec((size, 2 * width), lambda i: (i, 0))
    return pl.pallas_call(
        functools.partial(sum_rows_kernel, count),
        grid=(tokens // size,),
        in_specs=[pl.BlockSpec((size, units), lambda i: (i, 0))] * count
        + [pl.BlockSpec((width, units), lambda i: (0, at))] * (2 * count)
        + [full] * len(before),
        out_specs=full,
        out_shape=shape((tokens, 2 * width), jnp.float32),
        compiler_params=params(),
        cost_estimate=cost(4 * count * tokens * units * width, 8 * tokens * width),
    )(*rows, *own_weights, *sib_weights, *before)


def head_grads_kernel(own_ref, sib_ref, *refs):
    out_ref = refs[-1]
    count = (len(refs) - 1) // 2
    own = refs[0].shape[1]
    for k in range(count):
        total = mm(own_ref[...], refs[k][...], 1, 0) + mm(sib_ref[...], refs[count + k][...], 1, 0)
        out_ref[:, k * own : (k + 1) * own] = total.astype(jnp.bfloat16)


def head_grads(grads, own_weights, sib_weights):
    tokens, width = grads.shape[0], grads.shape[1] // 2
    count = len(own_weights)
    units = own_weights[0].shape[1] // 4
    size = min(256, tokens)
    return pl.pallas_call(
        head_grads_kernel,
        grid=(tokens // size,),
        in_specs=halves_of(size, width) + [pl.BlockSpec((width, units), lambda i: (0, 3))] * (2 * count),
        out_specs=pl.BlockSpec((size, count * units), lambda i: (i, 0)),
        out_shape=shape((tokens, count * units)),
        compiler_params=params(),
        cost_estimate=cost(4 * count * tokens * width * units, 8 * tokens * width),
    )(grads, grads, *own_weights, *sib_weights)


def head_products_kernel(*refs):
    normed, grads = refs[:2], refs[2:4]
    heads_ref, attended_ref = refs[4:6]
    outs, sum_ref = refs[6:8], refs[8]
    split = heads_ref.shape[1]
    for i in range(2):
        outs[i][:, :split] = mm(normed[i][...], heads_ref[...], 0, 0).astype(jnp.bfloat16)
        outs[i][:, split:] = mm(grads[i][...], attended_ref[...], 0, 0).astype(jnp.bfloat16)

    @pl.when(pl.program_id(0) == 0)
    def _():
        sum_ref[...] = jnp.sum(heads_ref[...].astype(jnp.float32), axis=0, keepdims=True)


def head_products(normed, grads, head_grad, attended):
    tokens, width = normed.shape[0], normed.shape[1] // 2
    split, own = head_grad.shape[1], attended.shape[1]
    size = min(512, width)
    blocks = width // size
    left = [pl.BlockSpec((tokens, size), lambda d, h=h: (0, h * blocks + d)) for h in range(2)]
    out = pl.BlockSpec((size, split + own), lambda d: (d, 0))
    return pl.pallas_call(
        head_products_kernel,
        grid=(width // size,),
        in_specs=left * 2
        + [pl.BlockSpec((tokens, split), lambda d: (0, 0)), pl.BlockSpec((tokens, own), lambda d: (0, 0))],
        out_specs=[out, out, pl.BlockSpec((1, split), lambda d: (0, 0))],
        out_shape=[shape((width, split + own))] * 2 + [shape((1, split), jnp.float32)],
        compiler_params=params(),
        cost_estimate=cost(4 * tokens * width * (split + own), 12 * tokens * width),
    )(normed, normed, grads, grads, head_grad, attended)


def block_at(half, width, place):
    block = width // 4
    return pl.ds(pl.multiple_of(half * width + place * block, block), block)


def norm_two_kernel(
    index_ref, rows_ref, came_ref, own_ref, sib_ref, vectors_ref, hidden_ref, normed_ref, stats_ref
):
    width = own_ref.shape[1]
    block = width // 4
    for half, tokens_ref in enumerate((own_ref, sib_ref)):
        for i in range(4):
            at = block_at(half, width, index_ref[1] ^ i)
            span = slice(half * width + i * block, half * width + (i + 1) * block)
            hidden_ref[:, span] = (
                tokens_ref[:, i * block : (i + 1) * block].astype(jnp.float32)
                + rows_ref[:, at]
                + came_ref[:, at].astype(jnp.float32)
                + vectors_ref[4:5, span]
            )
    hidden = hidden_ref[...]
    average = jnp.mean(hidden, axis=1, keepdims=True)
    centered = hidden - average
    inverse = lax.rsqrt(jnp.mean(centered * centered, axis=1, keepdims=True) + norm_eps)
    normed_ref[...] = (centered * inverse * vectors_ref[2:3, :] + vectors_ref[3:4, :]).astype(jnp.bfloat16)
    lane = lax.broadcasted_iota(jnp.int32, stats_ref.shape, 1)
    stats_ref[...] = jnp.where(lane == 0, average, inverse)


def my_rows(size, columns, blocks):
    return pl.BlockSpec((size, columns), lambda i, s: (s[0] * blocks + i, 0))


def norm_two(index, rows, came, own, sib, vectors):
    tokens, features = came.shape
    size = tokens // 2
    mine = my_rows(size, features // 2, 2)
    plain = pl.BlockSpec((size, features), lambda i, s: (i, 0))
    return pl.pallas_call(
        norm_two_kernel,
        grid_spec=pltpu.PrefetchScalarGridSpec(
            num_scalar_prefetch=1,
            grid=(2,),
            in_specs=[
                my_rows(size, features, 2),
                plain,
                mine,
                mine,
                pl.BlockSpec(vectors.shape, lambda i, s: (0, 0)),
            ],
            out_specs=[plain, plain, pl.BlockSpec((size, 128), lambda i, s: (i, 0))],
        ),
        out_shape=[
            shape((tokens, features), jnp.float32),
            shape((tokens, features)),
            shape((tokens, 128), jnp.float32),
        ],
        compiler_params=params(),
        cost_estimate=cost(0, 16 * tokens * features),
    )(index, rows, came, own, sib, vectors)


def norm_pull(grads, normal, inverse, gain):
    scaled = grads * gain
    return inverse * (
        scaled
        - jnp.mean(scaled, axis=1, keepdims=True)
        - normal * jnp.mean(scaled * normal, axis=1, keepdims=True)
    )


def add_sums(sums_ref, parts):
    rows = [jnp.sum(p, axis=0, keepdims=True) for p in parts]
    rows += [jnp.zeros_like(rows[0])] * (8 - len(rows))
    total = jnp.concatenate(rows, axis=0)

    @pl.when(pl.program_id(0) == 0)
    def _():
        sums_ref[...] = total

    @pl.when(pl.program_id(0) > 0)
    def _():
        sums_ref[...] += total


def norm_two_back_kernel(index_ref, *refs):
    here, x_top, y_top, x_bottom, y_bottom, hidden_ref, stats_ref, branch_ref, vectors_ref = refs[:9]
    grad_ref, blocks_ref, mirror_ref, sums_ref = refs[9:]
    f32 = jnp.float32
    top = pl.program_id(0) == 0
    from_x = jnp.where(top, x_top[...].astype(f32), x_bottom[...].astype(f32))
    from_y = jnp.where(top, y_top[...].astype(f32), y_bottom[...].astype(f32))
    grads = here[...].astype(f32) + from_x + from_y
    inverse = stats_ref[:, 1:2]
    normal = (hidden_ref[...] - stats_ref[:, :1]) * inverse
    branch = branch_ref[...].astype(f32)
    total = branch + norm_pull(grads, normal, inverse, vectors_ref[2:3, :])
    grad_ref[...] = total
    rounded = total.astype(jnp.bfloat16)
    width = rounded.shape[1] // 2
    block = width // 4
    for half in range(2):
        for i in range(4):
            part = rounded[:, half * width + i * block : half * width + (i + 1) * block]
            place = index_ref[1] ^ i
            blocks_ref[:, block_at(half, width, place)] = part
            mirror_ref[:, block_at(1 - half, width, place)] = part
    add_sums(sums_ref, (grads * normal, grads, rounded.astype(f32), branch))


def norm_two_back(index, parts, hidden, stats, branch, vectors):
    tokens, features = hidden.shape
    size = tokens // 2
    plain = pl.BlockSpec((size, features), lambda i, s: (i, 0))
    once = pl.BlockSpec((size, features), lambda i, s: (0, 0))
    return pl.pallas_call(
        norm_two_back_kernel,
        grid_spec=pltpu.PrefetchScalarGridSpec(
            num_scalar_prefetch=1,
            grid=(2,),
            in_specs=[plain]
            + [once] * 4
            + [
                plain,
                pl.BlockSpec((size, 128), lambda i, s: (i, 0)),
                plain,
                pl.BlockSpec(vectors.shape, lambda i, s: (0, 0)),
            ],
            out_specs=[plain] * 3 + [pl.BlockSpec((8, features), lambda i, s: (0, 0))],
        ),
        out_shape=[
            shape((tokens, features), jnp.float32),
            shape((tokens, features)),
            shape((tokens, features)),
            shape((8, features), jnp.float32),
        ],
        compiler_params=params(),
        cost_estimate=cost(0, 24 * tokens * features),
    )(index, *parts, hidden, stats, branch, vectors)


def norm_one_back_kernel(index_ref, *refs):
    rows_ref, came_ref, own_ref, sib_ref, stats_ref, out_own, out_sib, keep_ref, hidden_ref = refs[:9]
    vectors_ref, own_grad, sib_grad, sums_ref, grads_ref = refs[9:]
    f32 = jnp.float32
    width = own_ref.shape[1]
    block = width // 4
    for half in range(2):
        for i in range(4):
            at = block_at(half, width, index_ref[1] ^ i)
            span = slice(half * width + i * block, half * width + (i + 1) * block)
            grads_ref[:, span] = rows_ref[:, at] + came_ref[:, at].astype(f32)
    grads = grads_ref[...]
    inverse = stats_ref[:, 1:2]
    tokens = jnp.concatenate([own_ref[...], sib_ref[...]], axis=1).astype(f32)
    normal = (tokens - stats_ref[:, :1]) * inverse
    total = hidden_ref[...] + norm_pull(grads, normal, inverse, vectors_ref[0:1, :])
    dropped = 1.0 - keep_ref[...]
    own_grad[...] = out_own[...].astype(f32) * dropped + total[:, :width]
    sib_grad[...] = out_sib[...].astype(f32) * dropped + total[:, width:]
    add_sums(sums_ref, (grads * normal, grads))


def norm_one_back(index, rows, came, own, sib, stats, out_own, out_sib, keep, hidden, vectors):
    tokens, features = came.shape
    size, width = tokens // 2, features // 2
    plain = pl.BlockSpec((size, features), lambda i, s: (i, 0))
    half_wide = pl.BlockSpec((size, width), lambda i, s: (i, 0))
    return pl.pallas_call(
        norm_one_back_kernel,
        grid_spec=pltpu.PrefetchScalarGridSpec(
            num_scalar_prefetch=1,
            grid=(2,),
            in_specs=[
                my_rows(size, features, 2),
                plain,
                my_rows(size, width, 2),
                my_rows(size, width, 2),
                my_rows(size, 128, 2),
                my_rows(size, width, 2),
                half_wide,
                pl.BlockSpec((size, 1), lambda i, s: (i, 0)),
                plain,
                pl.BlockSpec(vectors.shape, lambda i, s: (0, 0)),
            ],
            out_specs=[half_wide, half_wide, pl.BlockSpec((8, features), lambda i, s: (0, 0))],
            scratch_shapes=[pltpu.VMEM((size, features), jnp.float32)],
        ),
        out_shape=[shape((tokens, width), jnp.float32)] * 2 + [shape((8, features), jnp.float32)],
        compiler_params=params(),
        cost_estimate=cost(0, 24 * tokens * features),
    )(index, rows, came, own, sib, stats, out_own, out_sib, keep, hidden, vectors)


def select_piece(refs, step, use):
    for j in range(3):

        @pl.when(step == j)
        def _():
            use(refs[j][...])

    @pl.when(step == 3)
    def _():
        use(jnp.concatenate([refs[3][...], refs[4][...]], axis=0))


def place_heads_kernel(index_ref, *refs):
    pieces, outs = refs[:5], refs[5:]
    own = pieces[0].shape[1] // 8

    def use(piece):
        for which in range(2):
            at = pl.multiple_of((index_ref[0] ^ which) * own, own)
            for m in range(4):
                part = piece[:, (4 * which + m) * own : (4 * which + m + 1) * own].astype(jnp.float32)
                if m < 3:
                    outs[m][:, pl.ds(at, own)] = part
                else:
                    outs[m][pl.ds(at, own), :] = part.T

    select_piece(pieces, pl.program_id(0), use)


def place_heads(index, pieces):
    block, columns = pieces[0].shape
    units, width = columns // 4, 4 * block
    whole = [pl.BlockSpec(p.shape, lambda j, s: (0, 0)) for p in pieces]
    return pl.pallas_call(
        place_heads_kernel,
        grid_spec=pltpu.PrefetchScalarGridSpec(
            num_scalar_prefetch=1,
            grid=(4,),
            in_specs=whole,
            out_specs=[pl.BlockSpec((block, units), lambda j, s: (s[1] ^ j, 0))] * 3
            + [pl.BlockSpec((units, block), lambda j, s: (0, s[1] ^ j))],
        ),
        out_shape=[shape((width, units), jnp.float32)] * 3 + [shape((units, width), jnp.float32)],
        compiler_params=params(),
        cost_estimate=cost(0, 24 * width * units),
    )(index, *pieces)


def place_ff_kernel(*refs):
    pieces, (up_out, down_out) = refs[:-2], refs[-2:]
    rows = pieces[0].shape[1]
    quarter = pieces[0].shape[2] // 2
    for part, piece in enumerate(pieces):
        span = slice(part * rows, (part + 1) * rows)
        up_out[span, :] = piece[0, :, :quarter].astype(jnp.float32)
        down_out[:, span] = piece[0, :, quarter:].astype(jnp.float32).T


def place_ff(pieces):
    count, rows, columns = pieces[0].shape
    width, quarter = rows * len(pieces), columns // 2
    return pl.pallas_call(
        place_ff_kernel,
        grid=(count,),
        in_specs=[pl.BlockSpec((1, rows, columns), lambda j: (j, 0, 0))] * len(pieces),
        out_specs=[
            pl.BlockSpec((width, quarter), lambda j: (0, j)),
            pl.BlockSpec((quarter, width), lambda j: (j, 0)),
        ],
        out_shape=[
            shape((width, count * quarter), jnp.float32),
            shape((count * quarter, width), jnp.float32),
        ],
        compiler_params=params(),
        cost_estimate=cost(0, 48 * width * quarter),
    )(*pieces)


def join_kernel(index_ref, mine_ref, first_ref, second_ref, out_ref):
    step = pl.program_id(0)

    @pl.when(step < 2)
    def _():
        out_ref[...] = mine_ref[...]

    @pl.when(step == 2)
    def _():
        out_ref[...] = first_ref[...]

    @pl.when(step == 3)
    def _():
        out_ref[...] = second_ref[...]


def join_tokens(index, mine, first, second):
    tokens, width = mine.shape
    size = tokens // 2
    once = pl.BlockSpec((size, width), lambda i, s: (0, 0))
    return pl.pallas_call(
        join_kernel,
        grid_spec=pltpu.PrefetchScalarGridSpec(
            num_scalar_prefetch=1,
            grid=(4,),
            in_specs=[pl.BlockSpec((size, width), lambda i, s: (jnp.minimum(i, 1), 0)), once, once],
            out_specs=pl.BlockSpec(
                (size, width), lambda i, s: (jnp.where(i < 2, s[0] * 2 + i, (1 - s[0]) * 2 + i - 2), 0)
            ),
        ),
        out_shape=shape((2 * tokens, width), mine.dtype),
        compiler_params=params(),
        cost_estimate=cost(0, 8 * tokens * width),
    )(index, mine, first, second)


def layer_out_kernel(*refs):
    here, x_top, y_top, x_bottom, y_bottom, hidden_ref, own_ref, sib_ref, keep_ref, vectors_ref = refs[1:11]
    own_out, sib_out = refs[11:]
    f32 = jnp.float32
    width = own_ref.shape[1]
    top = pl.program_id(0) == 0
    from_x = jnp.where(top, x_top[...].astype(f32), x_bottom[...].astype(f32))
    from_y = jnp.where(top, y_top[...].astype(f32), y_bottom[...].astype(f32))
    total = hidden_ref[...] + here[...].astype(f32) + from_x + from_y + vectors_ref[5:6, :]
    keep = keep_ref[...] > 0.5
    own_out[...] = jnp.where(keep, total[:, :width], own_ref[...].astype(f32))
    sib_out[...] = jnp.where(keep, total[:, width:], sib_ref[...].astype(f32))


def layer_rows(index, parts, hidden, own, sib, keep, vectors):
    tokens, features = hidden.shape
    size, width = tokens // 2, features // 2
    plain = pl.BlockSpec((size, features), lambda i, s: (i, 0))
    half_wide = pl.BlockSpec((size, width), lambda i, s: (i, 0))
    return pl.pallas_call(
        layer_out_kernel,
        grid_spec=pltpu.PrefetchScalarGridSpec(
            num_scalar_prefetch=1,
            grid=(2,),
            in_specs=[plain]
            + [pl.BlockSpec((size, features), lambda i, s: (0, 0))] * 4
            + [
                plain,
                my_rows(size, width, 2),
                my_rows(size, width, 2),
                pl.BlockSpec((size, 1), lambda i, s: (i, 0)),
                pl.BlockSpec(vectors.shape, lambda i, s: (0, 0)),
            ],
            out_specs=[half_wide, half_wide],
        ),
        out_shape=[shape((tokens, width), jnp.float32)] * 2,
        compiler_params=params(),
        cost_estimate=cost(0, 20 * tokens * features),
    )(index, *parts, hidden, own, sib, keep, vectors)


def body_local(
    tokens_in,
    out_grad,
    segment_ids,
    active_lengths,
    norm1_gain,
    norm1_shift,
    query_weight,
    query_bias,
    key_weight,
    value_weight,
    value_bias,
    out_weight,
    out_bias,
    norm2_gain,
    norm2_shift,
    up_weight,
    up_bias,
    down_weight,
    down_bias,
):
    f32, bf16 = jnp.float32, jnp.bfloat16
    rows, width = tokens_in.shape
    ring = lax.axis_size("col")
    row_i = lax.axis_index("row")
    plane_i = lax.axis_index("dp")
    col_i = lax.axis_index("col")
    own = query_weight.shape[1] // 2
    block = width // 4
    quarter = up_weight.shape[1] // 4
    unit = quarter // 2
    half = rows // 2
    order = Order()
    plane, column = Plane(order), Link(order)
    index = jnp.stack([row_i, plane_i, col_i]).astype(jnp.int32)

    def cut(values, start, size):
        return lax.dynamic_slice_in_dim(values, start, size, axis=0)

    def mirrored(values):
        return jnp.concatenate([values[:, width:], values[:, :width]], axis=1)

    def my_tokens(values):
        return cut(values, row_i * half, half)

    def other_tokens(values):
        return cut(values, (1 - row_i) * half, half)

    tokens_sib = order.swap(tokens_in)
    out_grad_sib = swap(other_tokens(out_grad))

    mine = jnp.concatenate(
        [
            cut(query_bias, row_i * own, own),
            jnp.zeros((own,), f32),
            cut(value_bias, row_i * own, own),
            cut(up_bias, plane_i * quarter, quarter),
        ]
    )
    small = [mine] + [
        lax.ppermute(mine, "col", [(i, (i + k) % ring) for i in range(ring)]) for k in range(1, ring)
    ]

    sources = (query_weight, key_weight, value_weight, out_weight)
    piece = order.run(pack_heads, after(index, mine), sources, 1)
    pieces = [jnp.concatenate([piece[0], swap(piece[1])], axis=0)]
    column.last = small[1:]
    pieces.append(column.send(step_up, pieces[0]))

    active_all = active_rows(segment_ids, active_lengths)
    active_here = my_tokens(cut(active_all, col_i * rows, rows))
    keep_mask = active_here.astype(f32)[:, None]
    out_grads = jnp.concatenate([my_tokens(out_grad), out_grad_sib], axis=1).astype(f32)
    branch_mine = (after(out_grads, *order.tokens) * keep_mask).astype(bf16)
    branch_first = plane.both(branch_mine[: half // 2], branch_mine[: half // 2])
    ff_piece = order.run(pack_ff, index, up_weight, down_weight)
    ff_pieces = lax.all_gather(ff_piece, ("row", "col"))
    vectors = jnp.stack([norm1_gain, norm1_shift, norm2_gain, norm2_shift, out_bias, down_bias])
    vectors_sib = swap(vectors)
    vectors_all = jnp.concatenate([vectors, vectors_sib], axis=1)
    pieces.append(column.send(step_up, pieces[1]))
    near = plane.both(pieces[1], pieces[1])
    here = order.run(pack_heads, index, sources, 4)
    own_parts, other_rows = [here[0]], [order.swap(here[1])]
    normed_one, stats_one = order.run(
        norm_rows,
        index,
        tokens_in,
        tokens_sib,
        jnp.concatenate([vectors[:2], vectors_sib[:2]], axis=0),
    )

    segment_row = picked(segment_ids, col_i)
    member = (segment_row[:, None] == jnp.arange(active_lengths.shape[1])).astype(jnp.int32)
    counts = jnp.sum(member, axis=0)
    first_row = jnp.sum(member * (jnp.cumsum(counts) - counts), axis=1)[None, :]

    heads, attended = [], []

    def attend_project(k):
        heads.append(
            order.run(project, normed_one, own_parts[k], other_rows[k], small[k][None, : 3 * own])
        )

    def attend(k):
        attended.append(order.run(local_forward, heads[k], first_row))

    def stack(k, near, far):
        own_part, other_part = order.run(stack_pieces, [pieces[k], *near, *far])
        own_parts.append(own_part)
        other_rows.append(other_part)

    attend_project(0)
    attend(0)
    far = plane.far(*near)
    pieces.append(column.send(step_up, pieces[2]))
    last_near, last_far = near, far
    near = plane.both(pieces[2], pieces[2])
    stack(1, last_near, last_far)
    attend_project(1)
    attend(1)
    far = plane.far(*near)
    last_near, last_far = near, far
    near = plane.both(pieces[3], pieces[3])
    stack(2, last_near, last_far)
    attend_project(2)
    attend(2)
    far = plane.far(*near)
    last_near, last_far = near, far
    branch_far = plane.far(*branch_first)
    stack(3, last_near, last_far)
    before = order.run(sum_rows, attended[:3], own_parts[:3], other_rows[:3], 3)
    second_near = plane.both(branch_mine[half // 2 :], branch_mine[half // 2 :])
    attend_project(3)
    attend(3)
    second_far = plane.far(*second_near)
    attention_rows = order.run(sum_rows, attended[3:], own_parts[3:], other_rows[3:], 3, (before,))
    arrived = swap(order.tie(mirrored(other_tokens(attention_rows)).astype(bf16)))

    order.tokens.append(ff_pieces)
    hidden_one, normed_two, stats_two = order.run(
        norm_two, index, attention_rows, arrived, tokens_in, tokens_sib, vectors_all
    )

    normed = [normed_two, *plane.both(normed_two, normed_two)]
    branch_all = jnp.concatenate(
        [branch_mine]
        + [part for pair in zip(branch_first, second_near) for part in pair]
        + [*branch_far, *second_far],
        axis=0,
    )
    def by_column(relative):
        places = jnp.mod(col_i - jnp.arange(ring), ring)
        return jnp.take(relative, places, axis=0)

    ff_biases = by_column(jnp.stack([s[None, 3 * own :] for s in small]))
    ff_rows, up_sums, grad_parts, down_parts = [], [], [], []

    def feed_forward(j):
        grads, part = (branch_all, j) if j > 0 else (branch_mine, 0)
        results = order.run(ffn_rows_of, index, normed[j], grads, part, ff_pieces, ff_biases)
        for kept, result in zip((ff_rows, up_sums, grad_parts, down_parts), results):
            kept.append(result)

    def top(values):
        return values[: half // 2]

    def bottom(values):
        return values[half // 2 :]

    def second_steps(parts, via_x, via_y):
        via_x, via_y = after((via_x, via_y), *order.tokens)
        return plane.both(add_rounded(bottom(parts[1]), via_y), add_rounded(top(parts[2]), via_x))

    def weight_grads(part):
        return order.run(weight_products, normed, branch_all, ff_rows, part)

    feed_forward(0)
    normed_far = plane.far(normed[1], normed[2])
    feed_forward(1)
    x_top = plane.x.send(step_x, top(grad_parts[1]))
    feed_forward(2)
    y_bottom = plane.y.send(step_y, bottom(grad_parts[2]))
    normed.append(jnp.concatenate(normed_far, axis=0))
    feed_forward(3)
    via_x, via_y = plane.both(top(grad_parts[3]), bottom(grad_parts[3]))
    ff_mine = weight_grads(0)
    x_bottom, y_top = second_steps(grad_parts, via_x, via_y)
    ff_other = order.swap(weight_grads(1))

    hidden_grad, grad_mine, grad_mirror, sums_two = order.run(
        norm_two_back,
        index,
        (grad_parts[0], x_top, y_top, x_bottom, y_bottom),
        hidden_one,
        stats_two,
        branch_mine,
        vectors_all,
    )
    down_x_top, down_y_bottom = plane.both(top(down_parts[1]), bottom(down_parts[2]))
    grad_others = [order.swap(top(grad_mirror)), order.swap(bottom(grad_mirror))]
    grad_rows = order.run(join_tokens, index, grad_mine, *grad_others)

    ff_grads = []
    for part in range(2):
        span = slice(part * width // 2, (part + 1) * width // 2)
        total = order.tie(add_rounded(ff_mine[:, span], ff_other[:, span]))
        total = lax.psum_scatter(total, "col", scatter_dimension=0, tiled=False)
        ff_grads.append(lax.all_gather(total, "dp"))

    down_via_x, down_via_y = plane.both(top(down_parts[3]), bottom(down_parts[3]), True)
    head_grad = order.run(head_grads, grad_rows, own_parts, other_rows)
    head_rows, bias_rows, group_parts = [None] * ring, [None] * ring, [None] * ring

    def backward(k):
        head_rows[k] = order.run(
            lambda h, g, f: local_backward(h, g, k, f), heads[k], head_grad, first_row
        )

    def head_weights(k):
        *group_parts[k], bias_rows[k] = order.run(
            head_products, normed_one, grad_rows, head_rows[k], attended[k]
        )

    def part_of(k, j, which):
        return group_parts[k][which][j * block : (j + 1) * block]

    def first_messages(k):
        return plane.both(part_of(k, 3, 0), part_of(k, 3, 1), True)

    def second_messages(k, via):
        via_x, via_y = after(via, *order.tokens)
        return plane.both(
            jnp.concatenate([part_of(k, 1, 0), add_rounded(part_of(k, 1, 1), via_y)], axis=1),
            jnp.concatenate([add_rounded(part_of(k, 2, 0), via_x), part_of(k, 2, 1)], axis=1),
            k == 0,
        )

    def group_total(k, came, total):
        came_x, came_y = after(came, *order.tokens)
        here = jnp.concatenate([part_of(k, 0, 0), part_of(k, 0, 1)], axis=1)
        here = here.astype(f32) + came_x.astype(f32) + came_y.astype(f32)
        if total is not None:
            here = here + total.astype(f32)
        return here.astype(bf16)

    def layer_out_rows():
        own_out, sib_out = order.run(
            layer_rows,
            index,
            (down_parts[0], down_x_top, down_y_top, down_x_bottom, down_y_bottom),
            hidden_one,
            tokens_in,
            tokens_sib,
            keep_mask,
            vectors_all,
        )
        return own_out, order.swap(top(sib_out)), order.swap(bottom(sib_out))

    vias, came = [None] * ring, [None] * ring
    backward(3)
    head_weights(3)
    down_x_bottom, down_y_top = second_steps(down_parts, down_via_x, down_via_y)
    vias[3] = first_messages(3)
    backward(2)
    head_weights(2)
    vias[2] = first_messages(2)
    came[3] = second_messages(3, vias[3])
    order.tokens += [down_x_bottom, down_y_top]
    backward(1)
    head_weights(1)
    vias[1] = first_messages(1)
    came[2] = second_messages(2, vias[2])
    backward(0)
    order.tokens += came[3]
    head_weights(0)
    vias[0] = first_messages(0)
    came[1] = second_messages(1, vias[1])
    total = column.send(step_down, group_total(3, came[3], None))
    order.tokens += came[2]
    back_rows = order.run(sum_rows, head_rows, own_parts, other_rows, 0)
    came[0] = second_messages(0, vias[0])
    arrived = order.swap(mirrored(other_tokens(back_rows)).astype(bf16))
    total = column.send(step_down, add_rounded(total, group_total(2, came[2], None)))
    layer_parts = layer_out_rows()

    input_mine, input_other, sums_one = order.run(
        norm_one_back,
        index,
        back_rows,
        arrived,
        tokens_in,
        tokens_sib,
        stats_one,
        out_grad,
        out_grad_sib,
        keep_mask,
        hidden_grad,
        vectors_all,
    )
    input_others = [order.swap(top(input_other)), order.swap(bottom(input_other))]
    total = column.send(step_down, add_rounded(total, group_total(1, came[1], None)))
    layer_out = order.run(join_tokens, index, *layer_parts)

    row_hot = (jnp.arange(2) == row_i).astype(f32)
    plane_hot = (jnp.arange(4) == plane_i).astype(f32)
    head_bias = by_column(jnp.stack(bias_rows)).reshape(ring, 3, 1, own) * row_hot[:, None]
    up_bias_part = sum(up_sums) * plane_hot[:, None]
    bias_vector = jnp.concatenate([head_bias.reshape(ring, -1), up_bias_part.reshape(ring, -1)], axis=1)
    feature_sums = jnp.concatenate([sums_one[:2], sums_two[:4]], axis=0)
    summed = jnp.concatenate([bias_vector.reshape(-1), feature_sums[:, :width].reshape(-1)])
    summed = summed + swap(
        jnp.concatenate([bias_vector.reshape(-1), feature_sums[:, width:].reshape(-1)])
    )

    summed = order.tie(summed)
    summed = summed + plane.x.send(step_x, summed)
    summed = summed + plane.y.send(step_y, summed)
    total = group_total(0, came[0], total)
    total = jnp.concatenate([total[:, : 4 * own], swap(total[:, 4 * own :])], axis=1)
    near = plane.both(total, total)
    step = 1
    while step < ring:
        pairs = [(i, i ^ step) for i in range(ring)]
        summed = summed + column.send(lambda v: lax.ppermute(v, "col", pairs), summed)
        step *= 2
    input_grad = order.run(join_tokens, index, input_mine, *input_others)
    far = plane.far(*near)
    up_weight_grad, down_weight_grad = order.run(place_ff, ff_grads)
    query_weight_grad, key_weight_grad, value_weight_grad, out_weight_grad = order.run(
        place_heads, index, [total, *near, *far]
    )

    bias_here = picked(summed[: bias_vector.size].reshape(ring, -1), col_i)
    own_here = summed[bias_vector.size :].reshape(6, width)
    size = 2 * own
    return (
        layer_out,
        input_grad,
        own_here[0],
        own_here[1],
        query_weight_grad,
        bias_here[:size],
        key_weight_grad,
        value_weight_grad,
        bias_here[2 * size : 3 * size],
        out_weight_grad,
        own_here[4],
        own_here[2],
        own_here[3],
        up_weight_grad,
        bias_here[3 * size :],
        down_weight_grad,
        own_here[5],
    )


def body(tokens_in, out_grad, segment_ids, *rest):
    ring = lax.axis_size("col")
    local = (
        lax.axis_size("dp") == 4
        and lax.axis_size("row") == 2
        and ring == 4
        and tokens_in.shape[0] == segment_ids.shape[1]
    )
    chosen = body_local if local else body_general
    return chosen(tokens_in, out_grad, segment_ids, *rest)


def solution(mesh):
    placed = (
        P(("dp", "col"), "row"),
        P(("dp", "col"), "row"),
        P("dp", None),
        P("dp", None),
        P("row"),
        P("row"),
        P("row", "col"),
        P("col"),
        P("row", "col"),
        P("row", "col"),
        P("col"),
        P("col", "row"),
        P("row"),
        P("row"),
        P("row"),
        P("row", "col"),
        P("col"),
        P("col", "row"),
        P("row"),
    )
    return jax.shard_map(
        body,
        mesh=mesh,
        in_specs=placed,
        out_specs=(
            P(("dp", "col"), "row"),
            P(("dp", "col"), "row"),
            P("row"),
            P("row"),
            P("row", "col"),
            P("col"),
            P("row", "col"),
            P("row", "col"),
            P("col"),
            P("col", "row"),
            P("row"),
            P("row"),
            P("row"),
            P("row", "col"),
            P("col"),
            P("col", "row"),
            P("row"),
        ),
        check_vma=False,
    )
```
